32 devices in a mesh: group: 2 (over y), shard: 16 (over z, x, core).
Axes of the slice: x: 2, y: 2, z: 4, core: 2. Of those that a mesh axis runs over, the one named last changes fastest.
Arguments:
- activations: bfloat16 [2, 128, 64, 1024], P('group', 'shard'), may hold values from -7 to 7
- out_grad: bfloat16 [2, 128, 64, 1024], P('group', None, 'shard'), may hold values from -1.5 to 1.5
- embedding: bfloat16 [512, 1024], replicated, may hold values from -6 to 6
- counts: int32 [2, 2], P('group'), may hold values from 0 to 64, as said below
- offsets: int32 [2, 2], P('group'), may hold values from 0 to 2, as said below
- layout: int32 [2, 64], P('group'), may hold values from 0 to 511
Outputs:
- input_grad: bfloat16 [2, 128, 64, 1024], P('group', 'shard')
- embedding_grad: float32 [512, 1024], P('group')
The draws below stay inside these ranges and needn't reach their ends.
Inputs may be any that keep to these rules, and one draw needn't show every extreme that they name: `counts`: A used session slot holds 19 to 256 electrodes; slots after the used ones hold 0. `offsets`: used session slots come first; the first starts at block 0 and each next one where the previous ends, a session taking ceil(count / 32) blocks, all sessions together exactly 2 blocks; unused slots hold 2.
All inputs are finite; a program needn't handle non-finite values.
Results may differ from the reference program's by a relative error of at most 0.012.
The reference program's roundings to bfloat16 on the way (of `embedded`, `weights`, `mixed`, `grad_scores` and `mixed_grad`) count: a program that leaves them out, or rounds other values in their place, can miss the bound.
Values may be sent and summed in bfloat16 or wider, within the bound.
No kernel may reach another device: no remote copies, remote signals or barrier semaphores. Data moves between devices by JAX's collectives and lax.ppermute only.
A program may use at most 64 MiB of HBM per device.

```python
import math
import jax
import jax.numpy as jnp
from jax import lax

D = 1024
HEADS = 16
TEMPLATES = 512
PATCHES = 128
BLOCK = 32
MIN_ELEC = 19
SESS_BLOCKS = 8
NE = 64
N_GROUP = 2


def session_table(key):
    key_cut = jax.random.fold_in(key, 11)
    key_short = jax.random.fold_in(key, 12)
    blocks = NE // BLOCK
    position = jnp.arange(blocks, dtype=jnp.int32)
    boundary = (position % SESS_BLOCKS == 0).astype(jnp.int32)
    starts = jax.random.randint(key_cut, (N_GROUP, blocks), 0, 2, dtype=jnp.int32)
    starts = jnp.maximum(starts, boundary[None, :])
    first_group = (jnp.arange(N_GROUP, dtype=jnp.int32) == 0)[:, None]
    starts = jnp.where(first_group, boundary[None, :], starts)
    owner_index = jnp.cumsum(starts, axis=1) - 1
    member = owner_index[:, :, None] == position[None, None, :]
    offsets = jnp.min(jnp.where(member, position[None, :, None], blocks), axis=1)
    span_blocks = jnp.sum(member.astype(jnp.int32), axis=1)
    shortfall = jax.random.randint(key_short, (N_GROUP, blocks), 0, BLOCK, dtype=jnp.int32)
    shortfall = jnp.where(first_group & (position[None, :] == 0), 0, shortfall)
    counts = jnp.maximum(span_blocks * BLOCK - shortfall, MIN_ELEC)
    counts = jnp.where(span_blocks > 0, counts, 0)
    return (counts.astype(jnp.int32), offsets.astype(jnp.int32))


def draw_counts(key, part):
    return session_table(key)[0]


def draw_offsets(key, part):
    return session_table(key)[1]


def draw_activations(key, part):
    key_value = jax.random.fold_in(key, 21)
    shape = (N_GROUP, PATCHES, NE, D)
    values = jnp.clip(jax.random.normal(key_value, shape, jnp.float32), -6.0, 6.0)
    return values.astype(jnp.bfloat16)


def with_ends(drawn, stream_key, low, high):
    extent = drawn.shape
    index_at = [jax.random.randint(jax.random.fold_in(stream_key, axis), (), 0, extent[axis]) for axis in range(len(extent))]
    drawn = drawn.at[tuple(index_at)].set(low)
    longest = extent.index(max(extent))
    index_at[longest] = (index_at[longest] + 1) % extent[longest]
    return drawn.at[tuple(index_at)].set(high)


def block_levels(rng, dims, pieces, least, largest):
    loudness, own = 1.0, jax.random.fold_in(rng, 6)
    for dim, parts in pieces:
        heights = jnp.exp(jax.random.uniform(jax.random.fold_in(own, dim), (parts,), jnp.float32, least / len(pieces), largest / len(pieces)))
        loudness = loudness * jnp.repeat(heights, dims[dim] // parts).reshape([-1 if axis == dim else 1 for axis in range(len(dims))])
    return loudness


def scatter_about(key, shape, scale, bound, split=(), kind=jnp.bfloat16):
    values = scale * jax.random.normal(key, shape, jnp.float32)
    if split:
        values = values * block_levels(key, shape, split, -0.22, 0.18)
    return jnp.clip(values, -bound, bound).astype(kind)


def setup_inputs(seed: int = 0) -> dict:
    splits = jax.random.split(jax.random.key(seed), 7)
    return {
        "activations": draw_activations(jax.random.fold_in(splits[6], 71), 0),
        "out_grad": scatter_about(splits[1], (N_GROUP, PATCHES, NE, D), 0.25, 1.5, ((0, 2), (2, 16))),
        "embedding": scatter_about(splits[2], (TEMPLATES, D), 1.0, 6.0),
        "counts": draw_counts(jax.random.fold_in(splits[6], 71), 0),
        "offsets": draw_offsets(jax.random.fold_in(splits[6], 71), 0),
        "layout": with_ends(jax.random.randint(splits[5], (N_GROUP, NE), 0, TEMPLATES), jax.random.fold_in(splits[5], 1), 0, TEMPLATES - 1).astype(jnp.int32),
    }


def product(form, left, right):
    return jnp.einsum(form, left.astype(jnp.float32), right.astype(jnp.float32), precision=lax.Precision.HIGHEST)

def attend(values, allowed):
    length = values.shape[0]
    head_split = values.reshape(length, HEADS, -1)
    score_scale = 0.5 / math.sqrt(head_split.shape[-1])
    scores = product('qhd,khd->hqk', head_split, head_split) * score_scale
    scores = jnp.where(allowed[None], scores, -1e+30)
    row_max = lax.optimization_barrier(jnp.max(scores, axis=-1, keepdims=True))
    exponent = jnp.exp(scores - row_max)
    weights = (exponent / lax.optimization_barrier(jnp.sum(exponent, axis=-1, keepdims=True))).astype(jnp.bfloat16)
    attended = product('hqk,khd->qhd', weights, head_split)
    return (head_split, weights, attended)

def attend_back(values, allowed, cotangent):
    head_split, weights, attended = attend(values, allowed)
    length = values.shape[0]
    score_scale = 0.5 / math.sqrt(head_split.shape[-1])
    grad_heads = cotangent.reshape(length, HEADS, -1)
    row_delta = lax.optimization_barrier(jnp.sum(grad_heads.astype(jnp.float32) * attended, axis=-1))
    grad_weights = product('qhd,khd->hqk', grad_heads, head_split)
    grad_scores = (weights.astype(jnp.float32) * (grad_weights - jnp.transpose(row_delta)[:, :, None])).astype(jnp.bfloat16)
    grad_values = score_scale * (product('hqk,khd->qhd', grad_scores, head_split) + product('hqk,qhd->khd', grad_scores, head_split))
    grad_values = grad_values + product('hqk,qhd->khd', weights, grad_heads)
    return grad_values.reshape(length, -1)

def session_pairs(counts, offsets, electrodes):
    slot_index = jnp.arange(electrodes, dtype=jnp.int32)
    block_index = slot_index // BLOCK
    member = (offsets[None, :] <= block_index[:, None]).astype(jnp.int32)
    session = lax.optimization_barrier(jnp.sum(member, axis=1)) - 1
    chosen = (jnp.arange(offsets.shape[0], dtype=jnp.int32)[None, :] == session[:, None]).astype(jnp.int32)
    first_slot = lax.optimization_barrier(jnp.sum(chosen * offsets[None, :], axis=1)) * BLOCK
    live_count = lax.optimization_barrier(jnp.sum(chosen * counts[None, :], axis=1))
    is_live = slot_index - first_slot < live_count
    return (session[:, None] == session[None, :]) & is_live[None, :]

def reference(activations, out_grad, embedding, counts, offsets, layout):
    input_rows = []
    tables = jnp.zeros((TEMPLATES, D), jnp.float32)
    full_mask = jnp.ones((PATCHES, PATCHES), dtype=bool)
    for group_index in range(N_GROUP):
        allowed = session_pairs(counts[group_index], offsets[group_index], NE)
        onehot = (layout[group_index][:, None] == jnp.arange(TEMPLATES, dtype=jnp.int32)[None, :]).astype(jnp.float32)
        layout_rows = jnp.dot(onehot, embedding.astype(jnp.float32), precision=lax.Precision.HIGHEST)
        embedded = (activations[group_index].astype(jnp.float32) + layout_rows[None]).astype(jnp.bfloat16)

        def spatial(values):
            return (values.astype(jnp.float32) + attend(values, allowed)[2].reshape(NE, D)).astype(jnp.bfloat16)
        mixed = lax.map(spatial, embedded)

        def temporal(couple):
            values, cotangent = couple
            return (cotangent.astype(jnp.float32) + attend_back(values, full_mask, cotangent)).astype(jnp.bfloat16)
        mixed_grad = lax.map(temporal, (jnp.moveaxis(mixed, 1, 0), jnp.moveaxis(out_grad[group_index], 1, 0)))
        mixed_grad = jnp.moveaxis(mixed_grad, 0, 1)

        def spatial_back(couple):
            values, cotangent = couple
            return cotangent.astype(jnp.float32) + attend_back(values, allowed, cotangent)
        full_grad = lax.map(spatial_back, (embedded, mixed_grad))
        input_rows.append(full_grad.astype(jnp.bfloat16))
        electrode_grad = lax.optimization_barrier(jnp.sum(full_grad, axis=0))
        tables = tables + jnp.dot(jnp.transpose(onehot), electrode_grad, precision=lax.Precision.HIGHEST)
    return (jnp.stack(input_rows), tables)
```

```python
import functools
import math

import jax
import jax.numpy as jnp
from jax import lax
from jax.experimental import pallas as pl
from jax.experimental.pallas import tpu as pltpu
from jax.sharding import PartitionSpec as P

HEADS = 16
BLOCK = 32
LANES = 128
MASKED = -1e30


def dot(left, right, over):
    return lax.dot_general(
        left, right, (((over[0],), (over[1],)), ((), ())), preferred_element_type=jnp.float32
    )


def head_rows(pair, width):
    lane = lax.broadcasted_iota(jnp.int32, pair.shape, 1)
    zero = jnp.zeros_like(pair)
    return jnp.concatenate(
        [jnp.where(lane < width, pair, zero), jnp.where(lane < width, zero, pair)], axis=0
    )


def head_columns(rows, width):
    count = rows.shape[0] // 2
    lane = lax.broadcasted_iota(jnp.int32, (count, rows.shape[1]), 1)
    return jnp.where(lane < width, rows[:count], rows[count:])


def weights_by_key(values, scaled, bias):
    scores = dot(values, scaled, (1, 1))
    if bias is not None:
        scores = scores + bias
    exponent = jnp.exp(scores - jnp.max(scores, axis=0, keepdims=True))
    share = 1.0 / jnp.sum(exponent, axis=0, keepdims=True)
    return (exponent * share).astype(jnp.bfloat16)


def back(values, cotangent, bias, width):
    score_scale = 0.5 / math.sqrt(width)
    scaled_pair = values * jnp.asarray(score_scale, values.dtype)
    scaled = head_rows(scaled_pair, width)
    heads_grad = head_rows(cotangent, width)
    weights = weights_by_key(values, scaled, bias)
    grad_weights = dot(values, heads_grad, (1, 1))
    wide = weights.astype(jnp.float32)
    delta = jnp.sum(wide * grad_weights, axis=0, keepdims=True)
    grad_scores = (wide * (grad_weights - delta)).astype(jnp.bfloat16)
    by_key = dot(
        jnp.concatenate([weights, grad_scores], axis=1),
        jnp.concatenate([heads_grad, scaled], axis=0),
        (1, 0),
    )
    by_query = head_columns(dot(grad_scores, scaled_pair, (0, 0)), width)
    return by_key + by_query


def pair_bias(counts, offsets, slots):
    def sessions(slot):
        block = slot // BLOCK
        session = jnp.full(slot.shape, -1, jnp.int32)
        for j in range(offsets.shape[1]):
            session = session + (offsets[0, j] <= block).astype(jnp.int32)
        return session

    key_slot = lax.broadcasted_iota(jnp.int32, (slots, 2 * slots), 0)
    query_slot = lax.broadcasted_iota(jnp.int32, (slots, 2 * slots), 1) % slots
    key_session = sessions(key_slot)
    first = jnp.zeros_like(key_slot)
    live = jnp.zeros_like(key_slot)
    for j in range(offsets.shape[1]):
        chosen = key_session == j
        first = jnp.where(chosen, offsets[0, j] * BLOCK, first)
        live = jnp.where(chosen, counts[0, j], live)
    allowed = (key_session == sessions(query_slot)) & (key_slot - first < live)
    return jnp.where(allowed, 0.0, MASKED)


def columns_at(step):
    return pl.ds(pl.multiple_of(step * LANES, LANES), LANES)


def spatial_kernel(
    width, counts, offsets, layout, embedding, tokens, embedded, mixed, rows, bias, by_electrode
):
    patches, slots, model = tokens.shape
    templates = embedding.shape[0]
    bias[...] = pair_bias(counts, offsets, slots)
    spread = lax.broadcasted_iota(jnp.int32, (templates, slots), 0) == layout[...]
    rows[...] = dot(spread.astype(jnp.float32).astype(jnp.bfloat16), embedding[...], (0, 0))

    def pair(step, carry):
        columns = columns_at(step)
        for p in range(patches):
            values = (tokens[p, :, columns].astype(jnp.float32) + rows[:, columns]).astype(
                jnp.bfloat16
            )
            embedded[p, :, columns] = values
            score_scale = jnp.asarray(0.5 / math.sqrt(width), values.dtype)
            weights = weights_by_key(values, head_rows(values * score_scale, width), bias[...])
            attended = head_columns(dot(weights, values, (0, 0)), width)
            by_electrode[pl.ds(p, slots, stride=patches), :] = (
                values.astype(jnp.float32) + attended
            )
        mixed[:, columns] = by_electrode[...].astype(jnp.bfloat16)
        return carry

    lax.fori_loop(0, model // LANES, pair, 0)


def temporal_kernel(width, parts, mixed, out_grad, mixed_grad, received, returned):
    electrodes, patches, model = out_grad.shape
    local = patches // parts

    def pair(step, carry):
        columns = columns_at(step)
        received[...] = mixed[:, columns].astype(jnp.float32)
        for e in range(electrodes):
            places = [
                pl.ds(e * local + p, parts, stride=electrodes * local) for p in range(local)
            ]
            values = jnp.concatenate([received[place, :] for place in places], axis=0)
            values = values.astype(jnp.bfloat16)
            cotangent = out_grad[e, :, columns]
            grad = cotangent.astype(jnp.float32) + back(values, cotangent, None, width)
            for p, place in enumerate(places):
                returned[place, :] = grad[p * parts : (p + 1) * parts]
        mixed_grad[:, columns] = returned[...].astype(jnp.bfloat16)
        return carry

    lax.fori_loop(0, model // LANES, pair, 0)


def spatial_back_kernel(
    width, counts, offsets, embedded, mixed_grad, input_grad, electrode_grad, bias, received
):
    patches, slots, model = embedded.shape
    bias[...] = pair_bias(counts, offsets, slots)

    def pair(step, carry):
        columns = columns_at(step)
        received[...] = mixed_grad[:, columns].astype(jnp.float32)
        total = jnp.zeros((slots, LANES), jnp.float32)
        for p in range(patches):
            arrived = received[pl.ds(p, slots, stride=patches), :]
            cotangent = arrived.astype(jnp.bfloat16)
            grad = arrived + back(embedded[p, :, columns], cotangent, bias[...], width)
            input_grad[p, :, columns] = grad.astype(jnp.bfloat16)
            total = total + grad
        electrode_grad[:, columns] = total
        return carry

    lax.fori_loop(0, model // LANES, pair, 0)


def table_kernel(groups, *refs):
    layouts, sums, table = refs[:groups], refs[groups], refs[groups + 1]
    owner = lax.axis_index("group")
    rows, model = table.shape
    slots = sums.shape[0] // groups
    template = lax.broadcasted_iota(jnp.int32, (rows, slots), 0) + owner * rows
    total = jnp.zeros((rows, model), jnp.float32)
    for away in range(groups):
        spread = (template == layouts[away][...]).astype(jnp.float32).astype(jnp.bfloat16)
        origin = lax.rem(owner + groups - away, groups)
        rest = sums[pl.ds(pl.multiple_of(origin * slots, slots), slots), :]
        for _ in range(3):
            part = rest.astype(jnp.bfloat16)
            total = total + dot(spread, part, (1, 0))
            rest = rest - part.astype(jnp.float32)
    table[...] = total


VMEM = pl.BlockSpec(memory_space=pltpu.VMEM)
SMEM = pl.BlockSpec(memory_space=pltpu.SMEM)
PARAMS = pltpu.CompilerParams(vmem_limit_bytes=48 * 1024 * 1024)


def body(activations, out_grad, embedding, counts, offsets, layout):
    tokens = activations[0]
    local, slots, model = tokens.shape
    groups = lax.axis_size("group")
    parts = lax.axis_size("shard")
    patches = local * parts
    own = slots // parts
    width = model // HEADS
    templates = embedding.shape[0]

    layouts = [layout] + [
        lax.ppermute(layout, "group", [(i, (i + away) % groups) for i in range(groups)])
        for away in range(1, groups)
    ]

    embedded, mixed = pl.pallas_call(
        functools.partial(spatial_kernel, width),
        out_shape=(
            jax.ShapeDtypeStruct(tokens.shape, jnp.bfloat16),
            jax.ShapeDtypeStruct((slots * local, model), jnp.bfloat16),
        ),
        in_specs=[SMEM, SMEM, VMEM, VMEM, VMEM],
        out_specs=(VMEM, VMEM),
        scratch_shapes=[
            pltpu.VMEM((slots, model), jnp.float32),
            pltpu.VMEM((slots, 2 * slots), jnp.float32),
            pltpu.VMEM((slots * local, LANES), jnp.float32),
        ],
        compiler_params=PARAMS,
        name="spatial",
    )(counts, offsets, layout, embedding, tokens)

    gathered = lax.all_to_all(mixed, "shard", split_axis=0, concat_axis=0, tiled=True)
    cotangent = out_grad[0].reshape(parts, local, own, model)
    cotangent = jnp.transpose(cotangent, (2, 1, 0, 3)).reshape(own, patches, model)

    mixed_grad = pl.pallas_call(
        functools.partial(temporal_kernel, width, parts),
        out_shape=jax.ShapeDtypeStruct(gathered.shape, jnp.bfloat16),
        in_specs=[VMEM, VMEM],
        out_specs=VMEM,
        scratch_shapes=[
            pltpu.VMEM((own * patches, LANES), jnp.float32),
            pltpu.VMEM((own * patches, LANES), jnp.float32),
        ],
        compiler_params=PARAMS,
        name="temporal",
    )(gathered, cotangent)

    returned = lax.all_to_all(mixed_grad, "shard", split_axis=0, concat_axis=0, tiled=True)

    input_grad, electrode_grad = pl.pallas_call(
        functools.partial(spatial_back_kernel, width),
        out_shape=(
            jax.ShapeDtypeStruct(tokens.shape, jnp.bfloat16),
            jax.ShapeDtypeStruct((slots, model), jnp.float32),
        ),
        in_specs=[SMEM, SMEM, VMEM, VMEM],
        out_specs=(VMEM, VMEM),
        scratch_shapes=[
            pltpu.VMEM((slots, 2 * slots), jnp.float32),
            pltpu.VMEM((slots * local, LANES), jnp.float32),
        ],
        compiler_params=PARAMS,
        name="spatial_back",
    )(counts, offsets, embedded, returned)

    shares = lax.all_to_all(
        electrode_grad.reshape(parts, own, model), "shard", split_axis=0, concat_axis=0, tiled=True
    )
    share = jnp.sum(shares, axis=0)
    everyone = lax.all_to_all(
        jnp.broadcast_to(share[None], (groups * parts, own, model)),
        ("group", "shard"),
        split_axis=0,
        concat_axis=0,
        tiled=True,
    )
    table_grad = pl.pallas_call(
        functools.partial(table_kernel, groups),
        out_shape=jax.ShapeDtypeStruct((templates // groups, model), jnp.float32),
        in_specs=[VMEM] * (groups + 1),
        out_specs=VMEM,
        compiler_params=PARAMS,
        name="table",
    )(*layouts, everyone.reshape(groups * slots, model))
    return (input_grad[None], table_grad)


def solution(mesh):
    placed = (
        P("group", "shard", None, None),
        P("group", None, "shard", None),
        P(),
        P("group", None),
        P("group", None),
        P("group", None),
    )
    return jax.shard_map(
        body,
        mesh=mesh,
        in_specs=placed,
        out_specs=(P("group", "shard", None, None), P("group", None)),
        check_vma=False,
    )
```

```python
import functools
import math

import jax
import jax.numpy as jnp
from jax import lax
from jax.experimental import pallas as pl
from jax.experimental.pallas import tpu as pltpu
from jax.sharding import PartitionSpec as P

HEADS = 16
BLOCK = 32
LANES = 128
MASKED = -1e30
CHUNKS = 1
GROUP = 4


def dot(left, right, over):
    return lax.dot_general(
        left, right, (((over[0],), (over[1],)), ((), ())), preferred_element_type=jnp.float32
    )


def head_masks(width, scale):
    lane = lax.broadcasted_iota(jnp.int32, (1, LANES), 1)
    first = jnp.where(lane < width, scale, 0.0).astype(jnp.bfloat16)
    second = jnp.where(lane < width, 0.0, scale).astype(jnp.bfloat16)
    return first, second


def head_rows(pair, masks):
    return jnp.concatenate([pair * masks[0], pair * masks[1]], axis=0)


def head_columns(rows, width):
    count = rows.shape[0] // 2
    lane = lax.broadcasted_iota(jnp.int32, (count, rows.shape[1]), 1)
    return jnp.where(lane < width, rows[:count], rows[count:])


def each(function, *lists):
    return [function(*items) for items in zip(*lists)]


def weights_by_key(scores):
    tops = each(lambda s: jnp.max(s, axis=0, keepdims=True), scores)
    exponents = each(lambda s, t: jnp.exp(s - t), scores, tops)
    shares = each(lambda e: 1.0 / jnp.sum(e, axis=0, keepdims=True), exponents)
    return each(lambda e, r: (e * r).astype(jnp.bfloat16), exponents, shares)


def back(values, scaled, cotangents, weights, grad_weights, heads_grads, width):
    wide = each(lambda w: w.astype(jnp.float32), weights)
    deltas = each(lambda w, g: jnp.sum(w * g, axis=0, keepdims=True), wide, grad_weights)
    grad_scores = each(
        lambda w, g, d: (w * (g - d)).astype(jnp.bfloat16), wide, grad_weights, deltas
    )
    by_key = each(
        lambda w, g, hg, hv: dot(
            jnp.concatenate([w, g], axis=1), jnp.concatenate([hg, hv], axis=0), (1, 0)
        ),
        weights,
        grad_scores,
        heads_grads,
        scaled,
    )
    score_scale = 0.5 / math.sqrt(width)
    by_query = each(lambda g, v: head_columns(dot(g, v, (0, 0)), width), grad_scores, values)
    return each(
        lambda c, k, q: c.astype(jnp.float32) + (k + score_scale * q),
        cotangents,
        by_key,
        by_query,
    )


def pair_bias(counts, offsets, slots):
    def sessions(slot):
        block = slot // BLOCK
        session = jnp.full(slot.shape, -1, jnp.int32)
        for j in range(offsets.shape[1]):
            session = session + (offsets[0, j] <= block).astype(jnp.int32)
        return session

    key_slot = lax.broadcasted_iota(jnp.int32, (slots, 2 * slots), 0)
    query_slot = lax.broadcasted_iota(jnp.int32, (slots, 2 * slots), 1) % slots
    key_session = sessions(key_slot)
    first = jnp.zeros_like(key_slot)
    live = jnp.zeros_like(key_slot)
    for j in range(offsets.shape[1]):
        chosen = key_session == j
        first = jnp.where(chosen, offsets[0, j] * BLOCK, first)
        live = jnp.where(chosen, counts[0, j], live)
    allowed = (key_session == sessions(query_slot)) & (key_slot - first < live)
    return jnp.where(allowed, 0.0, MASKED)


def columns_at(step, first=0):
    return pl.ds(pl.multiple_of(first + step * LANES, LANES), LANES)


def in_groups(count, size):
    return [range(start, min(start + size, count)) for start in range(0, count, size)]


def spatial_kernel(
    width, first, counts, offsets, layout, embedding, tokens,
    embedded, weights, mixed, rows, bias, by_electrode,
):
    patches, slots, model = embedded.shape
    templates = embedding.shape[0]
    score_masks = head_masks(width, 0.5 / math.sqrt(width))
    bias[...] = pair_bias(counts, offsets, slots)
    spread = lax.broadcasted_iota(jnp.int32, (templates, slots), 0) == layout[...]
    rows[...] = dot(
        spread.astype(jnp.float32).astype(jnp.bfloat16),
        embedding[:, first : first + model],
        (0, 0),
    )

    def pair(step, carry):
        source, columns = columns_at(step, first), columns_at(step)
        added = rows[:, columns]
        for group in in_groups(patches, GROUP):
            values = [
                (tokens[p, :, source].astype(jnp.float32) + added).astype(jnp.bfloat16)
                for p in group
            ]
            scores = each(
                lambda v: dot(v, head_rows(v, score_masks), (1, 1)) + bias[...], values
            )
            shares = weights_by_key(scores)
            attended = each(lambda w, v: head_columns(dot(w, v, (0, 0)), width), shares, values)
            for p, value, share, result in zip(group, values, shares, attended):
                embedded[p, :, columns] = value
                weights[p, step] = share
                by_electrode[pl.ds(p, slots, stride=patches), :] = (
                    value.astype(jnp.float32) + result
                )
        mixed[:, columns] = by_electrode[...].astype(jnp.bfloat16)
        return carry

    lax.fori_loop(0, model // LANES, pair, 0)


def temporal_kernel(width, parts, first, mixed, out_grad, mixed_grad, received, returned):
    electrodes, patches, _ = out_grad.shape
    model = mixed.shape[1]
    local = patches // parts
    score_masks = head_masks(width, 0.5 / math.sqrt(width))
    ones = head_masks(width, 1.0)

    def pair(step, carry):
        columns = columns_at(step)
        received[...] = mixed[:, columns].astype(jnp.float32)
        for group in in_groups(electrodes, GROUP // 2):
            places = [
                [pl.ds(e * local + p, parts, stride=electrodes * local) for p in range(local)]
                for e in group
            ]
            values = each(
                lambda place: jnp.concatenate([received[rows, :] for rows in place], axis=0).astype(
                    jnp.bfloat16
                ),
                places,
            )
            cotangents = [out_grad[e, :, columns_at(step, first)] for e in group]
            scaled = each(lambda v: head_rows(v, score_masks), values)
            scores = each(lambda v, s: dot(v, s, (1, 1)), values, scaled)
            heads_grads = each(lambda g: head_rows(g, ones), cotangents)
            grad_weights = each(lambda v, g: dot(v, g, (1, 1)), values, heads_grads)
            shares = weights_by_key(scores)
            grads = back(values, scaled, cotangents, shares, grad_weights, heads_grads, width)
            for place, grad in zip(places, grads):
                for p, rows in enumerate(place):
                    returned[rows, :] = grad[p * parts : (p + 1) * parts]
        mixed_grad[:, columns] = returned[...].astype(jnp.bfloat16)
        return carry

    lax.fori_loop(0, model // LANES, pair, 0)


def spatial_back_kernel(
    width, embedded, weights, mixed_grad, input_grad, electrode_grad, received
):
    patches, slots, model = embedded.shape
    score_masks = head_masks(width, 0.5 / math.sqrt(width))
    ones = head_masks(width, 1.0)

    def pair(step, carry):
        columns = columns_at(step)
        received[...] = mixed_grad[:, columns].astype(jnp.float32)
        total = jnp.zeros((slots, LANES), jnp.float32)
        for group in in_groups(patches, GROUP):
            cotangents = [
                received[pl.ds(p, slots, stride=patches), :].astype(jnp.bfloat16) for p in group
            ]
            values = [embedded[p, :, columns] for p in group]
            shares = [weights[p, step] for p in group]
            scaled = each(lambda v: head_rows(v, score_masks), values)
            heads_grads = each(lambda g: head_rows(g, ones), cotangents)
            grad_weights = each(lambda v, g: dot(v, g, (1, 1)), values, heads_grads)
            grads = back(values, scaled, cotangents, shares, grad_weights, heads_grads, width)
            for p, grad in zip(group, grads):
                input_grad[p, :, columns] = grad.astype(jnp.bfloat16)
                total = total + grad
        electrode_grad[:, columns] = total.astype(jnp.bfloat16)
        return carry

    lax.fori_loop(0, model // LANES, pair, 0)


def table_kernel(groups, *refs):
    layouts, sums, table = refs[:groups], refs[groups], refs[groups + 1]
    owner = lax.axis_index("group")
    rows, model = table.shape
    slots = sums.shape[0] // groups
    template = lax.broadcasted_iota(jnp.int32, (rows, slots), 0) + owner * rows
    total = jnp.zeros((rows, model), jnp.float32)
    for away in range(groups):
        spread = (template == layouts[away][...]).astype(jnp.float32).astype(jnp.bfloat16)
        origin = lax.rem(owner + groups - away, groups)
        part = sums[pl.ds(pl.multiple_of(origin * slots, slots), slots), :]
        total = total + dot(spread, part, (1, 0))
    table[...] = total


VMEM = pl.BlockSpec(memory_space=pltpu.VMEM)
SMEM = pl.BlockSpec(memory_space=pltpu.SMEM)
PARAMS = pltpu.CompilerParams(vmem_limit_bytes=48 * 1024 * 1024)


def body(activations, out_grad, embedding, counts, offsets, layout):
    tokens = activations[0]
    local, slots, model = tokens.shape
    groups = lax.axis_size("group")
    parts = lax.axis_size("shard")
    patches = local * parts
    own = slots // parts
    width = model // HEADS
    templates = embedding.shape[0]
    chunk = model // CHUNKS
    pairs = chunk // LANES

    layouts = [layout] + [
        lax.ppermute(layout, "group", [(i, (i + away) % groups) for i in range(groups)])
        for away in range(1, groups)
    ]
    cotangent = out_grad[0].reshape(parts, local, own, model)
    cotangent = jnp.transpose(cotangent, (2, 1, 0, 3)).reshape(own, patches, model)

    firsts = [index * chunk for index in range(CHUNKS)]
    forward = [
        pl.pallas_call(
            functools.partial(spatial_kernel, width, first),
            out_shape=(
                jax.ShapeDtypeStruct((local, slots, chunk), jnp.bfloat16),
                jax.ShapeDtypeStruct((local, pairs, slots, 2 * slots), jnp.bfloat16),
                jax.ShapeDtypeStruct((slots * local, chunk), jnp.bfloat16),
            ),
            in_specs=[SMEM, SMEM, VMEM, VMEM, VMEM],
            out_specs=(VMEM, VMEM, VMEM),
            scratch_shapes=[
                pltpu.VMEM((slots, chunk), jnp.float32),
                pltpu.VMEM((slots, 2 * slots), jnp.float32),
                pltpu.VMEM((slots * local, LANES), jnp.float32),
            ],
            compiler_params=PARAMS,
            name="spatial",
        )(counts, offsets, layout, embedding, tokens)
        for first in firsts
    ]
    gathered = [
        lax.all_to_all(mixed, "shard", split_axis=0, concat_axis=0, tiled=True)
        for _, _, mixed in forward
    ]
    mixed_grads = [
        pl.pallas_call(
            functools.partial(temporal_kernel, width, parts, first),
            out_shape=jax.ShapeDtypeStruct(arrived.shape, jnp.bfloat16),
            in_specs=[VMEM, VMEM],
            out_specs=VMEM,
            scratch_shapes=[
                pltpu.VMEM((own * patches, LANES), jnp.float32),
                pltpu.VMEM((own * patches, LANES), jnp.float32),
            ],
            compiler_params=PARAMS,
            name="temporal",
        )(arrived, cotangent)
        for first, arrived in zip(firsts, gathered)
    ]
    returned = [
        lax.all_to_all(grad, "shard", split_axis=0, concat_axis=0, tiled=True)
        for grad in mixed_grads
    ]
    backward = [
        pl.pallas_call(
            functools.partial(spatial_back_kernel, width),
            out_shape=(
                jax.ShapeDtypeStruct((local, slots, chunk), jnp.bfloat16),
                jax.ShapeDtypeStruct((slots, chunk), jnp.bfloat16),
            ),
            in_specs=[VMEM, VMEM, VMEM],
            out_specs=(VMEM, VMEM),
            scratch_shapes=[pltpu.VMEM((slots * local, LANES), jnp.float32)],
            compiler_params=PARAMS,
            name="spatial_back",
        )(embedded, weights, arrived)
        for (embedded, weights, _), arrived in zip(forward, returned)
    ]
    input_grad = jnp.concatenate([grad for grad, _ in backward], axis=2)
    electrode_grad = jnp.concatenate([grad for _, grad in backward], axis=1)

    shares = lax.all_to_all(
        electrode_grad.reshape(parts, own, model), "shard", split_axis=0, concat_axis=0, tiled=True
    )
    share = jnp.sum(shares.astype(jnp.float32), axis=0).astype(jnp.bfloat16)
    everyone = lax.all_to_all(
        jnp.broadcast_to(share[None], (groups * parts, own, model)),
        ("group", "shard"),
        split_axis=0,
        concat_axis=0,
        tiled=True,
    )
    table_grad = pl.pallas_call(
        functools.partial(table_kernel, groups),
        out_shape=jax.ShapeDtypeStruct((templates // groups, model), jnp.float32),
        in_specs=[VMEM] * (groups + 1),
        out_specs=VMEM,
        compiler_params=PARAMS,
        name="table",
    )(*layouts, everyone.reshape(groups * slots, model))
    return (input_grad[None], table_grad)


def solution(mesh):
    placed = (
        P("group", "shard", None, None),
        P("group", None, "shard", None),
        P(),
        P("group", None),
        P("group", None),
        P("group", None),
    )
    return jax.shard_map(
        body,
        mesh=mesh,
        in_specs=placed,
        out_specs=(P("group", "shard", None, None), P("group", None)),
        check_vma=False,
    )
```

```python
import functools
import math

import jax
import jax.numpy as jnp
from jax import lax
from jax.experimental import pallas as pl
from jax.experimental.pallas import tpu as pltpu
from jax.sharding import PartitionSpec as P

HEADS = 16
BLOCK = 32
LANES = 128
MASKED = -1e30
CHUNKS = 2
GROUP = 4


def dot(left, right, over):
    return lax.dot_general(
        left, right, (((over[0],), (over[1],)), ((), ())), preferred_element_type=jnp.float32
    )


def head_masks(width, scale):
    lane = lax.broadcasted_iota(jnp.int32, (1, LANES), 1)
    first = jnp.where(lane < width, scale, 0.0).astype(jnp.bfloat16)
    second = jnp.where(lane < width, 0.0, scale).astype(jnp.bfloat16)
    return first, second


def head_rows(pair, masks):
    return jnp.concatenate([pair * masks[0], pair * masks[1]], axis=0)


def head_columns(rows, width):
    count = rows.shape[0] // 2
    lane = lax.broadcasted_iota(jnp.int32, (count, rows.shape[1]), 1)
    return jnp.where(lane < width, rows[:count], rows[count:])


def each(function, *lists):
    return [function(*items) for items in zip(*lists)]


def weights_by_key(scores):
    tops = each(lambda s: jnp.max(s, axis=0, keepdims=True), scores)
    exponents = each(lambda s, t: jnp.exp(s - t), scores, tops)
    shares = each(lambda e: 1.0 / jnp.sum(e, axis=0, keepdims=True), exponents)
    return each(lambda e, r: (e * r).astype(jnp.bfloat16), exponents, shares)


def back(values, scaled, cotangents, weights, grad_weights, heads_grads, width):
    wide = each(lambda w: w.astype(jnp.float32), weights)
    deltas = each(lambda w, g: jnp.sum(w * g, axis=0, keepdims=True), wide, grad_weights)
    grad_scores = each(
        lambda w, g, d: (w * (g - d)).astype(jnp.bfloat16), wide, grad_weights, deltas
    )
    by_key = each(
        lambda w, g, hg, hv: dot(
            jnp.concatenate([w, g], axis=1), jnp.concatenate([hg, hv], axis=0), (1, 0)
        ),
        weights,
        grad_scores,
        heads_grads,
        scaled,
    )
    score_scale = 0.5 / math.sqrt(width)
    by_query = each(lambda g, v: head_columns(dot(g, v, (0, 0)), width), grad_scores, values)
    return each(
        lambda c, k, q: c.astype(jnp.float32) + (k + score_scale * q),
        cotangents,
        by_key,
        by_query,
    )


def pair_bias(counts, offsets, slots):
    def sessions(slot):
        block = slot // BLOCK
        session = jnp.full(slot.shape, -1, jnp.int32)
        for j in range(offsets.shape[1]):
            session = session + (offsets[0, j] <= block).astype(jnp.int32)
        return session

    key_slot = lax.broadcasted_iota(jnp.int32, (slots, 2 * slots), 0)
    query_slot = lax.broadcasted_iota(jnp.int32, (slots, 2 * slots), 1) % slots
    key_session = sessions(key_slot)
    first = jnp.zeros_like(key_slot)
    live = jnp.zeros_like(key_slot)
    for j in range(offsets.shape[1]):
        chosen = key_session == j
        first = jnp.where(chosen, offsets[0, j] * BLOCK, first)
        live = jnp.where(chosen, counts[0, j], live)
    allowed = (key_session == sessions(query_slot)) & (key_slot - first < live)
    return jnp.where(allowed, 0.0, MASKED)


def columns_at(step, first=0):
    return pl.ds(pl.multiple_of(first + step * LANES, LANES), LANES)


def in_groups(count, size):
    return [range(start, min(start + size, count)) for start in range(0, count, size)]


def spatial_kernel(
    width, first, counts, offsets, layout, embedding, tokens,
    embedded, weights, mixed, rows, bias, by_electrode,
):
    patches, slots, model = embedded.shape
    templates = embedding.shape[0]
    score_masks = head_masks(width, 0.5 / math.sqrt(width))
    bias[...] = pair_bias(counts, offsets, slots)
    spread = lax.broadcasted_iota(jnp.int32, (templates, slots), 0) == layout[...]
    rows[...] = dot(
        spread.astype(jnp.float32).astype(jnp.bfloat16),
        embedding[:, first : first + model],
        (0, 0),
    )

    def pair(step, carry):
        source, columns = columns_at(step, first), columns_at(step)
        added = rows[:, columns]
        for group in in_groups(patches, GROUP):
            values = [
                (tokens[p, :, source].astype(jnp.float32) + added).astype(jnp.bfloat16)
                for p in group
            ]
            scores = each(
                lambda v: dot(v, head_rows(v, score_masks), (1, 1)) + bias[...], values
            )
            shares = weights_by_key(scores)
            attended = each(lambda w, v: head_columns(dot(w, v, (0, 0)), width), shares, values)
            for p, value, share, result in zip(group, values, shares, attended):
                embedded[p, :, columns] = value
                weights[p, step] = share
                by_electrode[pl.ds(p, slots, stride=patches), :] = (
                    value.astype(jnp.float32) + result
                )
        mixed[:, columns] = by_electrode[...].astype(jnp.bfloat16)
        return carry

    lax.fori_loop(0, model // LANES, pair, 0)


def temporal_kernel(width, parts, first, mixed, out_grad, mixed_grad, received, returned):
    electrodes, patches, _ = out_grad.shape
    model = mixed.shape[1]
    local = patches // parts
    score_masks = head_masks(width, 0.5 / math.sqrt(width))
    ones = head_masks(width, 1.0)

    def pair(step, carry):
        columns = columns_at(step)
        received[...] = mixed[:, columns].astype(jnp.float32)
        for group in in_groups(electrodes, GROUP // 2):
            places = [
                [pl.ds(e * local + p, parts, stride=electrodes * local) for p in range(local)]
                for e in group
            ]
            values = each(
                lambda place: jnp.concatenate([received[rows, :] for rows in place], axis=0).astype(
                    jnp.bfloat16
                ),
                places,
            )
            cotangents = [out_grad[e, :, columns_at(step, first)] for e in group]
            scaled = each(lambda v: head_rows(v, score_masks), values)
            scores = each(lambda v, s: dot(v, s, (1, 1)), values, scaled)
            heads_grads = each(lambda g: head_rows(g, ones), cotangents)
            grad_weights = each(lambda v, g: dot(v, g, (1, 1)), values, heads_grads)
            shares = weights_by_key(scores)
            grads = back(values, scaled, cotangents, shares, grad_weights, heads_grads, width)
            for place, grad in zip(places, grads):
                for p, rows in enumerate(place):
                    returned[rows, :] = grad[p * parts : (p + 1) * parts]
        mixed_grad[:, columns] = returned[...].astype(jnp.bfloat16)
        return carry

    lax.fori_loop(0, model // LANES, pair, 0)


def spatial_back_kernel(width, embedded, weights, mixed_grad, *refs):
    input_grad, electrode_grad, received = refs[-3:]
    patches, slots, model = embedded.shape
    score_masks = head_masks(width, 0.5 / math.sqrt(width))
    ones = head_masks(width, 1.0)

    def pair(step, carry):
        columns = columns_at(step)
        received[...] = mixed_grad[:, columns].astype(jnp.float32)
        total = jnp.zeros((slots, LANES), jnp.float32)
        for group in in_groups(patches, GROUP):
            cotangents = [
                received[pl.ds(p, slots, stride=patches), :].astype(jnp.bfloat16) for p in group
            ]
            values = [embedded[p, :, columns] for p in group]
            shares = [weights[p, step] for p in group]
            scaled = each(lambda v: head_rows(v, score_masks), values)
            heads_grads = each(lambda g: head_rows(g, ones), cotangents)
            grad_weights = each(lambda v, g: dot(v, g, (1, 1)), values, heads_grads)
            grads = back(values, scaled, cotangents, shares, grad_weights, heads_grads, width)
            for p, grad in zip(group, grads):
                input_grad[p, :, columns] = grad.astype(jnp.bfloat16)
                total = total + grad
        electrode_grad[:, columns] = total.astype(jnp.bfloat16)
        return carry

    lax.fori_loop(0, model // LANES, pair, 0)


def table_kernel(groups, *refs):
    layouts, sums, table = refs[:groups], refs[groups], refs[groups + 1]
    owner = lax.axis_index("group")
    rows, model = table.shape
    slots = sums.shape[0] // groups
    template = lax.broadcasted_iota(jnp.int32, (rows, slots), 0) + owner * rows
    total = jnp.zeros((rows, model), jnp.float32)
    for away in range(groups):
        spread = (template == layouts[away][...]).astype(jnp.float32).astype(jnp.bfloat16)
        origin = lax.rem(owner + groups - away, groups)
        part = sums[pl.ds(pl.multiple_of(origin * slots, slots), slots), :]
        total = total + dot(spread, part, (1, 0))
    table[...] = total


VMEM = pl.BlockSpec(memory_space=pltpu.VMEM)
SMEM = pl.BlockSpec(memory_space=pltpu.SMEM)
PARAMS = pltpu.CompilerParams(vmem_limit_bytes=48 * 1024 * 1024)


def body(activations, out_grad, embedding, counts, offsets, layout):
    tokens = activations[0]
    local, slots, model = tokens.shape
    groups = lax.axis_size("group")
    parts = lax.axis_size("shard")
    patches = local * parts
    own = slots // parts
    width = model // HEADS
    templates = embedding.shape[0]
    chunk = model // CHUNKS
    pairs = chunk // LANES

    layouts = [layout] + [
        lax.ppermute(layout, "group", [(i, (i + away) % groups) for i in range(groups)])
        for away in range(1, groups)
    ]
    cotangent = out_grad[0].reshape(parts, local, own, model)
    cotangent = jnp.transpose(cotangent, (2, 1, 0, 3)).reshape(own, patches, model)

    firsts = [index * chunk for index in range(CHUNKS)]
    forward = [
        pl.pallas_call(
            functools.partial(spatial_kernel, width, first),
            out_shape=(
                jax.ShapeDtypeStruct((local, slots, chunk), jnp.bfloat16),
                jax.ShapeDtypeStruct((local, pairs, slots, 2 * slots), jnp.bfloat16),
                jax.ShapeDtypeStruct((slots * local, chunk), jnp.bfloat16),
            ),
            in_specs=[SMEM, SMEM, VMEM, VMEM, VMEM],
            out_specs=(VMEM, VMEM, VMEM),
            scratch_shapes=[
                pltpu.VMEM((slots, chunk), jnp.float32),
                pltpu.VMEM((slots, 2 * slots), jnp.float32),
                pltpu.VMEM((slots * local, LANES), jnp.float32),
            ],
            compiler_params=PARAMS,
            name="spatial",
        )(counts, offsets, layout, embedding, tokens)
        for first in firsts
    ]
    gathered = [
        lax.all_to_all(mixed, "shard", split_axis=0, concat_axis=0, tiled=True)
        for _, _, mixed in forward
    ]
    mixed_grads = [
        pl.pallas_call(
            functools.partial(temporal_kernel, width, parts, first),
            out_shape=jax.ShapeDtypeStruct(arrived.shape, jnp.bfloat16),
            in_specs=[VMEM, VMEM],
            out_specs=VMEM,
            scratch_shapes=[
                pltpu.VMEM((own * patches, LANES), jnp.float32),
                pltpu.VMEM((own * patches, LANES), jnp.float32),
            ],
            compiler_params=PARAMS,
            name="temporal",
        )(arrived, cotangent)
        for first, arrived in zip(firsts, gathered)
    ]
    returned = [
        lax.all_to_all(grad, "shard", split_axis=0, concat_axis=0, tiled=True)
        for grad in mixed_grads
    ]
    done = []
    for index, (embedded, weights, _) in enumerate(forward):
        done = pl.pallas_call(
            functools.partial(spatial_back_kernel, width),
            grid=(1,),
            out_shape=(
                jax.ShapeDtypeStruct(tokens.shape, jnp.bfloat16),
                jax.ShapeDtypeStruct((slots, model), jnp.bfloat16),
            ),
            in_specs=[VMEM, VMEM, VMEM] + [pl.BlockSpec(memory_space=pl.ANY)] * len(done),
            out_specs=(
                pl.BlockSpec((local, slots, chunk), lambda i, index=index: (0, 0, index)),
                pl.BlockSpec((slots, chunk), lambda i, index=index: (0, index)),
            ),
            scratch_shapes=[pltpu.VMEM((slots * local, LANES), jnp.float32)],
            input_output_aliases={3 + place: place for place in range(len(done))},
            compiler_params=PARAMS,
            name="spatial_back",
        )(embedded, weights, returned[index], *done)
    input_grad, electrode_grad = done

    shares = lax.all_to_all(
        electrode_grad.reshape(parts, own, model), "shard", split_axis=0, concat_axis=0, tiled=True
    )
    share = jnp.sum(shares.astype(jnp.float32), axis=0).astype(jnp.bfloat16)
    everyone = lax.all_to_all(
        jnp.broadcast_to(share[None], (groups * parts, own, model)),
        ("group", "shard"),
        split_axis=0,
        concat_axis=0,
        tiled=True,
    )
    table_grad = pl.pallas_call(
        functools.partial(table_kernel, groups),
        out_shape=jax.ShapeDtypeStruct((templates // groups, model), jnp.float32),
        in_specs=[VMEM] * (groups + 1),
        out_specs=VMEM,
        compiler_params=PARAMS,
        name="table",
    )(*layouts, everyone.reshape(groups * slots, model))
    return (input_grad[None], table_grad)


def solution(mesh):
    placed = (
        P("group", "shard", None, None),
        P("group", None, "shard", None),
        P(),
        P("group", None),
        P("group", None),
        P("group", None),
    )
    return jax.shard_map(
        body,
        mesh=mesh,
        in_specs=placed,
        out_specs=(P("group", "shard", None, None), P("group", None)),
        check_vma=False,
    )
```

```python
import functools
import math

import jax
import jax.numpy as jnp
from jax import lax
from jax.experimental import pallas as pl
from jax.experimental.pallas import tpu as pltpu
from jax.sharding import PartitionSpec as P

HEADS = 16
BLOCK = 32
LANES = 128
MASKED = -1e30
CHUNKS = 1
GROUP = 4


def dot(left, right, over):
    return lax.dot_general(
        left, right, (((over[0],), (over[1],)), ((), ())), preferred_element_type=jnp.float32
    )


def head_masks(width, scale):
    lane = lax.broadcasted_iota(jnp.int32, (1, LANES), 1)
    first = jnp.where(lane < width, scale, 0.0).astype(jnp.bfloat16)
    second = jnp.where(lane < width, 0.0, scale).astype(jnp.bfloat16)
    return first, second


def head_rows(pair, masks):
    return jnp.concatenate([pair * masks[0], pair * masks[1]], axis=0)


def head_columns(rows, width):
    count = rows.shape[0] // 2
    lane = lax.broadcasted_iota(jnp.int32, (count, rows.shape[1]), 1)
    return jnp.where(lane < width, rows[:count], rows[count:])


def each(function, *lists):
    return [function(*items) for items in zip(*lists)]


def weights_by_key(scores):
    tops = each(lambda s: jnp.max(s, axis=0, keepdims=True), scores)
    exponents = each(lambda s, t: jnp.exp(s - t), scores, tops)
    shares = each(lambda e: 1.0 / jnp.sum(e, axis=0, keepdims=True), exponents)
    return each(lambda e, r: (e * r).astype(jnp.bfloat16), exponents, shares)


def back(values, scaled, cotangents, weights, grad_weights, heads_grads, width):
    wide = each(lambda w: w.astype(jnp.float32), weights)
    deltas = each(lambda w, g: jnp.sum(w * g, axis=0, keepdims=True), wide, grad_weights)
    grad_scores = each(
        lambda w, g, d: (w * (g - d)).astype(jnp.bfloat16), wide, grad_weights, deltas
    )
    by_key = each(
        lambda w, g, hg, hv: dot(
            jnp.concatenate([w, g], axis=1), jnp.concatenate([hg, hv], axis=0), (1, 0)
        ),
        weights,
        grad_scores,
        heads_grads,
        scaled,
    )
    score_scale = 0.5 / math.sqrt(width)
    by_query = each(lambda g, v: head_columns(dot(g, v, (0, 0)), width), grad_scores, values)
    return each(
        lambda c, k, q: c.astype(jnp.float32) + (k + score_scale * q),
        cotangents,
        by_key,
        by_query,
    )


def pair_bias(counts, offsets, slots):
    def sessions(slot):
        block = slot // BLOCK
        session = jnp.full(slot.shape, -1, jnp.int32)
        for j in range(offsets.shape[1]):
            session = session + (offsets[0, j] <= block).astype(jnp.int32)
        return session

    key_slot = lax.broadcasted_iota(jnp.int32, (slots, 2 * slots), 0)
    query_slot = lax.broadcasted_iota(jnp.int32, (slots, 2 * slots), 1) % slots
    key_session = sessions(key_slot)
    first = jnp.zeros_like(key_slot)
    live = jnp.zeros_like(key_slot)
    for j in range(offsets.shape[1]):
        chosen = key_session == j
        first = jnp.where(chosen, offsets[0, j] * BLOCK, first)
        live = jnp.where(chosen, counts[0, j], live)
    allowed = (key_session == sessions(query_slot)) & (key_slot - first < live)
    return jnp.where(allowed, 0.0, MASKED)


def columns_at(step, first=0):
    return pl.ds(pl.multiple_of(first + step * LANES, LANES), LANES)


def in_groups(count, size):
    return [range(start, min(start + size, count)) for start in range(0, count, size)]


def partner_rows(away, count):
    partner = lax.bitwise_xor(lax.axis_index("shard"), away)
    return pl.ds(pl.multiple_of(partner * count, count), count)


def spatial_kernel(
    width, first, counts, offsets, layout, embedding, tokens, embedded, weights, *refs
):
    mixed, (rows, bias, by_electrode) = refs[:-3], refs[-3:]
    patches, slots, model = embedded.shape
    templates = embedding.shape[0]
    score_masks = head_masks(width, 0.5 / math.sqrt(width))
    bias[...] = pair_bias(counts, offsets, slots)
    spread = lax.broadcasted_iota(jnp.int32, (templates, slots), 0) == layout[...]
    rows[...] = dot(
        spread.astype(jnp.float32).astype(jnp.bfloat16),
        embedding[:, first : first + model],
        (0, 0),
    )

    def pair(step, carry):
        source, columns = columns_at(step, first), columns_at(step)
        added = rows[:, columns]
        for group in in_groups(patches, GROUP):
            values = [
                (tokens[p, :, source].astype(jnp.float32) + added).astype(jnp.bfloat16)
                for p in group
            ]
            scores = each(
                lambda v: dot(v, head_rows(v, score_masks), (1, 1)) + bias[...], values
            )
            shares = weights_by_key(scores)
            attended = each(lambda w, v: head_columns(dot(w, v, (0, 0)), width), shares, values)
            for p, value, share, result in zip(group, values, shares, attended):
                embedded[p, :, columns] = value
                weights[p, step] = share
                by_electrode[pl.ds(p, slots, stride=patches), :] = (
                    value.astype(jnp.float32) + result
                )
        for away, block in enumerate(mixed):
            block[:, columns] = by_electrode[partner_rows(away, block.shape[0]), :].astype(
                jnp.bfloat16
            )
        return carry

    lax.fori_loop(0, model // LANES, pair, 0)


def temporal_kernel(width, parts, first, out_grad, *refs):
    mixed, mixed_grad, (received, returned) = refs[:parts], refs[parts:-2], refs[-2:]
    electrodes, patches, _ = out_grad.shape
    model = mixed[0].shape[1]
    local = patches // parts
    score_masks = head_masks(width, 0.5 / math.sqrt(width))
    ones = head_masks(width, 1.0)

    def pair(step, carry):
        columns = columns_at(step)
        for away, block in enumerate(mixed):
            received[partner_rows(away, block.shape[0]), :] = block[:, columns].astype(jnp.float32)
        for group in in_groups(electrodes, GROUP // 2):
            places = [
                [pl.ds(e * local + p, parts, stride=electrodes * local) for p in range(local)]
                for e in group
            ]
            values = each(
                lambda place: jnp.concatenate([received[rows, :] for rows in place], axis=0).astype(
                    jnp.bfloat16
                ),
                places,
            )
            cotangents = [out_grad[e, :, columns_at(step, first)] for e in group]
            scaled = each(lambda v: head_rows(v, score_masks), values)
            scores = each(lambda v, s: dot(v, s, (1, 1)), values, scaled)
            heads_grads = each(lambda g: head_rows(g, ones), cotangents)
            grad_weights = each(lambda v, g: dot(v, g, (1, 1)), values, heads_grads)
            shares = weights_by_key(scores)
            grads = back(values, scaled, cotangents, shares, grad_weights, heads_grads, width)
            for place, grad in zip(places, grads):
                for p, rows in enumerate(place):
                    returned[rows, :] = grad[p * parts : (p + 1) * parts]
        for away, block in enumerate(mixed_grad):
            block[:, columns] = returned[partner_rows(away, block.shape[0]), :].astype(jnp.bfloat16)
        return carry

    lax.fori_loop(0, model // LANES, pair, 0)


def spatial_back_kernel(width, parts, embedded, weights, *refs):
    mixed_grad, (input_grad, electrode_grad, received) = refs[:parts], refs[-3:]
    patches, slots, model = embedded.shape
    score_masks = head_masks(width, 0.5 / math.sqrt(width))
    ones = head_masks(width, 1.0)

    def pair(step, carry):
        columns = columns_at(step)
        for away, block in enumerate(mixed_grad):
            received[partner_rows(away, block.shape[0]), :] = block[:, columns].astype(jnp.float32)
        total = jnp.zeros((slots, LANES), jnp.float32)
        for group in in_groups(patches, GROUP):
            cotangents = [
                received[pl.ds(p, slots, stride=patches), :].astype(jnp.bfloat16) for p in group
            ]
            values = [embedded[p, :, columns] for p in group]
            shares = [weights[p, step] for p in group]
            scaled = each(lambda v: head_rows(v, score_masks), values)
            heads_grads = each(lambda g: head_rows(g, ones), cotangents)
            grad_weights = each(lambda v, g: dot(v, g, (1, 1)), values, heads_grads)
            grads = back(values, scaled, cotangents, shares, grad_weights, heads_grads, width)
            for p, grad in zip(group, grads):
                input_grad[p, :, columns] = grad.astype(jnp.bfloat16)
                total = total + grad
        electrode_grad[:, columns] = total.astype(jnp.bfloat16)
        return carry

    lax.fori_loop(0, model // LANES, pair, 0)


def table_kernel(groups, *refs):
    layouts, sums, table = refs[:groups], refs[groups], refs[groups + 1]
    owner = lax.axis_index("group")
    rows, model = table.shape
    slots = sums.shape[0] // groups
    template = lax.broadcasted_iota(jnp.int32, (rows, slots), 0) + owner * rows
    total = jnp.zeros((rows, model), jnp.float32)
    for away in range(groups):
        spread = (template == layouts[away][...]).astype(jnp.float32).astype(jnp.bfloat16)
        origin = lax.rem(owner + groups - away, groups)
        part = sums[pl.ds(pl.multiple_of(origin * slots, slots), slots), :]
        total = total + dot(spread, part, (1, 0))
    table[...] = total


VMEM = pl.BlockSpec(memory_space=pltpu.VMEM)
SMEM = pl.BlockSpec(memory_space=pltpu.SMEM)
PARAMS = pltpu.CompilerParams(vmem_limit_bytes=48 * 1024 * 1024)


def exchange(blocks):
    count = len(blocks)
    return [blocks[0]] + [
        lax.ppermute(block, "shard", [(i, i ^ away) for i in range(count)])
        for away, block in enumerate(blocks)
        if away
    ]


def body(activations, out_grad, embedding, counts, offsets, layout):
    tokens = activations[0]
    local, slots, model = tokens.shape
    groups = lax.axis_size("group")
    parts = lax.axis_size("shard")
    patches = local * parts
    own = slots // parts
    width = model // HEADS
    templates = embedding.shape[0]
    chunk = model // CHUNKS
    pairs = chunk // LANES

    layouts = [layout] + [
        lax.ppermute(layout, "group", [(i, (i + away) % groups) for i in range(groups)])
        for away in range(1, groups)
    ]
    cotangent = out_grad[0].reshape(parts, local, own, model)
    cotangent = jnp.transpose(cotangent, (2, 1, 0, 3)).reshape(own, patches, model)

    firsts = [index * chunk for index in range(CHUNKS)]
    forward = [
        pl.pallas_call(
            functools.partial(spatial_kernel, width, first),
            out_shape=(
                jax.ShapeDtypeStruct((local, slots, chunk), jnp.bfloat16),
                jax.ShapeDtypeStruct((local, pairs, slots, 2 * slots), jnp.bfloat16),
            )
            + (jax.ShapeDtypeStruct((own * local, chunk), jnp.bfloat16),) * parts,
            in_specs=[SMEM, SMEM, VMEM, VMEM, VMEM],
            out_specs=(VMEM,) * (2 + parts),
            scratch_shapes=[
                pltpu.VMEM((slots, chunk), jnp.float32),
                pltpu.VMEM((slots, 2 * slots), jnp.float32),
                pltpu.VMEM((slots * local, LANES), jnp.float32),
            ],
            compiler_params=PARAMS,
            name="spatial",
        )(counts, offsets, layout, embedding, tokens)
        for first in firsts
    ]
    gathered = [exchange(mixed) for _, _, *mixed in forward]
    mixed_grads = [
        pl.pallas_call(
            functools.partial(temporal_kernel, width, parts, first),
            out_shape=(jax.ShapeDtypeStruct((own * local, chunk), jnp.bfloat16),) * parts,
            in_specs=[VMEM] * (1 + parts),
            out_specs=(VMEM,) * parts,
            scratch_shapes=[
                pltpu.VMEM((own * patches, LANES), jnp.float32),
                pltpu.VMEM((own * patches, LANES), jnp.float32),
            ],
            compiler_params=PARAMS,
            name="temporal",
        )(cotangent, *arrived)
        for first, arrived in zip(firsts, gathered)
    ]
    returned = [exchange(blocks) for blocks in mixed_grads]
    done = []
    for index, (embedded, weights, *_) in enumerate(forward):
        done = pl.pallas_call(
            functools.partial(spatial_back_kernel, width, parts),
            grid=(1,),
            out_shape=(
                jax.ShapeDtypeStruct(tokens.shape, jnp.bfloat16),
                jax.ShapeDtypeStruct((slots, model), jnp.bfloat16),
            ),
            in_specs=[VMEM] * (2 + parts) + [pl.BlockSpec(memory_space=pl.ANY)] * len(done),
            out_specs=(
                pl.BlockSpec((local, slots, chunk), lambda i, index=index: (0, 0, index)),
                pl.BlockSpec((slots, chunk), lambda i, index=index: (0, index)),
            ),
            scratch_shapes=[pltpu.VMEM((slots * local, LANES), jnp.float32)],
            input_output_aliases={2 + parts + place: place for place in range(len(done))},
            compiler_params=PARAMS,
            name="spatial_back",
        )(embedded, weights, *returned[index], *done)
    input_grad, electrode_grad = done

    shares = lax.all_to_all(
        electrode_grad.reshape(parts, own, model), "shard", split_axis=0, concat_axis=0, tiled=True
    )
    share = jnp.sum(shares.astype(jnp.float32), axis=0).astype(jnp.bfloat16)
    everyone = lax.all_to_all(
        jnp.broadcast_to(share[None], (groups * parts, own, model)),
        ("group", "shard"),
        split_axis=0,
        concat_axis=0,
        tiled=True,
    )
    table_grad = pl.pallas_call(
        functools.partial(table_kernel, groups),
        out_shape=jax.ShapeDtypeStruct((templates // groups, model), jnp.float32),
        in_specs=[VMEM] * (groups + 1),
        out_specs=VMEM,
        compiler_params=PARAMS,
        name="table",
    )(*layouts, everyone.reshape(groups * slots, model))
    return (input_grad[None], table_grad)


def solution(mesh):
    placed = (
        P("group", "shard", None, None),
        P("group", None, "shard", None),
        P(),
        P("group", None),
        P("group", None),
        P("group", None),
    )
    return jax.shard_map(
        body,
        mesh=mesh,
        in_specs=placed,
        out_specs=(P("group", "shard", None, None), P("group", None)),
        check_vma=False,
    )
```

```python
import functools
import math

import jax
import jax.numpy as jnp
from jax import lax
from jax.experimental import pallas as pl
from jax.experimental.pallas import tpu as pltpu
from jax.sharding import PartitionSpec as P

HEADS = 16
BLOCK = 32
LANES = 128
MASKED = -1e30
STEP = 256
GROUP = 4


def dot(left, right, over):
    return lax.dot_general(
        left, right, (((over[0],), (over[1],)), ((), ())), preferred_element_type=jnp.float32
    )


def head_masks(width, scale):
    lane = lax.broadcasted_iota(jnp.int32, (1, LANES), 1)
    first = jnp.where(lane < width, scale, 0.0).astype(jnp.bfloat16)
    second = jnp.where(lane < width, 0.0, scale).astype(jnp.bfloat16)
    return first, second


def head_rows(pair, masks):
    return jnp.concatenate([pair * masks[0], pair * masks[1]], axis=0)


def head_columns(rows, width):
    count = rows.shape[0] // 2
    lane = lax.broadcasted_iota(jnp.int32, (count, rows.shape[1]), 1)
    return jnp.where(lane < width, rows[:count], rows[count:])


def each(function, *lists):
    return [function(*items) for items in zip(*lists)]


def weights_by_key(scores):
    tops = each(lambda s: jnp.max(s, axis=0, keepdims=True), scores)
    exponents = each(lambda s, t: jnp.exp(s - t), scores, tops)
    shares = each(lambda e: 1.0 / jnp.sum(e, axis=0, keepdims=True), exponents)
    return each(lambda e, r: (e * r).astype(jnp.bfloat16), exponents, shares)


def by_query(shares, values, width):
    if 2 * values[0].shape[0] != LANES or len(values) % 2:
        return each(lambda s, v: head_columns(dot(s, v, (0, 0)), width), shares, values)
    results = []
    for first in range(0, len(values), 2):
        turned = jnp.transpose(jnp.concatenate(shares[first : first + 2], axis=0))
        one, other = values[first : first + 2]
        zero = jnp.zeros_like(one)
        apart = jnp.concatenate(
            [jnp.concatenate([one, zero], axis=1), jnp.concatenate([zero, other], axis=1)], axis=0
        )
        both = dot(turned, apart, (1, 0))
        results += [head_columns(both[:, :LANES], width), head_columns(both[:, LANES:], width)]
    return results


def back(values, scaled, cotangents, weights, grad_weights, heads_grads, width):
    wide = each(lambda w: w.astype(jnp.float32), weights)
    deltas = each(lambda w, g: jnp.sum(w * g, axis=0, keepdims=True), wide, grad_weights)
    grad_scores = each(
        lambda w, g, d: (w * (g - d)).astype(jnp.bfloat16), wide, grad_weights, deltas
    )
    length = values[0].shape[0]
    whole = length % LANES == 0
    both_ways = grad_scores
    if whole:
        both_ways = each(
            lambda g: jnp.concatenate(
                [
                    g[:, start : start + length] + jnp.transpose(g[:, start : start + length])
                    for start in (0, length)
                ],
                axis=1,
            ),
            grad_scores,
        )
    grads = each(
        lambda c, w, g, hg, hv: c.astype(jnp.float32)
        + dot(jnp.concatenate([w, g], axis=1), jnp.concatenate([hg, hv], axis=0), (1, 0)),
        cotangents,
        weights,
        both_ways,
        heads_grads,
        scaled,
    )
    if whole:
        return grads
    score_scale = 0.5 / math.sqrt(width)
    rest = by_query(grad_scores, values, width)
    return each(lambda g, r: g + score_scale * r, grads, rest)


def pair_bias(counts, offsets, slots):
    def sessions(slot):
        block = slot // BLOCK
        session = jnp.full(slot.shape, -1, jnp.int32)
        for j in range(offsets.shape[1]):
            session = session + (offsets[0, j] <= block).astype(jnp.int32)
        return session

    key_slot = lax.broadcasted_iota(jnp.int32, (slots, 2 * slots), 0)
    query_slot = lax.broadcasted_iota(jnp.int32, (slots, 2 * slots), 1) % slots
    key_session = sessions(key_slot)
    first = jnp.zeros_like(key_slot)
    live = jnp.zeros_like(key_slot)
    for j in range(offsets.shape[1]):
        chosen = key_session == j
        first = jnp.where(chosen, offsets[0, j] * BLOCK, first)
        live = jnp.where(chosen, counts[0, j], live)
    allowed = (key_session == sessions(query_slot)) & (key_slot - first < live)
    return jnp.where(allowed, 0.0, MASKED)


def pairs_of(model):
    return [pl.ds(start, LANES) for start in range(0, model, LANES)]


def in_groups(count, size):
    return [range(start, min(start + size, count)) for start in range(0, count, size)]


def spatial_kernel(
    width, counts, offsets, layout, embedding, tokens,
    embedded, weights, mixed, spread, bias, by_electrode,
):
    patches, slots, model = embedded.shape
    templates = embedding.shape[0]
    score_masks = head_masks(width, 0.5 / math.sqrt(width))

    @pl.when(pl.program_id(0) == 0)
    def _():
        bias[...] = pair_bias(counts, offsets, slots)
        chosen = lax.broadcasted_iota(jnp.int32, (templates, slots), 0) == layout[...]
        spread[...] = jnp.transpose(chosen.astype(jnp.float32)).astype(jnp.bfloat16)

    rows = dot(spread[...], embedding[...], (1, 0))
    for pair, columns in enumerate(pairs_of(model)):
        added = rows[:, pair * LANES : (pair + 1) * LANES]
        for group in in_groups(patches, GROUP):
            values = [
                (tokens[p, :, columns].astype(jnp.float32) + added).astype(jnp.bfloat16)
                for p in group
            ]
            scores = each(
                lambda v: dot(v, head_rows(v, score_masks), (1, 1)) + bias[...], values
            )
            shares = weights_by_key(scores)
            attended = by_query(shares, values, width)
            for p, value, share, result in zip(group, values, shares, attended):
                embedded[p, :, columns] = value
                weights[p, pair] = share
                by_electrode[pair, pl.ds(p, slots, stride=patches), :] = (
                    value.astype(jnp.float32) + result
                )
        mixed[:, columns] = by_electrode[pair].astype(jnp.bfloat16)


def temporal_kernel(width, parts, mixed, out_grad, mixed_grad, received, returned):
    electrodes, patches, model = out_grad.shape
    local = patches // parts
    score_masks = head_masks(width, 0.5 / math.sqrt(width))
    ones = head_masks(width, 1.0)
    for pair, columns in enumerate(pairs_of(model)):
        received[pair] = mixed[:, columns].astype(jnp.float32)
        for group in in_groups(electrodes, GROUP // 2):
            places = [
                [pl.ds(e * local + p, parts, stride=electrodes * local) for p in range(local)]
                for e in group
            ]
            values = each(
                lambda place: jnp.concatenate(
                    [received[pair, rows, :] for rows in place], axis=0
                ).astype(jnp.bfloat16),
                places,
            )
            cotangents = [out_grad[e, :, columns] for e in group]
            scaled = each(lambda v: head_rows(v, score_masks), values)
            scores = each(lambda v, s: dot(v, s, (1, 1)), values, scaled)
            heads_grads = each(lambda g: head_rows(g, ones), cotangents)
            grad_weights = each(lambda v, g: dot(v, g, (1, 1)), values, heads_grads)
            shares = weights_by_key(scores)
            grads = back(values, scaled, cotangents, shares, grad_weights, heads_grads, width)
            for place, grad in zip(places, grads):
                for p, rows in enumerate(place):
                    returned[pair, rows, :] = grad[p * parts : (p + 1) * parts]
        mixed_grad[:, columns] = returned[pair].astype(jnp.bfloat16)


def spatial_back_kernel(
    width, embedded, weights, mixed_grad, input_grad, electrode_grad, received
):
    patches, slots, model = embedded.shape
    score_masks = head_masks(width, 0.5 / math.sqrt(width))
    ones = head_masks(width, 1.0)
    for pair, columns in enumerate(pairs_of(model)):
        received[pair] = mixed_grad[:, columns].astype(jnp.float32)
        total = jnp.zeros((slots, LANES), jnp.float32)
        for group in in_groups(patches, GROUP):
            cotangents = [
                received[pair, pl.ds(p, slots, stride=patches), :].astype(jnp.bfloat16)
                for p in group
            ]
            values = [embedded[p, :, columns] for p in group]
            shares = [weights[p, pair] for p in group]
            scaled = each(lambda v: head_rows(v, score_masks), values)
            heads_grads = each(lambda g: head_rows(g, ones), cotangents)
            grad_weights = each(lambda v, g: dot(v, g, (1, 1)), values, heads_grads)
            grads = back(values, scaled, cotangents, shares, grad_weights, heads_grads, width)
            for p, grad in zip(group, grads):
                input_grad[p, :, columns] = grad.astype(jnp.bfloat16)
                total = total + grad
        electrode_grad[:, columns] = total.astype(jnp.bfloat16)


def table_kernel(groups, *refs):
    layouts, sums, table = refs[:groups], refs[groups], refs[groups + 1]
    owner = lax.axis_index("group")
    rows, model = table.shape
    slots = sums.shape[0] // groups
    template = lax.broadcasted_iota(jnp.int32, (rows, slots), 0) + owner * rows
    total = jnp.zeros((rows, model), jnp.float32)
    for away in range(groups):
        spread = (template == layouts[away][...]).astype(jnp.float32).astype(jnp.bfloat16)
        origin = lax.rem(owner + groups - away, groups)
        part = sums[pl.ds(pl.multiple_of(origin * slots, slots), slots), :]
        total = total + dot(spread, part, (1, 0))
    table[...] = total


VMEM = pl.BlockSpec(memory_space=pltpu.VMEM)
SMEM = pl.BlockSpec(memory_space=pltpu.SMEM)
PARAMS = pltpu.CompilerParams(vmem_limit_bytes=32 * 1024 * 1024)


def body(activations, out_grad, embedding, counts, offsets, layout):
    tokens = activations[0]
    local, slots, model = tokens.shape
    groups = lax.axis_size("group")
    parts = lax.axis_size("shard")
    patches = local * parts
    own = slots // parts
    width = model // HEADS
    templates = embedding.shape[0]
    pairs = STEP // LANES
    steps = model // STEP

    layouts = [layout] + [
        lax.ppermute(layout, "group", [(i, (i + away) % groups) for i in range(groups)])
        for away in range(1, groups)
    ]
    cotangent = out_grad[0].reshape(parts, local, own, model)
    cotangent = jnp.transpose(cotangent, (2, 1, 0, 3)).reshape(own, patches, model)

    flat = pl.BlockSpec((slots * local, STEP), lambda step: (0, step))
    planes = pl.BlockSpec((local, slots, STEP), lambda step: (0, 0, step))
    squares = pl.BlockSpec((local, pairs, slots, 2 * slots), lambda step: (0, step, 0, 0))
    flat_shape = jax.ShapeDtypeStruct((slots * local, model), jnp.bfloat16)
    plane_shape = jax.ShapeDtypeStruct(tokens.shape, jnp.bfloat16)
    flat_scratch = pltpu.VMEM((pairs, slots * local, LANES), jnp.float32)

    embedded, weights, mixed = pl.pallas_call(
        functools.partial(spatial_kernel, width),
        grid=(steps,),
        out_shape=(
            plane_shape,
            jax.ShapeDtypeStruct((local, model // LANES, slots, 2 * slots), jnp.bfloat16),
            flat_shape,
        ),
        in_specs=[SMEM, SMEM, VMEM, pl.BlockSpec((templates, STEP), lambda step: (0, step)), planes],
        out_specs=(planes, squares, flat),
        scratch_shapes=[
            pltpu.VMEM((slots, templates), jnp.bfloat16),
            pltpu.VMEM((slots, 2 * slots), jnp.float32),
            flat_scratch,
        ],
        compiler_params=PARAMS,
        name="spatial",
    )(counts, offsets, layout, embedding, tokens)

    gathered = lax.all_to_all(mixed, "shard", split_axis=0, concat_axis=0, tiled=True)
    mixed_grad = pl.pallas_call(
        functools.partial(temporal_kernel, width, parts),
        grid=(steps,),
        out_shape=flat_shape,
        in_specs=[flat, pl.BlockSpec((own, patches, STEP), lambda step: (0, 0, step))],
        out_specs=flat,
        scratch_shapes=[flat_scratch, flat_scratch],
        compiler_params=PARAMS,
        name="temporal",
    )(gathered, cotangent)

    returned = lax.all_to_all(mixed_grad, "shard", split_axis=0, concat_axis=0, tiled=True)
    input_grad, electrode_grad = pl.pallas_call(
        functools.partial(spatial_back_kernel, width),
        grid=(steps,),
        out_shape=(plane_shape, jax.ShapeDtypeStruct((slots, model), jnp.bfloat16)),
        in_specs=[planes, squares, flat],
        out_specs=(planes, pl.BlockSpec((slots, STEP), lambda step: (0, step))),
        scratch_shapes=[flat_scratch],
        compiler_params=PARAMS,
        name="spatial_back",
    )(embedded, weights, returned)

    shares = lax.all_to_all(
        electrode_grad.reshape(parts, own, model), "shard", split_axis=0, concat_axis=0, tiled=True
    )
    share = jnp.sum(shares.astype(jnp.float32), axis=0).astype(jnp.bfloat16)
    everyone = lax.all_to_all(
        jnp.broadcast_to(share[None], (groups * parts, own, model)),
        ("group", "shard"),
        split_axis=0,
        concat_axis=0,
        tiled=True,
    )
    table_grad = pl.pallas_call(
        functools.partial(table_kernel, groups),
        out_shape=jax.ShapeDtypeStruct((templates // groups, model), jnp.float32),
        in_specs=[VMEM] * (groups + 1),
        out_specs=VMEM,
        compiler_params=PARAMS,
        name="table",
    )(*layouts, everyone.reshape(groups * slots, model))
    return (input_grad[None], table_grad)


def solution(mesh):
    placed = (
        P("group", "shard", None, None),
        P("group", None, "shard", None),
        P(),
        P("group", None),
        P("group", None),
        P("group", None),
    )
    return jax.shard_map(
        body,
        mesh=mesh,
        in_specs=placed,
        out_specs=(P("group", "shard", None, None), P("group", None)),
        check_vma=False,
    )
```

```python
import functools
import math

import jax
import jax.numpy as jnp
from jax import lax
from jax.experimental import pallas as pl
from jax.experimental.pallas import tpu as pltpu
from jax.sharding import PartitionSpec as P

HEADS = 16
BLOCK = 32
LANES = 128
MASKED = -1e30
SUBLANES = 8
STEP = 256
GROUP = 4


def dot(left, right, over):
    return lax.dot_general(
        left, right, (((over[0],), (over[1],)), ((), ())), preferred_element_type=jnp.float32
    )


def head_masks(width, scale):
    lane = lax.broadcasted_iota(jnp.int32, (1, LANES), 1)
    first = jnp.where(lane < width, scale, 0.0).astype(jnp.bfloat16)
    second = jnp.where(lane < width, 0.0, scale).astype(jnp.bfloat16)
    return first, second


def head_rows(pair, masks):
    return jnp.concatenate([pair * masks[0], pair * masks[1]], axis=0)


def head_columns(rows, width):
    count = rows.shape[0] // 2
    lane = lax.broadcasted_iota(jnp.int32, (count, rows.shape[1]), 1)
    return jnp.where(lane < width, rows[:count], rows[count:])


def each(function, *lists):
    return [function(*items) for items in zip(*lists)]


def weights_by_key(scores):
    tops = each(lambda s: jnp.max(s, axis=0, keepdims=True), scores)
    exponents = each(lambda s, t: jnp.exp(s - t), scores, tops)
    shares = each(lambda e: 1.0 / jnp.sum(e, axis=0, keepdims=True), exponents)
    return each(lambda e, r: (e * r).astype(jnp.bfloat16), exponents, shares)


def by_query(shares, values, width):
    if 2 * values[0].shape[0] != LANES or len(values) % 2:
        return each(lambda s, v: head_columns(dot(s, v, (0, 0)), width), shares, values)
    results = []
    for first in range(0, len(values), 2):
        turned = jnp.transpose(jnp.concatenate(shares[first : first + 2], axis=0))
        one, other = values[first : first + 2]
        zero = jnp.zeros_like(one)
        apart = jnp.concatenate(
            [jnp.concatenate([one, zero], axis=1), jnp.concatenate([zero, other], axis=1)], axis=0
        )
        both = dot(turned, apart, (1, 0))
        results += [head_columns(both[:, :LANES], width), head_columns(both[:, LANES:], width)]
    return results


def back(values, scaled, cotangents, weights, grad_weights, heads_grads, width):
    wide = each(lambda w: w.astype(jnp.float32), weights)
    deltas = each(lambda w, g: jnp.sum(w * g, axis=0, keepdims=True), wide, grad_weights)
    grad_scores = each(
        lambda w, g, d: (w * (g - d)).astype(jnp.bfloat16), wide, grad_weights, deltas
    )
    length = values[0].shape[0]
    whole = length % LANES == 0
    both_ways = grad_scores
    if whole:
        both_ways = each(
            lambda g: jnp.concatenate(
                [
                    g[:, start : start + length] + jnp.transpose(g[:, start : start + length])
                    for start in (0, length)
                ],
                axis=1,
            ),
            grad_scores,
        )
    grads = each(
        lambda c, w, g, hg, hv: c.astype(jnp.float32)
        + dot(jnp.concatenate([w, g], axis=1), jnp.concatenate([hg, hv], axis=0), (1, 0)),
        cotangents,
        weights,
        both_ways,
        heads_grads,
        scaled,
    )
    if whole:
        return grads
    score_scale = 0.5 / math.sqrt(width)
    rest = by_query(grad_scores, values, width)
    return each(lambda g, r: g + score_scale * r, grads, rest)


def pair_bias(counts, offsets, slots):
    def sessions(slot):
        block = slot // BLOCK
        session = jnp.full(slot.shape, -1, jnp.int32)
        for j in range(offsets.shape[1]):
            session = session + (offsets[0, j] <= block).astype(jnp.int32)
        return session

    key_slot = lax.broadcasted_iota(jnp.int32, (slots, 2 * slots), 0)
    query_slot = lax.broadcasted_iota(jnp.int32, (slots, 2 * slots), 1) % slots
    key_session = sessions(key_slot)
    first = jnp.zeros_like(key_slot)
    live = jnp.zeros_like(key_slot)
    for j in range(offsets.shape[1]):
        chosen = key_session == j
        first = jnp.where(chosen, offsets[0, j] * BLOCK, first)
        live = jnp.where(chosen, counts[0, j], live)
    allowed = (key_session == sessions(query_slot)) & (key_slot - first < live)
    return jnp.where(allowed, 0.0, MASKED)


def pairs_of(model):
    return [pl.ds(start, LANES) for start in range(0, model, LANES)]


def in_groups(count, size):
    return [range(start, min(start + size, count)) for start in range(0, count, size)]


def turned_stride(patches):
    return patches + 1 if patches % SUBLANES == 0 else patches


def turned_scratch(pairs, slots, patches):
    return pltpu.VMEM((pairs, slots * turned_stride(patches), LANES), jnp.float32)


def read_turned(ref, pair, slots, patches):
    stride = turned_stride(patches)
    if stride == patches:
        return ref[pair]
    pieces = [ref[pair, pl.ds(slot * stride, patches), :] for slot in range(slots)]
    return jnp.concatenate(pieces, axis=0)


def write_turned(ref, pair, rows, slots, patches):
    stride = turned_stride(patches)
    if stride == patches:
        ref[pair] = rows
        return
    for slot in range(slots):
        ref[pair, pl.ds(slot * stride, patches), :] = rows[slot * patches : (slot + 1) * patches]


def of_patch(patch, slots, patches):
    return pl.ds(patch, slots, stride=turned_stride(patches))


def spatial_kernel(
    width, counts, offsets, layout, embedding, tokens,
    embedded, weights, mixed, spread, bias, by_electrode,
):
    patches, slots, model = embedded.shape
    templates = embedding.shape[0]
    score_masks = head_masks(width, 0.5 / math.sqrt(width))

    @pl.when(pl.program_id(0) == 0)
    def _():
        bias[...] = pair_bias(counts, offsets, slots)
        chosen = lax.broadcasted_iota(jnp.int32, (templates, slots), 0) == layout[...]
        spread[...] = jnp.transpose(chosen.astype(jnp.float32)).astype(jnp.bfloat16)

    rows = dot(spread[...], embedding[...], (1, 0))
    for pair, columns in enumerate(pairs_of(model)):
        added = rows[:, pair * LANES : (pair + 1) * LANES]
        for group in in_groups(patches, GROUP):
            values = [
                (tokens[p, :, columns].astype(jnp.float32) + added).astype(jnp.bfloat16)
                for p in group
            ]
            scores = each(
                lambda v: dot(v, head_rows(v, score_masks), (1, 1)) + bias[...], values
            )
            shares = weights_by_key(scores)
            attended = by_query(shares, values, width)
            for p, value, share, result in zip(group, values, shares, attended):
                embedded[p, :, columns] = value
                weights[p, pair] = share
                by_electrode[pair, of_patch(p, slots, patches), :] = (
                    value.astype(jnp.float32) + result
                )
        mixed[:, columns] = read_turned(by_electrode, pair, slots, patches).astype(jnp.bfloat16)


def patches_first(local):
    return local % SUBLANES != 0


def electrode_rows(electrode, electrodes, parts, local):
    start, step = electrode * local, electrodes * local
    if patches_first(local):
        return [pl.ds(start + p, parts, stride=step) for p in range(local)]
    return [pl.ds(start + part * step, local) for part in range(parts)]


def temporal_kernel(width, parts, mixed, out_grad, mixed_grad, received, returned):
    electrodes, patches, model = out_grad.shape
    local = patches // parts
    score_masks = head_masks(width, 0.5 / math.sqrt(width))
    ones = head_masks(width, 1.0)
    for pair, columns in enumerate(pairs_of(model)):
        received[pair] = mixed[:, columns].astype(jnp.float32)
        for group in in_groups(electrodes, GROUP // 2):
            places = [electrode_rows(e, electrodes, parts, local) for e in group]
            values = each(
                lambda place: jnp.concatenate(
                    [received[pair, rows, :] for rows in place], axis=0
                ).astype(jnp.bfloat16),
                places,
            )
            cotangents = [out_grad[e, :, columns] for e in group]
            scaled = each(lambda v: head_rows(v, score_masks), values)
            scores = each(lambda v, s: dot(v, s, (1, 1)), values, scaled)
            heads_grads = each(lambda g: head_rows(g, ones), cotangents)
            grad_weights = each(lambda v, g: dot(v, g, (1, 1)), values, heads_grads)
            shares = weights_by_key(scores)
            grads = back(values, scaled, cotangents, shares, grad_weights, heads_grads, width)
            for place, grad in zip(places, grads):
                start = 0
                for rows in place:
                    returned[pair, rows, :] = grad[start : start + rows.size]
                    start += rows.size
        mixed_grad[:, columns] = returned[pair].astype(jnp.bfloat16)


def spatial_back_kernel(
    width, embedded, weights, mixed_grad, input_grad, electrode_grad, received
):
    patches, slots, model = embedded.shape
    score_masks = head_masks(width, 0.5 / math.sqrt(width))
    ones = head_masks(width, 1.0)
    for pair, columns in enumerate(pairs_of(model)):
        arrived = mixed_grad[:, columns].astype(jnp.float32)
        write_turned(received, pair, arrived, slots, patches)
        total = jnp.zeros((slots, LANES), jnp.float32)
        for group in in_groups(patches, GROUP):
            cotangents = [
                received[pair, of_patch(p, slots, patches), :].astype(jnp.bfloat16)
                for p in group
            ]
            values = [embedded[p, :, columns] for p in group]
            shares = [weights[p, pair] for p in group]
            scaled = each(lambda v: head_rows(v, score_masks), values)
            heads_grads = each(lambda g: head_rows(g, ones), cotangents)
            grad_weights = each(lambda v, g: dot(v, g, (1, 1)), values, heads_grads)
            grads = back(values, scaled, cotangents, shares, grad_weights, heads_grads, width)
            for p, grad in zip(group, grads):
                input_grad[p, :, columns] = grad.astype(jnp.bfloat16)
                total = total + grad
        electrode_grad[:, columns] = total.astype(jnp.bfloat16)


def table_kernel(groups, *refs):
    layouts, sums, table = refs[:groups], refs[groups], refs[groups + 1]
    owner = lax.axis_index("group")
    rows, model = table.shape
    slots = sums.shape[0] // groups
    template = lax.broadcasted_iota(jnp.int32, (rows, slots), 0) + owner * rows
    total = jnp.zeros((rows, model), jnp.float32)
    for away in range(groups):
        spread = (template == layouts[away][...]).astype(jnp.float32).astype(jnp.bfloat16)
        origin = lax.rem(owner + groups - away, groups)
        part = sums[pl.ds(pl.multiple_of(origin * slots, slots), slots), :]
        total = total + dot(spread, part, (1, 0))
    table[...] = total


VMEM = pl.BlockSpec(memory_space=pltpu.VMEM)
SMEM = pl.BlockSpec(memory_space=pltpu.SMEM)
PARAMS = pltpu.CompilerParams(vmem_limit_bytes=32 * 1024 * 1024)


def body(activations, out_grad, embedding, counts, offsets, layout):
    tokens = activations[0]
    local, slots, model = tokens.shape
    groups = lax.axis_size("group")
    parts = lax.axis_size("shard")
    patches = local * parts
    own = slots // parts
    width = model // HEADS
    templates = embedding.shape[0]
    pairs = STEP // LANES
    steps = model // STEP

    layouts = [layout] + [
        lax.ppermute(layout, "group", [(i, (i + away) % groups) for i in range(groups)])
        for away in range(1, groups)
    ]
    order = (2, 1, 0, 3) if patches_first(local) else (2, 0, 1, 3)
    cotangent = jnp.transpose(out_grad[0].reshape(parts, local, own, model), order)
    cotangent = cotangent.reshape(own, patches, model)

    flat = pl.BlockSpec((slots * local, STEP), lambda step: (0, step))
    planes = pl.BlockSpec((local, slots, STEP), lambda step: (0, 0, step))
    squares = pl.BlockSpec((local, pairs, slots, 2 * slots), lambda step: (0, step, 0, 0))
    flat_shape = jax.ShapeDtypeStruct((slots * local, model), jnp.bfloat16)
    plane_shape = jax.ShapeDtypeStruct(tokens.shape, jnp.bfloat16)
    flat_scratch = pltpu.VMEM((pairs, slots * local, LANES), jnp.float32)
    turned = turned_scratch(pairs, slots, local)

    embedded, weights, mixed = pl.pallas_call(
        functools.partial(spatial_kernel, width),
        grid=(steps,),
        out_shape=(
            plane_shape,
            jax.ShapeDtypeStruct((local, model // LANES, slots, 2 * slots), jnp.bfloat16),
            flat_shape,
        ),
        in_specs=[SMEM, SMEM, VMEM, pl.BlockSpec((templates, STEP), lambda step: (0, step)), planes],
        out_specs=(planes, squares, flat),
        scratch_shapes=[
            pltpu.VMEM((slots, templates), jnp.bfloat16),
            pltpu.VMEM((slots, 2 * slots), jnp.float32),
            turned,
        ],
        compiler_params=pltpu.CompilerParams(vmem_limit_bytes=56 * 1024 * 1024),
        name="spatial",
    )(counts, offsets, layout, embedding, tokens)

    gathered = lax.all_to_all(mixed, "shard", split_axis=0, concat_axis=0, tiled=True)
    mixed_grad = pl.pallas_call(
        functools.partial(temporal_kernel, width, parts),
        grid=(steps,),
        out_shape=flat_shape,
        in_specs=[flat, pl.BlockSpec((own, patches, STEP), lambda step: (0, 0, step))],
        out_specs=flat,
        scratch_shapes=[flat_scratch, flat_scratch],
        compiler_params=PARAMS,
        name="temporal",
    )(gathered, cotangent)

    returned = lax.all_to_all(mixed_grad, "shard", split_axis=0, concat_axis=0, tiled=True)
    input_grad, electrode_grad = pl.pallas_call(
        functools.partial(spatial_back_kernel, width),
        grid=(steps,),
        out_shape=(plane_shape, jax.ShapeDtypeStruct((slots, model), jnp.bfloat16)),
        in_specs=[planes, squares, flat],
        out_specs=(planes, pl.BlockSpec((slots, STEP), lambda step: (0, step))),
        scratch_shapes=[turned],
        compiler_params=PARAMS,
        name="spatial_back",
    )(embedded, weights, returned)

    shares = lax.all_to_all(
        electrode_grad.reshape(parts, own, model), "shard", split_axis=0, concat_axis=0, tiled=True
    )
    share = jnp.sum(shares.astype(jnp.float32), axis=0).astype(jnp.bfloat16)
    everyone = lax.all_to_all(
        jnp.broadcast_to(share[None], (groups * parts, own, model)),
        ("group", "shard"),
        split_axis=0,
        concat_axis=0,
        tiled=True,
    )
    table_grad = pl.pallas_call(
        functools.partial(table_kernel, groups),
        out_shape=jax.ShapeDtypeStruct((templates // groups, model), jnp.float32),
        in_specs=[VMEM] * (groups + 1),
        out_specs=VMEM,
        compiler_params=PARAMS,
        name="table",
    )(*layouts, everyone.reshape(groups * slots, model))
    return (input_grad[None], table_grad)


def solution(mesh):
    placed = (
        P("group", "shard", None, None),
        P("group", None, "shard", None),
        P(),
        P("group", None),
        P("group", None),
        P("group", None),
    )
    return jax.shard_map(
        body,
        mesh=mesh,
        in_specs=placed,
        out_specs=(P("group", "shard", None, None), P("group", None)),
        check_vma=False,
    )
```

```python
import functools
import math

import jax
import jax.numpy as jnp
from jax import lax
from jax.experimental import pallas as pl
from jax.experimental.pallas import tpu as pltpu
from jax.sharding import PartitionSpec as P

HEADS = 16
BLOCK = 32
LANES = 128
MASKED = -1e30
SUBLANES = 8
STEP = 256
GROUP = 4


def dot(left, right, over):
    return lax.dot_general(
        left, right, (((over[0],), (over[1],)), ((), ())), preferred_element_type=jnp.float32
    )


def head_masks(width, scale):
    lane = lax.broadcasted_iota(jnp.int32, (1, LANES), 1)
    first = jnp.where(lane < width, scale, 0.0).astype(jnp.bfloat16)
    second = jnp.where(lane < width, 0.0, scale).astype(jnp.bfloat16)
    return first, second


def head_rows(pair, masks):
    return jnp.concatenate([pair * masks[0], pair * masks[1]], axis=0)


def head_blocks(pair, width):
    turned = jnp.transpose(pair)
    zero = jnp.zeros((width, pair.shape[0]), pair.dtype)
    return jnp.concatenate(
        [
            jnp.concatenate([turned[:width], zero], axis=0),
            jnp.concatenate([zero, turned[width:]], axis=0),
        ],
        axis=1,
    )


def head_columns(rows, width):
    count = rows.shape[0] // 2
    lane = lax.broadcasted_iota(jnp.int32, (count, rows.shape[1]), 1)
    return jnp.where(lane < width, rows[:count], rows[count:])


def each(function, *lists):
    return [function(*items) for items in zip(*lists)]


def weights_by_key(scores):
    tops = each(lambda s: jnp.max(s, axis=0, keepdims=True), scores)
    exponents = each(lambda s, t: jnp.exp(s - t), scores, tops)
    shares = each(lambda e: 1.0 / jnp.sum(e, axis=0, keepdims=True), exponents)
    return each(lambda e, r: (e * r).astype(jnp.bfloat16), exponents, shares)


def by_query(shares, values, width):
    if 2 * values[0].shape[0] != LANES or len(values) % 2:
        return each(lambda s, v: head_columns(dot(s, v, (0, 0)), width), shares, values)
    results = []
    for first in range(0, len(values), 2):
        turned = jnp.transpose(jnp.concatenate(shares[first : first + 2], axis=0))
        one, other = values[first : first + 2]
        zero = jnp.zeros_like(one)
        apart = jnp.concatenate(
            [jnp.concatenate([one, zero], axis=1), jnp.concatenate([zero, other], axis=1)], axis=0
        )
        both = dot(turned, apart, (1, 0))
        results += [head_columns(both[:, :LANES], width), head_columns(both[:, LANES:], width)]
    return results


def back(values, scaled, cotangents, weights, grad_weights, heads_grads, width):
    wide = each(lambda w: w.astype(jnp.float32), weights)
    deltas = each(lambda w, g: jnp.sum(w * g, axis=0, keepdims=True), wide, grad_weights)
    grad_scores = each(
        lambda w, g, d: (w * (g - d)).astype(jnp.bfloat16), wide, grad_weights, deltas
    )
    length = values[0].shape[0]
    whole = length % LANES == 0
    both_ways = grad_scores
    if whole:
        both_ways = each(
            lambda g: jnp.concatenate(
                [
                    g[:, start : start + length] + jnp.transpose(g[:, start : start + length])
                    for start in (0, length)
                ],
                axis=1,
            ),
            grad_scores,
        )
    grads = each(
        lambda c, w, g, hg, hv: c.astype(jnp.float32)
        + dot(jnp.concatenate([w, g], axis=1), jnp.concatenate([hg, hv], axis=0), (1, 0)),
        cotangents,
        weights,
        both_ways,
        heads_grads,
        scaled,
    )
    if whole:
        return grads
    score_scale = 0.5 / math.sqrt(width)
    rest = by_query(grad_scores, values, width)
    return each(lambda g, r: g + score_scale * r, grads, rest)


def pair_bias(counts, offsets, slots):
    def sessions(slot):
        block = slot // BLOCK
        session = jnp.full(slot.shape, -1, jnp.int32)
        for j in range(offsets.shape[1]):
            session = session + (offsets[0, j] <= block).astype(jnp.int32)
        return session

    key_slot = lax.broadcasted_iota(jnp.int32, (slots, 2 * slots), 0)
    query_slot = lax.broadcasted_iota(jnp.int32, (slots, 2 * slots), 1) % slots
    key_session = sessions(key_slot)
    first = jnp.zeros_like(key_slot)
    live = jnp.zeros_like(key_slot)
    for j in range(offsets.shape[1]):
        chosen = key_session == j
        first = jnp.where(chosen, offsets[0, j] * BLOCK, first)
        live = jnp.where(chosen, counts[0, j], live)
    allowed = (key_session == sessions(query_slot)) & (key_slot - first < live)
    return jnp.where(allowed, 0.0, MASKED)


def pairs_of(model):
    return [pl.ds(start, LANES) for start in range(0, model, LANES)]


def in_groups(count, size):
    return [range(start, min(start + size, count)) for start in range(0, count, size)]


def turned_stride(patches):
    return patches + 1 if patches % SUBLANES == 0 else patches


def turned_scratch(pairs, slots, patches):
    return pltpu.VMEM((pairs, slots * turned_stride(patches), LANES), jnp.float32)


def read_turned(ref, pair, slots, patches):
    stride = turned_stride(patches)
    if stride == patches:
        return ref[pair]
    pieces = [ref[pair, pl.ds(slot * stride, patches), :] for slot in range(slots)]
    return jnp.concatenate(pieces, axis=0)


def write_turned(ref, pair, rows, slots, patches):
    stride = turned_stride(patches)
    if stride == patches:
        ref[pair] = rows
        return
    for slot in range(slots):
        ref[pair, pl.ds(slot * stride, patches), :] = rows[slot * patches : (slot + 1) * patches]


def of_patch(patch, slots, patches):
    return pl.ds(patch, slots, stride=turned_stride(patches))


def attention(width, tokens, added, bias, group, columns):
    score_masks = head_masks(width, 0.5 / math.sqrt(width))
    values = [
        (tokens[p, :, columns].astype(jnp.float32) + added).astype(jnp.bfloat16) for p in group
    ]
    scores = each(lambda v: dot(v, head_rows(v, score_masks), (1, 1)) + bias[...], values)
    return values, weights_by_key(scores)


def spatial_kernel(
    width, counts, offsets, layout, embedding, tokens, rows, mixed, spread, bias, by_electrode
):
    patches, slots, model = tokens.shape
    templates = embedding.shape[0]

    @pl.when(pl.program_id(0) == 0)
    def _():
        bias[...] = pair_bias(counts, offsets, slots)
        chosen = lax.broadcasted_iota(jnp.int32, (templates, slots), 0) == layout[...]
        spread[...] = jnp.transpose(chosen.astype(jnp.float32)).astype(jnp.bfloat16)

    chosen_rows = dot(spread[...], embedding[...], (1, 0))
    rows[...] = chosen_rows.astype(jnp.bfloat16)
    for pair, columns in enumerate(pairs_of(model)):
        added = chosen_rows[:, pair * LANES : (pair + 1) * LANES]
        for group in in_groups(patches, GROUP):
            values, shares = attention(width, tokens, added, bias, group, columns)
            attended = by_query(shares, values, width)
            for p, value, result in zip(group, values, attended):
                by_electrode[pair, of_patch(p, slots, patches), :] = (
                    value.astype(jnp.float32) + result
                )
        mixed[:, columns] = read_turned(by_electrode, pair, slots, patches).astype(jnp.bfloat16)


def weights_kernel(width, counts, offsets, rows, tokens, embedded, weights, bias):
    patches, slots, model = tokens.shape

    @pl.when(pl.program_id(0) == 0)
    def _():
        bias[...] = pair_bias(counts, offsets, slots)

    for pair, columns in enumerate(pairs_of(model)):
        added = rows[:, columns].astype(jnp.float32)
        for group in in_groups(patches, GROUP):
            values, shares = attention(width, tokens, added, bias, group, columns)
            for p, value, share in zip(group, values, shares):
                embedded[p, :, columns] = value
                weights[p, pair] = share


def patches_first(local):
    return local % SUBLANES != 0


def electrode_rows(electrode, electrodes, parts, local):
    start, step = electrode * local, electrodes * local
    if patches_first(local):
        return [pl.ds(start + p, parts, stride=step) for p in range(local)]
    return [pl.ds(start + part * step, local) for part in range(parts)]


def temporal_kernel(width, parts, mixed, out_grad, mixed_grad, received, returned):
    electrodes, patches, model = out_grad.shape
    local = patches // parts
    score_masks = head_masks(width, 0.5 / math.sqrt(width))
    ones = head_masks(width, 1.0)
    score_scale = jnp.asarray(0.5 / math.sqrt(width), jnp.bfloat16)
    for pair, columns in enumerate(pairs_of(model)):
        received[pair] = mixed[:, columns].astype(jnp.float32)
        for group in in_groups(electrodes, GROUP // 2):
            places = [electrode_rows(e, electrodes, parts, local) for e in group]
            values = each(
                lambda place: jnp.concatenate(
                    [received[pair, rows, :] for rows in place], axis=0
                ).astype(jnp.bfloat16),
                places,
            )
            cotangents = [out_grad[e, :, columns] for e in group]
            scaled = each(lambda v: head_rows(v, score_masks), values)
            heads_grads = each(lambda g: head_rows(g, ones), cotangents)
            scaled_values = each(lambda v: v * score_scale, values)
            scores = each(lambda v, s: dot(v, head_blocks(s, width), (1, 0)), values, scaled_values)
            grad_weights = each(
                lambda v, g: dot(v, head_blocks(g, width), (1, 0)), values, cotangents
            )
            shares = weights_by_key(scores)
            grads = back(values, scaled, cotangents, shares, grad_weights, heads_grads, width)
            for place, grad in zip(places, grads):
                start = 0
                for rows in place:
                    returned[pair, rows, :] = grad[start : start + rows.size]
                    start += rows.size
        mixed_grad[:, columns] = returned[pair].astype(jnp.bfloat16)


def spatial_back_kernel(
    width, embedded, weights, mixed_grad, input_grad, electrode_grad, received
):
    patches, slots, model = embedded.shape
    score_masks = head_masks(width, 0.5 / math.sqrt(width))
    ones = head_masks(width, 1.0)
    for pair, columns in enumerate(pairs_of(model)):
        arrived = mixed_grad[:, columns].astype(jnp.float32)
        write_turned(received, pair, arrived, slots, patches)
        total = jnp.zeros((slots, LANES), jnp.float32)
        for group in in_groups(patches, 2 * GROUP):
            cotangents = [
                received[pair, of_patch(p, slots, patches), :].astype(jnp.bfloat16)
                for p in group
            ]
            values = [embedded[p, :, columns] for p in group]
            shares = [weights[p, pair] for p in group]
            scaled = each(lambda v: head_rows(v, score_masks), values)
            heads_grads = each(lambda g: head_rows(g, ones), cotangents)
            grad_weights = each(lambda v, g: dot(v, g, (1, 1)), values, heads_grads)
            grads = back(values, scaled, cotangents, shares, grad_weights, heads_grads, width)
            for p, grad in zip(group, grads):
                input_grad[p, :, columns] = grad.astype(jnp.bfloat16)
                total = total + grad
        electrode_grad[:, columns] = total.astype(jnp.bfloat16)


def table_kernel(groups, *refs):
    layouts, sums, table = refs[:groups], refs[groups], refs[groups + 1]
    owner = lax.axis_index("group")
    rows, model = table.shape
    slots = sums.shape[0] // groups
    template = lax.broadcasted_iota(jnp.int32, (rows, slots), 0) + owner * rows
    total = jnp.zeros((rows, model), jnp.float32)
    for away in range(groups):
        spread = (template == layouts[away][...]).astype(jnp.float32).astype(jnp.bfloat16)
        origin = lax.rem(owner + groups - away, groups)
        part = sums[pl.ds(pl.multiple_of(origin * slots, slots), slots), :]
        total = total + dot(spread, part, (1, 0))
    table[...] = total


VMEM = pl.BlockSpec(memory_space=pltpu.VMEM)
SMEM = pl.BlockSpec(memory_space=pltpu.SMEM)
PARAMS = pltpu.CompilerParams(vmem_limit_bytes=32 * 1024 * 1024)


def body(activations, out_grad, embedding, counts, offsets, layout):
    tokens = activations[0]
    local, slots, model = tokens.shape
    groups = lax.axis_size("group")
    parts = lax.axis_size("shard")
    patches = local * parts
    own = slots // parts
    width = model // HEADS
    templates = embedding.shape[0]
    pairs = STEP // LANES
    steps = model // STEP

    layouts = [layout] + [
        lax.ppermute(layout, "group", [(i, (i + away) % groups) for i in range(groups)])
        for away in range(1, groups)
    ]
    order = (2, 1, 0, 3) if patches_first(local) else (2, 0, 1, 3)
    cotangent = jnp.transpose(out_grad[0].reshape(parts, local, own, model), order)
    cotangent = cotangent.reshape(own, patches, model)

    flat = pl.BlockSpec((slots * local, STEP), lambda step: (0, step))
    planes = pl.BlockSpec((local, slots, STEP), lambda step: (0, 0, step))
    squares = pl.BlockSpec((local, pairs, slots, 2 * slots), lambda step: (0, step, 0, 0))
    flat_shape = jax.ShapeDtypeStruct((slots * local, model), jnp.bfloat16)
    plane_shape = jax.ShapeDtypeStruct(tokens.shape, jnp.bfloat16)
    flat_scratch = pltpu.VMEM((pairs, slots * local, LANES), jnp.float32)
    turned = turned_scratch(pairs, slots, local)

    strip = pl.BlockSpec((slots, STEP), lambda step: (0, step))
    strip_shape = jax.ShapeDtypeStruct((slots, model), jnp.bfloat16)
    rows, mixed = pl.pallas_call(
        functools.partial(spatial_kernel, width),
        grid=(steps,),
        out_shape=(strip_shape, flat_shape),
        in_specs=[SMEM, SMEM, VMEM, pl.BlockSpec((templates, STEP), lambda step: (0, step)), planes],
        out_specs=(strip, flat),
        scratch_shapes=[
            pltpu.VMEM((slots, templates), jnp.bfloat16),
            pltpu.VMEM((slots, 2 * slots), jnp.float32),
            turned,
        ],
        compiler_params=pltpu.CompilerParams(vmem_limit_bytes=56 * 1024 * 1024),
        name="spatial",
    )(counts, offsets, layout, embedding, tokens)
    embedded, weights = pl.pallas_call(
        functools.partial(weights_kernel, width),
        grid=(steps,),
        out_shape=(
            plane_shape,
            jax.ShapeDtypeStruct((local, model // LANES, slots, 2 * slots), jnp.bfloat16),
        ),
        in_specs=[SMEM, SMEM, strip, planes],
        out_specs=(planes, squares),
        scratch_shapes=[pltpu.VMEM((slots, 2 * slots), jnp.float32)],
        compiler_params=PARAMS,
        cost_estimate=pl.CostEstimate(
            flops=4 * local * slots * slots * model, bytes_accessed=6 * tokens.size, transcendentals=0
        ),
        name="weights",
    )(counts, offsets, rows, tokens)

    gathered = lax.all_to_all(mixed, "shard", split_axis=0, concat_axis=0, tiled=True)
    mixed_grad = pl.pallas_call(
        functools.partial(temporal_kernel, width, parts),
        grid=(steps,),
        out_shape=flat_shape,
        in_specs=[flat, pl.BlockSpec((own, patches, STEP), lambda step: (0, 0, step))],
        out_specs=flat,
        scratch_shapes=[flat_scratch, flat_scratch],
        compiler_params=PARAMS,
        name="temporal",
    )(gathered, cotangent)

    returned = lax.all_to_all(mixed_grad, "shard", split_axis=0, concat_axis=0, tiled=True)
    input_grad, electrode_grad = pl.pallas_call(
        functools.partial(spatial_back_kernel, width),
        grid=(steps,),
        out_shape=(plane_shape, strip_shape),
        in_specs=[planes, squares, flat],
        out_specs=(planes, strip),
        scratch_shapes=[turned],
        compiler_params=PARAMS,
        name="spatial_back",
    )(embedded, weights, returned)

    shares = lax.all_to_all(
        electrode_grad.reshape(parts, own, model), "shard", split_axis=0, concat_axis=0, tiled=True
    )
    share = jnp.sum(shares.astype(jnp.float32), axis=0).astype(jnp.bfloat16)
    everyone = lax.all_to_all(
        jnp.broadcast_to(share[None], (groups * parts, own, model)),
        ("group", "shard"),
        split_axis=0,
        concat_axis=0,
        tiled=True,
    )
    table_grad = pl.pallas_call(
        functools.partial(table_kernel, groups),
        out_shape=jax.ShapeDtypeStruct((templates // groups, model), jnp.float32),
        in_specs=[VMEM] * (groups + 1),
        out_specs=VMEM,
        compiler_params=PARAMS,
        name="table",
    )(*layouts, everyone.reshape(groups * slots, model))
    return (input_grad[None], table_grad)


def solution(mesh):
    placed = (
        P("group", "shard", None, None),
        P("group", None, "shard", None),
        P(),
        P("group", None),
        P("group", None),
        P("group", None),
    )
    return jax.shard_map(
        body,
        mesh=mesh,
        in_specs=placed,
        out_specs=(P("group", "shard", None, None), P("group", None)),
        check_vma=False,
    )
```

```python
import functools
import math

import jax
import jax.numpy as jnp
from jax import lax
from jax.experimental import pallas as pl
from jax.experimental.pallas import tpu as pltpu
from jax.sharding import PartitionSpec as P

HEADS = 16
BLOCK = 32
LANES = 128
MASKED = -1e30
SUBLANES = 8
STEP = 256
SPATIAL_GROUP = 16
TEMPORAL_GROUP = 4


def dot(left, right, over):
    return lax.dot_general(
        left, right, (((over[0],), (over[1],)), ((), ())), preferred_element_type=jnp.float32
    )


def head_masks(width, scale):
    lane = lax.broadcasted_iota(jnp.int32, (1, LANES), 1)
    first = jnp.where(lane < width, scale, 0.0).astype(jnp.bfloat16)
    second = jnp.where(lane < width, 0.0, scale).astype(jnp.bfloat16)
    return first, second


def head_rows(pair, masks):
    return jnp.concatenate([pair * masks[0], pair * masks[1]], axis=0)


def head_columns(rows, width):
    count = rows.shape[0] // 2
    lane = lax.broadcasted_iota(jnp.int32, (count, rows.shape[1]), 1)
    return jnp.where(lane < width, rows[:count], rows[count:])


def each(function, *lists):
    return [function(*items) for items in zip(*lists)]


def weights_by_key(scores):
    tops = each(lambda s: jnp.max(s, axis=0, keepdims=True), scores)
    exponents = each(lambda s, t: jnp.exp(s - t), scores, tops)
    shares = each(lambda e: 1.0 / jnp.sum(e, axis=0, keepdims=True), exponents)
    return each(lambda e, r: (e * r).astype(jnp.bfloat16), exponents, shares)


def by_query(shares, values, width):
    if 2 * values[0].shape[0] != LANES or len(values) % 2:
        return each(lambda s, v: head_columns(dot(s, v, (0, 0)), width), shares, values)
    results = []
    for first in range(0, len(values), 2):
        turned = jnp.transpose(jnp.concatenate(shares[first : first + 2], axis=0))
        one, other = values[first : first + 2]
        zero = jnp.zeros_like(one)
        apart = jnp.concatenate(
            [jnp.concatenate([one, zero], axis=1), jnp.concatenate([zero, other], axis=1)], axis=0
        )
        both = dot(turned, apart, (1, 0))
        results += [head_columns(both[:, :LANES], width), head_columns(both[:, LANES:], width)]
    return results


def back(values, scaled, cotangents, weights, grad_weights, heads_grads, width):
    wide = each(lambda w: w.astype(jnp.float32), weights)
    deltas = each(lambda w, g: jnp.sum(w * g, axis=0, keepdims=True), wide, grad_weights)
    grad_scores = each(
        lambda w, g, d: (w * (g - d)).astype(jnp.bfloat16), wide, grad_weights, deltas
    )
    length = values[0].shape[0]
    whole = length % LANES == 0
    both_ways = grad_scores
    if whole:
        both_ways = each(
            lambda g: jnp.concatenate(
                [
                    g[:, start : start + length] + jnp.transpose(g[:, start : start + length])
                    for start in (0, length)
                ],
                axis=1,
            ),
            grad_scores,
        )
    grads = each(
        lambda c, w, g, hg, hv: c.astype(jnp.float32)
        + dot(jnp.concatenate([w, g], axis=1), jnp.concatenate([hg, hv], axis=0), (1, 0)),
        cotangents,
        weights,
        both_ways,
        heads_grads,
        scaled,
    )
    if whole:
        return grads
    score_scale = 0.5 / math.sqrt(width)
    rest = by_query(grad_scores, values, width)
    return each(lambda g, r: g + score_scale * r, grads, rest)


def pair_bias(counts, offsets, slots):
    def sessions(slot):
        block = slot // BLOCK
        session = jnp.full(slot.shape, -1, jnp.int32)
        for j in range(offsets.shape[1]):
            session = session + (offsets[0, j] <= block).astype(jnp.int32)
        return session

    key_slot = lax.broadcasted_iota(jnp.int32, (slots, 2 * slots), 0)
    query_slot = lax.broadcasted_iota(jnp.int32, (slots, 2 * slots), 1) % slots
    key_session = sessions(key_slot)
    first = jnp.zeros_like(key_slot)
    live = jnp.zeros_like(key_slot)
    for j in range(offsets.shape[1]):
        chosen = key_session == j
        first = jnp.where(chosen, offsets[0, j] * BLOCK, first)
        live = jnp.where(chosen, counts[0, j], live)
    allowed = (key_session == sessions(query_slot)) & (key_slot - first < live)
    return jnp.where(allowed, 0.0, MASKED)


def pair_columns(pair):
    return pl.ds(pair * LANES, LANES)


def in_groups(pairs, rows, size):
    items = [(pair, row) for pair in range(pairs) for row in range(rows)]
    return [items[start : start + size] for start in range(0, len(items), size)]


def turned_stride(patches):
    return patches + 1 if patches % SUBLANES == 0 else patches


def turned_scratch(pairs, slots, patches):
    return pltpu.VMEM((pairs, slots * turned_stride(patches), LANES), jnp.float32)


def read_turned(ref, pair, slots, patches):
    stride = turned_stride(patches)
    if stride == patches:
        return ref[pair]
    pieces = [ref[pair, pl.ds(slot * stride, patches), :] for slot in range(slots)]
    return jnp.concatenate(pieces, axis=0)


def write_turned(ref, pair, rows, slots, patches):
    stride = turned_stride(patches)
    if stride == patches:
        ref[pair] = rows
        return
    for slot in range(slots):
        ref[pair, pl.ds(slot * stride, patches), :] = rows[slot * patches : (slot + 1) * patches]


def of_patch(patch, slots, patches):
    return pl.ds(patch, slots, stride=turned_stride(patches))


def attention(width, tokens, rows, bias, group):
    score_masks = head_masks(width, 0.5 / math.sqrt(width))
    values = [
        (
            tokens[p, :, pair_columns(pair)].astype(jnp.float32)
            + rows[:, pair * LANES : (pair + 1) * LANES]
        ).astype(jnp.bfloat16)
        for pair, p in group
    ]
    scores = each(lambda v: dot(v, head_rows(v, score_masks), (1, 1)) + bias[...], values)
    return values, weights_by_key(scores)


def spatial_kernel(
    width, counts, offsets, layout, embedding, tokens, rows, mixed, spread, bias, by_electrode
):
    patches, slots, model = tokens.shape
    templates = embedding.shape[0]
    pairs = model // LANES

    @pl.when(pl.program_id(0) == 0)
    def _():
        bias[...] = pair_bias(counts, offsets, slots)
        chosen = lax.broadcasted_iota(jnp.int32, (templates, slots), 0) == layout[...]
        spread[...] = jnp.transpose(chosen.astype(jnp.float32)).astype(jnp.bfloat16)

    chosen_rows = dot(spread[...], embedding[...], (1, 0))
    rows[...] = chosen_rows.astype(jnp.bfloat16)
    for group in in_groups(pairs, patches, SPATIAL_GROUP):
        values, shares = attention(width, tokens, chosen_rows, bias, group)
        attended = by_query(shares, values, width)
        for (pair, p), value, result in zip(group, values, attended):
            by_electrode[pair, of_patch(p, slots, patches), :] = value.astype(jnp.float32) + result
    for pair in range(pairs):
        mixed[:, pair_columns(pair)] = read_turned(by_electrode, pair, slots, patches).astype(
            jnp.bfloat16
        )


def weights_kernel(width, counts, offsets, rows, tokens, embedded, weights, bias):
    patches, slots, model = tokens.shape

    @pl.when(pl.program_id(0) == 0)
    def _():
        bias[...] = pair_bias(counts, offsets, slots)

    added = rows[...].astype(jnp.float32)
    for group in in_groups(model // LANES, patches, SPATIAL_GROUP):
        values, shares = attention(width, tokens, added, bias, group)
        for (pair, p), value, share in zip(group, values, shares):
            embedded[p, :, pair_columns(pair)] = value
            weights[p, pair] = share


def patches_first(local):
    return local % SUBLANES != 0


def electrode_rows(electrode, electrodes, parts, local):
    start, step = electrode * local, electrodes * local
    if patches_first(local):
        return [pl.ds(start + p, parts, stride=step) for p in range(local)]
    return [pl.ds(start + part * step, local) for part in range(parts)]


def temporal_kernel(width, parts, mixed, out_grad, mixed_grad, received, returned):
    electrodes, patches, model = out_grad.shape
    local = patches // parts
    pairs = model // LANES
    score_masks = head_masks(width, 0.5 / math.sqrt(width))
    ones = head_masks(width, 1.0)
    for pair in range(pairs):
        received[pair] = mixed[:, pair_columns(pair)].astype(jnp.float32)
    for group in in_groups(pairs, electrodes, TEMPORAL_GROUP):
        places = [electrode_rows(e, electrodes, parts, local) for _, e in group]
        values = each(
            lambda item, place: jnp.concatenate(
                [received[item[0], rows, :] for rows in place], axis=0
            ).astype(jnp.bfloat16),
            group,
            places,
        )
        cotangents = [out_grad[e, :, pair_columns(pair)] for pair, e in group]
        scaled = each(lambda v: head_rows(v, score_masks), values)
        scores = each(lambda v, s: dot(v, s, (1, 1)), values, scaled)
        heads_grads = each(lambda g: head_rows(g, ones), cotangents)
        grad_weights = each(lambda v, g: dot(v, g, (1, 1)), values, heads_grads)
        shares = weights_by_key(scores)
        grads = back(values, scaled, cotangents, shares, grad_weights, heads_grads, width)
        for (pair, _), place, grad in zip(group, places, grads):
            start = 0
            for rows in place:
                returned[pair, rows, :] = grad[start : start + rows.size]
                start += rows.size
    for pair in range(pairs):
        mixed_grad[:, pair_columns(pair)] = returned[pair].astype(jnp.bfloat16)


def spatial_back_kernel(
    width, embedded, weights, mixed_grad, input_grad, electrode_grad, received
):
    patches, slots, model = embedded.shape
    pairs = model // LANES
    score_masks = head_masks(width, 0.5 / math.sqrt(width))
    ones = head_masks(width, 1.0)
    totals = [jnp.zeros((slots, LANES), jnp.float32) for _ in range(pairs)]
    for pair in range(pairs):
        arrived = mixed_grad[:, pair_columns(pair)].astype(jnp.float32)
        write_turned(received, pair, arrived, slots, patches)
    for group in in_groups(pairs, patches, SPATIAL_GROUP):
        cotangents = [
            received[pair, of_patch(p, slots, patches), :].astype(jnp.bfloat16)
            for pair, p in group
        ]
        values = [embedded[p, :, pair_columns(pair)] for pair, p in group]
        shares = [weights[p, pair] for pair, p in group]
        scaled = each(lambda v: head_rows(v, score_masks), values)
        heads_grads = each(lambda g: head_rows(g, ones), cotangents)
        grad_weights = each(lambda v, g: dot(v, g, (1, 1)), values, heads_grads)
        grads = back(values, scaled, cotangents, shares, grad_weights, heads_grads, width)
        for (pair, p), grad in zip(group, grads):
            input_grad[p, :, pair_columns(pair)] = grad.astype(jnp.bfloat16)
            totals[pair] = totals[pair] + grad
    for pair in range(pairs):
        electrode_grad[:, pair_columns(pair)] = totals[pair].astype(jnp.bfloat16)


def table_kernel(groups, *refs):
    layouts, sums, table = refs[:groups], refs[groups], refs[groups + 1]
    owner = lax.axis_index("group")
    rows, model = table.shape
    slots = sums.shape[0] // groups
    template = lax.broadcasted_iota(jnp.int32, (rows, slots), 0) + owner * rows
    total = jnp.zeros((rows, model), jnp.float32)
    for away in range(groups):
        spread = (template == layouts[away][...]).astype(jnp.float32).astype(jnp.bfloat16)
        origin = lax.rem(owner + groups - away, groups)
        part = sums[pl.ds(pl.multiple_of(origin * slots, slots), slots), :]
        total = total + dot(spread, part, (1, 0))
    table[...] = total


VMEM = pl.BlockSpec(memory_space=pltpu.VMEM)
SMEM = pl.BlockSpec(memory_space=pltpu.SMEM)
PARAMS = pltpu.CompilerParams(vmem_limit_bytes=32 * 1024 * 1024)
STREAMED = pltpu.CompilerParams(vmem_limit_bytes=56 * 1024 * 1024)


def body(activations, out_grad, embedding, counts, offsets, layout):
    tokens = activations[0]
    local, slots, model = tokens.shape
    groups = lax.axis_size("group")
    parts = lax.axis_size("shard")
    patches = local * parts
    own = slots // parts
    width = model // HEADS
    templates = embedding.shape[0]
    pairs = STEP // LANES
    steps = model // STEP

    layouts = [layout] + [
        lax.ppermute(layout, "group", [(i, (i + away) % groups) for i in range(groups)])
        for away in range(1, groups)
    ]
    order = (2, 1, 0, 3) if patches_first(local) else (2, 0, 1, 3)
    cotangent = jnp.transpose(out_grad[0].reshape(parts, local, own, model), order)
    cotangent = cotangent.reshape(own, patches, model)

    flat = pl.BlockSpec((slots * local, STEP), lambda step: (0, step))
    planes = pl.BlockSpec((local, slots, STEP), lambda step: (0, 0, step))
    squares = pl.BlockSpec((local, pairs, slots, 2 * slots), lambda step: (0, step, 0, 0))
    flat_shape = jax.ShapeDtypeStruct((slots * local, model), jnp.bfloat16)
    plane_shape = jax.ShapeDtypeStruct(tokens.shape, jnp.bfloat16)
    flat_scratch = pltpu.VMEM((pairs, slots * local, LANES), jnp.float32)
    turned = turned_scratch(pairs, slots, local)

    strip = pl.BlockSpec((slots, STEP), lambda step: (0, step))
    strip_shape = jax.ShapeDtypeStruct((slots, model), jnp.bfloat16)
    rows, mixed = pl.pallas_call(
        functools.partial(spatial_kernel, width),
        grid=(steps,),
        out_shape=(strip_shape, flat_shape),
        in_specs=[SMEM, SMEM, VMEM, pl.BlockSpec((templates, STEP), lambda step: (0, step)), planes],
        out_specs=(strip, flat),
        scratch_shapes=[
            pltpu.VMEM((slots, templates), jnp.bfloat16),
            pltpu.VMEM((slots, 2 * slots), jnp.float32),
            turned,
        ],
        compiler_params=STREAMED,
        name="spatial",
    )(counts, offsets, layout, embedding, tokens)
    embedded, weights = pl.pallas_call(
        functools.partial(weights_kernel, width),
        grid=(steps,),
        out_shape=(
            plane_shape,
            jax.ShapeDtypeStruct((local, model // LANES, slots, 2 * slots), jnp.bfloat16),
        ),
        in_specs=[SMEM, SMEM, strip, planes],
        out_specs=(planes, squares),
        scratch_shapes=[pltpu.VMEM((slots, 2 * slots), jnp.float32)],
        compiler_params=PARAMS,
        cost_estimate=pl.CostEstimate(
            flops=4 * local * slots * slots * model, bytes_accessed=6 * tokens.size, transcendentals=0
        ),
        name="weights",
    )(counts, offsets, rows, tokens)

    gathered = lax.all_to_all(mixed, "shard", split_axis=0, concat_axis=0, tiled=True)
    mixed_grad = pl.pallas_call(
        functools.partial(temporal_kernel, width, parts),
        grid=(steps,),
        out_shape=flat_shape,
        in_specs=[flat, pl.BlockSpec((own, patches, STEP), lambda step: (0, 0, step))],
        out_specs=flat,
        scratch_shapes=[flat_scratch, flat_scratch],
        compiler_params=PARAMS,
        name="temporal",
    )(gathered, cotangent)

    returned = lax.all_to_all(mixed_grad, "shard", split_axis=0, concat_axis=0, tiled=True)
    input_grad, electrode_grad = pl.pallas_call(
        functools.partial(spatial_back_kernel, width),
        grid=(steps,),
        out_shape=(plane_shape, strip_shape),
        in_specs=[planes, squares, flat],
        out_specs=(planes, strip),
        scratch_shapes=[turned],
        compiler_params=STREAMED,
        name="spatial_back",
    )(embedded, weights, returned)

    shares = lax.all_to_all(
        electrode_grad.reshape(parts, own, model), "shard", split_axis=0, concat_axis=0, tiled=True
    )
    share = jnp.sum(shares.astype(jnp.float32), axis=0).astype(jnp.bfloat16)
    everyone = lax.all_to_all(
        jnp.broadcast_to(share[None], (groups * parts, own, model)),
        ("group", "shard"),
        split_axis=0,
        concat_axis=0,
        tiled=True,
    )
    table_grad = pl.pallas_call(
        functools.partial(table_kernel, groups),
        out_shape=jax.ShapeDtypeStruct((templates // groups, model), jnp.float32),
        in_specs=[VMEM] * (groups + 1),
        out_specs=VMEM,
        compiler_params=PARAMS,
        name="table",
    )(*layouts, everyone.reshape(groups * slots, model))
    return (input_grad[None], table_grad)


def solution(mesh):
    placed = (
        P("group", "shard", None, None),
        P("group", None, "shard", None),
        P(),
        P("group", None),
        P("group", None),
        P("group", None),
    )
    return jax.shard_map(
        body,
        mesh=mesh,
        in_specs=placed,
        out_specs=(P("group", "shard", None, None), P("group", None)),
        check_vma=False,
    )
```

```python
import functools
import math

import jax
import jax.numpy as jnp
from jax import lax
from jax.experimental import pallas as pl
from jax.experimental.pallas import tpu as pltpu
from jax.sharding import PartitionSpec as P

HEADS = 16
BLOCK = 32
LANES = 128
MASKED = -1e30
SUBLANES = 8
STEP = 256
PIECES = 4
SPATIAL_GROUP = 16
TEMPORAL_GROUP = 8


def dot(left, right, over):
    return lax.dot_general(
        left, right, (((over[0],), (over[1],)), ((), ())), preferred_element_type=jnp.float32
    )


def head_masks(width, scale):
    lane = lax.broadcasted_iota(jnp.int32, (1, LANES), 1)
    first = jnp.where(lane < width, scale, 0.0).astype(jnp.bfloat16)
    second = jnp.where(lane < width, 0.0, scale).astype(jnp.bfloat16)
    return first, second


def head_rows(pair, masks):
    return jnp.concatenate([pair * masks[0], pair * masks[1]], axis=0)


def head_columns(rows, width):
    count = rows.shape[0] // 2
    lane = lax.broadcasted_iota(jnp.int32, (count, rows.shape[1]), 1)
    return jnp.where(lane < width, rows[:count], rows[count:])


def each(function, *lists):
    return [function(*items) for items in zip(*lists)]


def weights_by_key(scores):
    tops = each(lambda s: jnp.max(s, axis=0, keepdims=True), scores)
    exponents = each(lambda s, t: jnp.exp(s - t), scores, tops)
    shares = each(lambda e: 1.0 / jnp.sum(e, axis=0, keepdims=True), exponents)
    return each(lambda e, r: (e * r).astype(jnp.bfloat16), exponents, shares)


def by_query(shares, values, width):
    if 2 * values[0].shape[0] != LANES or len(values) % 2:
        return each(lambda s, v: head_columns(dot(s, v, (0, 0)), width), shares, values)
    results = []
    for first in range(0, len(values), 2):
        turned = jnp.transpose(jnp.concatenate(shares[first : first + 2], axis=0))
        one, other = values[first : first + 2]
        zero = jnp.zeros_like(one)
        apart = jnp.concatenate(
            [jnp.concatenate([one, zero], axis=1), jnp.concatenate([zero, other], axis=1)], axis=0
        )
        both = dot(turned, apart, (1, 0))
        results += [head_columns(both[:, :LANES], width), head_columns(both[:, LANES:], width)]
    return results


def back(values, scaled, cotangents, weights, grad_weights, heads_grads, width):
    wide = each(lambda w: w.astype(jnp.float32), weights)
    deltas = each(lambda w, g: jnp.sum(w * g, axis=0, keepdims=True), wide, grad_weights)
    grad_scores = each(
        lambda w, g, d: (w * (g - d)).astype(jnp.bfloat16), wide, grad_weights, deltas
    )
    length = values[0].shape[0]
    whole = length % LANES == 0
    both_ways = grad_scores
    if whole:
        both_ways = each(
            lambda g: jnp.concatenate(
                [
                    g[:, start : start + length] + jnp.transpose(g[:, start : start + length])
                    for start in (0, length)
                ],
                axis=1,
            ),
            grad_scores,
        )
    grads = each(
        lambda c, w, g, hg, hv: c.astype(jnp.float32)
        + dot(jnp.concatenate([w, g], axis=1), jnp.concatenate([hg, hv], axis=0), (1, 0)),
        cotangents,
        weights,
        both_ways,
        heads_grads,
        scaled,
    )
    if whole:
        return grads
    score_scale = 0.5 / math.sqrt(width)
    rest = by_query(grad_scores, values, width)
    return each(lambda g, r: g + score_scale * r, grads, rest)


def pair_bias(counts, offsets, slots):
    def sessions(slot):
        block = slot // BLOCK
        session = jnp.full(slot.shape, -1, jnp.int32)
        for j in range(offsets.shape[1]):
            session = session + (offsets[0, j] <= block).astype(jnp.int32)
        return session

    key_slot = lax.broadcasted_iota(jnp.int32, (slots, 2 * slots), 0)
    query_slot = lax.broadcasted_iota(jnp.int32, (slots, 2 * slots), 1) % slots
    key_session = sessions(key_slot)
    first = jnp.zeros_like(key_slot)
    live = jnp.zeros_like(key_slot)
    for j in range(offsets.shape[1]):
        chosen = key_session == j
        first = jnp.where(chosen, offsets[0, j] * BLOCK, first)
        live = jnp.where(chosen, counts[0, j], live)
    allowed = (key_session == sessions(query_slot)) & (key_slot - first < live)
    return jnp.where(allowed, 0.0, MASKED)


def pair_columns(pair):
    return pl.ds(pair * LANES, LANES)


def in_groups(pairs, rows, size):
    items = [(pair, row) for pair in range(pairs) for row in range(rows)]
    return [items[start : start + size] for start in range(0, len(items), size)]


def turned_stride(patches):
    return patches + 1 if patches % SUBLANES == 0 else patches


def turned_scratch(pairs, slots, patches):
    return pltpu.VMEM((pairs, slots * turned_stride(patches), LANES), jnp.float32)


def read_turned(ref, pair, slots, patches):
    stride = turned_stride(patches)
    if stride == patches:
        return ref[pair]
    pieces = [ref[pair, pl.ds(slot * stride, patches), :] for slot in range(slots)]
    return jnp.concatenate(pieces, axis=0)


def write_turned(ref, pair, rows, slots, patches):
    stride = turned_stride(patches)
    if stride == patches:
        ref[pair] = rows
        return
    for slot in range(slots):
        ref[pair, pl.ds(slot * stride, patches), :] = rows[slot * patches : (slot + 1) * patches]


def of_patch(patch, slots, patches):
    return pl.ds(patch, slots, stride=turned_stride(patches))


def attention(width, tokens, rows, bias, group):
    score_masks = head_masks(width, 0.5 / math.sqrt(width))
    values = [
        (
            tokens[p, :, pair_columns(pair)].astype(jnp.float32)
            + rows[:, pair * LANES : (pair + 1) * LANES]
        ).astype(jnp.bfloat16)
        for pair, p in group
    ]
    scores = each(lambda v: dot(v, head_rows(v, score_masks), (1, 1)) + bias[...], values)
    return values, weights_by_key(scores)


def spatial_kernel(
    width, counts, offsets, layout, embedding, tokens, rows, mixed, spread, bias, by_electrode
):
    patches, slots, model = tokens.shape
    templates = embedding.shape[0]
    pairs = model // LANES

    @pl.when(pl.program_id(0) == 0)
    def _():
        bias[...] = pair_bias(counts, offsets, slots)
        chosen = lax.broadcasted_iota(jnp.int32, (templates, slots), 0) == layout[...]
        spread[...] = jnp.transpose(chosen.astype(jnp.float32)).astype(jnp.bfloat16)

    chosen_rows = dot(spread[...], embedding[...], (1, 0))
    rows[...] = chosen_rows.astype(jnp.bfloat16)
    for group in in_groups(pairs, patches, SPATIAL_GROUP):
        values, shares = attention(width, tokens, chosen_rows, bias, group)
        attended = by_query(shares, values, width)
        for (pair, p), value, result in zip(group, values, attended):
            by_electrode[pair, of_patch(p, slots, patches), :] = value.astype(jnp.float32) + result
    for pair in range(pairs):
        mixed[:, pair_columns(pair)] = read_turned(by_electrode, pair, slots, patches).astype(
            jnp.bfloat16
        )


def weights_kernel(width, counts, offsets, rows, tokens, embedded, weights, bias):
    patches, slots, model = tokens.shape

    @pl.when(pl.program_id(0) == 0)
    def _():
        bias[...] = pair_bias(counts, offsets, slots)

    added = rows[...].astype(jnp.float32)
    for group in in_groups(model // LANES, patches, SPATIAL_GROUP):
        values, shares = attention(width, tokens, added, bias, group)
        for (pair, p), value, share in zip(group, values, shares):
            embedded[p, :, pair_columns(pair)] = value
            weights[p, pair] = share


def patches_first(local):
    return local % SUBLANES != 0


def electrode_rows(electrode, electrodes, parts, local):
    start, step = electrode * local, electrodes * local
    if patches_first(local):
        return [pl.ds(start + p, parts, stride=step) for p in range(local)]
    return [pl.ds(start + part * step, local) for part in range(parts)]


def temporal_kernel(width, parts, mixed, out_grad, mixed_grad, received, returned):
    electrodes, patches, model = out_grad.shape
    local = patches // parts
    pairs = model // LANES
    score_masks = head_masks(width, 0.5 / math.sqrt(width))
    ones = head_masks(width, 1.0)
    for pair in range(pairs):
        received[pair] = mixed[:, pair_columns(pair)].astype(jnp.float32)
    for group in in_groups(pairs, electrodes, TEMPORAL_GROUP):
        places = [electrode_rows(e, electrodes, parts, local) for _, e in group]
        values = each(
            lambda item, place: jnp.concatenate(
                [received[item[0], rows, :] for rows in place], axis=0
            ).astype(jnp.bfloat16),
            group,
            places,
        )
        cotangents = [out_grad[e, :, pair_columns(pair)] for pair, e in group]
        scaled = each(lambda v: head_rows(v, score_masks), values)
        scores = each(lambda v, s: dot(v, s, (1, 1)), values, scaled)
        heads_grads = each(lambda g: head_rows(g, ones), cotangents)
        grad_weights = each(lambda v, g: dot(v, g, (1, 1)), values, heads_grads)
        shares = weights_by_key(scores)
        grads = back(values, scaled, cotangents, shares, grad_weights, heads_grads, width)
        for (pair, _), place, grad in zip(group, places, grads):
            start = 0
            for rows in place:
                returned[pair, rows, :] = grad[start : start + rows.size]
                start += rows.size
    for pair in range(pairs):
        mixed_grad[:, pair_columns(pair)] = returned[pair].astype(jnp.bfloat16)


def spatial_back_kernel(
    width, all_embedded, all_weights, mixed_grad, input_grad, electrode_grad,
    received, kept_embedded, kept_weights, arrived_sems,
):
    patches, slots, model = input_grad.shape
    pairs = model // LANES
    step = pl.program_id(0)

    def copies(at):
        columns, places = pl.ds(at * model, model), pl.ds(at * pairs, pairs)
        return (
            pltpu.make_async_copy(
                all_embedded.at[:, :, columns], kept_embedded.at[at], arrived_sems.at[at, 0]
            ),
            pltpu.make_async_copy(
                all_weights.at[:, places], kept_weights.at[at], arrived_sems.at[at, 1]
            ),
        )

    @pl.when(step == 0)
    def _():
        for at in range(kept_embedded.shape[0]):
            for copy in copies(at):
                copy.start()

    for at in range(kept_embedded.shape[0]):

        @pl.when(step == at)
        def _():
            for copy in copies(at):
                copy.wait()

    embedded, weights = kept_embedded.at[step], kept_weights.at[step]
    score_masks = head_masks(width, 0.5 / math.sqrt(width))
    ones = head_masks(width, 1.0)
    totals = [jnp.zeros((slots, LANES), jnp.float32) for _ in range(pairs)]
    for pair in range(pairs):
        arrived = mixed_grad[:, pair_columns(pair)].astype(jnp.float32)
        write_turned(received, pair, arrived, slots, patches)
    for group in in_groups(pairs, patches, SPATIAL_GROUP):
        cotangents = [
            received[pair, of_patch(p, slots, patches), :].astype(jnp.bfloat16)
            for pair, p in group
        ]
        values = [embedded[p, :, pair_columns(pair)] for pair, p in group]
        shares = [weights[p, pair] for pair, p in group]
        scaled = each(lambda v: head_rows(v, score_masks), values)
        heads_grads = each(lambda g: head_rows(g, ones), cotangents)
        grad_weights = each(lambda v, g: dot(v, g, (1, 1)), values, heads_grads)
        grads = back(values, scaled, cotangents, shares, grad_weights, heads_grads, width)
        for (pair, p), grad in zip(group, grads):
            input_grad[p, :, pair_columns(pair)] = grad.astype(jnp.bfloat16)
            totals[pair] = totals[pair] + grad
    for pair in range(pairs):
        electrode_grad[:, pair_columns(pair)] = totals[pair].astype(jnp.bfloat16)


def share_kernel(shares, everyone):
    total = shares[0].astype(jnp.float32)
    for part in range(1, shares.shape[0]):
        total = total + shares[part].astype(jnp.float32)
    everyone[...] = jnp.broadcast_to(total.astype(jnp.bfloat16)[None], everyone.shape)


def table_kernel(groups, *refs):
    layouts, sums, (table, pieces, sems) = refs[:groups], refs[groups], refs[groups + 1 :]
    owner = lax.axis_index("group")
    count, rows, model = pieces.shape
    slots = sums.shape[0] // groups
    parts = []
    for away in range(groups):
        origin = lax.rem(owner + groups - away, groups)
        parts.append(sums[pl.ds(pl.multiple_of(origin * slots, slots), slots), :])
    sources = jnp.concatenate(parts, axis=0)
    layout = jnp.concatenate([ref[...] for ref in layouts], axis=1)
    copies = []
    for piece in range(count):
        first = owner * (count * rows) + piece * rows
        template = lax.broadcasted_iota(jnp.int32, (rows, groups * slots), 0) + first
        spread = (template == layout).astype(jnp.float32).astype(jnp.bfloat16)
        pieces[piece] = dot(spread, sources, (1, 0))
        copy = pltpu.make_async_copy(
            pieces.at[piece], table.at[pl.ds(piece * rows, rows)], sems.at[piece]
        )
        copy.start()
        copies.append(copy)
    for copy in copies:
        copy.wait()


VMEM = pl.BlockSpec(memory_space=pltpu.VMEM)
SMEM = pl.BlockSpec(memory_space=pltpu.SMEM)
HBM = pl.BlockSpec(memory_space=pltpu.HBM)
PARAMS = pltpu.CompilerParams(vmem_limit_bytes=32 * 1024 * 1024)
STREAMED = pltpu.CompilerParams(vmem_limit_bytes=56 * 1024 * 1024)


def body(activations, out_grad, embedding, counts, offsets, layout):
    tokens = activations[0]
    local, slots, model = tokens.shape
    groups = lax.axis_size("group")
    parts = lax.axis_size("shard")
    patches = local * parts
    own = slots // parts
    width = model // HEADS
    templates = embedding.shape[0]
    pairs = STEP // LANES
    steps = model // STEP

    layouts = [layout] + [
        lax.ppermute(layout, "group", [(i, (i + away) % groups) for i in range(groups)])
        for away in range(1, groups)
    ]
    order = (2, 1, 0, 3) if patches_first(local) else (2, 0, 1, 3)
    cotangent = jnp.transpose(out_grad[0].reshape(parts, local, own, model), order)
    cotangent = cotangent.reshape(own, patches, model)

    flat = pl.BlockSpec((slots * local, STEP), lambda step: (0, step))
    planes = pl.BlockSpec((local, slots, STEP), lambda step: (0, 0, step))
    squares = pl.BlockSpec((local, pairs, slots, 2 * slots), lambda step: (0, step, 0, 0))
    flat_shape = jax.ShapeDtypeStruct((slots * local, model), jnp.bfloat16)
    plane_shape = jax.ShapeDtypeStruct(tokens.shape, jnp.bfloat16)
    flat_scratch = pltpu.VMEM((pairs, slots * local, LANES), jnp.float32)
    turned = turned_scratch(pairs, slots, local)

    strip = pl.BlockSpec((slots, STEP), lambda step: (0, step))
    strip_shape = jax.ShapeDtypeStruct((slots, model), jnp.bfloat16)
    rows, mixed = pl.pallas_call(
        functools.partial(spatial_kernel, width),
        grid=(steps,),
        out_shape=(strip_shape, flat_shape),
        in_specs=[SMEM, SMEM, VMEM, pl.BlockSpec((templates, STEP), lambda step: (0, step)), planes],
        out_specs=(strip, flat),
        scratch_shapes=[
            pltpu.VMEM((slots, templates), jnp.bfloat16),
            pltpu.VMEM((slots, 2 * slots), jnp.float32),
            turned,
        ],
        compiler_params=STREAMED,
        name="spatial",
    )(counts, offsets, layout, embedding, tokens)
    embedded, weights = pl.pallas_call(
        functools.partial(weights_kernel, width),
        grid=(steps,),
        out_shape=(
            plane_shape,
            jax.ShapeDtypeStruct((local, model // LANES, slots, 2 * slots), jnp.bfloat16),
        ),
        in_specs=[SMEM, SMEM, strip, planes],
        out_specs=(planes, squares),
        scratch_shapes=[pltpu.VMEM((slots, 2 * slots), jnp.float32)],
        compiler_params=PARAMS,
        cost_estimate=pl.CostEstimate(
            flops=4 * local * slots * slots * model, bytes_accessed=6 * tokens.size, transcendentals=0
        ),
        name="weights",
    )(counts, offsets, rows, tokens)

    gathered = lax.all_to_all(mixed, "shard", split_axis=0, concat_axis=0, tiled=True)
    mixed_grad = pl.pallas_call(
        functools.partial(temporal_kernel, width, parts),
        grid=(steps,),
        out_shape=flat_shape,
        in_specs=[flat, pl.BlockSpec((own, patches, STEP), lambda step: (0, 0, step))],
        out_specs=flat,
        scratch_shapes=[flat_scratch, flat_scratch],
        compiler_params=PARAMS,
        name="temporal",
    )(gathered, cotangent)

    returned = lax.all_to_all(mixed_grad, "shard", split_axis=0, concat_axis=0, tiled=True)
    input_grad, electrode_grad = pl.pallas_call(
        functools.partial(spatial_back_kernel, width),
        grid=(steps,),
        out_shape=(plane_shape, strip_shape),
        in_specs=[HBM, HBM, flat],
        out_specs=(planes, strip),
        scratch_shapes=[
            turned,
            pltpu.VMEM((steps, local, slots, STEP), jnp.bfloat16),
            pltpu.VMEM((steps, local, pairs, slots, 2 * slots), jnp.bfloat16),
            pltpu.SemaphoreType.DMA((steps, 2)),
        ],
        compiler_params=PARAMS,
        name="spatial_back",
    )(embedded, weights, returned)

    shares = lax.all_to_all(
        electrode_grad.reshape(parts, own, model), "shard", split_axis=0, concat_axis=0, tiled=True
    )
    everyone = pl.pallas_call(
        share_kernel,
        out_shape=jax.ShapeDtypeStruct((groups * parts, own, model), jnp.bfloat16),
        in_specs=[VMEM],
        out_specs=VMEM,
        compiler_params=PARAMS,
        name="share",
    )(shares)
    everyone = lax.all_to_all(
        everyone, ("group", "shard"), split_axis=0, concat_axis=0, tiled=True
    )
    table_rows = templates // groups
    table_grad = pl.pallas_call(
        functools.partial(table_kernel, groups),
        out_shape=jax.ShapeDtypeStruct((table_rows, model), jnp.float32),
        in_specs=[VMEM] * (groups + 1),
        out_specs=HBM,
        scratch_shapes=[
            pltpu.VMEM((PIECES, table_rows // PIECES, model), jnp.float32),
            pltpu.SemaphoreType.DMA((PIECES,)),
        ],
        compiler_params=PARAMS,
        name="table",
    )(*layouts, everyone.reshape(groups * slots, model))
    return (input_grad[None], table_grad)


def solution(mesh):
    placed = (
        P("group", "shard", None, None),
        P("group", None, "shard", None),
        P(),
        P("group", None),
        P("group", None),
        P("group", None),
    )
    return jax.shard_map(
        body,
        mesh=mesh,
        in_specs=placed,
        out_specs=(P("group", "shard", None, None), P("group", None)),
        check_vma=False,
    )
```

```python
import functools
import math

import jax
import jax.numpy as jnp
from jax import lax
from jax.experimental import pallas as pl
from jax.experimental.pallas import tpu as pltpu
from jax.sharding import PartitionSpec as P

HEADS = 16
BLOCK = 32
LANES = 128
MASKED = -1e30
SUBLANES = 8
STEP = 256
CHUNKS = 2
PLANE = 4
PIECES = 4
SPATIAL_GROUP = 16
TEMPORAL_GROUP = 8


def dot(left, right, over):
    return lax.dot_general(
        left, right, (((over[0],), (over[1],)), ((), ())), preferred_element_type=jnp.float32
    )


def head_masks(width, scale):
    lane = lax.broadcasted_iota(jnp.int32, (1, LANES), 1)
    first = jnp.where(lane < width, scale, 0.0).astype(jnp.bfloat16)
    second = jnp.where(lane < width, 0.0, scale).astype(jnp.bfloat16)
    return first, second


def head_rows(pair, masks):
    return jnp.concatenate([pair * masks[0], pair * masks[1]], axis=0)


def head_columns(rows, width):
    count = rows.shape[0] // 2
    lane = lax.broadcasted_iota(jnp.int32, (count, rows.shape[1]), 1)
    return jnp.where(lane < width, rows[:count], rows[count:])


def each(function, *lists):
    return [function(*items) for items in zip(*lists)]


def weights_by_key(scores):
    tops = each(lambda s: jnp.max(s, axis=0, keepdims=True), scores)
    exponents = each(lambda s, t: jnp.exp(s - t), scores, tops)
    shares = each(lambda e: 1.0 / jnp.sum(e, axis=0, keepdims=True), exponents)
    return each(lambda e, r: (e * r).astype(jnp.bfloat16), exponents, shares)


def by_query(shares, values, width):
    if 2 * values[0].shape[0] != LANES or len(values) % 2:
        return each(lambda s, v: head_columns(dot(s, v, (0, 0)), width), shares, values)
    results = []
    for first in range(0, len(values), 2):
        turned = jnp.transpose(jnp.concatenate(shares[first : first + 2], axis=0))
        one, other = values[first : first + 2]
        zero = jnp.zeros_like(one)
        apart = jnp.concatenate(
            [jnp.concatenate([one, zero], axis=1), jnp.concatenate([zero, other], axis=1)], axis=0
        )
        both = dot(turned, apart, (1, 0))
        results += [head_columns(both[:, :LANES], width), head_columns(both[:, LANES:], width)]
    return results


def back(values, scaled, cotangents, weights, grad_weights, heads_grads, width):
    wide = each(lambda w: w.astype(jnp.float32), weights)
    deltas = each(lambda w, g: jnp.sum(w * g, axis=0, keepdims=True), wide, grad_weights)
    grad_scores = each(
        lambda w, g, d: (w * (g - d)).astype(jnp.bfloat16), wide, grad_weights, deltas
    )
    length = values[0].shape[0]
    whole = length % LANES == 0
    both_ways = grad_scores
    if whole:
        both_ways = each(
            lambda g: jnp.concatenate(
                [
                    g[:, start : start + length] + jnp.transpose(g[:, start : start + length])
                    for start in (0, length)
                ],
                axis=1,
            ),
            grad_scores,
        )
    grads = each(
        lambda c, w, g, hg, hv: c.astype(jnp.float32)
        + dot(jnp.concatenate([w, g], axis=1), jnp.concatenate([hg, hv], axis=0), (1, 0)),
        cotangents,
        weights,
        both_ways,
        heads_grads,
        scaled,
    )
    if whole:
        return grads
    score_scale = 0.5 / math.sqrt(width)
    rest = by_query(grad_scores, values, width)
    return each(lambda g, r: g + score_scale * r, grads, rest)


def pair_bias(counts, offsets, slots):
    def sessions(slot):
        block = slot // BLOCK
        session = jnp.full(slot.shape, -1, jnp.int32)
        for j in range(offsets.shape[1]):
            session = session + (offsets[0, j] <= block).astype(jnp.int32)
        return session

    key_slot = lax.broadcasted_iota(jnp.int32, (slots, 2 * slots), 0)
    query_slot = lax.broadcasted_iota(jnp.int32, (slots, 2 * slots), 1) % slots
    key_session = sessions(key_slot)
    first = jnp.zeros_like(key_slot)
    live = jnp.zeros_like(key_slot)
    for j in range(offsets.shape[1]):
        chosen = key_session == j
        first = jnp.where(chosen, offsets[0, j] * BLOCK, first)
        live = jnp.where(chosen, counts[0, j], live)
    allowed = (key_session == sessions(query_slot)) & (key_slot - first < live)
    return jnp.where(allowed, 0.0, MASKED)


def pair_columns(pair):
    return pl.ds(pair * LANES, LANES)


def in_groups(pairs, rows, size):
    items = [(pair, row) for pair in range(pairs) for row in range(rows)]
    return [items[start : start + size] for start in range(0, len(items), size)]


def of_patch(patch, slots, patches):
    return pl.ds(patch, slots, stride=patches)


def partner_rows(away, count):
    partner = lax.bitwise_xor(lax.axis_index("shard"), away)
    return pl.ds(pl.multiple_of(partner * count, count), count)


def send_blocks(blocks, pair, rows):
    for far, block in enumerate(blocks):
        for near in range(block.shape[0]):
            place = partner_rows(far * block.shape[0] + near, block.shape[1])
            block[near, :, pair_columns(pair)] = rows[pair, place, :].astype(jnp.bfloat16)


def take_blocks(blocks, pair, rows):
    for near, block in enumerate(blocks):
        for far in range(block.shape[0]):
            place = partner_rows(far * len(blocks) + near, block.shape[1])
            rows[pair, place, :] = block[far, :, pair_columns(pair)].astype(jnp.float32)


def attention(width, tokens, rows, bias, group):
    score_masks = head_masks(width, 0.5 / math.sqrt(width))
    values = [
        (
            tokens[p, :, pair_columns(pair)].astype(jnp.float32)
            + rows[:, pair * LANES : (pair + 1) * LANES]
        ).astype(jnp.bfloat16)
        for pair, p in group
    ]
    scores = each(lambda v: dot(v, head_rows(v, score_masks), (1, 1)) + bias[...], values)
    return values, weights_by_key(scores)


def spatial_kernel(width, counts, offsets, layout, embedding, tokens, embedded, weights, *refs):
    mixed, (spread, bias, by_electrode) = refs[:-3], refs[-3:]
    patches, slots, model = tokens.shape
    templates = embedding.shape[0]
    pairs = model // LANES

    @pl.when(pl.program_id(0) == 0)
    def _():
        bias[...] = pair_bias(counts, offsets, slots)
        chosen = lax.broadcasted_iota(jnp.int32, (templates, slots), 0) == layout[...]
        spread[...] = jnp.transpose(chosen.astype(jnp.float32)).astype(jnp.bfloat16)

    rows = dot(spread[...], embedding[...], (1, 0))
    for group in in_groups(pairs, patches, SPATIAL_GROUP):
        values, shares = attention(width, tokens, rows, bias, group)
        attended = by_query(shares, values, width)
        for (pair, p), value, share, result in zip(group, values, shares, attended):
            embedded[p, :, pair_columns(pair)] = value
            weights[p, pair] = share
            by_electrode[pair, of_patch(p, slots, patches), :] = value.astype(jnp.float32) + result
    for pair in range(pairs):
        send_blocks(mixed, pair, by_electrode)


def patches_first(local):
    return local % SUBLANES != 0


def electrode_rows(electrode, electrodes, parts, local):
    start, step = electrode * local, electrodes * local
    if patches_first(local):
        return [pl.ds(start + p, parts, stride=step) for p in range(local)]
    return [pl.ds(start + part * step, local) for part in range(parts)]


def temporal_kernel(width, parts, plane, out_grad, *refs):
    mixed, mixed_grad, (received, returned) = refs[:plane], refs[plane:-2], refs[-2:]
    electrodes, patches, model = out_grad.shape
    local = patches // parts
    pairs = model // LANES
    score_masks = head_masks(width, 0.5 / math.sqrt(width))
    ones = head_masks(width, 1.0)
    for pair in range(pairs):
        take_blocks(mixed, pair, received)
    for group in in_groups(pairs, electrodes, TEMPORAL_GROUP):
        places = [electrode_rows(e, electrodes, parts, local) for _, e in group]
        values = each(
            lambda item, place: jnp.concatenate(
                [received[item[0], rows, :] for rows in place], axis=0
            ).astype(jnp.bfloat16),
            group,
            places,
        )
        cotangents = [out_grad[e, :, pair_columns(pair)] for pair, e in group]
        scaled = each(lambda v: head_rows(v, score_masks), values)
        scores = each(lambda v, s: dot(v, s, (1, 1)), values, scaled)
        heads_grads = each(lambda g: head_rows(g, ones), cotangents)
        grad_weights = each(lambda v, g: dot(v, g, (1, 1)), values, heads_grads)
        shares = weights_by_key(scores)
        grads = back(values, scaled, cotangents, shares, grad_weights, heads_grads, width)
        for (pair, _), place, grad in zip(group, places, grads):
            start = 0
            for rows in place:
                returned[pair, rows, :] = grad[start : start + rows.size]
                start += rows.size
    for pair in range(pairs):
        send_blocks(mixed_grad, pair, returned)


def spatial_back_kernel(width, plane, embedded, weights, *refs):
    mixed_grad, (input_grad, electrode_grad, received) = refs[:plane], refs[-3:]
    patches, slots, model = embedded.shape
    pairs = model // LANES
    score_masks = head_masks(width, 0.5 / math.sqrt(width))
    ones = head_masks(width, 1.0)
    totals = [jnp.zeros((slots, LANES), jnp.float32) for _ in range(pairs)]
    for pair in range(pairs):
        take_blocks(mixed_grad, pair, received)
    for group in in_groups(pairs, patches, SPATIAL_GROUP):
        cotangents = [
            received[pair, of_patch(p, slots, patches), :].astype(jnp.bfloat16)
            for pair, p in group
        ]
        values = [embedded[p, :, pair_columns(pair)] for pair, p in group]
        shares = [weights[p, pair] for pair, p in group]
        scaled = each(lambda v: head_rows(v, score_masks), values)
        heads_grads = each(lambda g: head_rows(g, ones), cotangents)
        grad_weights = each(lambda v, g: dot(v, g, (1, 1)), values, heads_grads)
        grads = back(values, scaled, cotangents, shares, grad_weights, heads_grads, width)
        for (pair, p), grad in zip(group, grads):
            input_grad[p, :, pair_columns(pair)] = grad.astype(jnp.bfloat16)
            totals[pair] = totals[pair] + grad
    for pair in range(pairs):
        electrode_grad[:, pair_columns(pair)] = totals[pair].astype(jnp.bfloat16)


def repack_kernel(count, *refs):
    sources, targets, sems = refs[:count], refs[count:-1], refs[-1]
    copies = [
        pltpu.make_async_copy(source.at[near], target.at[far], sems.at[far, near])
        for far, source in enumerate(sources)
        for near, target in enumerate(targets)
    ]
    for copy in copies:
        copy.start()
    for copy in copies:
        copy.wait()


def share_kernel(shares, everyone):
    total = shares[0].astype(jnp.float32)
    for part in range(1, shares.shape[0]):
        total = total + shares[part].astype(jnp.float32)
    everyone[...] = jnp.broadcast_to(total.astype(jnp.bfloat16)[None], everyone.shape)


def table_kernel(groups, *refs):
    layouts, sums, (table, pieces, sems) = refs[:groups], refs[groups], refs[groups + 1 :]
    owner = lax.axis_index("group")
    count, rows, model = pieces.shape
    slots = sums.shape[0] // groups
    parts = []
    for away in range(groups):
        origin = lax.rem(owner + groups - away, groups)
        parts.append(sums[pl.ds(pl.multiple_of(origin * slots, slots), slots), :])
    sources = jnp.concatenate(parts, axis=0)
    layout = jnp.concatenate([ref[...] for ref in layouts], axis=1)
    copies = []
    for piece in range(count):
        first = owner * (count * rows) + piece * rows
        template = lax.broadcasted_iota(jnp.int32, (rows, groups * slots), 0) + first
        spread = (template == layout).astype(jnp.float32).astype(jnp.bfloat16)
        pieces[piece] = dot(spread, sources, (1, 0))
        copy = pltpu.make_async_copy(
            pieces.at[piece], table.at[pl.ds(piece * rows, rows)], sems.at[piece]
        )
        copy.start()
        copies.append(copy)
    for copy in copies:
        copy.wait()


VMEM = pl.BlockSpec(memory_space=pltpu.VMEM)
SMEM = pl.BlockSpec(memory_space=pltpu.SMEM)
HBM = pl.BlockSpec(memory_space=pltpu.HBM)
ANY = pl.BlockSpec(memory_space=pl.ANY)
PARAMS = pltpu.CompilerParams(vmem_limit_bytes=32 * 1024 * 1024)
STREAMED = pltpu.CompilerParams(vmem_limit_bytes=56 * 1024 * 1024)


def exchange(blocks):
    far_count, (plane, rows, columns) = len(blocks), blocks[0].shape
    parts = far_count * plane
    arrived = {0: blocks[0]}
    for far in reversed(range(1, far_count)):
        arrived[far] = lax.ppermute(
            blocks[far], "shard", [(i, i ^ (far * plane)) for i in range(parts)]
        )
    packed = pl.pallas_call(
        functools.partial(repack_kernel, far_count),
        out_shape=(jax.ShapeDtypeStruct((far_count, rows, columns), jnp.bfloat16),) * plane,
        in_specs=[ANY] * far_count,
        out_specs=(ANY,) * plane,
        scratch_shapes=[pltpu.SemaphoreType.DMA((far_count, plane))],
        compiler_params=PARAMS,
        name="repack",
    )(*[arrived[far] for far in range(far_count)])
    return [packed[0]] + [
        lax.ppermute(packed[near], "shard", [(i, i ^ near) for i in range(parts)])
        for near in range(1, plane)
    ]


def body(activations, out_grad, embedding, counts, offsets, layout):
    tokens = activations[0]
    local, slots, model = tokens.shape
    groups = lax.axis_size("group")
    parts = lax.axis_size("shard")
    patches = local * parts
    own = slots // parts
    width = model // HEADS
    templates = embedding.shape[0]
    pairs = STEP // LANES
    chunk = model // CHUNKS
    steps = chunk // STEP
    far_count = parts // PLANE
    assert parts == far_count * PLANE and parts & (parts - 1) == 0

    layouts = [layout] + [
        lax.ppermute(layout, "group", [(i, (i + away) % groups) for i in range(groups)])
        for away in range(1, groups)
    ]
    order = (2, 1, 0, 3) if patches_first(local) else (2, 0, 1, 3)
    cotangent = jnp.transpose(out_grad[0].reshape(parts, local, own, model), order)
    cotangent = cotangent.reshape(own, patches, model)

    def last(shape, first=0):
        lead = (0,) * (len(shape) - 1)
        return pl.BlockSpec(shape, lambda step: lead + (first + step,))

    squares = pl.BlockSpec((local, pairs, slots, 2 * slots), lambda step: (0, step, 0, 0))
    planes = last((local, slots, STEP))
    block = own * local
    far_specs = (last((PLANE, block, STEP)),) * far_count
    far_shapes = (jax.ShapeDtypeStruct((PLANE, block, chunk), jnp.bfloat16),) * far_count
    near_specs = [last((far_count, block, STEP))] * PLANE
    flat_scratch = pltpu.VMEM((pairs, slots * local, LANES), jnp.float32)

    forward = [
        pl.pallas_call(
            functools.partial(spatial_kernel, width),
            grid=(steps,),
            out_shape=(
                jax.ShapeDtypeStruct((local, slots, chunk), jnp.bfloat16),
                jax.ShapeDtypeStruct((local, chunk // LANES, slots, 2 * slots), jnp.bfloat16),
            )
            + far_shapes,
            in_specs=[
                SMEM,
                SMEM,
                VMEM,
                last((templates, STEP), index * steps),
                last((local, slots, STEP), index * steps),
            ],
            out_specs=(planes, squares) + far_specs,
            scratch_shapes=[
                pltpu.VMEM((slots, templates), jnp.bfloat16),
                pltpu.VMEM((slots, 2 * slots), jnp.float32),
                flat_scratch,
            ],
            compiler_params=STREAMED,
            name="spatial",
        )(counts, offsets, layout, embedding, tokens)
        for index in range(CHUNKS)
    ]
    gathered = [exchange(mixed) for _, _, *mixed in forward]
    mixed_grads = [
        pl.pallas_call(
            functools.partial(temporal_kernel, width, parts, PLANE),
            grid=(steps,),
            out_shape=far_shapes,
            in_specs=[last((own, patches, STEP), index * steps)] + near_specs,
            out_specs=far_specs,
            scratch_shapes=[flat_scratch, flat_scratch],
            compiler_params=PARAMS,
            name="temporal",
        )(cotangent, *arrived)
        for index, arrived in enumerate(gathered)
    ]
    returned = [exchange(blocks) for blocks in mixed_grads]
    done = []
    for index, (embedded, weights, *_) in enumerate(forward):
        done = pl.pallas_call(
            functools.partial(spatial_back_kernel, width, PLANE),
            grid=(steps,),
            out_shape=(
                jax.ShapeDtypeStruct(tokens.shape, jnp.bfloat16),
                jax.ShapeDtypeStruct((slots, model), jnp.bfloat16),
            ),
            in_specs=[planes, squares] + near_specs + [ANY] * len(done),
            out_specs=(
                last((local, slots, STEP), index * steps),
                last((slots, STEP), index * steps),
            ),
            scratch_shapes=[flat_scratch],
            input_output_aliases={2 + PLANE + place: place for place in range(len(done))},
            compiler_params=PARAMS,
            name="spatial_back",
        )(embedded, weights, *returned[index], *done)
    input_grad, electrode_grad = done

    shares = lax.all_to_all(
        electrode_grad.reshape(parts, own, model), "shard", split_axis=0, concat_axis=0, tiled=True
    )
    everyone = pl.pallas_call(
        share_kernel,
        out_shape=jax.ShapeDtypeStruct((groups * parts, own, model), jnp.bfloat16),
        in_specs=[VMEM],
        out_specs=VMEM,
        compiler_params=PARAMS,
        name="share",
    )(shares)
    everyone = lax.all_to_all(
        everyone, ("group", "shard"), split_axis=0, concat_axis=0, tiled=True
    )
    table_rows = templates // groups
    table_grad = pl.pallas_call(
        functools.partial(table_kernel, groups),
        out_shape=jax.ShapeDtypeStruct((table_rows, model), jnp.float32),
        in_specs=[VMEM] * (groups + 1),
        out_specs=HBM,
        scratch_shapes=[
            pltpu.VMEM((PIECES, table_rows // PIECES, model), jnp.float32),
            pltpu.SemaphoreType.DMA((PIECES,)),
        ],
        compiler_params=PARAMS,
        name="table",
    )(*layouts, everyone.reshape(groups * slots, model))
    return (input_grad[None], table_grad)


def solution(mesh):
    placed = (
        P("group", "shard", None, None),
        P("group", None, "shard", None),
        P(),
        P("group", None),
        P("group", None),
        P("group", None),
    )
    return jax.shard_map(
        body,
        mesh=mesh,
        in_specs=placed,
        out_specs=(P("group", "shard", None, None), P("group", None)),
        check_vma=False,
    )
```

```python
import functools
import math

import jax
import jax.numpy as jnp
from jax import lax
from jax.experimental import pallas as pl
from jax.experimental.pallas import tpu as pltpu
from jax.sharding import PartitionSpec as P

HEADS = 16
BLOCK = 32
LANES = 128
MASKED = -1e30
SUBLANES = 8
STEP = 256
CHUNKS = 2
PLANE = 4
PIECES = 4
SPATIAL_GROUP = 16
TEMPORAL_GROUP = 8


def dot(left, right, over):
    return lax.dot_general(
        left, right, (((over[0],), (over[1],)), ((), ())), preferred_element_type=jnp.float32
    )


def head_masks(width, scale):
    lane = lax.broadcasted_iota(jnp.int32, (1, LANES), 1)
    first = jnp.where(lane < width, scale, 0.0).astype(jnp.bfloat16)
    second = jnp.where(lane < width, 0.0, scale).astype(jnp.bfloat16)
    return first, second


def head_rows(pair, masks):
    return jnp.concatenate([pair * masks[0], pair * masks[1]], axis=0)


def head_columns(rows, width):
    count = rows.shape[0] // 2
    lane = lax.broadcasted_iota(jnp.int32, (count, rows.shape[1]), 1)
    return jnp.where(lane < width, rows[:count], rows[count:])


def each(function, *lists):
    return [function(*items) for items in zip(*lists)]


def weights_by_key(scores):
    tops = each(lambda s: jnp.max(s, axis=0, keepdims=True), scores)
    exponents = each(lambda s, t: jnp.exp(s - t), scores, tops)
    shares = each(lambda e: 1.0 / jnp.sum(e, axis=0, keepdims=True), exponents)
    return each(lambda e, r: (e * r).astype(jnp.bfloat16), exponents, shares)


def by_query(shares, values, width):
    if 2 * values[0].shape[0] != LANES or len(values) % 2:
        return each(lambda s, v: head_columns(dot(s, v, (0, 0)), width), shares, values)
    results = []
    for first in range(0, len(values), 2):
        turned = jnp.transpose(jnp.concatenate(shares[first : first + 2], axis=0))
        one, other = values[first : first + 2]
        zero = jnp.zeros_like(one)
        apart = jnp.concatenate(
            [jnp.concatenate([one, zero], axis=1), jnp.concatenate([zero, other], axis=1)], axis=0
        )
        both = dot(turned, apart, (1, 0))
        results += [head_columns(both[:, :LANES], width), head_columns(both[:, LANES:], width)]
    return results


def back(values, scaled, cotangents, weights, grad_weights, heads_grads, width):
    wide = each(lambda w: w.astype(jnp.float32), weights)
    deltas = each(lambda w, g: jnp.sum(w * g, axis=0, keepdims=True), wide, grad_weights)
    grad_scores = each(
        lambda w, g, d: (w * (g - d)).astype(jnp.bfloat16), wide, grad_weights, deltas
    )
    length = values[0].shape[0]
    whole = length % LANES == 0
    both_ways = grad_scores
    if whole:
        both_ways = each(
            lambda g: jnp.concatenate(
                [
                    g[:, start : start + length] + jnp.transpose(g[:, start : start + length])
                    for start in (0, length)
                ],
                axis=1,
            ),
            grad_scores,
        )
    grads = each(
        lambda c, w, g, hg, hv: c.astype(jnp.float32)
        + dot(jnp.concatenate([w, g], axis=1), jnp.concatenate([hg, hv], axis=0), (1, 0)),
        cotangents,
        weights,
        both_ways,
        heads_grads,
        scaled,
    )
    if whole:
        return grads
    score_scale = 0.5 / math.sqrt(width)
    rest = by_query(grad_scores, values, width)
    return each(lambda g, r: g + score_scale * r, grads, rest)


def pair_bias(counts, offsets, slots):
    def sessions(slot):
        block = slot // BLOCK
        session = jnp.full(slot.shape, -1, jnp.int32)
        for j in range(offsets.shape[1]):
            session = session + (offsets[0, j] <= block).astype(jnp.int32)
        return session

    key_slot = lax.broadcasted_iota(jnp.int32, (slots, 2 * slots), 0)
    query_slot = lax.broadcasted_iota(jnp.int32, (slots, 2 * slots), 1) % slots
    key_session = sessions(key_slot)
    first = jnp.zeros_like(key_slot)
    live = jnp.zeros_like(key_slot)
    for j in range(offsets.shape[1]):
        chosen = key_session == j
        first = jnp.where(chosen, offsets[0, j] * BLOCK, first)
        live = jnp.where(chosen, counts[0, j], live)
    allowed = (key_session == sessions(query_slot)) & (key_slot - first < live)
    return jnp.where(allowed, 0.0, MASKED)


def pair_columns(pair):
    return pl.ds(pair * LANES, LANES)


def in_groups(pairs, rows, size):
    items = [(pair, row) for pair in range(pairs) for row in range(rows)]
    return [items[start : start + size] for start in range(0, len(items), size)]


def of_patch(patch, slots, patches):
    return pl.ds(patch, slots, stride=patches)


def partner_rows(away, count):
    partner = lax.bitwise_xor(lax.axis_index("shard"), away)
    return pl.ds(pl.multiple_of(partner * count, count), count)


def send_blocks(blocks, pair, rows):
    for far, block in enumerate(blocks):
        for near in range(block.shape[0]):
            place = partner_rows(far * block.shape[0] + near, block.shape[1])
            block[near, :, pair_columns(pair)] = rows[pair, place, :].astype(jnp.bfloat16)


def take_blocks(blocks, pair, rows):
    for near, block in enumerate(blocks):
        for far in range(block.shape[0]):
            place = partner_rows(far * len(blocks) + near, block.shape[1])
            rows[pair, place, :] = block[far, :, pair_columns(pair)].astype(jnp.float32)


def attention(width, tokens, rows, bias, group):
    score_masks = head_masks(width, 0.5 / math.sqrt(width))
    values = [
        (
            tokens[p, :, pair_columns(pair)].astype(jnp.float32)
            + rows[:, pair * LANES : (pair + 1) * LANES]
        ).astype(jnp.bfloat16)
        for pair, p in group
    ]
    scores = each(lambda v: dot(v, head_rows(v, score_masks), (1, 1)) + bias[...], values)
    return values, weights_by_key(scores)


def spatial_kernel(width, counts, offsets, layout, embedding, tokens, embedded, weights, *refs):
    mixed, (spread, bias, by_electrode) = refs[:-3], refs[-3:]
    patches, slots, model = tokens.shape
    templates = embedding.shape[0]
    pairs = model // LANES

    @pl.when(pl.program_id(0) == 0)
    def _():
        bias[...] = pair_bias(counts, offsets, slots)
        chosen = lax.broadcasted_iota(jnp.int32, (templates, slots), 0) == layout[...]
        spread[...] = jnp.transpose(chosen.astype(jnp.float32)).astype(jnp.bfloat16)

    rows = dot(spread[...], embedding[...], (1, 0))
    for group in in_groups(pairs, patches, SPATIAL_GROUP):
        values, shares = attention(width, tokens, rows, bias, group)
        attended = by_query(shares, values, width)
        for (pair, p), value, share, result in zip(group, values, shares, attended):
            embedded[p, :, pair_columns(pair)] = value
            weights[p, pair] = share
            by_electrode[pair, of_patch(p, slots, patches), :] = value.astype(jnp.float32) + result
    for pair in range(pairs):
        send_blocks(mixed, pair, by_electrode)


def patches_first(local):
    return local % SUBLANES != 0


def electrode_rows(electrode, electrodes, parts, local):
    start, step = electrode * local, electrodes * local
    if patches_first(local):
        return [pl.ds(start + p, parts, stride=step) for p in range(local)]
    return [pl.ds(start + part * step, local) for part in range(parts)]


def temporal_kernel(width, parts, plane, out_grad, *refs):
    mixed, mixed_grad, (received, returned) = refs[:plane], refs[plane:-2], refs[-2:]
    electrodes, patches, model = out_grad.shape
    local = patches // parts
    pairs = model // LANES
    score_masks = head_masks(width, 0.5 / math.sqrt(width))
    ones = head_masks(width, 1.0)
    for pair in range(pairs):
        take_blocks(mixed, pair, received)
    for group in in_groups(pairs, electrodes, TEMPORAL_GROUP):
        places = [electrode_rows(e, electrodes, parts, local) for _, e in group]
        values = each(
            lambda item, place: jnp.concatenate(
                [received[item[0], rows, :] for rows in place], axis=0
            ).astype(jnp.bfloat16),
            group,
            places,
        )
        cotangents = [out_grad[e, :, pair_columns(pair)] for pair, e in group]
        scaled = each(lambda v: head_rows(v, score_masks), values)
        scores = each(lambda v, s: dot(v, s, (1, 1)), values, scaled)
        heads_grads = each(lambda g: head_rows(g, ones), cotangents)
        grad_weights = each(lambda v, g: dot(v, g, (1, 1)), values, heads_grads)
        shares = weights_by_key(scores)
        grads = back(values, scaled, cotangents, shares, grad_weights, heads_grads, width)
        for (pair, _), place, grad in zip(group, places, grads):
            start = 0
            for rows in place:
                returned[pair, rows, :] = grad[start : start + rows.size]
                start += rows.size
    for pair in range(pairs):
        send_blocks(mixed_grad, pair, returned)


def spatial_back_kernel(width, plane, embedded, weights, *refs):
    mixed_grad, (input_grad, electrode_grad, received) = refs[:plane], refs[-3:]
    patches, slots, model = embedded.shape
    pairs = model // LANES
    score_masks = head_masks(width, 0.5 / math.sqrt(width))
    ones = head_masks(width, 1.0)
    totals = [jnp.zeros((slots, LANES), jnp.float32) for _ in range(pairs)]
    for pair in range(pairs):
        take_blocks(mixed_grad, pair, received)
    for group in in_groups(pairs, patches, SPATIAL_GROUP):
        cotangents = [
            received[pair, of_patch(p, slots, patches), :].astype(jnp.bfloat16)
            for pair, p in group
        ]
        values = [embedded[p, :, pair_columns(pair)] for pair, p in group]
        shares = [weights[p, pair] for pair, p in group]
        scaled = each(lambda v: head_rows(v, score_masks), values)
        heads_grads = each(lambda g: head_rows(g, ones), cotangents)
        grad_weights = each(lambda v, g: dot(v, g, (1, 1)), values, heads_grads)
        grads = back(values, scaled, cotangents, shares, grad_weights, heads_grads, width)
        for (pair, p), grad in zip(group, grads):
            input_grad[p, :, pair_columns(pair)] = grad.astype(jnp.bfloat16)
            totals[pair] = totals[pair] + grad
    for pair in range(pairs):
        electrode_grad[:, pair_columns(pair)] = totals[pair].astype(jnp.bfloat16)


def repack_kernel(far_count, plane, *refs):
    sources, targets, sems = refs[:far_count], refs[-1 - plane : -1], refs[-1]
    copies = [
        pltpu.make_async_copy(source.at[near], target.at[far], sems.at[far, near])
        for far, source in enumerate(sources)
        for near, target in enumerate(targets)
    ]
    for copy in copies:
        copy.start()
    for copy in copies:
        copy.wait()


def share_kernel(shares, everyone):
    total = shares[0].astype(jnp.float32)
    for part in range(1, shares.shape[0]):
        total = total + shares[part].astype(jnp.float32)
    everyone[...] = jnp.broadcast_to(total.astype(jnp.bfloat16)[None], everyone.shape)


def table_kernel(groups, *refs):
    layouts, sums, (table, pieces, sems) = refs[:groups], refs[groups], refs[groups + 1 :]
    owner = lax.axis_index("group")
    count, rows, model = pieces.shape
    slots = sums.shape[0] // groups
    parts = []
    for away in range(groups):
        origin = lax.rem(owner + groups - away, groups)
        parts.append(sums[pl.ds(pl.multiple_of(origin * slots, slots), slots), :])
    sources = jnp.concatenate(parts, axis=0)
    layout = jnp.concatenate([ref[...] for ref in layouts], axis=1)
    copies = []
    for piece in range(count):
        first = owner * (count * rows) + piece * rows
        template = lax.broadcasted_iota(jnp.int32, (rows, groups * slots), 0) + first
        spread = (template == layout).astype(jnp.float32).astype(jnp.bfloat16)
        pieces[piece] = dot(spread, sources, (1, 0))
        copy = pltpu.make_async_copy(
            pieces.at[piece], table.at[pl.ds(piece * rows, rows)], sems.at[piece]
        )
        copy.start()
        copies.append(copy)
    for copy in copies:
        copy.wait()


VMEM = pl.BlockSpec(memory_space=pltpu.VMEM)
SMEM = pl.BlockSpec(memory_space=pltpu.SMEM)
HBM = pl.BlockSpec(memory_space=pltpu.HBM)
ANY = pl.BlockSpec(memory_space=pl.ANY)
PARAMS = pltpu.CompilerParams(vmem_limit_bytes=32 * 1024 * 1024)
STREAMED = pltpu.CompilerParams(vmem_limit_bytes=56 * 1024 * 1024)


def exchange(blocks, following):
    far_count, (plane, rows, columns) = len(blocks), blocks[0].shape
    parts = far_count * plane
    arrived = {0: blocks[0]}
    for far in reversed(range(1, far_count)):
        arrived[far] = lax.ppermute(
            blocks[far], "shard", [(i, i ^ (far * plane)) for i in range(parts)]
        )
    results = pl.pallas_call(
        functools.partial(repack_kernel, far_count, plane),
        out_shape=tuple(jax.ShapeDtypeStruct(x.shape, x.dtype) for x in following)
        + (jax.ShapeDtypeStruct((far_count, rows, columns), jnp.bfloat16),) * plane,
        in_specs=[ANY] * (far_count + len(following)),
        out_specs=(ANY,) * (len(following) + plane),
        scratch_shapes=[pltpu.SemaphoreType.DMA((far_count, plane))],
        input_output_aliases={far_count + place: place for place in range(len(following))},
        compiler_params=PARAMS,
        name="repack",
    )(*[arrived[far] for far in range(far_count)], *following)
    following, packed = results[: len(following)], results[len(following) :]
    near_blocks = [packed[0]] + [
        lax.ppermute(packed[near], "shard", [(i, i ^ near) for i in range(parts)])
        for near in range(1, plane)
    ]
    return near_blocks, list(following)


def body(activations, out_grad, embedding, counts, offsets, layout):
    tokens = activations[0]
    local, slots, model = tokens.shape
    groups = lax.axis_size("group")
    parts = lax.axis_size("shard")
    patches = local * parts
    own = slots // parts
    width = model // HEADS
    templates = embedding.shape[0]
    pairs = STEP // LANES
    chunk = model // CHUNKS
    steps = chunk // STEP
    far_count = parts // PLANE
    assert parts == far_count * PLANE and parts & (parts - 1) == 0

    layouts = [layout] + [
        lax.ppermute(layout, "group", [(i, (i + away) % groups) for i in range(groups)])
        for away in range(1, groups)
    ]
    order = (2, 1, 0, 3) if patches_first(local) else (2, 0, 1, 3)
    cotangent = jnp.transpose(out_grad[0].reshape(parts, local, own, model), order)
    cotangent = cotangent.reshape(own, patches, model)

    def last(shape, first=0):
        lead = (0,) * (len(shape) - 1)
        return pl.BlockSpec(shape, lambda step: lead + (first + step,))

    squares = pl.BlockSpec((local, pairs, slots, 2 * slots), lambda step: (0, step, 0, 0))
    planes = last((local, slots, STEP))
    block = own * local
    far_specs = (last((PLANE, block, STEP)),) * far_count
    far_shapes = (jax.ShapeDtypeStruct((PLANE, block, chunk), jnp.bfloat16),) * far_count
    near_specs = [last((far_count, block, STEP))] * PLANE
    flat_scratch = pltpu.VMEM((pairs, slots * local, LANES), jnp.float32)

    forward = [
        pl.pallas_call(
            functools.partial(spatial_kernel, width),
            grid=(steps,),
            out_shape=(
                jax.ShapeDtypeStruct((local, slots, chunk), jnp.bfloat16),
                jax.ShapeDtypeStruct((local, chunk // LANES, slots, 2 * slots), jnp.bfloat16),
            )
            + far_shapes,
            in_specs=[
                SMEM,
                SMEM,
                VMEM,
                last((templates, STEP), index * steps),
                last((local, slots, STEP), index * steps),
            ],
            out_specs=(planes, squares) + far_specs,
            scratch_shapes=[
                pltpu.VMEM((slots, templates), jnp.bfloat16),
                pltpu.VMEM((slots, 2 * slots), jnp.float32),
                flat_scratch,
            ],
            compiler_params=STREAMED,
            name="spatial",
        )(counts, offsets, layout, embedding, tokens)
        for index in range(CHUNKS)
    ]
    def temporal(index, arrived):
        return pl.pallas_call(
            functools.partial(temporal_kernel, width, parts, PLANE),
            grid=(steps,),
            out_shape=far_shapes,
            in_specs=[last((own, patches, STEP), index * steps)] + near_specs,
            out_specs=far_specs,
            scratch_shapes=[flat_scratch, flat_scratch],
            compiler_params=PARAMS,
            name="temporal",
        )(cotangent, *arrived)

    def spatial_back(index, arrived, before):
        embedded, weights = forward[index][:2]
        return pl.pallas_call(
            functools.partial(spatial_back_kernel, width, PLANE),
            grid=(steps,),
            out_shape=(
                jax.ShapeDtypeStruct(tokens.shape, jnp.bfloat16),
                jax.ShapeDtypeStruct((slots, model), jnp.bfloat16),
            ),
            in_specs=[planes, squares] + near_specs + [ANY] * len(before),
            out_specs=(
                last((local, slots, STEP), index * steps),
                last((slots, STEP), index * steps),
            ),
            scratch_shapes=[flat_scratch],
            input_output_aliases={2 + PLANE + place: place for place in range(len(before))},
            compiler_params=PARAMS,
            name="spatial_back",
        )(embedded, weights, *arrived, *before)

    blocks = list(forward[0][2:])
    gathered = []
    for index in range(CHUNKS):
        if index + 1 < CHUNKS:
            following = list(forward[index + 1][2:])
        else:
            following = temporal(0, gathered[0])
        arrived, blocks = exchange(blocks, following)
        gathered.append(arrived)
    done = []
    for index in range(CHUNKS):
        if index + 1 < CHUNKS:
            following = temporal(index + 1, gathered[index + 1])
        else:
            following = done
        arrived, blocks = exchange(blocks, following)
        done = spatial_back(index, arrived, blocks if index + 1 == CHUNKS else done)
    input_grad, electrode_grad = done

    shares = lax.all_to_all(
        electrode_grad.reshape(parts, own, model), "shard", split_axis=0, concat_axis=0, tiled=True
    )
    everyone = pl.pallas_call(
        share_kernel,
        out_shape=jax.ShapeDtypeStruct((groups * parts, own, model), jnp.bfloat16),
        in_specs=[VMEM],
        out_specs=VMEM,
        compiler_params=PARAMS,
        name="share",
    )(shares)
    everyone = lax.all_to_all(
        everyone, ("group", "shard"), split_axis=0, concat_axis=0, tiled=True
    )
    table_rows = templates // groups
    table_grad = pl.pallas_call(
        functools.partial(table_kernel, groups),
        out_shape=jax.ShapeDtypeStruct((table_rows, model), jnp.float32),
        in_specs=[VMEM] * (groups + 1),
        out_specs=HBM,
        scratch_shapes=[
            pltpu.VMEM((PIECES, table_rows // PIECES, model), jnp.float32),
            pltpu.SemaphoreType.DMA((PIECES,)),
        ],
        compiler_params=PARAMS,
        name="table",
    )(*layouts, everyone.reshape(groups * slots, model))
    return (input_grad[None], table_grad)


def solution(mesh):
    placed = (
        P("group", "shard", None, None),
        P("group", None, "shard", None),
        P(),
        P("group", None),
        P("group", None),
        P("group", None),
    )
    return jax.shard_map(
        body,
        mesh=mesh,
        in_specs=placed,
        out_specs=(P("group", "shard", None, None), P("group", None)),
        check_vma=False,
    )
```

```python
import functools
import math

import jax
import jax.numpy as jnp
from jax import lax
from jax.experimental import pallas as pl
from jax.experimental.pallas import tpu as pltpu
from jax.sharding import PartitionSpec as P

HEADS = 16
BLOCK = 32
LANES = 128
MASKED = -1e30
SUBLANES = 8
STEP = 256
CHUNKS = 2
PLANE = 4
PIECES = 4
SPATIAL_GROUP = 16
TEMPORAL_GROUP = 8


def dot(left, right, over):
    return lax.dot_general(
        left, right, (((over[0],), (over[1],)), ((), ())), preferred_element_type=jnp.float32
    )


def head_masks(width, scale):
    lane = lax.broadcasted_iota(jnp.int32, (1, LANES), 1)
    first = jnp.where(lane < width, scale, 0.0).astype(jnp.bfloat16)
    second = jnp.where(lane < width, 0.0, scale).astype(jnp.bfloat16)
    return first, second


def head_rows(pair, masks):
    return jnp.concatenate([pair * masks[0], pair * masks[1]], axis=0)


def head_columns(rows, width):
    count = rows.shape[0] // 2
    lane = lax.broadcasted_iota(jnp.int32, (count, rows.shape[1]), 1)
    return jnp.where(lane < width, rows[:count], rows[count:])


def each(function, *lists):
    return [function(*items) for items in zip(*lists)]


def weights_by_key(scores):
    tops = each(lambda s: jnp.max(s, axis=0, keepdims=True), scores)
    exponents = each(lambda s, t: jnp.exp(s - t), scores, tops)
    shares = each(lambda e: 1.0 / jnp.sum(e, axis=0, keepdims=True), exponents)
    return each(lambda e, r: (e * r).astype(jnp.bfloat16), exponents, shares)


def by_query(shares, values, width):
    if 2 * values[0].shape[0] != LANES or len(values) % 2:
        return each(lambda s, v: head_columns(dot(s, v, (0, 0)), width), shares, values)
    results = []
    for first in range(0, len(values), 2):
        turned = jnp.transpose(jnp.concatenate(shares[first : first + 2], axis=0))
        one, other = values[first : first + 2]
        zero = jnp.zeros_like(one)
        apart = jnp.concatenate(
            [jnp.concatenate([one, zero], axis=1), jnp.concatenate([zero, other], axis=1)], axis=0
        )
        both = dot(turned, apart, (1, 0))
        results += [head_columns(both[:, :LANES], width), head_columns(both[:, LANES:], width)]
    return results


def back(values, scaled, cotangents, weights, grad_weights, heads_grads, width):
    wide = each(lambda w: w.astype(jnp.float32), weights)
    deltas = each(lambda w, g: jnp.sum(w * g, axis=0, keepdims=True), wide, grad_weights)
    grad_scores = each(
        lambda w, g, d: (w * (g - d)).astype(jnp.bfloat16), wide, grad_weights, deltas
    )
    length = values[0].shape[0]
    whole = length % LANES == 0
    both_ways = grad_scores
    if whole:
        both_ways = each(
            lambda g: jnp.concatenate(
                [
                    g[:, start : start + length] + jnp.transpose(g[:, start : start + length])
                    for start in (0, length)
                ],
                axis=1,
            ),
            grad_scores,
        )
    grads = each(
        lambda c, w, g, hg, hv: c.astype(jnp.float32)
        + dot(jnp.concatenate([w, g], axis=1), jnp.concatenate([hg, hv], axis=0), (1, 0)),
        cotangents,
        weights,
        both_ways,
        heads_grads,
        scaled,
    )
    if whole:
        return grads
    score_scale = 0.5 / math.sqrt(width)
    rest = by_query(grad_scores, values, width)
    return each(lambda g, r: g + score_scale * r, grads, rest)


def pair_bias(counts, offsets, slots):
    def sessions(slot):
        block = slot // BLOCK
        session = jnp.full(slot.shape, -1, jnp.int32)
        for j in range(offsets.shape[1]):
            session = session + (offsets[0, j] <= block).astype(jnp.int32)
        return session

    key_slot = lax.broadcasted_iota(jnp.int32, (slots, 2 * slots), 0)
    query_slot = lax.broadcasted_iota(jnp.int32, (slots, 2 * slots), 1) % slots
    key_session = sessions(key_slot)
    first = jnp.zeros_like(key_slot)
    live = jnp.zeros_like(key_slot)
    for j in range(offsets.shape[1]):
        chosen = key_session == j
        first = jnp.where(chosen, offsets[0, j] * BLOCK, first)
        live = jnp.where(chosen, counts[0, j], live)
    allowed = (key_session == sessions(query_slot)) & (key_slot - first < live)
    return jnp.where(allowed, 0.0, MASKED)


def pair_columns(pair):
    return pl.ds(pair * LANES, LANES)


def in_groups(pairs, rows, size):
    items = [(pair, row) for pair in range(pairs) for row in range(rows)]
    return [items[start : start + size] for start in range(0, len(items), size)]


def of_patch(patch, slots, patches):
    return pl.ds(patch, slots, stride=patches)


def partner_rows(away, count):
    partner = lax.bitwise_xor(lax.axis_index("shard"), away)
    return pl.ds(pl.multiple_of(partner * count, count), count)


def send_blocks(blocks, pair, rows):
    for far, block in enumerate(blocks):
        for near in range(block.shape[0]):
            place = partner_rows(far * block.shape[0] + near, block.shape[1])
            block[near, :, pair_columns(pair)] = rows[pair, place, :].astype(jnp.bfloat16)


def take_blocks(blocks, pair, rows):
    for near, block in enumerate(blocks):
        for far in range(block.shape[0]):
            place = partner_rows(far * len(blocks) + near, block.shape[1])
            rows[pair, place, :] = block[far, :, pair_columns(pair)].astype(jnp.float32)


def attention(width, tokens, rows, bias, group):
    score_masks = head_masks(width, 0.5 / math.sqrt(width))
    values = [
        (
            tokens[p, :, pair_columns(pair)].astype(jnp.float32)
            + rows[:, pair * LANES : (pair + 1) * LANES]
        ).astype(jnp.bfloat16)
        for pair, p in group
    ]
    scores = each(lambda v: dot(v, head_rows(v, score_masks), (1, 1)) + bias[...], values)
    return values, weights_by_key(scores)


def spatial_kernel(width, counts, offsets, layout, embedding, tokens, embedded, weights, *refs):
    mixed, (spread, bias, by_electrode) = refs[:-3], refs[-3:]
    patches, slots, model = tokens.shape
    templates = embedding.shape[0]
    pairs = model // LANES

    @pl.when(pl.program_id(0) == 0)
    def _():
        bias[...] = pair_bias(counts, offsets, slots)
        chosen = lax.broadcasted_iota(jnp.int32, (templates, slots), 0) == layout[...]
        spread[...] = jnp.transpose(chosen.astype(jnp.float32)).astype(jnp.bfloat16)

    rows = dot(spread[...], embedding[...], (1, 0))
    for group in in_groups(pairs, patches, SPATIAL_GROUP):
        values, shares = attention(width, tokens, rows, bias, group)
        attended = by_query(shares, values, width)
        for (pair, p), value, share, result in zip(group, values, shares, attended):
            embedded[p, :, pair_columns(pair)] = value
            weights[p, pair] = share
            by_electrode[pair, of_patch(p, slots, patches), :] = value.astype(jnp.float32) + result
    for pair in range(pairs):
        send_blocks(mixed, pair, by_electrode)


def patches_first(local):
    return local % SUBLANES != 0


def electrode_rows(electrode, electrodes, parts, local):
    start, step = electrode * local, electrodes * local
    if patches_first(local):
        return [pl.ds(start + p, parts, stride=step) for p in range(local)]
    return [pl.ds(start + part * step, local) for part in range(parts)]


def temporal_kernel(width, parts, plane, out_grad, *refs):
    mixed, mixed_grad, (token, received, returned) = refs[:plane], refs[plane:-3], refs[-3:]
    token[...] = jnp.zeros_like(token)
    electrodes, patches, model = out_grad.shape
    local = patches // parts
    pairs = model // LANES
    score_masks = head_masks(width, 0.5 / math.sqrt(width))
    ones = head_masks(width, 1.0)
    for pair in range(pairs):
        take_blocks(mixed, pair, received)
    for group in in_groups(pairs, electrodes, TEMPORAL_GROUP):
        places = [electrode_rows(e, electrodes, parts, local) for _, e in group]
        values = each(
            lambda item, place: jnp.concatenate(
                [received[item[0], rows, :] for rows in place], axis=0
            ).astype(jnp.bfloat16),
            group,
            places,
        )
        cotangents = [out_grad[e, :, pair_columns(pair)] for pair, e in group]
        scaled = each(lambda v: head_rows(v, score_masks), values)
        scores = each(lambda v, s: dot(v, s, (1, 1)), values, scaled)
        heads_grads = each(lambda g: head_rows(g, ones), cotangents)
        grad_weights = each(lambda v, g: dot(v, g, (1, 1)), values, heads_grads)
        shares = weights_by_key(scores)
        grads = back(values, scaled, cotangents, shares, grad_weights, heads_grads, width)
        for (pair, _), place, grad in zip(group, places, grads):
            start = 0
            for rows in place:
                returned[pair, rows, :] = grad[start : start + rows.size]
                start += rows.size
    for pair in range(pairs):
        send_blocks(mixed_grad, pair, returned)


def spatial_back_kernel(width, plane, embedded, weights, *refs):
    mixed_grad, (input_grad, electrode_grad, token, received) = refs[:plane], refs[-4:]
    token[...] = jnp.zeros_like(token)
    patches, slots, model = embedded.shape
    pairs = model // LANES
    score_masks = head_masks(width, 0.5 / math.sqrt(width))
    ones = head_masks(width, 1.0)
    totals = [jnp.zeros((slots, LANES), jnp.float32) for _ in range(pairs)]
    for pair in range(pairs):
        take_blocks(mixed_grad, pair, received)
    for group in in_groups(pairs, patches, SPATIAL_GROUP):
        cotangents = [
            received[pair, of_patch(p, slots, patches), :].astype(jnp.bfloat16)
            for pair, p in group
        ]
        values = [embedded[p, :, pair_columns(pair)] for pair, p in group]
        shares = [weights[p, pair] for pair, p in group]
        scaled = each(lambda v: head_rows(v, score_masks), values)
        heads_grads = each(lambda g: head_rows(g, ones), cotangents)
        grad_weights = each(lambda v, g: dot(v, g, (1, 1)), values, heads_grads)
        grads = back(values, scaled, cotangents, shares, grad_weights, heads_grads, width)
        for (pair, p), grad in zip(group, grads):
            input_grad[p, :, pair_columns(pair)] = grad.astype(jnp.bfloat16)
            totals[pair] = totals[pair] + grad
    for pair in range(pairs):
        electrode_grad[:, pair_columns(pair)] = totals[pair].astype(jnp.bfloat16)


def repack_kernel(far_count, plane, *refs):
    sources, targets, sems = refs[:far_count], refs[-1 - plane : -1], refs[-1]
    copies = [
        pltpu.make_async_copy(source.at[near], target.at[far], sems.at[far, near])
        for far, source in enumerate(sources)
        for near, target in enumerate(targets)
    ]
    for copy in copies:
        copy.start()
    for copy in copies:
        copy.wait()


def share_kernel(shares, everyone):
    total = shares[0].astype(jnp.float32)
    for part in range(1, shares.shape[0]):
        total = total + shares[part].astype(jnp.float32)
    everyone[...] = jnp.broadcast_to(total.astype(jnp.bfloat16)[None], everyone.shape)


def table_kernel(groups, *refs):
    layouts, sums, (table, pieces, sems) = refs[:groups], refs[groups], refs[groups + 1 :]
    owner = lax.axis_index("group")
    count, rows, model = pieces.shape
    slots = sums.shape[0] // groups
    parts = []
    for away in range(groups):
        origin = lax.rem(owner + groups - away, groups)
        parts.append(sums[pl.ds(pl.multiple_of(origin * slots, slots), slots), :])
    sources = jnp.concatenate(parts, axis=0)
    layout = jnp.concatenate([ref[...] for ref in layouts], axis=1)
    copies = []
    for piece in range(count):
        first = owner * (count * rows) + piece * rows
        template = lax.broadcasted_iota(jnp.int32, (rows, groups * slots), 0) + first
        spread = (template == layout).astype(jnp.float32).astype(jnp.bfloat16)
        pieces[piece] = dot(spread, sources, (1, 0))
        copy = pltpu.make_async_copy(
            pieces.at[piece], table.at[pl.ds(piece * rows, rows)], sems.at[piece]
        )
        copy.start()
        copies.append(copy)
    for copy in copies:
        copy.wait()


VMEM = pl.BlockSpec(memory_space=pltpu.VMEM)
SMEM = pl.BlockSpec(memory_space=pltpu.SMEM)
HBM = pl.BlockSpec(memory_space=pltpu.HBM)
ANY = pl.BlockSpec(memory_space=pl.ANY)
PARAMS = pltpu.CompilerParams(vmem_limit_bytes=32 * 1024 * 1024)
STREAMED = pltpu.CompilerParams(vmem_limit_bytes=56 * 1024 * 1024)


def exchange(blocks, tokens):
    far_count, (plane, rows, columns) = len(blocks), blocks[0].shape
    parts = far_count * plane
    arrived = {0: blocks[0]}
    for far in reversed(range(1, far_count)):
        arrived[far] = lax.ppermute(
            blocks[far], "shard", [(i, i ^ (far * plane)) for i in range(parts)]
        )
    packed = pl.pallas_call(
        functools.partial(repack_kernel, far_count, plane),
        out_shape=(jax.ShapeDtypeStruct((far_count, rows, columns), jnp.bfloat16),) * plane,
        in_specs=[ANY] * (far_count + len(tokens)),
        out_specs=(ANY,) * plane,
        scratch_shapes=[pltpu.SemaphoreType.DMA((far_count, plane))],
        compiler_params=PARAMS,
        name="repack",
    )(*[arrived[far] for far in range(far_count)], *tokens)
    return [packed[0]] + [
        lax.ppermute(packed[near], "shard", [(i, i ^ near) for i in range(parts)])
        for near in range(1, plane)
    ]


def body(activations, out_grad, embedding, counts, offsets, layout):
    tokens = activations[0]
    local, slots, model = tokens.shape
    groups = lax.axis_size("group")
    parts = lax.axis_size("shard")
    patches = local * parts
    own = slots // parts
    width = model // HEADS
    templates = embedding.shape[0]
    pairs = STEP // LANES
    chunk = model // CHUNKS
    steps = chunk // STEP
    far_count = parts // PLANE
    assert parts == far_count * PLANE and parts & (parts - 1) == 0

    layouts = [layout] + [
        lax.ppermute(layout, "group", [(i, (i + away) % groups) for i in range(groups)])
        for away in range(1, groups)
    ]
    order = (2, 1, 0, 3) if patches_first(local) else (2, 0, 1, 3)
    cotangent = jnp.transpose(out_grad[0].reshape(parts, local, own, model), order)
    cotangent = cotangent.reshape(own, patches, model)

    def last(shape, first=0):
        lead = (0,) * (len(shape) - 1)
        return pl.BlockSpec(shape, lambda step: lead + (first + step,))

    squares = pl.BlockSpec((local, pairs, slots, 2 * slots), lambda step: (0, step, 0, 0))
    planes = last((local, slots, STEP))
    block = own * local
    far_specs = (last((PLANE, block, STEP)),) * far_count
    far_shapes = (jax.ShapeDtypeStruct((PLANE, block, chunk), jnp.bfloat16),) * far_count
    near_specs = [last((far_count, block, STEP))] * PLANE
    flat_scratch = pltpu.VMEM((pairs, slots * local, LANES), jnp.float32)

    forward = [
        pl.pallas_call(
            functools.partial(spatial_kernel, width),
            grid=(steps,),
            out_shape=(
                jax.ShapeDtypeStruct((local, slots, chunk), jnp.bfloat16),
                jax.ShapeDtypeStruct((local, chunk // LANES, slots, 2 * slots), jnp.bfloat16),
            )
            + far_shapes,
            in_specs=[
                SMEM,
                SMEM,
                VMEM,
                last((templates, STEP), index * steps),
                last((local, slots, STEP), index * steps),
            ],
            out_specs=(planes, squares) + far_specs,
            scratch_shapes=[
                pltpu.VMEM((slots, templates), jnp.bfloat16),
                pltpu.VMEM((slots, 2 * slots), jnp.float32),
                flat_scratch,
            ],
            compiler_params=STREAMED,
            name="spatial",
        )(counts, offsets, layout, embedding, tokens)
        for index in range(CHUNKS)
    ]
    token_shape = jax.ShapeDtypeStruct((SUBLANES, LANES), jnp.float32)
    token_spec = pl.BlockSpec((SUBLANES, LANES), lambda step: (0, 0))

    def temporal(index, arrived):
        return pl.pallas_call(
            functools.partial(temporal_kernel, width, parts, PLANE),
            grid=(steps,),
            out_shape=far_shapes + (token_shape,),
            in_specs=[last((own, patches, STEP), index * steps)] + near_specs,
            out_specs=far_specs + (token_spec,),
            scratch_shapes=[flat_scratch, flat_scratch],
            compiler_params=PARAMS,
            name="temporal",
        )(cotangent, *arrived)

    def spatial_back(index, arrived, before):
        embedded, weights = forward[index][:2]
        return pl.pallas_call(
            functools.partial(spatial_back_kernel, width, PLANE),
            grid=(steps,),
            out_shape=(
                jax.ShapeDtypeStruct(tokens.shape, jnp.bfloat16),
                jax.ShapeDtypeStruct((slots, model), jnp.bfloat16),
                token_shape,
            ),
            in_specs=[planes, squares] + near_specs + [ANY] * len(before),
            out_specs=(
                last((local, slots, STEP), index * steps),
                last((slots, STEP), index * steps),
                token_spec,
            ),
            scratch_shapes=[flat_scratch],
            input_output_aliases={2 + PLANE + place: place for place in range(len(before))},
            compiler_params=PARAMS,
            name="spatial_back",
        )(embedded, weights, *arrived, *before)

    mixed_grads, tokens_made = [], []
    for index in range(CHUNKS):
        arrived = exchange(forward[index][2:], tokens_made)
        *blocks, made = temporal(index, arrived)
        mixed_grads.append(blocks)
        tokens_made = [made]
    done, tokens_made = [], []
    for index in range(CHUNKS):
        arrived = exchange(mixed_grads[index], tokens_made)
        *done, made = spatial_back(index, arrived, done)
        tokens_made = [made]
    input_grad, electrode_grad = done

    shares = lax.all_to_all(
        electrode_grad.reshape(parts, own, model), "shard", split_axis=0, concat_axis=0, tiled=True
    )
    everyone = pl.pallas_call(
        share_kernel,
        out_shape=jax.ShapeDtypeStruct((groups * parts, own, model), jnp.bfloat16),
        in_specs=[VMEM],
        out_specs=VMEM,
        compiler_params=PARAMS,
        name="share",
    )(shares)
    everyone = lax.all_to_all(
        everyone, ("group", "shard"), split_axis=0, concat_axis=0, tiled=True
    )
    table_rows = templates // groups
    table_grad = pl.pallas_call(
        functools.partial(table_kernel, groups),
        out_shape=jax.ShapeDtypeStruct((table_rows, model), jnp.float32),
        in_specs=[VMEM] * (groups + 1),
        out_specs=HBM,
        scratch_shapes=[
            pltpu.VMEM((PIECES, table_rows // PIECES, model), jnp.float32),
            pltpu.SemaphoreType.DMA((PIECES,)),
        ],
        compiler_params=PARAMS,
        name="table",
    )(*layouts, everyone.reshape(groups * slots, model))
    return (input_grad[None], table_grad)


def solution(mesh):
    placed = (
        P("group", "shard", None, None),
        P("group", None, "shard", None),
        P(),
        P("group", None),
        P("group", None),
        P("group", None),
    )
    return jax.shard_map(
        body,
        mesh=mesh,
        in_specs=placed,
        out_specs=(P("group", "shard", None, None), P("group", None)),
        check_vma=False,
    )
```

```python
import functools
import math

import jax
import jax.numpy as jnp
from jax import lax
from jax.experimental import pallas as pl
from jax.experimental.pallas import tpu as pltpu
from jax.sharding import PartitionSpec as P

HEADS = 16
BLOCK = 32
LANES = 128
MASKED = -1e30
SUBLANES = 8
STEP = 256
CHUNKS = 2
PLANE = 4
PIECES = 4
SPATIAL_GROUP = 16
TEMPORAL_GROUP = 8


def dot(left, right, over):
    return lax.dot_general(
        left, right, (((over[0],), (over[1],)), ((), ())), preferred_element_type=jnp.float32
    )


def head_masks(width, scale):
    lane = lax.broadcasted_iota(jnp.int32, (1, LANES), 1)
    first = jnp.where(lane < width, scale, 0.0).astype(jnp.bfloat16)
    second = jnp.where(lane < width, 0.0, scale).astype(jnp.bfloat16)
    return first, second


def head_rows(pair, masks):
    return jnp.concatenate([pair * masks[0], pair * masks[1]], axis=0)


def head_columns(rows, width):
    count = rows.shape[0] // 2
    lane = lax.broadcasted_iota(jnp.int32, (count, rows.shape[1]), 1)
    return jnp.where(lane < width, rows[:count], rows[count:])


def each(function, *lists):
    return [function(*items) for items in zip(*lists)]


def weights_by_key(scores):
    tops = each(lambda s: jnp.max(s, axis=0, keepdims=True), scores)
    exponents = each(lambda s, t: jnp.exp(s - t), scores, tops)
    shares = each(lambda e: 1.0 / jnp.sum(e, axis=0, keepdims=True), exponents)
    return each(lambda e, r: (e * r).astype(jnp.bfloat16), exponents, shares)


def by_query(shares, values, width):
    if 2 * values[0].shape[0] != LANES or len(values) % 2:
        return each(lambda s, v: head_columns(dot(s, v, (0, 0)), width), shares, values)
    results = []
    for first in range(0, len(values), 2):
        turned = jnp.transpose(jnp.concatenate(shares[first : first + 2], axis=0))
        one, other = values[first : first + 2]
        zero = jnp.zeros_like(one)
        apart = jnp.concatenate(
            [jnp.concatenate([one, zero], axis=1), jnp.concatenate([zero, other], axis=1)], axis=0
        )
        both = dot(turned, apart, (1, 0))
        results += [head_columns(both[:, :LANES], width), head_columns(both[:, LANES:], width)]
    return results


def back(values, scaled, cotangents, weights, grad_weights, heads_grads, width):
    wide = each(lambda w: w.astype(jnp.float32), weights)
    deltas = each(lambda w, g: jnp.sum(w * g, axis=0, keepdims=True), wide, grad_weights)
    grad_scores = each(
        lambda w, g, d: (w * (g - d)).astype(jnp.bfloat16), wide, grad_weights, deltas
    )
    length = values[0].shape[0]
    whole = length % LANES == 0
    both_ways = grad_scores
    if whole:
        both_ways = each(
            lambda g: jnp.concatenate(
                [
                    g[:, start : start + length] + jnp.transpose(g[:, start : start + length])
                    for start in (0, length)
                ],
                axis=1,
            ),
            grad_scores,
        )
    grads = each(
        lambda c, w, g, hg, hv: c.astype(jnp.float32)
        + dot(jnp.concatenate([w, g], axis=1), jnp.concatenate([hg, hv], axis=0), (1, 0)),
        cotangents,
        weights,
        both_ways,
        heads_grads,
        scaled,
    )
    if whole:
        return grads
    score_scale = 0.5 / math.sqrt(width)
    rest = by_query(grad_scores, values, width)
    return each(lambda g, r: g + score_scale * r, grads, rest)


def pair_bias(counts, offsets, slots):
    def sessions(slot):
        block = slot // BLOCK
        session = jnp.full(slot.shape, -1, jnp.int32)
        for j in range(offsets.shape[1]):
            session = session + (offsets[0, j] <= block).astype(jnp.int32)
        return session

    key_slot = lax.broadcasted_iota(jnp.int32, (slots, 2 * slots), 0)
    query_slot = lax.broadcasted_iota(jnp.int32, (slots, 2 * slots), 1) % slots
    key_session = sessions(key_slot)
    first = jnp.zeros_like(key_slot)
    live = jnp.zeros_like(key_slot)
    for j in range(offsets.shape[1]):
        chosen = key_session == j
        first = jnp.where(chosen, offsets[0, j] * BLOCK, first)
        live = jnp.where(chosen, counts[0, j], live)
    allowed = (key_session == sessions(query_slot)) & (key_slot - first < live)
    return jnp.where(allowed, 0.0, MASKED)


def pair_columns(pair):
    return pl.ds(pair * LANES, LANES)


def in_groups(pairs, rows, size):
    items = [(pair, row) for pair in range(pairs) for row in range(rows)]
    return [items[start : start + size] for start in range(0, len(items), size)]


def of_patch(patch, slots, patches):
    return pl.ds(patch, slots, stride=patches)


def partner_rows(away, count):
    partner = lax.bitwise_xor(lax.axis_index("shard"), away)
    return pl.ds(pl.multiple_of(partner * count, count), count)


def send_blocks(blocks, pair, rows):
    for far, block in enumerate(blocks):
        for near in range(block.shape[0]):
            place = partner_rows(far * block.shape[0] + near, block.shape[1])
            block[near, :, pair_columns(pair)] = rows[pair, place, :].astype(jnp.bfloat16)


def take_blocks(blocks, pair, rows):
    for near, block in enumerate(blocks):
        for far in range(block.shape[0]):
            place = partner_rows(far * len(blocks) + near, block.shape[1])
            rows[pair, place, :] = block[far, :, pair_columns(pair)].astype(jnp.float32)


def attention(width, tokens, rows, bias, group):
    score_masks = head_masks(width, 0.5 / math.sqrt(width))
    values = [
        (
            tokens[p, :, pair_columns(pair)].astype(jnp.float32)
            + rows[:, pair * LANES : (pair + 1) * LANES]
        ).astype(jnp.bfloat16)
        for pair, p in group
    ]
    scores = each(lambda v: dot(v, head_rows(v, score_masks), (1, 1)) + bias[...], values)
    return values, weights_by_key(scores)


def spatial_kernel(width, counts, offsets, layout, embedding, tokens, embedded, weights, *refs):
    mixed, (token, spread, bias, by_electrode) = refs[:-4], refs[-4:]
    token[...] = jnp.zeros_like(token)
    patches, slots, model = tokens.shape
    templates = embedding.shape[0]
    pairs = model // LANES

    @pl.when(pl.program_id(0) == 0)
    def _():
        bias[...] = pair_bias(counts, offsets, slots)
        chosen = lax.broadcasted_iota(jnp.int32, (templates, slots), 0) == layout[...]
        spread[...] = jnp.transpose(chosen.astype(jnp.float32)).astype(jnp.bfloat16)

    rows = dot(spread[...], embedding[...], (1, 0))
    for group in in_groups(pairs, patches, SPATIAL_GROUP):
        values, shares = attention(width, tokens, rows, bias, group)
        attended = by_query(shares, values, width)
        for (pair, p), value, share, result in zip(group, values, shares, attended):
            embedded[p, :, pair_columns(pair)] = value
            weights[p, pair] = share
            by_electrode[pair, of_patch(p, slots, patches), :] = value.astype(jnp.float32) + result
    for pair in range(pairs):
        send_blocks(mixed, pair, by_electrode)


def patches_first(local):
    return local % SUBLANES != 0


def electrode_rows(electrode, electrodes, parts, local):
    start, step = electrode * local, electrodes * local
    if patches_first(local):
        return [pl.ds(start + p, parts, stride=step) for p in range(local)]
    return [pl.ds(start + part * step, local) for part in range(parts)]


def temporal_kernel(width, parts, plane, out_grad, *refs):
    mixed, mixed_grad, (token, received, returned) = refs[:plane], refs[plane:-3], refs[-3:]
    token[...] = jnp.zeros_like(token)
    electrodes, patches, model = out_grad.shape
    local = patches // parts
    pairs = model // LANES
    score_masks = head_masks(width, 0.5 / math.sqrt(width))
    ones = head_masks(width, 1.0)
    for pair in range(pairs):
        take_blocks(mixed, pair, received)
    for group in in_groups(pairs, electrodes, TEMPORAL_GROUP):
        places = [electrode_rows(e, electrodes, parts, local) for _, e in group]
        values = each(
            lambda item, place: jnp.concatenate(
                [received[item[0], rows, :] for rows in place], axis=0
            ).astype(jnp.bfloat16),
            group,
            places,
        )
        cotangents = [out_grad[e, :, pair_columns(pair)] for pair, e in group]
        scaled = each(lambda v: head_rows(v, score_masks), values)
        scores = each(lambda v, s: dot(v, s, (1, 1)), values, scaled)
        heads_grads = each(lambda g: head_rows(g, ones), cotangents)
        grad_weights = each(lambda v, g: dot(v, g, (1, 1)), values, heads_grads)
        shares = weights_by_key(scores)
        grads = back(values, scaled, cotangents, shares, grad_weights, heads_grads, width)
        for (pair, _), place, grad in zip(group, places, grads):
            start = 0
            for rows in place:
                returned[pair, rows, :] = grad[start : start + rows.size]
                start += rows.size
    for pair in range(pairs):
        send_blocks(mixed_grad, pair, returned)


def spatial_back_kernel(width, plane, embedded, weights, *refs):
    mixed_grad, (input_grad, electrode_grad, token, received) = refs[:plane], refs[-4:]
    token[...] = jnp.zeros_like(token)
    patches, slots, model = embedded.shape
    pairs = model // LANES
    score_masks = head_masks(width, 0.5 / math.sqrt(width))
    ones = head_masks(width, 1.0)
    totals = [jnp.zeros((slots, LANES), jnp.float32) for _ in range(pairs)]
    for pair in range(pairs):
        take_blocks(mixed_grad, pair, received)
    for group in in_groups(pairs, patches, SPATIAL_GROUP):
        cotangents = [
            received[pair, of_patch(p, slots, patches), :].astype(jnp.bfloat16)
            for pair, p in group
        ]
        values = [embedded[p, :, pair_columns(pair)] for pair, p in group]
        shares = [weights[p, pair] for pair, p in group]
        scaled = each(lambda v: head_rows(v, score_masks), values)
        heads_grads = each(lambda g: head_rows(g, ones), cotangents)
        grad_weights = each(lambda v, g: dot(v, g, (1, 1)), values, heads_grads)
        grads = back(values, scaled, cotangents, shares, grad_weights, heads_grads, width)
        for (pair, p), grad in zip(group, grads):
            input_grad[p, :, pair_columns(pair)] = grad.astype(jnp.bfloat16)
            totals[pair] = totals[pair] + grad
    for pair in range(pairs):
        electrode_grad[:, pair_columns(pair)] = totals[pair].astype(jnp.bfloat16)


def repack_kernel(far_count, plane, *refs):
    sources, targets, sems = refs[:far_count], refs[-1 - plane : -1], refs[-1]
    copies = [
        pltpu.make_async_copy(source.at[near], target.at[far], sems.at[far, near])
        for far, source in enumerate(sources)
        for near, target in enumerate(targets)
    ]
    for copy in copies:
        copy.start()
    for copy in copies:
        copy.wait()


def share_kernel(shares, everyone):
    total = shares[0].astype(jnp.float32)
    for part in range(1, shares.shape[0]):
        total = total + shares[part].astype(jnp.float32)
    everyone[...] = jnp.broadcast_to(total.astype(jnp.bfloat16)[None], everyone.shape)


def table_kernel(groups, *refs):
    layouts, sums, (table, pieces, sems) = refs[:groups], refs[groups], refs[groups + 1 :]
    owner = lax.axis_index("group")
    count, rows, model = pieces.shape
    slots = sums.shape[0] // groups
    parts = []
    for away in range(groups):
        origin = lax.rem(owner + groups - away, groups)
        parts.append(sums[pl.ds(pl.multiple_of(origin * slots, slots), slots), :])
    sources = jnp.concatenate(parts, axis=0)
    layout = jnp.concatenate([ref[...] for ref in layouts], axis=1)
    copies = []
    for piece in range(count):
        first = owner * (count * rows) + piece * rows
        template = lax.broadcasted_iota(jnp.int32, (rows, groups * slots), 0) + first
        spread = (template == layout).astype(jnp.float32).astype(jnp.bfloat16)
        pieces[piece] = dot(spread, sources, (1, 0))
        copy = pltpu.make_async_copy(
            pieces.at[piece], table.at[pl.ds(piece * rows, rows)], sems.at[piece]
        )
        copy.start()
        copies.append(copy)
    for copy in copies:
        copy.wait()


VMEM = pl.BlockSpec(memory_space=pltpu.VMEM)
SMEM = pl.BlockSpec(memory_space=pltpu.SMEM)
HBM = pl.BlockSpec(memory_space=pltpu.HBM)
ANY = pl.BlockSpec(memory_space=pl.ANY)
PARAMS = pltpu.CompilerParams(vmem_limit_bytes=32 * 1024 * 1024)
STREAMED = pltpu.CompilerParams(vmem_limit_bytes=56 * 1024 * 1024)


def exchange(blocks, tokens):
    far_count, (plane, rows, columns) = len(blocks), blocks[0].shape
    parts = far_count * plane
    arrived = {0: blocks[0]}
    for far in reversed(range(1, far_count)):
        arrived[far] = lax.ppermute(
            blocks[far], "shard", [(i, i ^ (far * plane)) for i in range(parts)]
        )
    packed = pl.pallas_call(
        functools.partial(repack_kernel, far_count, plane),
        out_shape=(jax.ShapeDtypeStruct((far_count, rows, columns), jnp.bfloat16),) * plane,
        in_specs=[ANY] * (far_count + len(tokens)),
        out_specs=(ANY,) * plane,
        scratch_shapes=[pltpu.SemaphoreType.DMA((far_count, plane))],
        compiler_params=PARAMS,
        name="repack",
    )(*[arrived[far] for far in range(far_count)], *tokens)
    return [packed[0]] + [
        lax.ppermute(packed[near], "shard", [(i, i ^ near) for i in range(parts)])
        for near in range(1, plane)
    ]


def body(activations, out_grad, embedding, counts, offsets, layout):
    tokens = activations[0]
    local, slots, model = tokens.shape
    groups = lax.axis_size("group")
    parts = lax.axis_size("shard")
    patches = local * parts
    own = slots // parts
    width = model // HEADS
    templates = embedding.shape[0]
    pairs = STEP // LANES
    chunk = model // CHUNKS
    steps = chunk // STEP
    far_count = parts // PLANE
    assert parts == far_count * PLANE and parts & (parts - 1) == 0

    layouts = [layout] + [
        lax.ppermute(layout, "group", [(i, (i + away) % groups) for i in range(groups)])
        for away in range(1, groups)
    ]
    order = (2, 1, 0, 3) if patches_first(local) else (2, 0, 1, 3)
    cotangent = jnp.transpose(out_grad[0].reshape(parts, local, own, model), order)
    cotangent = cotangent.reshape(own, patches, model)

    def last(shape, first=0):
        lead = (0,) * (len(shape) - 1)
        return pl.BlockSpec(shape, lambda step: lead + (first + step,))

    squares = pl.BlockSpec((local, pairs, slots, 2 * slots), lambda step: (0, step, 0, 0))
    planes = last((local, slots, STEP))
    block = own * local
    far_specs = (last((PLANE, block, STEP)),) * far_count
    far_shapes = (jax.ShapeDtypeStruct((PLANE, block, chunk), jnp.bfloat16),) * far_count
    near_specs = [last((far_count, block, STEP))] * PLANE
    flat_scratch = pltpu.VMEM((pairs, slots * local, LANES), jnp.float32)

    token_shape = jax.ShapeDtypeStruct((SUBLANES, LANES), jnp.float32)
    token_spec = pl.BlockSpec((SUBLANES, LANES), lambda step: (0, 0))

    forward = [
        pl.pallas_call(
            functools.partial(spatial_kernel, width),
            grid=(steps,),
            out_shape=(
                jax.ShapeDtypeStruct((local, slots, chunk), jnp.bfloat16),
                jax.ShapeDtypeStruct((local, chunk // LANES, slots, 2 * slots), jnp.bfloat16),
            )
            + far_shapes
            + (token_shape,),
            in_specs=[
                SMEM,
                SMEM,
                VMEM,
                last((templates, STEP), index * steps),
                last((local, slots, STEP), index * steps),
            ],
            out_specs=(planes, squares) + far_specs + (token_spec,),
            scratch_shapes=[
                pltpu.VMEM((slots, templates), jnp.bfloat16),
                pltpu.VMEM((slots, 2 * slots), jnp.float32),
                flat_scratch,
            ],
            compiler_params=STREAMED,
            name="spatial",
        )(counts, offsets, layout, embedding, tokens)
        for index in range(CHUNKS)
    ]
    def temporal(index, arrived):
        return pl.pallas_call(
            functools.partial(temporal_kernel, width, parts, PLANE),
            grid=(steps,),
            out_shape=far_shapes + (token_shape,),
            in_specs=[last((own, patches, STEP), index * steps)] + near_specs,
            out_specs=far_specs + (token_spec,),
            scratch_shapes=[flat_scratch, flat_scratch],
            compiler_params=PARAMS,
            name="temporal",
        )(cotangent, *arrived)

    def spatial_back(index, arrived, before):
        embedded, weights = forward[index][:2]
        return pl.pallas_call(
            functools.partial(spatial_back_kernel, width, PLANE),
            grid=(steps,),
            out_shape=(
                jax.ShapeDtypeStruct(tokens.shape, jnp.bfloat16),
                jax.ShapeDtypeStruct((slots, model), jnp.bfloat16),
                token_shape,
            ),
            in_specs=[planes, squares] + near_specs + [ANY] * len(before),
            out_specs=(
                last((local, slots, STEP), index * steps),
                last((slots, STEP), index * steps),
                token_spec,
            ),
            scratch_shapes=[flat_scratch],
            input_output_aliases={2 + PLANE + place: place for place in range(len(before))},
            compiler_params=PARAMS,
            name="spatial_back",
        )(embedded, weights, *arrived, *before)

    def ordered(*tokens_made):
        return [made for made in tokens_made if made is not None]

    mixed_grads, temporal_tokens = [], [None]
    for index in range(CHUNKS):
        ahead = forward[index + 1][-1] if index + 1 < CHUNKS else None
        arrived = exchange(forward[index][2:-1], ordered(ahead, temporal_tokens[-1]))
        *blocks, made = temporal(index, arrived)
        mixed_grads.append(blocks)
        temporal_tokens.append(made)
    done, made = [], None
    for index in range(CHUNKS):
        ahead = temporal_tokens[index + 2] if index + 1 < CHUNKS else None
        arrived = exchange(mixed_grads[index], ordered(ahead, made))
        *done, made = spatial_back(index, arrived, done)
    input_grad, electrode_grad = done

    shares = lax.all_to_all(
        electrode_grad.reshape(parts, own, model), "shard", split_axis=0, concat_axis=0, tiled=True
    )
    everyone = pl.pallas_call(
        share_kernel,
        out_shape=jax.ShapeDtypeStruct((groups * parts, own, model), jnp.bfloat16),
        in_specs=[VMEM],
        out_specs=VMEM,
        compiler_params=PARAMS,
        name="share",
    )(shares)
    everyone = lax.all_to_all(
        everyone, ("group", "shard"), split_axis=0, concat_axis=0, tiled=True
    )
    table_rows = templates // groups
    table_grad = pl.pallas_call(
        functools.partial(table_kernel, groups),
        out_shape=jax.ShapeDtypeStruct((table_rows, model), jnp.float32),
        in_specs=[VMEM] * (groups + 1),
        out_specs=HBM,
        scratch_shapes=[
            pltpu.VMEM((PIECES, table_rows // PIECES, model), jnp.float32),
            pltpu.SemaphoreType.DMA((PIECES,)),
        ],
        compiler_params=PARAMS,
        name="table",
    )(*layouts, everyone.reshape(groups * slots, model))
    return (input_grad[None], table_grad)


def solution(mesh):
    placed = (
        P("group", "shard", None, None),
        P("group", None, "shard", None),
        P(),
        P("group", None),
        P("group", None),
        P("group", None),
    )
    return jax.shard_map(
        body,
        mesh=mesh,
        in_specs=placed,
        out_specs=(P("group", "shard", None, None), P("group", None)),
        check_vma=False,
    )
```

```python
import functools
import math

import jax
import jax.numpy as jnp
from jax import lax
from jax.experimental import pallas as pl
from jax.experimental.pallas import tpu as pltpu
from jax.sharding import PartitionSpec as P

HEADS = 16
BLOCK = 32
LANES = 128
MASKED = -1e30
SUBLANES = 8
STEP = 256
PIECES = 4
SPATIAL_GROUP = 16
TEMPORAL_GROUP = 8


def dot(left, right, over):
    return lax.dot_general(
        left, right, (((over[0],), (over[1],)), ((), ())), preferred_element_type=jnp.float32
    )


def head_masks(width, scale):
    lane = lax.broadcasted_iota(jnp.int32, (1, LANES), 1)
    first = jnp.where(lane < width, scale, 0.0).astype(jnp.bfloat16)
    second = jnp.where(lane < width, 0.0, scale).astype(jnp.bfloat16)
    return first, second


def head_rows(pair, masks):
    return jnp.concatenate([pair * masks[0], pair * masks[1]], axis=0)


def head_columns(rows, width):
    count = rows.shape[0] // 2
    lane = lax.broadcasted_iota(jnp.int32, (count, rows.shape[1]), 1)
    return jnp.where(lane < width, rows[:count], rows[count:])


def each(function, *lists):
    return [function(*items) for items in zip(*lists)]


def weights_by_key(scores):
    tops = each(lambda s: jnp.max(s, axis=0, keepdims=True), scores)
    exponents = each(lambda s, t: jnp.exp(s - t), scores, tops)
    shares = each(lambda e: 1.0 / jnp.sum(e, axis=0, keepdims=True), exponents)
    return each(lambda e, r: (e * r).astype(jnp.bfloat16), exponents, shares)


def by_query(shares, values, width):
    if 2 * values[0].shape[0] != LANES or len(values) % 2:
        return each(lambda s, v: head_columns(dot(s, v, (0, 0)), width), shares, values)
    results = []
    for first in range(0, len(values), 2):
        turned = jnp.transpose(jnp.concatenate(shares[first : first + 2], axis=0))
        one, other = values[first : first + 2]
        zero = jnp.zeros_like(one)
        apart = jnp.concatenate(
            [jnp.concatenate([one, zero], axis=1), jnp.concatenate([zero, other], axis=1)], axis=0
        )
        both = dot(turned, apart, (1, 0))
        results += [head_columns(both[:, :LANES], width), head_columns(both[:, LANES:], width)]
    return results


def back(values, scaled, cotangents, weights, grad_weights, heads_grads, width):
    wide = each(lambda w: w.astype(jnp.float32), weights)
    deltas = each(lambda w, g: jnp.sum(w * g, axis=0, keepdims=True), wide, grad_weights)
    grad_scores = each(
        lambda w, g, d: (w * (g - d)).astype(jnp.bfloat16), wide, grad_weights, deltas
    )
    length = values[0].shape[0]
    whole = length % LANES == 0
    both_ways = grad_scores
    if whole:
        both_ways = each(
            lambda g: jnp.concatenate(
                [
                    g[:, start : start + length] + jnp.transpose(g[:, start : start + length])
                    for start in (0, length)
                ],
                axis=1,
            ),
            grad_scores,
        )
    grads = each(
        lambda c, w, g, hg, hv: c.astype(jnp.float32)
        + dot(jnp.concatenate([w, g], axis=1), jnp.concatenate([hg, hv], axis=0), (1, 0)),
        cotangents,
        weights,
        both_ways,
        heads_grads,
        scaled,
    )
    if whole:
        return grads
    score_scale = 0.5 / math.sqrt(width)
    rest = by_query(grad_scores, values, width)
    return each(lambda g, r: g + score_scale * r, grads, rest)


def pair_bias(counts, offsets, slots):
    def sessions(slot):
        block = slot // BLOCK
        session = jnp.full(slot.shape, -1, jnp.int32)
        for j in range(offsets.shape[1]):
            session = session + (offsets[0, j] <= block).astype(jnp.int32)
        return session

    key_slot = lax.broadcasted_iota(jnp.int32, (slots, 2 * slots), 0)
    query_slot = lax.broadcasted_iota(jnp.int32, (slots, 2 * slots), 1) % slots
    key_session = sessions(key_slot)
    first = jnp.zeros_like(key_slot)
    live = jnp.zeros_like(key_slot)
    for j in range(offsets.shape[1]):
        chosen = key_session == j
        first = jnp.where(chosen, offsets[0, j] * BLOCK, first)
        live = jnp.where(chosen, counts[0, j], live)
    allowed = (key_session == sessions(query_slot)) & (key_slot - first < live)
    return jnp.where(allowed, 0.0, MASKED)


def pair_columns(pair):
    return pl.ds(pair * LANES, LANES)


def in_groups(pairs, rows, size):
    items = [(pair, row) for pair in range(pairs) for row in range(rows)]
    return [items[start : start + size] for start in range(0, len(items), size)]


def of_patch(patch, slots, patches):
    return pl.ds(patch, slots, stride=patches)


def attention(width, tokens, rows, bias, group):
    score_masks = head_masks(width, 0.5 / math.sqrt(width))
    values = [
        (
            tokens[p, :, pair_columns(pair)].astype(jnp.float32)
            + rows[:, pair * LANES : (pair + 1) * LANES]
        ).astype(jnp.bfloat16)
        for pair, p in group
    ]
    scores = each(lambda v: dot(v, head_rows(v, score_masks), (1, 1)) + bias[...], values)
    return values, weights_by_key(scores)


def spatial_kernel(
    width, counts, offsets, layout, all_embedding, all_tokens, embedded, weights, mixed,
    spread, bias, by_electrode, kept_embedding, kept_tokens, sems,
):
    patches, slots, model = embedded.shape
    templates = all_embedding.shape[0]
    pairs = model // LANES
    step = pl.program_id(0)

    def copies(at):
        columns = pl.ds(at * model, model)
        return (
            pltpu.make_async_copy(
                all_tokens.at[:, :, columns], kept_tokens.at[at], sems.at[at, 0]
            ),
            pltpu.make_async_copy(
                all_embedding.at[:, columns], kept_embedding.at[at], sems.at[at, 1]
            ),
        )

    @pl.when(step == 0)
    def _():
        for at in range(kept_tokens.shape[0]):
            for copy in copies(at):
                copy.start()
        bias[...] = pair_bias(counts, offsets, slots)
        chosen = lax.broadcasted_iota(jnp.int32, (templates, slots), 0) == layout[...]
        spread[...] = jnp.transpose(chosen.astype(jnp.float32)).astype(jnp.bfloat16)

    for at in range(kept_tokens.shape[0]):

        @pl.when(step == at)
        def _():
            for copy in copies(at):
                copy.wait()

    tokens = kept_tokens.at[step]
    rows = dot(spread[...], kept_embedding[step], (1, 0))
    for group in in_groups(pairs, patches, SPATIAL_GROUP):
        values, shares = attention(width, tokens, rows, bias, group)
        attended = by_query(shares, values, width)
        for (pair, p), value, share, result in zip(group, values, shares, attended):
            embedded[p, :, pair_columns(pair)] = value
            weights[p, pair] = share
            by_electrode[pair, of_patch(p, slots, patches), :] = value.astype(jnp.float32) + result
    for pair in range(pairs):
        mixed[:, pair_columns(pair)] = by_electrode[pair].astype(jnp.bfloat16)


def patches_first(local):
    return local % SUBLANES != 0


def electrode_rows(electrode, electrodes, parts, local):
    start, step = electrode * local, electrodes * local
    if patches_first(local):
        return [pl.ds(start + p, parts, stride=step) for p in range(local)]
    return [pl.ds(start + part * step, local) for part in range(parts)]


def temporal_kernel(width, parts, mixed, out_grad, mixed_grad, received, returned):
    electrodes, patches, model = out_grad.shape
    local = patches // parts
    pairs = model // LANES
    score_masks = head_masks(width, 0.5 / math.sqrt(width))
    ones = head_masks(width, 1.0)
    for pair in range(pairs):
        received[pair] = mixed[:, pair_columns(pair)].astype(jnp.float32)
    for group in in_groups(pairs, electrodes, TEMPORAL_GROUP):
        places = [electrode_rows(e, electrodes, parts, local) for _, e in group]
        values = each(
            lambda item, place: jnp.concatenate(
                [received[item[0], rows, :] for rows in place], axis=0
            ).astype(jnp.bfloat16),
            group,
            places,
        )
        cotangents = [out_grad[e, :, pair_columns(pair)] for pair, e in group]
        scaled = each(lambda v: head_rows(v, score_masks), values)
        scores = each(lambda v, s: dot(v, s, (1, 1)), values, scaled)
        heads_grads = each(lambda g: head_rows(g, ones), cotangents)
        grad_weights = each(lambda v, g: dot(v, g, (1, 1)), values, heads_grads)
        shares = weights_by_key(scores)
        grads = back(values, scaled, cotangents, shares, grad_weights, heads_grads, width)
        for (pair, _), place, grad in zip(group, places, grads):
            start = 0
            for rows in place:
                returned[pair, rows, :] = grad[start : start + rows.size]
                start += rows.size
    for pair in range(pairs):
        mixed_grad[:, pair_columns(pair)] = returned[pair].astype(jnp.bfloat16)


def spatial_back_kernel(
    width, embedded, weights, mixed_grad, input_grad, electrode_grad, received
):
    patches, slots, model = embedded.shape
    pairs = model // LANES
    score_masks = head_masks(width, 0.5 / math.sqrt(width))
    ones = head_masks(width, 1.0)
    totals = [jnp.zeros((slots, LANES), jnp.float32) for _ in range(pairs)]
    for pair in range(pairs):
        received[pair] = mixed_grad[:, pair_columns(pair)].astype(jnp.float32)
    for group in in_groups(pairs, patches, SPATIAL_GROUP):
        cotangents = [
            received[pair, of_patch(p, slots, patches), :].astype(jnp.bfloat16)
            for pair, p in group
        ]
        values = [embedded[p, :, pair_columns(pair)] for pair, p in group]
        shares = [weights[p, pair] for pair, p in group]
        scaled = each(lambda v: head_rows(v, score_masks), values)
        heads_grads = each(lambda g: head_rows(g, ones), cotangents)
        grad_weights = each(lambda v, g: dot(v, g, (1, 1)), values, heads_grads)
        grads = back(values, scaled, cotangents, shares, grad_weights, heads_grads, width)
        for (pair, p), grad in zip(group, grads):
            input_grad[p, :, pair_columns(pair)] = grad.astype(jnp.bfloat16)
            totals[pair] = totals[pair] + grad
    for pair in range(pairs):
        electrode_grad[:, pair_columns(pair)] = totals[pair].astype(jnp.bfloat16)


def share_kernel(shares, everyone):
    total = shares[0].astype(jnp.float32)
    for part in range(1, shares.shape[0]):
        total = total + shares[part].astype(jnp.float32)
    everyone[...] = jnp.broadcast_to(total.astype(jnp.bfloat16)[None], everyone.shape)


def table_kernel(groups, *refs):
    layouts, sums, (table, pieces, sems) = refs[:groups], refs[groups], refs[groups + 1 :]
    owner = lax.axis_index("group")
    count, rows, model = pieces.shape
    slots = sums.shape[0] // groups
    parts = []
    for away in range(groups):
        origin = lax.rem(owner + groups - away, groups)
        parts.append(sums[pl.ds(pl.multiple_of(origin * slots, slots), slots), :])
    sources = jnp.concatenate(parts, axis=0)
    layout = jnp.concatenate([ref[...] for ref in layouts], axis=1)
    copies = []
    for piece in range(count):
        first = owner * (count * rows) + piece * rows
        template = lax.broadcasted_iota(jnp.int32, (rows, groups * slots), 0) + first
        spread = (template == layout).astype(jnp.float32).astype(jnp.bfloat16)
        pieces[piece] = dot(spread, sources, (1, 0))
        copy = pltpu.make_async_copy(
            pieces.at[piece], table.at[pl.ds(piece * rows, rows)], sems.at[piece]
        )
        copy.start()
        copies.append(copy)
    for copy in copies:
        copy.wait()


VMEM = pl.BlockSpec(memory_space=pltpu.VMEM)
SMEM = pl.BlockSpec(memory_space=pltpu.SMEM)
HBM = pl.BlockSpec(memory_space=pltpu.HBM)
PARAMS = pltpu.CompilerParams(vmem_limit_bytes=32 * 1024 * 1024)
STREAMED = pltpu.CompilerParams(vmem_limit_bytes=56 * 1024 * 1024)


def body(activations, out_grad, embedding, counts, offsets, layout):
    tokens = activations[0]
    local, slots, model = tokens.shape
    groups = lax.axis_size("group")
    parts = lax.axis_size("shard")
    patches = local * parts
    own = slots // parts
    width = model // HEADS
    templates = embedding.shape[0]
    pairs = STEP // LANES
    steps = model // STEP

    layouts = [layout] + [
        lax.ppermute(layout, "group", [(i, (i + away) % groups) for i in range(groups)])
        for away in range(1, groups)
    ]
    order = (2, 1, 0, 3) if patches_first(local) else (2, 0, 1, 3)
    cotangent = jnp.transpose(out_grad[0].reshape(parts, local, own, model), order)
    cotangent = cotangent.reshape(own, patches, model)

    flat = pl.BlockSpec((slots * local, STEP), lambda step: (0, step))
    planes = pl.BlockSpec((local, slots, STEP), lambda step: (0, 0, step))
    squares = pl.BlockSpec((local, pairs, slots, 2 * slots), lambda step: (0, step, 0, 0))
    flat_shape = jax.ShapeDtypeStruct((slots * local, model), jnp.bfloat16)
    plane_shape = jax.ShapeDtypeStruct(tokens.shape, jnp.bfloat16)
    flat_scratch = pltpu.VMEM((pairs, slots * local, LANES), jnp.float32)

    strip = pl.BlockSpec((slots, STEP), lambda step: (0, step))
    strip_shape = jax.ShapeDtypeStruct((slots, model), jnp.bfloat16)
    embedded, weights, mixed = pl.pallas_call(
        functools.partial(spatial_kernel, width),
        grid=(steps,),
        out_shape=(
            plane_shape,
            jax.ShapeDtypeStruct((local, model // LANES, slots, 2 * slots), jnp.bfloat16),
            flat_shape,
        ),
        in_specs=[SMEM, SMEM, VMEM, HBM, HBM],
        out_specs=(planes, squares, flat),
        scratch_shapes=[
            pltpu.VMEM((slots, templates), jnp.bfloat16),
            pltpu.VMEM((slots, 2 * slots), jnp.float32),
            flat_scratch,
            pltpu.VMEM((steps, templates, STEP), jnp.bfloat16),
            pltpu.VMEM((steps, local, slots, STEP), jnp.bfloat16),
            pltpu.SemaphoreType.DMA((steps, 2)),
        ],
        compiler_params=STREAMED,
        name="spatial",
    )(counts, offsets, layout, embedding, tokens)

    gathered = lax.all_to_all(mixed, "shard", split_axis=0, concat_axis=0, tiled=True)
    mixed_grad = pl.pallas_call(
        functools.partial(temporal_kernel, width, parts),
        grid=(steps,),
        out_shape=flat_shape,
        in_specs=[flat, pl.BlockSpec((own, patches, STEP), lambda step: (0, 0, step))],
        out_specs=flat,
        scratch_shapes=[flat_scratch, flat_scratch],
        compiler_params=PARAMS,
        name="temporal",
    )(gathered, cotangent)

    returned = lax.all_to_all(mixed_grad, "shard", split_axis=0, concat_axis=0, tiled=True)
    input_grad, electrode_grad = pl.pallas_call(
        functools.partial(spatial_back_kernel, width),
        grid=(steps,),
        out_shape=(plane_shape, strip_shape),
        in_specs=[planes, squares, flat],
        out_specs=(planes, strip),
        scratch_shapes=[flat_scratch],
        compiler_params=PARAMS,
        name="spatial_back",
    )(embedded, weights, returned)

    shares = lax.all_to_all(
        electrode_grad.reshape(parts, own, model), "shard", split_axis=0, concat_axis=0, tiled=True
    )
    everyone = pl.pallas_call(
        share_kernel,
        out_shape=jax.ShapeDtypeStruct((groups * parts, own, model), jnp.bfloat16),
        in_specs=[VMEM],
        out_specs=VMEM,
        compiler_params=PARAMS,
        name="share",
    )(shares)
    everyone = lax.all_to_all(
        everyone, ("group", "shard"), split_axis=0, concat_axis=0, tiled=True
    )
    table_rows = templates // groups
    table_grad = pl.pallas_call(
        functools.partial(table_kernel, groups),
        out_shape=jax.ShapeDtypeStruct((table_rows, model), jnp.float32),
        in_specs=[VMEM] * (groups + 1),
        out_specs=HBM,
        scratch_shapes=[
            pltpu.VMEM((PIECES, table_rows // PIECES, model), jnp.float32),
            pltpu.SemaphoreType.DMA((PIECES,)),
        ],
        compiler_params=PARAMS,
        name="table",
    )(*layouts, everyone.reshape(groups * slots, model))
    return (input_grad[None], table_grad)


def solution(mesh):
    placed = (
        P("group", "shard", None, None),
        P("group", None, "shard", None),
        P(),
        P("group", None),
        P("group", None),
        P("group", None),
    )
    return jax.shard_map(
        body,
        mesh=mesh,
        in_specs=placed,
        out_specs=(P("group", "shard", None, None), P("group", None)),
        check_vma=False,
    )
```

```python
import functools
import math

import jax
import jax.numpy as jnp
from jax import lax
from jax.experimental import pallas as pl
from jax.experimental.pallas import tpu as pltpu
from jax.sharding import PartitionSpec as P

HEADS = 16
BLOCK = 32
LANES = 128
MASKED = -1e30
SUBLANES = 8
STEP = 256
PIECES = 4
SPATIAL_GROUP = 16
TEMPORAL_GROUP = 8


def dot(left, right, over):
    return lax.dot_general(
        left, right, (((over[0],), (over[1],)), ((), ())), preferred_element_type=jnp.float32
    )


def head_masks(width, scale):
    lane = lax.broadcasted_iota(jnp.int32, (1, LANES), 1)
    first = jnp.where(lane < width, scale, 0.0).astype(jnp.bfloat16)
    second = jnp.where(lane < width, 0.0, scale).astype(jnp.bfloat16)
    return first, second


def head_rows(pair, masks):
    return jnp.concatenate([pair * masks[0], pair * masks[1]], axis=0)


def head_columns(rows, width):
    count = rows.shape[0] // 2
    lane = lax.broadcasted_iota(jnp.int32, (count, rows.shape[1]), 1)
    return jnp.where(lane < width, rows[:count], rows[count:])


def each(function, *lists):
    return [function(*items) for items in zip(*lists)]


def weights_by_key(scores):
    tops = each(lambda s: jnp.max(s, axis=0, keepdims=True), scores)
    exponents = each(lambda s, t: jnp.exp(s - t), scores, tops)
    shares = each(lambda e: 1.0 / jnp.sum(e, axis=0, keepdims=True), exponents)
    return each(lambda e, r: (e * r).astype(jnp.bfloat16), exponents, shares)


def by_query(shares, values, width):
    if 2 * values[0].shape[0] != LANES or len(values) % 2:
        return each(lambda s, v: head_columns(dot(s, v, (0, 0)), width), shares, values)
    results = []
    for first in range(0, len(values), 2):
        turned = jnp.transpose(jnp.concatenate(shares[first : first + 2], axis=0))
        one, other = values[first : first + 2]
        zero = jnp.zeros_like(one)
        apart = jnp.concatenate(
            [jnp.concatenate([one, zero], axis=1), jnp.concatenate([zero, other], axis=1)], axis=0
        )
        both = dot(turned, apart, (1, 0))
        results += [head_columns(both[:, :LANES], width), head_columns(both[:, LANES:], width)]
    return results


def back(values, scaled, cotangents, weights, grad_weights, heads_grads, width):
    wide = each(lambda w: w.astype(jnp.float32), weights)
    deltas = each(lambda w, g: jnp.sum(w * g, axis=0, keepdims=True), wide, grad_weights)
    grad_scores = each(
        lambda w, g, d: (w * (g - d)).astype(jnp.bfloat16), wide, grad_weights, deltas
    )
    length = values[0].shape[0]
    whole = length % LANES == 0
    both_ways = grad_scores
    if whole:
        both_ways = each(
            lambda g: jnp.concatenate(
                [
                    g[:, start : start + length] + jnp.transpose(g[:, start : start + length])
                    for start in (0, length)
                ],
                axis=1,
            ),
            grad_scores,
        )
    grads = each(
        lambda c, w, g, hg, hv: c.astype(jnp.float32)
        + dot(jnp.concatenate([w, g], axis=1), jnp.concatenate([hg, hv], axis=0), (1, 0)),
        cotangents,
        weights,
        both_ways,
        heads_grads,
        scaled,
    )
    if whole:
        return grads
    score_scale = 0.5 / math.sqrt(width)
    rest = by_query(grad_scores, values, width)
    return each(lambda g, r: g + score_scale * r, grads, rest)


def pair_bias(counts, offsets, slots):
    def sessions(slot):
        block = slot // BLOCK
        session = jnp.full(slot.shape, -1, jnp.int32)
        for j in range(offsets.shape[1]):
            session = session + (offsets[0, j] <= block).astype(jnp.int32)
        return session

    key_slot = lax.broadcasted_iota(jnp.int32, (slots, 2 * slots), 0)
    query_slot = lax.broadcasted_iota(jnp.int32, (slots, 2 * slots), 1) % slots
    key_session = sessions(key_slot)
    first = jnp.zeros_like(key_slot)
    live = jnp.zeros_like(key_slot)
    for j in range(offsets.shape[1]):
        chosen = key_session == j
        first = jnp.where(chosen, offsets[0, j] * BLOCK, first)
        live = jnp.where(chosen, counts[0, j], live)
    allowed = (key_session == sessions(query_slot)) & (key_slot - first < live)
    return jnp.where(allowed, 0.0, MASKED)


def pair_columns(pair):
    return pl.ds(pair * LANES, LANES)


def in_groups(pairs, rows, size):
    items = [(pair, row) for pair in range(pairs) for row in range(rows)]
    return [items[start : start + size] for start in range(0, len(items), size)]


def of_patch(patch, slots, patches):
    return pl.ds(patch, slots, stride=patches)


def attention(width, tokens, rows, bias, group):
    score_masks = head_masks(width, 0.5 / math.sqrt(width))
    values = [
        (
            tokens[p, :, pair_columns(pair)].astype(jnp.float32)
            + rows[:, pair * LANES : (pair + 1) * LANES]
        ).astype(jnp.bfloat16)
        for pair, p in group
    ]
    scores = each(lambda v: dot(v, head_rows(v, score_masks), (1, 1)) + bias[...], values)
    return values, weights_by_key(scores)


def spatial_kernel(
    width, counts, offsets, layout, embedding, tokens, rows, mixed, spread, bias, by_electrode
):
    patches, slots, model = tokens.shape
    templates = embedding.shape[0]
    pairs = model // LANES

    @pl.when(pl.program_id(0) == 0)
    def _():
        bias[...] = pair_bias(counts, offsets, slots)
        chosen = lax.broadcasted_iota(jnp.int32, (templates, slots), 0) == layout[...]
        spread[...] = jnp.transpose(chosen.astype(jnp.float32)).astype(jnp.bfloat16)

    chosen_rows = dot(spread[...], embedding[...], (1, 0))
    rows[...] = chosen_rows.astype(jnp.bfloat16)
    for group in in_groups(pairs, patches, SPATIAL_GROUP):
        values, shares = attention(width, tokens, chosen_rows, bias, group)
        attended = by_query(shares, values, width)
        for (pair, p), value, result in zip(group, values, attended):
            by_electrode[pair, of_patch(p, slots, patches), :] = value.astype(jnp.float32) + result
    for pair in range(pairs):
        mixed[:, pair_columns(pair)] = by_electrode[pair].astype(jnp.bfloat16)


def weights_kernel(width, counts, offsets, rows, tokens, embedded, weights, bias):
    patches, slots, model = tokens.shape

    @pl.when(pl.program_id(0) == 0)
    def _():
        bias[...] = pair_bias(counts, offsets, slots)

    added = rows[...].astype(jnp.float32)
    for group in in_groups(model // LANES, patches, SPATIAL_GROUP):
        values, shares = attention(width, tokens, added, bias, group)
        for (pair, p), value, share in zip(group, values, shares):
            embedded[p, :, pair_columns(pair)] = value
            weights[p, pair] = share


def patches_first(local):
    return local % SUBLANES != 0


def electrode_rows(electrode, electrodes, parts, local):
    start, step = electrode * local, electrodes * local
    if patches_first(local):
        return [pl.ds(start + p, parts, stride=step) for p in range(local)]
    return [pl.ds(start + part * step, local) for part in range(parts)]


def temporal_kernel(width, parts, mixed, out_grad, mixed_grad, received, returned):
    electrodes, patches, model = out_grad.shape
    local = patches // parts
    pairs = model // LANES
    score_masks = head_masks(width, 0.5 / math.sqrt(width))
    ones = head_masks(width, 1.0)
    for pair in range(pairs):
        received[pair] = mixed[:, pair_columns(pair)].astype(jnp.float32)
    for group in in_groups(pairs, electrodes, TEMPORAL_GROUP):
        places = [electrode_rows(e, electrodes, parts, local) for _, e in group]
        values = each(
            lambda item, place: jnp.concatenate(
                [received[item[0], rows, :] for rows in place], axis=0
            ).astype(jnp.bfloat16),
            group,
            places,
        )
        cotangents = [out_grad[e, :, pair_columns(pair)] for pair, e in group]
        scaled = each(lambda v: head_rows(v, score_masks), values)
        scores = each(lambda v, s: dot(v, s, (1, 1)), values, scaled)
        heads_grads = each(lambda g: head_rows(g, ones), cotangents)
        grad_weights = each(lambda v, g: dot(v, g, (1, 1)), values, heads_grads)
        shares = weights_by_key(scores)
        grads = back(values, scaled, cotangents, shares, grad_weights, heads_grads, width)
        for (pair, _), place, grad in zip(group, places, grads):
            start = 0
            for rows in place:
                returned[pair, rows, :] = grad[start : start + rows.size]
                start += rows.size
    for pair in range(pairs):
        mixed_grad[:, pair_columns(pair)] = returned[pair].astype(jnp.bfloat16)


def spatial_back_kernel(
    width, embedded, weights, mixed_grad, input_grad, electrode_grad, received
):
    patches, slots, model = embedded.shape
    pairs = model // LANES
    score_masks = head_masks(width, 0.5 / math.sqrt(width))
    ones = head_masks(width, 1.0)
    totals = [jnp.zeros((slots, LANES), jnp.float32) for _ in range(pairs)]
    for pair in range(pairs):
        received[pair] = mixed_grad[:, pair_columns(pair)].astype(jnp.float32)
    for group in in_groups(pairs, patches, SPATIAL_GROUP):
        cotangents = [
            received[pair, of_patch(p, slots, patches), :].astype(jnp.bfloat16)
            for pair, p in group
        ]
        values = [embedded[p, :, pair_columns(pair)] for pair, p in group]
        shares = [weights[p, pair] for pair, p in group]
        scaled = each(lambda v: head_rows(v, score_masks), values)
        heads_grads = each(lambda g: head_rows(g, ones), cotangents)
        grad_weights = each(lambda v, g: dot(v, g, (1, 1)), values, heads_grads)
        grads = back(values, scaled, cotangents, shares, grad_weights, heads_grads, width)
        for (pair, p), grad in zip(group, grads):
            input_grad[p, :, pair_columns(pair)] = grad.astype(jnp.bfloat16)
            totals[pair] = totals[pair] + grad
    for pair in range(pairs):
        electrode_grad[:, pair_columns(pair)] = totals[pair].astype(jnp.bfloat16)


def share_kernel(shares, everyone):
    total = shares[0].astype(jnp.float32)
    for part in range(1, shares.shape[0]):
        total = total + shares[part].astype(jnp.float32)
    everyone[...] = jnp.broadcast_to(total.astype(jnp.bfloat16)[None], everyone.shape)


def table_kernel(groups, *refs):
    layouts, sums, (table, pieces, sems) = refs[:groups], refs[groups], refs[groups + 1 :]
    owner = lax.axis_index("group")
    count, rows, model = pieces.shape
    slots = sums.shape[0] // groups
    parts = []
    for away in range(groups):
        origin = lax.rem(owner + groups - away, groups)
        parts.append(sums[pl.ds(pl.multiple_of(origin * slots, slots), slots), :])
    sources = jnp.concatenate(parts, axis=0)
    layout = jnp.concatenate([ref[...] for ref in layouts], axis=1)
    copies = []
    for piece in range(count):
        first = owner * (count * rows) + piece * rows
        template = lax.broadcasted_iota(jnp.int32, (rows, groups * slots), 0) + first
        spread = (template == layout).astype(jnp.float32).astype(jnp.bfloat16)
        pieces[piece] = dot(spread, sources, (1, 0))
        copy = pltpu.make_async_copy(
            pieces.at[piece], table.at[pl.ds(piece * rows, rows)], sems.at[piece]
        )
        copy.start()
        copies.append(copy)
    for copy in copies:
        copy.wait()


VMEM = pl.BlockSpec(memory_space=pltpu.VMEM)
SMEM = pl.BlockSpec(memory_space=pltpu.SMEM)
HBM = pl.BlockSpec(memory_space=pltpu.HBM)
PARAMS = pltpu.CompilerParams(vmem_limit_bytes=32 * 1024 * 1024)
STREAMED = pltpu.CompilerParams(vmem_limit_bytes=56 * 1024 * 1024)


def body(activations, out_grad, embedding, counts, offsets, layout):
    tokens = activations[0]
    local, slots, model = tokens.shape
    groups = lax.axis_size("group")
    parts = lax.axis_size("shard")
    patches = local * parts
    own = slots // parts
    width = model // HEADS
    templates = embedding.shape[0]
    pairs = STEP // LANES
    steps = model // STEP

    layouts = [layout] + [
        lax.ppermute(layout, "group", [(i, (i + away) % groups) for i in range(groups)])
        for away in range(1, groups)
    ]
    order = (2, 1, 0, 3) if patches_first(local) else (2, 0, 1, 3)
    cotangent = jnp.transpose(out_grad[0].reshape(parts, local, own, model), order)
    cotangent = cotangent.reshape(own, patches, model)

    flat = pl.BlockSpec((slots * local, STEP), lambda step: (0, step))
    planes = pl.BlockSpec((local, slots, STEP), lambda step: (0, 0, step))
    squares = pl.BlockSpec((local, pairs, slots, 2 * slots), lambda step: (0, step, 0, 0))
    flat_shape = jax.ShapeDtypeStruct((slots * local, model), jnp.bfloat16)
    plane_shape = jax.ShapeDtypeStruct(tokens.shape, jnp.bfloat16)
    flat_scratch = pltpu.VMEM((pairs, slots * local, LANES), jnp.float32)

    strip = pl.BlockSpec((slots, STEP), lambda step: (0, step))
    strip_shape = jax.ShapeDtypeStruct((slots, model), jnp.bfloat16)

    def narrow(*lead):
        return pl.BlockSpec(lead + (LANES,), lambda step: (0,) * len(lead) + (step,))

    rows, mixed = pl.pallas_call(
        functools.partial(spatial_kernel, width),
        grid=(model // LANES,),
        out_shape=(strip_shape, flat_shape),
        in_specs=[SMEM, SMEM, VMEM, narrow(templates), narrow(local, slots)],
        out_specs=(narrow(slots), narrow(slots * local)),
        scratch_shapes=[
            pltpu.VMEM((slots, templates), jnp.bfloat16),
            pltpu.VMEM((slots, 2 * slots), jnp.float32),
            pltpu.VMEM((1, slots * local, LANES), jnp.float32),
        ],
        compiler_params=STREAMED,
        name="spatial",
    )(counts, offsets, layout, embedding, tokens)
    embedded, weights = pl.pallas_call(
        functools.partial(weights_kernel, width),
        grid=(steps,),
        out_shape=(
            plane_shape,
            jax.ShapeDtypeStruct((local, model // LANES, slots, 2 * slots), jnp.bfloat16),
        ),
        in_specs=[SMEM, SMEM, strip, planes],
        out_specs=(planes, squares),
        scratch_shapes=[pltpu.VMEM((slots, 2 * slots), jnp.float32)],
        compiler_params=STREAMED,
        cost_estimate=pl.CostEstimate(
            flops=4 * local * slots * slots * model, bytes_accessed=6 * tokens.size, transcendentals=0
        ),
        name="weights",
    )(counts, offsets, rows, tokens)

    gathered = lax.all_to_all(mixed, "shard", split_axis=0, concat_axis=0, tiled=True)
    mixed_grad = pl.pallas_call(
        functools.partial(temporal_kernel, width, parts),
        grid=(steps,),
        out_shape=flat_shape,
        in_specs=[flat, pl.BlockSpec((own, patches, STEP), lambda step: (0, 0, step))],
        out_specs=flat,
        scratch_shapes=[flat_scratch, flat_scratch],
        compiler_params=PARAMS,
        name="temporal",
    )(gathered, cotangent)

    returned = lax.all_to_all(mixed_grad, "shard", split_axis=0, concat_axis=0, tiled=True)
    input_grad, electrode_grad = pl.pallas_call(
        functools.partial(spatial_back_kernel, width),
        grid=(steps,),
        out_shape=(plane_shape, strip_shape),
        in_specs=[planes, squares, flat],
        out_specs=(planes, strip),
        scratch_shapes=[flat_scratch],
        compiler_params=PARAMS,
        name="spatial_back",
    )(embedded, weights, returned)

    shares = lax.all_to_all(
        electrode_grad.reshape(parts, own, model), "shard", split_axis=0, concat_axis=0, tiled=True
    )
    everyone = pl.pallas_call(
        share_kernel,
        out_shape=jax.ShapeDtypeStruct((groups * parts, own, model), jnp.bfloat16),
        in_specs=[VMEM],
        out_specs=VMEM,
        compiler_params=PARAMS,
        name="share",
    )(shares)
    everyone = lax.all_to_all(
        everyone, ("group", "shard"), split_axis=0, concat_axis=0, tiled=True
    )
    table_rows = templates // groups
    table_grad = pl.pallas_call(
        functools.partial(table_kernel, groups),
        out_shape=jax.ShapeDtypeStruct((table_rows, model), jnp.float32),
        in_specs=[VMEM] * (groups + 1),
        out_specs=HBM,
        scratch_shapes=[
            pltpu.VMEM((PIECES, table_rows // PIECES, model), jnp.float32),
            pltpu.SemaphoreType.DMA((PIECES,)),
        ],
        compiler_params=PARAMS,
        name="table",
    )(*layouts, everyone.reshape(groups * slots, model))
    return (input_grad[None], table_grad)


def solution(mesh):
    placed = (
        P("group", "shard", None, None),
        P("group", None, "shard", None),
        P(),
        P("group", None),
        P("group", None),
        P("group", None),
    )
    return jax.shard_map(
        body,
        mesh=mesh,
        in_specs=placed,
        out_specs=(P("group", "shard", None, None), P("group", None)),
        check_vma=False,
    )
```

```python
import functools
import math

import jax
import jax.numpy as jnp
from jax import lax
from jax.experimental import pallas as pl
from jax.experimental.pallas import tpu as pltpu
from jax.sharding import PartitionSpec as P

HEADS = 16
BLOCK = 32
LANES = 128
MASKED = -1e30
SUBLANES = 8
STEP = 512
PIECES = 4
SPATIAL_GROUP = 16
TEMPORAL_GROUP = 8


def dot(left, right, over):
    return lax.dot_general(
        left, right, (((over[0],), (over[1],)), ((), ())), preferred_element_type=jnp.float32
    )


def head_masks(width, scale):
    lane = lax.broadcasted_iota(jnp.int32, (1, LANES), 1)
    first = jnp.where(lane < width, scale, 0.0).astype(jnp.bfloat16)
    second = jnp.where(lane < width, 0.0, scale).astype(jnp.bfloat16)
    return first, second


def head_rows(pair, masks):
    return jnp.concatenate([pair * masks[0], pair * masks[1]], axis=0)


def head_columns(rows, width):
    count = rows.shape[0] // 2
    lane = lax.broadcasted_iota(jnp.int32, (count, rows.shape[1]), 1)
    return jnp.where(lane < width, rows[:count], rows[count:])


def each(function, *lists):
    return [function(*items) for items in zip(*lists)]


def weights_by_key(scores):
    tops = each(lambda s: jnp.max(s, axis=0, keepdims=True), scores)
    exponents = each(lambda s, t: jnp.exp(s - t), scores, tops)
    shares = each(lambda e: 1.0 / jnp.sum(e, axis=0, keepdims=True), exponents)
    return each(lambda e, r: (e * r).astype(jnp.bfloat16), exponents, shares)


def by_query(shares, values, width):
    if 2 * values[0].shape[0] != LANES or len(values) % 2:
        return each(lambda s, v: head_columns(dot(s, v, (0, 0)), width), shares, values)
    results = []
    for first in range(0, len(values), 2):
        turned = jnp.transpose(jnp.concatenate(shares[first : first + 2], axis=0))
        one, other = values[first : first + 2]
        zero = jnp.zeros_like(one)
        apart = jnp.concatenate(
            [jnp.concatenate([one, zero], axis=1), jnp.concatenate([zero, other], axis=1)], axis=0
        )
        both = dot(turned, apart, (1, 0))
        results += [head_columns(both[:, :LANES], width), head_columns(both[:, LANES:], width)]
    return results


def back(values, scaled, cotangents, weights, grad_weights, heads_grads, width):
    wide = each(lambda w: w.astype(jnp.float32), weights)
    deltas = each(lambda w, g: jnp.sum(w * g, axis=0, keepdims=True), wide, grad_weights)
    grad_scores = each(
        lambda w, g, d: (w * (g - d)).astype(jnp.bfloat16), wide, grad_weights, deltas
    )
    length = values[0].shape[0]
    whole = length % LANES == 0
    both_ways = grad_scores
    if whole:
        both_ways = each(
            lambda g: jnp.concatenate(
                [
                    g[:, start : start + length] + jnp.transpose(g[:, start : start + length])
                    for start in (0, length)
                ],
                axis=1,
            ),
            grad_scores,
        )
    grads = each(
        lambda c, w, g, hg, hv: c.astype(jnp.float32)
        + dot(jnp.concatenate([w, g], axis=1), jnp.concatenate([hg, hv], axis=0), (1, 0)),
        cotangents,
        weights,
        both_ways,
        heads_grads,
        scaled,
    )
    if whole:
        return grads
    score_scale = 0.5 / math.sqrt(width)
    rest = by_query(grad_scores, values, width)
    return each(lambda g, r: g + score_scale * r, grads, rest)


def pair_bias(counts, offsets, slots):
    def sessions(slot):
        block = slot // BLOCK
        session = jnp.full(slot.shape, -1, jnp.int32)
        for j in range(offsets.shape[1]):
            session = session + (offsets[0, j] <= block).astype(jnp.int32)
        return session

    key_slot = lax.broadcasted_iota(jnp.int32, (slots, 2 * slots), 0)
    query_slot = lax.broadcasted_iota(jnp.int32, (slots, 2 * slots), 1) % slots
    key_session = sessions(key_slot)
    first = jnp.zeros_like(key_slot)
    live = jnp.zeros_like(key_slot)
    for j in range(offsets.shape[1]):
        chosen = key_session == j
        first = jnp.where(chosen, offsets[0, j] * BLOCK, first)
        live = jnp.where(chosen, counts[0, j], live)
    allowed = (key_session == sessions(query_slot)) & (key_slot - first < live)
    return jnp.where(allowed, 0.0, MASKED)


def pair_columns(pair):
    return pl.ds(pair * LANES, LANES)


def in_groups(pairs, rows, size):
    items = [(pair, row) for pair in range(pairs) for row in range(rows)]
    return [items[start : start + size] for start in range(0, len(items), size)]


def of_patch(patch, slots, patches):
    return pl.ds(patch, slots, stride=patches)


def attention(width, tokens, rows, bias, group):
    score_masks = head_masks(width, 0.5 / math.sqrt(width))
    values = [
        (
            tokens[p, :, pair_columns(pair)].astype(jnp.float32)
            + rows[:, pair * LANES : (pair + 1) * LANES]
        ).astype(jnp.bfloat16)
        for pair, p in group
    ]
    scores = each(lambda v: dot(v, head_rows(v, score_masks), (1, 1)) + bias[...], values)
    return values, weights_by_key(scores)


def spatial_kernel(
    width, counts, offsets, layout, embedding, tokens,
    embedded, weights, mixed, spread, bias, by_electrode,
):
    patches, slots, model = tokens.shape
    templates = embedding.shape[0]
    pairs = model // LANES

    @pl.when(pl.program_id(0) == 0)
    def _():
        bias[...] = pair_bias(counts, offsets, slots)
        chosen = lax.broadcasted_iota(jnp.int32, (templates, slots), 0) == layout[...]
        spread[...] = jnp.transpose(chosen.astype(jnp.float32)).astype(jnp.bfloat16)

    rows = dot(spread[...], embedding[...], (1, 0))
    for group in in_groups(pairs, patches, SPATIAL_GROUP):
        values, shares = attention(width, tokens, rows, bias, group)
        attended = by_query(shares, values, width)
        for (pair, p), value, share, result in zip(group, values, shares, attended):
            embedded[p, :, pair_columns(pair)] = value
            weights[p, pair] = share
            by_electrode[pair, of_patch(p, slots, patches), :] = value.astype(jnp.float32) + result
    for pair in range(pairs):
        mixed[:, pair_columns(pair)] = by_electrode[pair].astype(jnp.bfloat16)


def patches_first(local):
    return local % SUBLANES != 0


def electrode_rows(electrode, electrodes, parts, local):
    start, step = electrode * local, electrodes * local
    if patches_first(local):
        return [pl.ds(start + p, parts, stride=step) for p in range(local)]
    return [pl.ds(start + part * step, local) for part in range(parts)]


def temporal_kernel(width, parts, mixed, out_grad, mixed_grad, received, returned):
    electrodes, patches, model = out_grad.shape
    local = patches // parts
    pairs = model // LANES
    score_masks = head_masks(width, 0.5 / math.sqrt(width))
    ones = head_masks(width, 1.0)
    for pair in range(pairs):
        received[pair] = mixed[:, pair_columns(pair)].astype(jnp.float32)
    for group in in_groups(pairs, electrodes, TEMPORAL_GROUP):
        places = [electrode_rows(e, electrodes, parts, local) for _, e in group]
        values = each(
            lambda item, place: jnp.concatenate(
                [received[item[0], rows, :] for rows in place], axis=0
            ).astype(jnp.bfloat16),
            group,
            places,
        )
        cotangents = [out_grad[e, :, pair_columns(pair)] for pair, e in group]
        scaled = each(lambda v: head_rows(v, score_masks), values)
        scores = each(lambda v, s: dot(v, s, (1, 1)), values, scaled)
        heads_grads = each(lambda g: head_rows(g, ones), cotangents)
        grad_weights = each(lambda v, g: dot(v, g, (1, 1)), values, heads_grads)
        shares = weights_by_key(scores)
        grads = back(values, scaled, cotangents, shares, grad_weights, heads_grads, width)
        for (pair, _), place, grad in zip(group, places, grads):
            start = 0
            for rows in place:
                returned[pair, rows, :] = grad[start : start + rows.size]
                start += rows.size
    for pair in range(pairs):
        mixed_grad[:, pair_columns(pair)] = returned[pair].astype(jnp.bfloat16)


def spatial_back_kernel(
    width, embedded, weights, mixed_grad, input_grad, electrode_grad, received
):
    patches, slots, model = embedded.shape
    pairs = model // LANES
    score_masks = head_masks(width, 0.5 / math.sqrt(width))
    ones = head_masks(width, 1.0)
    totals = [jnp.zeros((slots, LANES), jnp.float32) for _ in range(pairs)]
    for pair in range(pairs):
        received[pair] = mixed_grad[:, pair_columns(pair)].astype(jnp.float32)
    for group in in_groups(pairs, patches, SPATIAL_GROUP):
        cotangents = [
            received[pair, of_patch(p, slots, patches), :].astype(jnp.bfloat16)
            for pair, p in group
        ]
        values = [embedded[p, :, pair_columns(pair)] for pair, p in group]
        shares = [weights[p, pair] for pair, p in group]
        scaled = each(lambda v: head_rows(v, score_masks), values)
        heads_grads = each(lambda g: head_rows(g, ones), cotangents)
        grad_weights = each(lambda v, g: dot(v, g, (1, 1)), values, heads_grads)
        grads = back(values, scaled, cotangents, shares, grad_weights, heads_grads, width)
        for (pair, p), grad in zip(group, grads):
            input_grad[p, :, pair_columns(pair)] = grad.astype(jnp.bfloat16)
            totals[pair] = totals[pair] + grad
    for pair in range(pairs):
        electrode_grad[:, pair_columns(pair)] = totals[pair].astype(jnp.bfloat16)


def share_kernel(shares, everyone):
    total = shares[0].astype(jnp.float32)
    for part in range(1, shares.shape[0]):
        total = total + shares[part].astype(jnp.float32)
    everyone[...] = jnp.broadcast_to(total.astype(jnp.bfloat16)[None], everyone.shape)


def table_kernel(groups, *refs):
    layouts, sums, (table, pieces, sems) = refs[:groups], refs[groups], refs[groups + 1 :]
    owner = lax.axis_index("group")
    count, rows, model = pieces.shape
    slots = sums.shape[0] // groups
    parts = []
    for away in range(groups):
        origin = lax.rem(owner + groups - away, groups)
        parts.append(sums[pl.ds(pl.multiple_of(origin * slots, slots), slots), :])
    sources = jnp.concatenate(parts, axis=0)
    layout = jnp.concatenate([ref[...] for ref in layouts], axis=1)
    copies = []
    for piece in range(count):
        first = owner * (count * rows) + piece * rows
        template = lax.broadcasted_iota(jnp.int32, (rows, groups * slots), 0) + first
        spread = (template == layout).astype(jnp.float32).astype(jnp.bfloat16)
        pieces[piece] = dot(spread, sources, (1, 0))
        copy = pltpu.make_async_copy(
            pieces.at[piece], table.at[pl.ds(piece * rows, rows)], sems.at[piece]
        )
        copy.start()
        copies.append(copy)
    for copy in copies:
        copy.wait()


VMEM = pl.BlockSpec(memory_space=pltpu.VMEM)
SMEM = pl.BlockSpec(memory_space=pltpu.SMEM)
HBM = pl.BlockSpec(memory_space=pltpu.HBM)
PARAMS = pltpu.CompilerParams(vmem_limit_bytes=32 * 1024 * 1024)
STREAMED = pltpu.CompilerParams(vmem_limit_bytes=56 * 1024 * 1024)


def body(activations, out_grad, embedding, counts, offsets, layout):
    tokens = activations[0]
    local, slots, model = tokens.shape
    groups = lax.axis_size("group")
    parts = lax.axis_size("shard")
    patches = local * parts
    own = slots // parts
    width = model // HEADS
    templates = embedding.shape[0]
    pairs = STEP // LANES
    steps = model // STEP

    layouts = [layout] + [
        lax.ppermute(layout, "group", [(i, (i + away) % groups) for i in range(groups)])
        for away in range(1, groups)
    ]
    order = (2, 1, 0, 3) if patches_first(local) else (2, 0, 1, 3)
    cotangent = jnp.transpose(out_grad[0].reshape(parts, local, own, model), order)
    cotangent = cotangent.reshape(own, patches, model)

    flat = pl.BlockSpec((slots * local, STEP), lambda step: (0, step))
    planes = pl.BlockSpec((local, slots, STEP), lambda step: (0, 0, step))
    squares = pl.BlockSpec((local, pairs, slots, 2 * slots), lambda step: (0, step, 0, 0))
    flat_shape = jax.ShapeDtypeStruct((slots * local, model), jnp.bfloat16)
    plane_shape = jax.ShapeDtypeStruct(tokens.shape, jnp.bfloat16)
    flat_scratch = pltpu.VMEM((pairs, slots * local, LANES), jnp.float32)

    strip = pl.BlockSpec((slots, STEP), lambda step: (0, step))
    strip_shape = jax.ShapeDtypeStruct((slots, model), jnp.bfloat16)
    embedded, weights, mixed = pl.pallas_call(
        functools.partial(spatial_kernel, width),
        grid=(steps,),
        out_shape=(
            plane_shape,
            jax.ShapeDtypeStruct((local, model // LANES, slots, 2 * slots), jnp.bfloat16),
            flat_shape,
        ),
        in_specs=[SMEM, SMEM, VMEM, pl.BlockSpec((templates, STEP), lambda step: (0, step)), planes],
        out_specs=(planes, squares, flat),
        scratch_shapes=[
            pltpu.VMEM((slots, templates), jnp.bfloat16),
            pltpu.VMEM((slots, 2 * slots), jnp.float32),
            flat_scratch,
        ],
        compiler_params=STREAMED,
        name="spatial",
    )(counts, offsets, layout, embedding, tokens)

    gathered = lax.all_to_all(mixed, "shard", split_axis=0, concat_axis=0, tiled=True)
    mixed_grad = pl.pallas_call(
        functools.partial(temporal_kernel, width, parts),
        grid=(steps,),
        out_shape=flat_shape,
        in_specs=[flat, pl.BlockSpec((own, patches, STEP), lambda step: (0, 0, step))],
        out_specs=flat,
        scratch_shapes=[flat_scratch, flat_scratch],
        compiler_params=PARAMS,
        name="temporal",
    )(gathered, cotangent)

    returned = lax.all_to_all(mixed_grad, "shard", split_axis=0, concat_axis=0, tiled=True)
    input_grad, electrode_grad = pl.pallas_call(
        functools.partial(spatial_back_kernel, width),
        grid=(steps,),
        out_shape=(plane_shape, strip_shape),
        in_specs=[planes, squares, flat],
        out_specs=(planes, strip),
        scratch_shapes=[flat_scratch],
        compiler_params=PARAMS,
        name="spatial_back",
    )(embedded, weights, returned)

    shares = lax.all_to_all(
        electrode_grad.reshape(parts, own, model), "shard", split_axis=0, concat_axis=0, tiled=True
    )
    everyone = pl.pallas_call(
        share_kernel,
        out_shape=jax.ShapeDtypeStruct((groups * parts, own, model), jnp.bfloat16),
        in_specs=[VMEM],
        out_specs=VMEM,
        compiler_params=PARAMS,
        name="share",
    )(shares)
    everyone = lax.all_to_all(
        everyone, ("group", "shard"), split_axis=0, concat_axis=0, tiled=True
    )
    table_rows = templates // groups
    table_grad = pl.pallas_call(
        functools.partial(table_kernel, groups),
        out_shape=jax.ShapeDtypeStruct((table_rows, model), jnp.float32),
        in_specs=[VMEM] * (groups + 1),
        out_specs=HBM,
        scratch_shapes=[
            pltpu.VMEM((PIECES, table_rows // PIECES, model), jnp.float32),
            pltpu.SemaphoreType.DMA((PIECES,)),
        ],
        compiler_params=PARAMS,
        name="table",
    )(*layouts, everyone.reshape(groups * slots, model))
    return (input_grad[None], table_grad)


def solution(mesh):
    placed = (
        P("group", "shard", None, None),
        P("group", None, "shard", None),
        P(),
        P("group", None),
        P("group", None),
        P("group", None),
    )
    return jax.shard_map(
        body,
        mesh=mesh,
        in_specs=placed,
        out_specs=(P("group", "shard", None, None), P("group", None)),
        check_vma=False,
    )
```

```python
import functools
import math

import jax
import jax.numpy as jnp
from jax import lax
from jax.experimental import pallas as pl
from jax.experimental.pallas import tpu as pltpu
from jax.sharding import PartitionSpec as P

HEADS = 16
BLOCK = 32
LANES = 128
MASKED = -1e30
SUBLANES = 8
STEP = 512
PIECES = 4
SPATIAL_GROUP = 32
TEMPORAL_GROUP = 16


def dot(left, right, over):
    return lax.dot_general(
        left, right, (((over[0],), (over[1],)), ((), ())), preferred_element_type=jnp.float32
    )


def head_masks(width, scale):
    lane = lax.broadcasted_iota(jnp.int32, (1, LANES), 1)
    first = jnp.where(lane < width, scale, 0.0).astype(jnp.bfloat16)
    second = jnp.where(lane < width, 0.0, scale).astype(jnp.bfloat16)
    return first, second


def head_rows(pair, masks):
    return jnp.concatenate([pair * masks[0], pair * masks[1]], axis=0)


def head_columns(rows, width):
    count = rows.shape[0] // 2
    lane = lax.broadcasted_iota(jnp.int32, (count, rows.shape[1]), 1)
    return jnp.where(lane < width, rows[:count], rows[count:])


def each(function, *lists):
    return [function(*items) for items in zip(*lists)]


def weights_by_key(scores):
    tops = each(lambda s: jnp.max(s, axis=0, keepdims=True), scores)
    exponents = each(lambda s, t: jnp.exp(s - t), scores, tops)
    shares = each(lambda e: 1.0 / jnp.sum(e, axis=0, keepdims=True), exponents)
    return each(lambda e, r: (e * r).astype(jnp.bfloat16), exponents, shares)


def by_query(shares, values, width):
    if 2 * values[0].shape[0] != LANES or len(values) % 2:
        return each(lambda s, v: head_columns(dot(s, v, (0, 0)), width), shares, values)
    results = []
    for first in range(0, len(values), 2):
        turned = jnp.transpose(jnp.concatenate(shares[first : first + 2], axis=0))
        one, other = values[first : first + 2]
        zero = jnp.zeros_like(one)
        apart = jnp.concatenate(
            [jnp.concatenate([one, zero], axis=1), jnp.concatenate([zero, other], axis=1)], axis=0
        )
        both = dot(turned, apart, (1, 0))
        results += [head_columns(both[:, :LANES], width), head_columns(both[:, LANES:], width)]
    return results


def back(values, scaled, cotangents, weights, grad_weights, heads_grads, width):
    wide = each(lambda w: w.astype(jnp.float32), weights)
    deltas = each(lambda w, g: jnp.sum(w * g, axis=0, keepdims=True), wide, grad_weights)
    grad_scores = each(
        lambda w, g, d: (w * (g - d)).astype(jnp.bfloat16), wide, grad_weights, deltas
    )
    length = values[0].shape[0]
    whole = length % LANES == 0
    both_ways = grad_scores
    if whole:
        both_ways = each(
            lambda g: jnp.concatenate(
                [
                    g[:, start : start + length] + jnp.transpose(g[:, start : start + length])
                    for start in (0, length)
                ],
                axis=1,
            ),
            grad_scores,
        )
    grads = each(
        lambda c, w, g, hg, hv: c.astype(jnp.float32)
        + dot(jnp.concatenate([w, g], axis=1), jnp.concatenate([hg, hv], axis=0), (1, 0)),
        cotangents,
        weights,
        both_ways,
        heads_grads,
        scaled,
    )
    if whole:
        return grads
    score_scale = 0.5 / math.sqrt(width)
    rest = by_query(grad_scores, values, width)
    return each(lambda g, r: g + score_scale * r, grads, rest)


def pair_bias(counts, offsets, slots):
    def sessions(slot):
        block = slot // BLOCK
        session = jnp.full(slot.shape, -1, jnp.int32)
        for j in range(offsets.shape[1]):
            session = session + (offsets[0, j] <= block).astype(jnp.int32)
        return session

    key_slot = lax.broadcasted_iota(jnp.int32, (slots, 2 * slots), 0)
    query_slot = lax.broadcasted_iota(jnp.int32, (slots, 2 * slots), 1) % slots
    key_session = sessions(key_slot)
    first = jnp.zeros_like(key_slot)
    live = jnp.zeros_like(key_slot)
    for j in range(offsets.shape[1]):
        chosen = key_session == j
        first = jnp.where(chosen, offsets[0, j] * BLOCK, first)
        live = jnp.where(chosen, counts[0, j], live)
    allowed = (key_session == sessions(query_slot)) & (key_slot - first < live)
    return jnp.where(allowed, 0.0, MASKED)


def pair_columns(pair):
    return pl.ds(pair * LANES, LANES)


def in_groups(pairs, rows, size):
    items = [(pair, row) for pair in range(pairs) for row in range(rows)]
    return [items[start : start + size] for start in range(0, len(items), size)]


def of_patch(patch, slots, patches):
    return pl.ds(patch, slots, stride=patches)


def attention(width, tokens, rows, bias, group):
    score_masks = head_masks(width, 0.5 / math.sqrt(width))
    values = [
        (
            tokens[p, :, pair_columns(pair)].astype(jnp.float32)
            + rows[:, pair * LANES : (pair + 1) * LANES]
        ).astype(jnp.bfloat16)
        for pair, p in group
    ]
    scores = each(lambda v: dot(v, head_rows(v, score_masks), (1, 1)) + bias[...], values)
    return values, weights_by_key(scores)


def spatial_kernel(
    width, counts, offsets, layout, embedding, tokens,
    embedded, weights, mixed, spread, bias, by_electrode,
):
    patches, slots, model = tokens.shape
    templates = embedding.shape[0]
    pairs = model // LANES

    @pl.when(pl.program_id(0) == 0)
    def _():
        bias[...] = pair_bias(counts, offsets, slots)
        chosen = lax.broadcasted_iota(jnp.int32, (templates, slots), 0) == layout[...]
        spread[...] = jnp.transpose(chosen.astype(jnp.float32)).astype(jnp.bfloat16)

    rows = dot(spread[...], embedding[...], (1, 0))
    for group in in_groups(pairs, patches, SPATIAL_GROUP):
        values, shares = attention(width, tokens, rows, bias, group)
        attended = by_query(shares, values, width)
        for (pair, p), value, share, result in zip(group, values, shares, attended):
            embedded[p, :, pair_columns(pair)] = value
            weights[p, pair] = share
            by_electrode[pair, of_patch(p, slots, patches), :] = value.astype(jnp.float32) + result
    for pair in range(pairs):
        mixed[:, pair_columns(pair)] = by_electrode[pair].astype(jnp.bfloat16)


def patches_first(local):
    return local % SUBLANES != 0


def electrode_rows(electrode, electrodes, parts, local):
    start, step = electrode * local, electrodes * local
    if patches_first(local):
        return [pl.ds(start + p, parts, stride=step) for p in range(local)]
    return [pl.ds(start + part * step, local) for part in range(parts)]


def temporal_kernel(width, parts, mixed, out_grad, mixed_grad, received, returned):
    electrodes, patches, model = out_grad.shape
    local = patches // parts
    pairs = model // LANES
    score_masks = head_masks(width, 0.5 / math.sqrt(width))
    ones = head_masks(width, 1.0)
    for pair in range(pairs):
        received[pair] = mixed[:, pair_columns(pair)].astype(jnp.float32)
    for group in in_groups(pairs, electrodes, TEMPORAL_GROUP):
        places = [electrode_rows(e, electrodes, parts, local) for _, e in group]
        values = each(
            lambda item, place: jnp.concatenate(
                [received[item[0], rows, :] for rows in place], axis=0
            ).astype(jnp.bfloat16),
            group,
            places,
        )
        cotangents = [out_grad[e, :, pair_columns(pair)] for pair, e in group]
        scaled = each(lambda v: head_rows(v, score_masks), values)
        scores = each(lambda v, s: dot(v, s, (1, 1)), values, scaled)
        heads_grads = each(lambda g: head_rows(g, ones), cotangents)
        grad_weights = each(lambda v, g: dot(v, g, (1, 1)), values, heads_grads)
        shares = weights_by_key(scores)
        grads = back(values, scaled, cotangents, shares, grad_weights, heads_grads, width)
        for (pair, _), place, grad in zip(group, places, grads):
            start = 0
            for rows in place:
                returned[pair, rows, :] = grad[start : start + rows.size]
                start += rows.size
    for pair in range(pairs):
        mixed_grad[:, pair_columns(pair)] = returned[pair].astype(jnp.bfloat16)


def spatial_back_kernel(
    width, embedded, weights, mixed_grad, input_grad, electrode_grad, received
):
    patches, slots, model = embedded.shape
    pairs = model // LANES
    score_masks = head_masks(width, 0.5 / math.sqrt(width))
    ones = head_masks(width, 1.0)
    totals = [jnp.zeros((slots, LANES), jnp.float32) for _ in range(pairs)]
    for pair in range(pairs):
        received[pair] = mixed_grad[:, pair_columns(pair)].astype(jnp.float32)
    for group in in_groups(pairs, patches, SPATIAL_GROUP):
        cotangents = [
            received[pair, of_patch(p, slots, patches), :].astype(jnp.bfloat16)
            for pair, p in group
        ]
        values = [embedded[p, :, pair_columns(pair)] for pair, p in group]
        shares = [weights[p, pair] for pair, p in group]
        scaled = each(lambda v: head_rows(v, score_masks), values)
        heads_grads = each(lambda g: head_rows(g, ones), cotangents)
        grad_weights = each(lambda v, g: dot(v, g, (1, 1)), values, heads_grads)
        grads = back(values, scaled, cotangents, shares, grad_weights, heads_grads, width)
        for (pair, p), grad in zip(group, grads):
            input_grad[p, :, pair_columns(pair)] = grad.astype(jnp.bfloat16)
            totals[pair] = totals[pair] + grad
    for pair in range(pairs):
        electrode_grad[:, pair_columns(pair)] = totals[pair].astype(jnp.bfloat16)


def share_kernel(shares, everyone):
    total = shares[0].astype(jnp.float32)
    for part in range(1, shares.shape[0]):
        total = total + shares[part].astype(jnp.float32)
    everyone[...] = jnp.broadcast_to(total.astype(jnp.bfloat16)[None], everyone.shape)


def table_kernel(groups, *refs):
    layouts, sums, (table, pieces, sems) = refs[:groups], refs[groups], refs[groups + 1 :]
    owner = lax.axis_index("group")
    count, rows, model = pieces.shape
    slots = sums.shape[0] // groups
    parts = []
    for away in range(groups):
        origin = lax.rem(owner + groups - away, groups)
        parts.append(sums[pl.ds(pl.multiple_of(origin * slots, slots), slots), :])
    sources = jnp.concatenate(parts, axis=0)
    layout = jnp.concatenate([ref[...] for ref in layouts], axis=1)
    copies = []
    for piece in range(count):
        first = owner * (count * rows) + piece * rows
        template = lax.broadcasted_iota(jnp.int32, (rows, groups * slots), 0) + first
        spread = (template == layout).astype(jnp.float32).astype(jnp.bfloat16)
        pieces[piece] = dot(spread, sources, (1, 0))
        copy = pltpu.make_async_copy(
            pieces.at[piece], table.at[pl.ds(piece * rows, rows)], sems.at[piece]
        )
        copy.start()
        copies.append(copy)
    for copy in copies:
        copy.wait()


VMEM = pl.BlockSpec(memory_space=pltpu.VMEM)
SMEM = pl.BlockSpec(memory_space=pltpu.SMEM)
HBM = pl.BlockSpec(memory_space=pltpu.HBM)
PARAMS = pltpu.CompilerParams(vmem_limit_bytes=32 * 1024 * 1024)
STREAMED = pltpu.CompilerParams(vmem_limit_bytes=56 * 1024 * 1024)


def body(activations, out_grad, embedding, counts, offsets, layout):
    tokens = activations[0]
    local, slots, model = tokens.shape
    groups = lax.axis_size("group")
    parts = lax.axis_size("shard")
    patches = local * parts
    own = slots // parts
    width = model // HEADS
    templates = embedding.shape[0]
    pairs = STEP // LANES
    steps = model // STEP

    layouts = [layout] + [
        lax.ppermute(layout, "group", [(i, (i + away) % groups) for i in range(groups)])
        for away in range(1, groups)
    ]
    order = (2, 1, 0, 3) if patches_first(local) else (2, 0, 1, 3)
    cotangent = jnp.transpose(out_grad[0].reshape(parts, local, own, model), order)
    cotangent = cotangent.reshape(own, patches, model)

    flat = pl.BlockSpec((slots * local, STEP), lambda step: (0, step))
    planes = pl.BlockSpec((local, slots, STEP), lambda step: (0, 0, step))
    squares = pl.BlockSpec((local, pairs, slots, 2 * slots), lambda step: (0, step, 0, 0))
    flat_shape = jax.ShapeDtypeStruct((slots * local, model), jnp.bfloat16)
    plane_shape = jax.ShapeDtypeStruct(tokens.shape, jnp.bfloat16)
    flat_scratch = pltpu.VMEM((pairs, slots * local, LANES), jnp.float32)

    strip = pl.BlockSpec((slots, STEP), lambda step: (0, step))
    strip_shape = jax.ShapeDtypeStruct((slots, model), jnp.bfloat16)
    embedded, weights, mixed = pl.pallas_call(
        functools.partial(spatial_kernel, width),
        grid=(steps,),
        out_shape=(
            plane_shape,
            jax.ShapeDtypeStruct((local, model // LANES, slots, 2 * slots), jnp.bfloat16),
            flat_shape,
        ),
        in_specs=[SMEM, SMEM, VMEM, pl.BlockSpec((templates, STEP), lambda step: (0, step)), planes],
        out_specs=(planes, squares, flat),
        scratch_shapes=[
            pltpu.VMEM((slots, templates), jnp.bfloat16),
            pltpu.VMEM((slots, 2 * slots), jnp.float32),
            flat_scratch,
        ],
        compiler_params=STREAMED,
        name="spatial",
    )(counts, offsets, layout, embedding, tokens)

    gathered = lax.all_to_all(mixed, "shard", split_axis=0, concat_axis=0, tiled=True)
    mixed_grad = pl.pallas_call(
        functools.partial(temporal_kernel, width, parts),
        grid=(steps,),
        out_shape=flat_shape,
        in_specs=[flat, pl.BlockSpec((own, patches, STEP), lambda step: (0, 0, step))],
        out_specs=flat,
        scratch_shapes=[flat_scratch, flat_scratch],
        compiler_params=PARAMS,
        name="temporal",
    )(gathered, cotangent)

    returned = lax.all_to_all(mixed_grad, "shard", split_axis=0, concat_axis=0, tiled=True)
    input_grad, electrode_grad = pl.pallas_call(
        functools.partial(spatial_back_kernel, width),
        grid=(steps,),
        out_shape=(plane_shape, strip_shape),
        in_specs=[planes, squares, flat],
        out_specs=(planes, strip),
        scratch_shapes=[flat_scratch],
        compiler_params=PARAMS,
        name="spatial_back",
    )(embedded, weights, returned)

    shares = lax.all_to_all(
        electrode_grad.reshape(parts, own, model), "shard", split_axis=0, concat_axis=0, tiled=True
    )
    everyone = pl.pallas_call(
        share_kernel,
        out_shape=jax.ShapeDtypeStruct((groups * parts, own, model), jnp.bfloat16),
        in_specs=[VMEM],
        out_specs=VMEM,
        compiler_params=PARAMS,
        name="share",
    )(shares)
    everyone = lax.all_to_all(
        everyone, ("group", "shard"), split_axis=0, concat_axis=0, tiled=True
    )
    table_rows = templates // groups
    table_grad = pl.pallas_call(
        functools.partial(table_kernel, groups),
        out_shape=jax.ShapeDtypeStruct((table_rows, model), jnp.float32),
        in_specs=[VMEM] * (groups + 1),
        out_specs=HBM,
        scratch_shapes=[
            pltpu.VMEM((PIECES, table_rows // PIECES, model), jnp.float32),
            pltpu.SemaphoreType.DMA((PIECES,)),
        ],
        compiler_params=PARAMS,
        name="table",
    )(*layouts, everyone.reshape(groups * slots, model))
    return (input_grad[None], table_grad)


def solution(mesh):
    placed = (
        P("group", "shard", None, None),
        P("group", None, "shard", None),
        P(),
        P("group", None),
        P("group", None),
        P("group", None),
    )
    return jax.shard_map(
        body,
        mesh=mesh,
        in_specs=placed,
        out_specs=(P("group", "shard", None, None), P("group", None)),
        check_vma=False,
    )
```

```python
import functools
import math

import jax
import jax.numpy as jnp
from jax import lax
from jax.experimental import pallas as pl
from jax.experimental.pallas import tpu as pltpu
from jax.sharding import PartitionSpec as P

HEADS = 16
BLOCK = 32
LANES = 128
MASKED = -1e30
SUBLANES = 8
STEP = 512
PIECES = 4
PLANE = 4
SPATIAL_GROUP = 32
TEMPORAL_GROUP = 8


def dot(left, right, over):
    return lax.dot_general(
        left, right, (((over[0],), (over[1],)), ((), ())), preferred_element_type=jnp.float32
    )


def head_masks(width, scale):
    lane = lax.broadcasted_iota(jnp.int32, (1, LANES), 1)
    first = jnp.where(lane < width, scale, 0.0).astype(jnp.bfloat16)
    second = jnp.where(lane < width, 0.0, scale).astype(jnp.bfloat16)
    return first, second


def head_rows(pair, masks):
    return jnp.concatenate([pair * masks[0], pair * masks[1]], axis=0)


def head_columns(rows, width):
    count = rows.shape[0] // 2
    lane = lax.broadcasted_iota(jnp.int32, (count, rows.shape[1]), 1)
    return jnp.where(lane < width, rows[:count], rows[count:])


def each(function, *lists):
    return [function(*items) for items in zip(*lists)]


def weights_by_key(scores):
    tops = each(lambda s: jnp.max(s, axis=0, keepdims=True), scores)
    exponents = each(lambda s, t: jnp.exp(s - t), scores, tops)
    shares = each(lambda e: 1.0 / jnp.sum(e, axis=0, keepdims=True), exponents)
    return each(lambda e, r: (e * r).astype(jnp.bfloat16), exponents, shares)


def by_query(shares, values, width):
    if 2 * values[0].shape[0] != LANES or len(values) % 2:
        return each(lambda s, v: head_columns(dot(s, v, (0, 0)), width), shares, values)
    results = []
    for first in range(0, len(values), 2):
        turned = jnp.transpose(jnp.concatenate(shares[first : first + 2], axis=0))
        one, other = values[first : first + 2]
        zero = jnp.zeros_like(one)
        apart = jnp.concatenate(
            [jnp.concatenate([one, zero], axis=1), jnp.concatenate([zero, other], axis=1)], axis=0
        )
        both = dot(turned, apart, (1, 0))
        results += [head_columns(both[:, :LANES], width), head_columns(both[:, LANES:], width)]
    return results


def back(values, scaled, cotangents, weights, grad_weights, heads_grads, width):
    wide = each(lambda w: w.astype(jnp.float32), weights)
    deltas = each(lambda w, g: jnp.sum(w * g, axis=0, keepdims=True), wide, grad_weights)
    grad_scores = each(
        lambda w, g, d: (w * (g - d)).astype(jnp.bfloat16), wide, grad_weights, deltas
    )
    length = values[0].shape[0]
    whole = length % LANES == 0
    both_ways = grad_scores
    if whole:
        both_ways = each(
            lambda g: jnp.concatenate(
                [
                    g[:, start : start + length] + jnp.transpose(g[:, start : start + length])
                    for start in (0, length)
                ],
                axis=1,
            ),
            grad_scores,
        )
    grads = each(
        lambda c, w, g, hg, hv: c.astype(jnp.float32)
        + dot(jnp.concatenate([w, g], axis=1), jnp.concatenate([hg, hv], axis=0), (1, 0)),
        cotangents,
        weights,
        both_ways,
        heads_grads,
        scaled,
    )
    if whole:
        return grads
    score_scale = 0.5 / math.sqrt(width)
    rest = by_query(grad_scores, values, width)
    return each(lambda g, r: g + score_scale * r, grads, rest)


def pair_bias(counts, offsets, slots):
    def sessions(slot):
        block = slot // BLOCK
        session = jnp.full(slot.shape, -1, jnp.int32)
        for j in range(offsets.shape[1]):
            session = session + (offsets[0, j] <= block).astype(jnp.int32)
        return session

    key_slot = lax.broadcasted_iota(jnp.int32, (slots, 2 * slots), 0)
    query_slot = lax.broadcasted_iota(jnp.int32, (slots, 2 * slots), 1) % slots
    key_session = sessions(key_slot)
    first = jnp.zeros_like(key_slot)
    live = jnp.zeros_like(key_slot)
    for j in range(offsets.shape[1]):
        chosen = key_session == j
        first = jnp.where(chosen, offsets[0, j] * BLOCK, first)
        live = jnp.where(chosen, counts[0, j], live)
    allowed = (key_session == sessions(query_slot)) & (key_slot - first < live)
    return jnp.where(allowed, 0.0, MASKED)


def pair_columns(pair):
    return pl.ds(pair * LANES, LANES)


def in_groups(pairs, rows, size):
    items = [(pair, row) for pair in range(pairs) for row in range(rows)]
    return [items[start : start + size] for start in range(0, len(items), size)]


def of_patch(patch, slots, patches):
    return pl.ds(patch, slots, stride=patches)


def attention(width, tokens, rows, bias, group):
    score_masks = head_masks(width, 0.5 / math.sqrt(width))
    values = [
        (
            tokens[p, :, pair_columns(pair)].astype(jnp.float32)
            + rows[:, pair * LANES : (pair + 1) * LANES]
        ).astype(jnp.bfloat16)
        for pair, p in group
    ]
    scores = each(lambda v: dot(v, head_rows(v, score_masks), (1, 1)) + bias[...], values)
    return values, weights_by_key(scores)


def spatial_kernel(
    width, counts, offsets, layout, embedding, tokens,
    embedded, weights, mixed, spread, bias, by_electrode,
):
    patches, slots, model = tokens.shape
    templates = embedding.shape[0]
    pairs = model // LANES

    @pl.when(pl.program_id(0) == 0)
    def _():
        bias[...] = pair_bias(counts, offsets, slots)
        chosen = lax.broadcasted_iota(jnp.int32, (templates, slots), 0) == layout[...]
        spread[...] = jnp.transpose(chosen.astype(jnp.float32)).astype(jnp.bfloat16)

    rows = dot(spread[...], embedding[...], (1, 0))
    for group in in_groups(pairs, patches, SPATIAL_GROUP):
        values, shares = attention(width, tokens, rows, bias, group)
        attended = by_query(shares, values, width)
        for (pair, p), value, share, result in zip(group, values, shares, attended):
            embedded[p, :, pair_columns(pair)] = value
            weights[p, pair] = share
            by_electrode[pair, of_patch(p, slots, patches), :] = value.astype(jnp.float32) + result
    for pair in range(pairs):
        mixed[:, pair_columns(pair)] = by_electrode[pair].astype(jnp.bfloat16)


def patches_first(local):
    return local % SUBLANES != 0


def electrode_rows(electrode, electrodes, parts, local):
    start, step = electrode * local, electrodes * local
    if patches_first(local):
        return [pl.ds(start + p, parts, stride=step) for p in range(local)]
    return [pl.ds(start + part * step, local) for part in range(parts)]


def temporal_kernel(width, parts, mixed, out_grad, mixed_grad, received, returned):
    electrodes, patches, model = out_grad.shape
    local = patches // parts
    pairs = model // LANES
    score_masks = head_masks(width, 0.5 / math.sqrt(width))
    ones = head_masks(width, 1.0)
    for pair in range(pairs):
        received[pair] = mixed[:, pair_columns(pair)].astype(jnp.float32)
    for group in in_groups(pairs, electrodes, TEMPORAL_GROUP):
        places = [electrode_rows(e, electrodes, parts, local) for _, e in group]
        values = each(
            lambda item, place: jnp.concatenate(
                [received[item[0], rows, :] for rows in place], axis=0
            ).astype(jnp.bfloat16),
            group,
            places,
        )
        cotangents = [out_grad[e, :, pair_columns(pair)] for pair, e in group]
        scaled = each(lambda v: head_rows(v, score_masks), values)
        scores = each(lambda v, s: dot(v, s, (1, 1)), values, scaled)
        heads_grads = each(lambda g: head_rows(g, ones), cotangents)
        grad_weights = each(lambda v, g: dot(v, g, (1, 1)), values, heads_grads)
        shares = weights_by_key(scores)
        grads = back(values, scaled, cotangents, shares, grad_weights, heads_grads, width)
        for (pair, _), place, grad in zip(group, places, grads):
            start = 0
            for rows in place:
                returned[pair, rows, :] = grad[start : start + rows.size]
                start += rows.size
    for pair in range(pairs):
        mixed_grad[:, pair_columns(pair)] = returned[pair].astype(jnp.bfloat16)


def plane_rows(away, count):
    place = lax.bitwise_xor(lax.rem(lax.axis_index("shard"), PLANE), away)
    return pl.ds(pl.multiple_of(place * count, count), count)


def spatial_back_kernel(width, embedded, weights, mixed_grad, input_grad, *refs):
    electrode_grads, (sums, received) = refs[:-2], refs[-2:]
    patches, slots, model = embedded.shape
    pairs = model // LANES
    score_masks = head_masks(width, 0.5 / math.sqrt(width))
    ones = head_masks(width, 1.0)
    totals = [jnp.zeros((slots, LANES), jnp.float32) for _ in range(pairs)]
    for pair in range(pairs):
        received[pair] = mixed_grad[:, pair_columns(pair)].astype(jnp.float32)
    for group in in_groups(pairs, patches, SPATIAL_GROUP):
        cotangents = [
            received[pair, of_patch(p, slots, patches), :].astype(jnp.bfloat16)
            for pair, p in group
        ]
        values = [embedded[p, :, pair_columns(pair)] for pair, p in group]
        shares = [weights[p, pair] for pair, p in group]
        scaled = each(lambda v: head_rows(v, score_masks), values)
        heads_grads = each(lambda g: head_rows(g, ones), cotangents)
        grad_weights = each(lambda v, g: dot(v, g, (1, 1)), values, heads_grads)
        grads = back(values, scaled, cotangents, shares, grad_weights, heads_grads, width)
        for (pair, p), grad in zip(group, grads):
            input_grad[p, :, pair_columns(pair)] = grad.astype(jnp.bfloat16)
            totals[pair] = totals[pair] + grad
    for pair in range(pairs):
        sums[pair] = totals[pair]
        for away, block in enumerate(electrode_grads):
            rows = sums[pair, plane_rows(away, block.shape[0]), :]
            block[:, pair_columns(pair)] = rows.astype(jnp.bfloat16)


def plane_sum_kernel(*refs):
    total = refs[0][...].astype(jnp.float32)
    for part in refs[1:-1]:
        total = total + part[...].astype(jnp.float32)
    refs[-1][...] = total.astype(jnp.bfloat16)


def far_sum_kernel(*refs):
    parts, (total, ordered) = refs[:-2], refs[-2:]
    place = lax.div(lax.axis_index("shard"), PLANE)
    for away, part in enumerate(parts):
        ordered[lax.bitwise_xor(place, away)] = part[...].astype(jnp.float32)
    result = ordered[0]
    for index in range(1, len(parts)):
        result = result + ordered[index]
    total[...] = result.astype(jnp.bfloat16)


def table_kernel(groups, *refs):
    layouts, blocks, (table, sources, pieces, sems) = refs[:groups], refs[groups:-4], refs[-4:]
    owner = lax.axis_index("group")
    count, rows, _ = pieces.shape
    slots = sources.shape[1]
    for away in range(groups):
        for near in range(PLANE):
            block = blocks[away * PLANE + near]
            sources[away, plane_rows(near, block.shape[0]), :] = block[...]
    copies = []
    for piece in range(count):
        first = owner * (count * rows) + piece * rows
        template = lax.broadcasted_iota(jnp.int32, (rows, slots), 0) + first
        total = jnp.zeros(pieces.shape[1:], jnp.float32)
        for away in range(groups):
            spread = (template == layouts[away][...]).astype(jnp.float32).astype(jnp.bfloat16)
            total = total + dot(spread, sources[away], (1, 0))
        pieces[piece] = total
        copy = pltpu.make_async_copy(
            pieces.at[piece], table.at[pl.ds(piece * rows, rows)], sems.at[piece]
        )
        copy.start()
        copies.append(copy)
    for copy in copies:
        copy.wait()


VMEM = pl.BlockSpec(memory_space=pltpu.VMEM)
SMEM = pl.BlockSpec(memory_space=pltpu.SMEM)
HBM = pl.BlockSpec(memory_space=pltpu.HBM)
PARAMS = pltpu.CompilerParams(vmem_limit_bytes=32 * 1024 * 1024)
STREAMED = pltpu.CompilerParams(vmem_limit_bytes=56 * 1024 * 1024)


def body(activations, out_grad, embedding, counts, offsets, layout):
    tokens = activations[0]
    local, slots, model = tokens.shape
    groups = lax.axis_size("group")
    parts = lax.axis_size("shard")
    patches = local * parts
    own = slots // parts
    width = model // HEADS
    templates = embedding.shape[0]
    pairs = STEP // LANES
    steps = model // STEP

    layouts = [layout] + [
        lax.ppermute(layout, "group", [(i, (i + away) % groups) for i in range(groups)])
        for away in range(1, groups)
    ]
    order = (2, 1, 0, 3) if patches_first(local) else (2, 0, 1, 3)
    cotangent = jnp.transpose(out_grad[0].reshape(parts, local, own, model), order)
    cotangent = cotangent.reshape(own, patches, model)

    flat = pl.BlockSpec((slots * local, STEP), lambda step: (0, step))
    planes = pl.BlockSpec((local, slots, STEP), lambda step: (0, 0, step))
    squares = pl.BlockSpec((local, pairs, slots, 2 * slots), lambda step: (0, step, 0, 0))
    flat_shape = jax.ShapeDtypeStruct((slots * local, model), jnp.bfloat16)
    plane_shape = jax.ShapeDtypeStruct(tokens.shape, jnp.bfloat16)
    flat_scratch = pltpu.VMEM((pairs, slots * local, LANES), jnp.float32)

    embedded, weights, mixed = pl.pallas_call(
        functools.partial(spatial_kernel, width),
        grid=(steps,),
        out_shape=(
            plane_shape,
            jax.ShapeDtypeStruct((local, model // LANES, slots, 2 * slots), jnp.bfloat16),
            flat_shape,
        ),
        in_specs=[SMEM, SMEM, VMEM, pl.BlockSpec((templates, STEP), lambda step: (0, step)), planes],
        out_specs=(planes, squares, flat),
        scratch_shapes=[
            pltpu.VMEM((slots, templates), jnp.bfloat16),
            pltpu.VMEM((slots, 2 * slots), jnp.float32),
            flat_scratch,
        ],
        compiler_params=STREAMED,
        name="spatial",
    )(counts, offsets, layout, embedding, tokens)

    gathered = lax.all_to_all(mixed, "shard", split_axis=0, concat_axis=0, tiled=True)
    mixed_grad = pl.pallas_call(
        functools.partial(temporal_kernel, width, parts),
        grid=(steps,),
        out_shape=flat_shape,
        in_specs=[flat, pl.BlockSpec((own, patches, STEP), lambda step: (0, 0, step))],
        out_specs=flat,
        scratch_shapes=[flat_scratch, flat_scratch],
        compiler_params=PARAMS,
        name="temporal",
    )(gathered, cotangent)

    returned = lax.all_to_all(mixed_grad, "shard", split_axis=0, concat_axis=0, tiled=True)
    kept = slots // PLANE
    input_grad, *sums = pl.pallas_call(
        functools.partial(spatial_back_kernel, width),
        grid=(steps,),
        out_shape=(plane_shape,) + (jax.ShapeDtypeStruct((kept, model), jnp.bfloat16),) * PLANE,
        in_specs=[planes, squares, flat],
        out_specs=(planes,) + (pl.BlockSpec((kept, STEP), lambda step: (0, step)),) * PLANE,
        scratch_shapes=[pltpu.VMEM((pairs, slots, LANES), jnp.float32), flat_scratch],
        compiler_params=PARAMS,
        name="spatial_back",
    )(embedded, weights, returned)

    def to_partner(array, away):
        if away == 0:
            return array
        return lax.ppermute(array, "shard", [(i, i ^ away) for i in range(parts)])

    far_count = parts // PLANE
    assert parts == far_count * PLANE and parts & (parts - 1) == 0
    kept_shape = jax.ShapeDtypeStruct((kept, model), jnp.bfloat16)
    plane_parts = [to_partner(block, away) for away, block in enumerate(sums)]
    plane_sum = pl.pallas_call(
        plane_sum_kernel,
        out_shape=kept_shape,
        in_specs=[VMEM] * PLANE,
        out_specs=VMEM,
        compiler_params=PARAMS,
        name="plane_sum",
    )(*plane_parts)
    far_parts = [to_partner(plane_sum, far * PLANE) for far in range(far_count)]
    total = pl.pallas_call(
        far_sum_kernel,
        out_shape=kept_shape,
        in_specs=[VMEM] * far_count,
        out_specs=VMEM,
        scratch_shapes=[pltpu.VMEM((far_count, kept, model), jnp.float32)],
        compiler_params=PARAMS,
        name="far_sum",
    )(*far_parts)
    totals = [total] + [
        lax.ppermute(total, "group", [(i, (i + away) % groups) for i in range(groups)])
        for away in range(1, groups)
    ]
    everyone = [to_partner(rows, near) for rows in totals for near in range(PLANE)]
    table_rows = templates // groups
    table_grad = pl.pallas_call(
        functools.partial(table_kernel, groups),
        out_shape=jax.ShapeDtypeStruct((table_rows, model), jnp.float32),
        in_specs=[VMEM] * (groups + groups * PLANE),
        out_specs=HBM,
        scratch_shapes=[
            pltpu.VMEM((groups, slots, model), jnp.bfloat16),
            pltpu.VMEM((PIECES, table_rows // PIECES, model), jnp.float32),
            pltpu.SemaphoreType.DMA((PIECES,)),
        ],
        compiler_params=PARAMS,
        name="table",
    )(*layouts, *everyone)
    return (input_grad[None], table_grad)


def solution(mesh):
    placed = (
        P("group", "shard", None, None),
        P("group", None, "shard", None),
        P(),
        P("group", None),
        P("group", None),
        P("group", None),
    )
    return jax.shard_map(
        body,
        mesh=mesh,
        in_specs=placed,
        out_specs=(P("group", "shard", None, None), P("group", None)),
        check_vma=False,
    )
```

```python
import functools
import math

import jax
import jax.numpy as jnp
from jax import lax
from jax.experimental import pallas as pl
from jax.experimental.pallas import tpu as pltpu
from jax.sharding import PartitionSpec as P

HEADS = 16
BLOCK = 32
LANES = 128
MASKED = -1e30
SUBLANES = 8
STEP = 512
PIECES = 4
SPATIAL_GROUP = 32
TEMPORAL_GROUP = 8


def dot(left, right, over):
    return lax.dot_general(
        left, right, (((over[0],), (over[1],)), ((), ())), preferred_element_type=jnp.float32
    )


def head_masks(width, scale):
    lane = lax.broadcasted_iota(jnp.int32, (1, LANES), 1)
    first = jnp.where(lane < width, scale, 0.0).astype(jnp.bfloat16)
    second = jnp.where(lane < width, 0.0, scale).astype(jnp.bfloat16)
    return first, second


def head_rows(pair, masks):
    return jnp.concatenate([pair * masks[0], pair * masks[1]], axis=0)


def head_columns(rows, width):
    count = rows.shape[0] // 2
    lane = lax.broadcasted_iota(jnp.int32, (count, rows.shape[1]), 1)
    return jnp.where(lane < width, rows[:count], rows[count:])


def each(function, *lists):
    return [function(*items) for items in zip(*lists)]


def weights_by_key(scores):
    tops = each(lambda s: jnp.max(s, axis=0, keepdims=True), scores)
    exponents = each(lambda s, t: jnp.exp(s - t), scores, tops)
    shares = each(lambda e: 1.0 / jnp.sum(e, axis=0, keepdims=True), exponents)
    return each(lambda e, r: (e * r).astype(jnp.bfloat16), exponents, shares)


def by_query(shares, values, width):
    if 2 * values[0].shape[0] != LANES or len(values) % 2:
        return each(lambda s, v: head_columns(dot(s, v, (0, 0)), width), shares, values)
    results = []
    for first in range(0, len(values), 2):
        turned = jnp.transpose(jnp.concatenate(shares[first : first + 2], axis=0))
        one, other = values[first : first + 2]
        zero = jnp.zeros_like(one)
        apart = jnp.concatenate(
            [jnp.concatenate([one, zero], axis=1), jnp.concatenate([zero, other], axis=1)], axis=0
        )
        both = dot(turned, apart, (1, 0))
        results += [head_columns(both[:, :LANES], width), head_columns(both[:, LANES:], width)]
    return results


def back(values, scaled, cotangents, weights, grad_weights, heads_grads, width):
    wide = each(lambda w: w.astype(jnp.float32), weights)
    deltas = each(lambda w, g: jnp.sum(w * g, axis=0, keepdims=True), wide, grad_weights)
    grad_scores = each(
        lambda w, g, d: (w * (g - d)).astype(jnp.bfloat16), wide, grad_weights, deltas
    )
    length = values[0].shape[0]
    whole = length % LANES == 0
    both_ways = grad_scores
    if whole:
        both_ways = each(
            lambda g: jnp.concatenate(
                [
                    g[:, start : start + length] + jnp.transpose(g[:, start : start + length])
                    for start in (0, length)
                ],
                axis=1,
            ),
            grad_scores,
        )
    grads = each(
        lambda c, w, g, hg, hv: c.astype(jnp.float32)
        + dot(jnp.concatenate([w, g], axis=1), jnp.concatenate([hg, hv], axis=0), (1, 0)),
        cotangents,
        weights,
        both_ways,
        heads_grads,
        scaled,
    )
    if whole:
        return grads
    score_scale = 0.5 / math.sqrt(width)
    rest = by_query(grad_scores, values, width)
    return each(lambda g, r: g + score_scale * r, grads, rest)


def pair_bias(counts, offsets, slots):
    def sessions(slot):
        block = slot // BLOCK
        session = jnp.full(slot.shape, -1, jnp.int32)
        for j in range(offsets.shape[1]):
            session = session + (offsets[0, j] <= block).astype(jnp.int32)
        return session

    key_slot = lax.broadcasted_iota(jnp.int32, (slots, 2 * slots), 0)
    query_slot = lax.broadcasted_iota(jnp.int32, (slots, 2 * slots), 1) % slots
    key_session = sessions(key_slot)
    first = jnp.zeros_like(key_slot)
    live = jnp.zeros_like(key_slot)
    for j in range(offsets.shape[1]):
        chosen = key_session == j
        first = jnp.where(chosen, offsets[0, j] * BLOCK, first)
        live = jnp.where(chosen, counts[0, j], live)
    allowed = (key_session == sessions(query_slot)) & (key_slot - first < live)
    return jnp.where(allowed, 0.0, MASKED)


def pair_columns(pair):
    return pl.ds(pair * LANES, LANES)


def in_groups(pairs, rows, size):
    items = [(pair, row) for pair in range(pairs) for row in range(rows)]
    return [items[start : start + size] for start in range(0, len(items), size)]


def of_patch(patch, slots, patches):
    return pl.ds(patch, slots, stride=patches)


def attention(width, tokens, rows, bias, group):
    score_masks = head_masks(width, 0.5 / math.sqrt(width))
    values = [
        (
            tokens[p, :, pair_columns(pair)].astype(jnp.float32)
            + rows[:, pair * LANES : (pair + 1) * LANES]
        ).astype(jnp.bfloat16)
        for pair, p in group
    ]
    scores = each(lambda v: dot(v, head_rows(v, score_masks), (1, 1)) + bias[...], values)
    return values, weights_by_key(scores)


def spatial_kernel(
    width, counts, offsets, layout, embedding, tokens,
    embedded, weights, mixed, spread, bias, by_electrode,
):
    patches, slots, model = tokens.shape
    templates = embedding.shape[0]
    pairs = model // LANES

    @pl.when(pl.program_id(0) == 0)
    def _():
        bias[...] = pair_bias(counts, offsets, slots)
        chosen = lax.broadcasted_iota(jnp.int32, (templates, slots), 0) == layout[...]
        spread[...] = jnp.transpose(chosen.astype(jnp.float32)).astype(jnp.bfloat16)

    rows = dot(spread[...], embedding[...], (1, 0))
    for group in in_groups(pairs, patches, SPATIAL_GROUP):
        values, shares = attention(width, tokens, rows, bias, group)
        attended = by_query(shares, values, width)
        for (pair, p), value, share, result in zip(group, values, shares, attended):
            embedded[p, :, pair_columns(pair)] = value
            weights[p, pair] = share
            by_electrode[pair, of_patch(p, slots, patches), :] = value.astype(jnp.float32) + result
    for pair in range(pairs):
        mixed[:, pair_columns(pair)] = by_electrode[pair].astype(jnp.bfloat16)


def patches_first(local):
    return local % SUBLANES != 0


def electrode_rows(electrode, electrodes, parts, local):
    start, step = electrode * local, electrodes * local
    if patches_first(local):
        return [pl.ds(start + p, parts, stride=step) for p in range(local)]
    return [pl.ds(start + part * step, local) for part in range(parts)]


def temporal_kernel(width, parts, mixed, out_grad, *refs):
    mixed_grad, received, returned = refs[-3:]
    electrodes, patches, model = out_grad.shape
    local = patches // parts
    pairs = model // LANES
    score_masks = head_masks(width, 0.5 / math.sqrt(width))
    ones = head_masks(width, 1.0)
    for pair in range(pairs):
        received[pair] = mixed[:, pair_columns(pair)].astype(jnp.float32)
    for group in in_groups(pairs, electrodes, TEMPORAL_GROUP):
        places = [electrode_rows(e, electrodes, parts, local) for _, e in group]
        values = each(
            lambda item, place: jnp.concatenate(
                [received[item[0], rows, :] for rows in place], axis=0
            ).astype(jnp.bfloat16),
            group,
            places,
        )
        cotangents = [out_grad[e, :, pair_columns(pair)] for pair, e in group]
        scaled = each(lambda v: head_rows(v, score_masks), values)
        scores = each(lambda v, s: dot(v, s, (1, 1)), values, scaled)
        heads_grads = each(lambda g: head_rows(g, ones), cotangents)
        grad_weights = each(lambda v, g: dot(v, g, (1, 1)), values, heads_grads)
        shares = weights_by_key(scores)
        grads = back(values, scaled, cotangents, shares, grad_weights, heads_grads, width)
        for (pair, _), place, grad in zip(group, places, grads):
            start = 0
            for rows in place:
                returned[pair, rows, :] = grad[start : start + rows.size]
                start += rows.size
    for pair in range(pairs):
        mixed_grad[:, pair_columns(pair)] = returned[pair].astype(jnp.bfloat16)


def half_rows(bit, away, count):
    here = lax.bitwise_and(lax.shift_right_logical(lax.axis_index("shard"), bit), 1)
    return pl.ds(pl.multiple_of(lax.bitwise_xor(here, away) * count, count), count)


def spatial_back_kernel(width, embedded, weights, mixed_grad, input_grad, *refs):
    electrode_grads, (sums, received) = refs[:-2], refs[-2:]
    patches, slots, model = embedded.shape
    pairs = model // LANES
    score_masks = head_masks(width, 0.5 / math.sqrt(width))
    ones = head_masks(width, 1.0)
    totals = [jnp.zeros((slots, LANES), jnp.float32) for _ in range(pairs)]
    for pair in range(pairs):
        received[pair] = mixed_grad[:, pair_columns(pair)].astype(jnp.float32)
    for group in in_groups(pairs, patches, SPATIAL_GROUP):
        cotangents = [
            received[pair, of_patch(p, slots, patches), :].astype(jnp.bfloat16)
            for pair, p in group
        ]
        values = [embedded[p, :, pair_columns(pair)] for pair, p in group]
        shares = [weights[p, pair] for pair, p in group]
        scaled = each(lambda v: head_rows(v, score_masks), values)
        heads_grads = each(lambda g: head_rows(g, ones), cotangents)
        grad_weights = each(lambda v, g: dot(v, g, (1, 1)), values, heads_grads)
        grads = back(values, scaled, cotangents, shares, grad_weights, heads_grads, width)
        for (pair, p), grad in zip(group, grads):
            input_grad[p, :, pair_columns(pair)] = grad.astype(jnp.bfloat16)
            totals[pair] = totals[pair] + grad
    for pair in range(pairs):
        sums[pair] = totals[pair]
        for away, block in enumerate(electrode_grads):
            rows = sums[pair, half_rows(0, away, block.shape[0]), :]
            block[:, pair_columns(pair)] = rows.astype(jnp.bfloat16)


def halve_kernel(bit, own, arrived, kept, sent, total):
    total[...] = own[...].astype(jnp.float32) + arrived[...].astype(jnp.float32)
    for away, block in enumerate((kept, sent)):
        block[...] = total[half_rows(bit, away, block.shape[0]), :].astype(jnp.bfloat16)


def add_kernel(own, arrived, total):
    total[...] = (own[...].astype(jnp.float32) + arrived[...].astype(jnp.float32)).astype(
        jnp.bfloat16
    )


def stack_kernel(*refs):
    for index, block in enumerate(refs[:-1]):
        refs[-1][index] = block[...]


def join_kernel(bit, own, arrived, joined):
    for away, block in enumerate((own, arrived)):
        joined[:, half_rows(bit, away, block.shape[1]), :] = block[...]


def table_kernel(groups, *refs):
    layouts, blocks, (table, sources, pieces, sems) = refs[:groups], refs[groups:-4], refs[-4:]
    owner = lax.axis_index("group")
    count, rows, _ = pieces.shape
    slots = sources.shape[1]
    join_kernel(0, *blocks, sources)
    copies = []
    for piece in range(count):
        first = owner * (count * rows) + piece * rows
        template = lax.broadcasted_iota(jnp.int32, (rows, slots), 0) + first
        total = jnp.zeros(pieces.shape[1:], jnp.float32)
        for away in range(groups):
            spread = (template == layouts[away][...]).astype(jnp.float32).astype(jnp.bfloat16)
            total = total + dot(spread, sources[away], (1, 0))
        pieces[piece] = total
        copy = pltpu.make_async_copy(
            pieces.at[piece], table.at[pl.ds(piece * rows, rows)], sems.at[piece]
        )
        copy.start()
        copies.append(copy)
    for copy in copies:
        copy.wait()


VMEM = pl.BlockSpec(memory_space=pltpu.VMEM)
SMEM = pl.BlockSpec(memory_space=pltpu.SMEM)
HBM = pl.BlockSpec(memory_space=pltpu.HBM)
PARAMS = pltpu.CompilerParams(vmem_limit_bytes=32 * 1024 * 1024)
STREAMED = pltpu.CompilerParams(vmem_limit_bytes=56 * 1024 * 1024)


def body(activations, out_grad, embedding, counts, offsets, layout):
    tokens = activations[0]
    local, slots, model = tokens.shape
    groups = lax.axis_size("group")
    parts = lax.axis_size("shard")
    patches = local * parts
    own = slots // parts
    width = model // HEADS
    templates = embedding.shape[0]
    pairs = STEP // LANES
    steps = model // STEP

    layouts = [layout] + [
        lax.ppermute(layout, "group", [(i, (i + away) % groups) for i in range(groups)])
        for away in range(1, groups)
    ]
    order = (2, 1, 0, 3) if patches_first(local) else (2, 0, 1, 3)
    cotangent = jnp.transpose(out_grad[0].reshape(parts, local, own, model), order)
    cotangent = cotangent.reshape(own, patches, model)

    flat = pl.BlockSpec((slots * local, STEP), lambda step: (0, step))
    planes = pl.BlockSpec((local, slots, STEP), lambda step: (0, 0, step))
    squares = pl.BlockSpec((local, pairs, slots, 2 * slots), lambda step: (0, step, 0, 0))
    flat_shape = jax.ShapeDtypeStruct((slots * local, model), jnp.bfloat16)
    plane_shape = jax.ShapeDtypeStruct(tokens.shape, jnp.bfloat16)
    flat_scratch = pltpu.VMEM((pairs, slots * local, LANES), jnp.float32)

    embedded, weights, mixed = pl.pallas_call(
        functools.partial(spatial_kernel, width),
        grid=(steps,),
        out_shape=(
            plane_shape,
            jax.ShapeDtypeStruct((local, model // LANES, slots, 2 * slots), jnp.bfloat16),
            flat_shape,
        ),
        in_specs=[SMEM, SMEM, VMEM, pl.BlockSpec((templates, STEP), lambda step: (0, step)), planes],
        out_specs=(planes, squares, flat),
        scratch_shapes=[
            pltpu.VMEM((slots, templates), jnp.bfloat16),
            pltpu.VMEM((slots, 2 * slots), jnp.float32),
            flat_scratch,
        ],
        compiler_params=STREAMED,
        name="spatial",
    )(counts, offsets, layout, embedding, tokens)

    gathered = lax.all_to_all(mixed, "shard", split_axis=0, concat_axis=0, tiled=True)
    mixed_grad = pl.pallas_call(
        functools.partial(temporal_kernel, width, parts),
        grid=(steps,),
        out_shape=flat_shape,
        in_specs=[flat, pl.BlockSpec((own, patches, STEP), lambda step: (0, 0, step))]
        + [pl.BlockSpec(memory_space=pl.ANY)] * (groups - 1),
        out_specs=flat,
        scratch_shapes=[flat_scratch, flat_scratch],
        compiler_params=PARAMS,
        name="temporal",
    )(gathered, cotangent, *layouts[1:])

    returned = lax.all_to_all(mixed_grad, "shard", split_axis=0, concat_axis=0, tiled=True)
    half, kept = slots // 2, slots // 4
    assert parts & (parts - 1) == 0 and parts >= 4
    input_grad, *halves = pl.pallas_call(
        functools.partial(spatial_back_kernel, width),
        grid=(steps,),
        out_shape=(plane_shape,) + (jax.ShapeDtypeStruct((half, model), jnp.bfloat16),) * 2,
        in_specs=[planes, squares, flat],
        out_specs=(planes,) + (pl.BlockSpec((half, STEP), lambda step: (0, step)),) * 2,
        scratch_shapes=[pltpu.VMEM((pairs, slots, LANES), jnp.float32), flat_scratch],
        compiler_params=PARAMS,
        name="spatial_back",
    )(embedded, weights, returned)

    def swap(array, bit):
        return lax.ppermute(array, "shard", [(i, i ^ (1 << bit)) for i in range(parts)])

    def small(kernel, shape, scratch=(), many=1):
        out = jax.ShapeDtypeStruct(shape, jnp.bfloat16)

        def call(*operands):
            return pl.pallas_call(
                kernel,
                out_shape=(out,) * many if many > 1 else out,
                in_specs=[VMEM] * len(operands),
                out_specs=(VMEM,) * many if many > 1 else VMEM,
                scratch_shapes=list(scratch),
                compiler_params=PARAMS,
                name="sums",
            )(*operands)

        return call

    own_half, other_half = halves
    own_rows, other_rows = small(
        functools.partial(halve_kernel, 1),
        (kept, model),
        [pltpu.VMEM((half, model), jnp.float32)],
        many=2,
    )(own_half, swap(other_half, 0))
    add = small(add_kernel, (kept, model))
    total = add(own_rows, swap(other_rows, 1))
    for bit in range(2, parts.bit_length() - 1):
        total = add(total, swap(total, bit))
    totals = [total] + [
        lax.ppermute(total, "group", [(i, (i + away) % groups) for i in range(groups)])
        for away in range(1, groups)
    ]
    stacked = small(stack_kernel, (groups, kept, model))(*totals)
    joined = small(functools.partial(join_kernel, 1), (groups, half, model))(
        stacked, swap(stacked, 1)
    )
    table_rows = templates // groups
    table_grad = pl.pallas_call(
        functools.partial(table_kernel, groups),
        out_shape=jax.ShapeDtypeStruct((table_rows, model), jnp.float32),
        in_specs=[VMEM] * (groups + 2),
        out_specs=HBM,
        scratch_shapes=[
            pltpu.VMEM((groups, slots, model), jnp.bfloat16),
            pltpu.VMEM((PIECES, table_rows // PIECES, model), jnp.float32),
            pltpu.SemaphoreType.DMA((PIECES,)),
        ],
        compiler_params=PARAMS,
        name="table",
    )(*layouts, joined, swap(joined, 0))
    return (input_grad[None], table_grad)


def solution(mesh):
    placed = (
        P("group", "shard", None, None),
        P("group", None, "shard", None),
        P(),
        P("group", None),
        P("group", None),
        P("group", None),
    )
    return jax.shard_map(
        body,
        mesh=mesh,
        in_specs=placed,
        out_specs=(P("group", "shard", None, None), P("group", None)),
        check_vma=False,
    )
```

```python
import functools
import math

import jax
import jax.numpy as jnp
from jax import lax
from jax.experimental import pallas as pl
from jax.experimental.pallas import tpu as pltpu
from jax.sharding import PartitionSpec as P

HEADS = 16
BLOCK = 32
LANES = 128
MASKED = -1e30
SUBLANES = 8
STEP = 512
PIECES = 4
PLANE = 4
SPATIAL_GROUP = 32
TEMPORAL_GROUP = 8


def dot(left, right, over):
    return lax.dot_general(
        left, right, (((over[0],), (over[1],)), ((), ())), preferred_element_type=jnp.float32
    )


def head_masks(width, scale):
    lane = lax.broadcasted_iota(jnp.int32, (1, LANES), 1)
    first = jnp.where(lane < width, scale, 0.0).astype(jnp.bfloat16)
    second = jnp.where(lane < width, 0.0, scale).astype(jnp.bfloat16)
    return first, second


def head_rows(pair, masks):
    return jnp.concatenate([pair * masks[0], pair * masks[1]], axis=0)


def head_columns(rows, width):
    count = rows.shape[0] // 2
    lane = lax.broadcasted_iota(jnp.int32, (count, rows.shape[1]), 1)
    return jnp.where(lane < width, rows[:count], rows[count:])


def each(function, *lists):
    return [function(*items) for items in zip(*lists)]


def weights_by_key(scores):
    tops = each(lambda s: jnp.max(s, axis=0, keepdims=True), scores)
    exponents = each(lambda s, t: jnp.exp(s - t), scores, tops)
    shares = each(lambda e: 1.0 / jnp.sum(e, axis=0, keepdims=True), exponents)
    return each(lambda e, r: (e * r).astype(jnp.bfloat16), exponents, shares)


def by_query(shares, values, width):
    if 2 * values[0].shape[0] != LANES or len(values) % 2:
        return each(lambda s, v: head_columns(dot(s, v, (0, 0)), width), shares, values)
    results = []
    for first in range(0, len(values), 2):
        turned = jnp.transpose(jnp.concatenate(shares[first : first + 2], axis=0))
        one, other = values[first : first + 2]
        zero = jnp.zeros_like(one)
        apart = jnp.concatenate(
            [jnp.concatenate([one, zero], axis=1), jnp.concatenate([zero, other], axis=1)], axis=0
        )
        both = dot(turned, apart, (1, 0))
        results += [head_columns(both[:, :LANES], width), head_columns(both[:, LANES:], width)]
    return results


def back(values, scaled, cotangents, weights, grad_weights, heads_grads, width):
    wide = each(lambda w: w.astype(jnp.float32), weights)
    deltas = each(lambda w, g: jnp.sum(w * g, axis=0, keepdims=True), wide, grad_weights)
    grad_scores = each(
        lambda w, g, d: (w * (g - d)).astype(jnp.bfloat16), wide, grad_weights, deltas
    )
    length = values[0].shape[0]
    whole = length % LANES == 0
    both_ways = grad_scores
    if whole:
        both_ways = each(
            lambda g: jnp.concatenate(
                [
                    g[:, start : start + length] + jnp.transpose(g[:, start : start + length])
                    for start in (0, length)
                ],
                axis=1,
            ),
            grad_scores,
        )
    grads = each(
        lambda c, w, g, hg, hv: c.astype(jnp.float32)
        + dot(jnp.concatenate([w, g], axis=1), jnp.concatenate([hg, hv], axis=0), (1, 0)),
        cotangents,
        weights,
        both_ways,
        heads_grads,
        scaled,
    )
    if whole:
        return grads
    score_scale = 0.5 / math.sqrt(width)
    rest = by_query(grad_scores, values, width)
    return each(lambda g, r: g + score_scale * r, grads, rest)


def pair_bias(counts, offsets, slots):
    def sessions(slot):
        block = slot // BLOCK
        session = jnp.full(slot.shape, -1, jnp.int32)
        for j in range(offsets.shape[1]):
            session = session + (offsets[0, j] <= block).astype(jnp.int32)
        return session

    key_slot = lax.broadcasted_iota(jnp.int32, (slots, 2 * slots), 0)
    query_slot = lax.broadcasted_iota(jnp.int32, (slots, 2 * slots), 1) % slots
    key_session = sessions(key_slot)
    first = jnp.zeros_like(key_slot)
    live = jnp.zeros_like(key_slot)
    for j in range(offsets.shape[1]):
        chosen = key_session == j
        first = jnp.where(chosen, offsets[0, j] * BLOCK, first)
        live = jnp.where(chosen, counts[0, j], live)
    allowed = (key_session == sessions(query_slot)) & (key_slot - first < live)
    return jnp.where(allowed, 0.0, MASKED)


def pair_columns(pair):
    return pl.ds(pair * LANES, LANES)


def in_groups(pairs, rows, size):
    items = [(pair, row) for pair in range(pairs) for row in range(rows)]
    return [items[start : start + size] for start in range(0, len(items), size)]


def of_patch(patch, slots, patches):
    return pl.ds(patch, slots, stride=patches)


def attention(width, tokens, rows, bias, group):
    score_masks = head_masks(width, 0.5 / math.sqrt(width))
    values = [
        (
            tokens[p, :, pair_columns(pair)].astype(jnp.float32)
            + rows[:, pair * LANES : (pair + 1) * LANES]
        ).astype(jnp.bfloat16)
        for pair, p in group
    ]
    scores = each(lambda v: dot(v, head_rows(v, score_masks), (1, 1)) + bias[...], values)
    return values, weights_by_key(scores)


def spatial_kernel(
    width, counts, offsets, layout, embedding, tokens, rows, mixed, spread, bias, by_electrode
):
    patches, slots, model = tokens.shape
    templates = embedding.shape[0]
    pairs = model // LANES

    @pl.when(pl.program_id(0) == 0)
    def _():
        bias[...] = pair_bias(counts, offsets, slots)
        chosen = lax.broadcasted_iota(jnp.int32, (templates, slots), 0) == layout[...]
        spread[...] = jnp.transpose(chosen.astype(jnp.float32)).astype(jnp.bfloat16)

    chosen_rows = dot(spread[...], embedding[...], (1, 0))
    rows[...] = chosen_rows.astype(jnp.bfloat16)
    for group in in_groups(pairs, patches, SPATIAL_GROUP):
        values, shares = attention(width, tokens, chosen_rows, bias, group)
        attended = by_query(shares, values, width)
        for (pair, p), value, result in zip(group, values, attended):
            by_electrode[pair, of_patch(p, slots, patches), :] = value.astype(jnp.float32) + result
    for pair in range(pairs):
        mixed[:, pair_columns(pair)] = by_electrode[pair].astype(jnp.bfloat16)


def weights_kernel(width, counts, offsets, rows, tokens, embedded, weights, made, bias):
    made[...] = jnp.zeros_like(made)
    patches, slots, model = tokens.shape

    @pl.when(pl.program_id(0) == 0)
    def _():
        bias[...] = pair_bias(counts, offsets, slots)

    added = rows[...].astype(jnp.float32)
    for group in in_groups(model // LANES, patches, SPATIAL_GROUP):
        values, shares = attention(width, tokens, added, bias, group)
        for (pair, p), value, share in zip(group, values, shares):
            embedded[p, :, pair_columns(pair)] = value
            weights[p, pair] = share


def patches_first(local):
    return local % SUBLANES != 0


def electrode_rows(electrode, electrodes, parts, local):
    start, step = electrode * local, electrodes * local
    if patches_first(local):
        return [pl.ds(start + p, parts, stride=step) for p in range(local)]
    return [pl.ds(start + part * step, local) for part in range(parts)]


def temporal_kernel(width, parts, mixed, out_grad, *refs):
    mixed_grad, received, returned = refs[-3:]
    electrodes, patches, model = out_grad.shape
    local = patches // parts
    pairs = model // LANES
    score_masks = head_masks(width, 0.5 / math.sqrt(width))
    ones = head_masks(width, 1.0)
    for pair in range(pairs):
        received[pair] = mixed[:, pair_columns(pair)].astype(jnp.float32)
    for group in in_groups(pairs, electrodes, TEMPORAL_GROUP):
        places = [electrode_rows(e, electrodes, parts, local) for _, e in group]
        values = each(
            lambda item, place: jnp.concatenate(
                [received[item[0], rows, :] for rows in place], axis=0
            ).astype(jnp.bfloat16),
            group,
            places,
        )
        cotangents = [out_grad[e, :, pair_columns(pair)] for pair, e in group]
        scaled = each(lambda v: head_rows(v, score_masks), values)
        scores = each(lambda v, s: dot(v, s, (1, 1)), values, scaled)
        heads_grads = each(lambda g: head_rows(g, ones), cotangents)
        grad_weights = each(lambda v, g: dot(v, g, (1, 1)), values, heads_grads)
        shares = weights_by_key(scores)
        grads = back(values, scaled, cotangents, shares, grad_weights, heads_grads, width)
        for (pair, _), place, grad in zip(group, places, grads):
            start = 0
            for rows in place:
                returned[pair, rows, :] = grad[start : start + rows.size]
                start += rows.size
    for pair in range(pairs):
        mixed_grad[:, pair_columns(pair)] = returned[pair].astype(jnp.bfloat16)


def plane_rows(away, count):
    place = lax.bitwise_xor(lax.rem(lax.axis_index("shard"), PLANE), away)
    return pl.ds(pl.multiple_of(place * count, count), count)


def spatial_back_kernel(width, embedded, weights, mixed_grad, input_grad, *refs):
    electrode_grads, (sums, received) = refs[:-2], refs[-2:]
    patches, slots, model = embedded.shape
    pairs = model // LANES
    score_masks = head_masks(width, 0.5 / math.sqrt(width))
    ones = head_masks(width, 1.0)
    totals = [jnp.zeros((slots, LANES), jnp.float32) for _ in range(pairs)]
    for pair in range(pairs):
        received[pair] = mixed_grad[:, pair_columns(pair)].astype(jnp.float32)
    for group in in_groups(pairs, patches, SPATIAL_GROUP):
        cotangents = [
            received[pair, of_patch(p, slots, patches), :].astype(jnp.bfloat16)
            for pair, p in group
        ]
        values = [embedded[p, :, pair_columns(pair)] for pair, p in group]
        shares = [weights[p, pair] for pair, p in group]
        scaled = each(lambda v: head_rows(v, score_masks), values)
        heads_grads = each(lambda g: head_rows(g, ones), cotangents)
        grad_weights = each(lambda v, g: dot(v, g, (1, 1)), values, heads_grads)
        grads = back(values, scaled, cotangents, shares, grad_weights, heads_grads, width)
        for (pair, p), grad in zip(group, grads):
            input_grad[p, :, pair_columns(pair)] = grad.astype(jnp.bfloat16)
            totals[pair] = totals[pair] + grad
    for pair in range(pairs):
        sums[pair] = totals[pair]
        for away, block in enumerate(electrode_grads):
            rows = sums[pair, plane_rows(away, block.shape[0]), :]
            block[:, pair_columns(pair)] = rows.astype(jnp.bfloat16)


def plane_sum_kernel(*refs):
    total = refs[0][...].astype(jnp.float32)
    for part in refs[1:-1]:
        total = total + part[...].astype(jnp.float32)
    refs[-1][...] = total.astype(jnp.bfloat16)


def far_sum_kernel(*refs):
    parts, (total, ordered) = refs[:-2], refs[-2:]
    place = lax.div(lax.axis_index("shard"), PLANE)
    for away, part in enumerate(parts):
        ordered[lax.bitwise_xor(place, away)] = part[...].astype(jnp.float32)
    result = ordered[0]
    for index in range(1, len(parts)):
        result = result + ordered[index]
    total[...] = result.astype(jnp.bfloat16)


def table_kernel(groups, *refs):
    layouts, blocks, (table, sources, pieces, sems) = refs[:groups], refs[groups:-4], refs[-4:]
    owner = lax.axis_index("group")
    count, rows, _ = pieces.shape
    slots = sources.shape[1]
    for away in range(groups):
        for near in range(PLANE):
            block = blocks[away * PLANE + near]
            sources[away, plane_rows(near, block.shape[0]), :] = block[...]
    copies = []
    for piece in range(count):
        first = owner * (count * rows) + piece * rows
        template = lax.broadcasted_iota(jnp.int32, (rows, slots), 0) + first
        total = jnp.zeros(pieces.shape[1:], jnp.float32)
        for away in range(groups):
            spread = (template == layouts[away][...]).astype(jnp.float32).astype(jnp.bfloat16)
            total = total + dot(spread, sources[away], (1, 0))
        pieces[piece] = total
        copy = pltpu.make_async_copy(
            pieces.at[piece], table.at[pl.ds(piece * rows, rows)], sems.at[piece]
        )
        copy.start()
        copies.append(copy)
    for copy in copies:
        copy.wait()


VMEM = pl.BlockSpec(memory_space=pltpu.VMEM)
SMEM = pl.BlockSpec(memory_space=pltpu.SMEM)
HBM = pl.BlockSpec(memory_space=pltpu.HBM)
PARAMS = pltpu.CompilerParams(vmem_limit_bytes=32 * 1024 * 1024)
STREAMED = pltpu.CompilerParams(vmem_limit_bytes=56 * 1024 * 1024)


def body(activations, out_grad, embedding, counts, offsets, layout):
    tokens = activations[0]
    local, slots, model = tokens.shape
    groups = lax.axis_size("group")
    parts = lax.axis_size("shard")
    patches = local * parts
    own = slots // parts
    width = model // HEADS
    templates = embedding.shape[0]
    pairs = STEP // LANES
    steps = model // STEP

    layouts = [layout] + [
        lax.ppermute(layout, "group", [(i, (i + away) % groups) for i in range(groups)])
        for away in range(1, groups)
    ]
    order = (2, 1, 0, 3) if patches_first(local) else (2, 0, 1, 3)
    cotangent = jnp.transpose(out_grad[0].reshape(parts, local, own, model), order)
    cotangent = cotangent.reshape(own, patches, model)

    flat = pl.BlockSpec((slots * local, STEP), lambda step: (0, step))
    planes = pl.BlockSpec((local, slots, STEP), lambda step: (0, 0, step))
    squares = pl.BlockSpec((local, pairs, slots, 2 * slots), lambda step: (0, step, 0, 0))
    flat_shape = jax.ShapeDtypeStruct((slots * local, model), jnp.bfloat16)
    plane_shape = jax.ShapeDtypeStruct(tokens.shape, jnp.bfloat16)
    flat_scratch = pltpu.VMEM((pairs, slots * local, LANES), jnp.float32)

    strip = pl.BlockSpec((slots, STEP), lambda step: (0, step))
    rows, mixed = pl.pallas_call(
        functools.partial(spatial_kernel, width),
        grid=(steps,),
        out_shape=(jax.ShapeDtypeStruct((slots, model), jnp.bfloat16), flat_shape),
        in_specs=[SMEM, SMEM, VMEM, pl.BlockSpec((templates, STEP), lambda step: (0, step)), planes],
        out_specs=(strip, flat),
        scratch_shapes=[
            pltpu.VMEM((slots, templates), jnp.bfloat16),
            pltpu.VMEM((slots, 2 * slots), jnp.float32),
            flat_scratch,
        ],
        compiler_params=STREAMED,
        name="spatial",
    )(counts, offsets, layout, embedding, tokens)
    embedded, weights, made = pl.pallas_call(
        functools.partial(weights_kernel, width),
        grid=(steps,),
        out_shape=(
            plane_shape,
            jax.ShapeDtypeStruct((local, model // LANES, slots, 2 * slots), jnp.bfloat16),
            jax.ShapeDtypeStruct((SUBLANES, LANES), jnp.float32),
        ),
        in_specs=[SMEM, SMEM, strip, planes],
        out_specs=(planes, squares, pl.BlockSpec((SUBLANES, LANES), lambda step: (0, 0))),
        scratch_shapes=[pltpu.VMEM((slots, 2 * slots), jnp.float32)],
        compiler_params=STREAMED,
        cost_estimate=pl.CostEstimate(
            flops=4 * local * slots * slots * model, bytes_accessed=6 * tokens.size, transcendentals=0
        ),
        name="weights",
    )(counts, offsets, rows, tokens)

    gathered = lax.all_to_all(mixed, "shard", split_axis=0, concat_axis=0, tiled=True)
    mixed_grad = pl.pallas_call(
        functools.partial(temporal_kernel, width, parts),
        grid=(steps,),
        out_shape=flat_shape,
        in_specs=[flat, pl.BlockSpec((own, patches, STEP), lambda step: (0, 0, step))]
        + [pl.BlockSpec(memory_space=pl.ANY)] * groups,
        out_specs=flat,
        scratch_shapes=[flat_scratch, flat_scratch],
        compiler_params=PARAMS,
        name="temporal",
    )(gathered, cotangent, made, *layouts[1:])

    returned = lax.all_to_all(mixed_grad, "shard", split_axis=0, concat_axis=0, tiled=True)
    kept = slots // PLANE
    input_grad, *sums = pl.pallas_call(
        functools.partial(spatial_back_kernel, width),
        grid=(steps,),
        out_shape=(plane_shape,) + (jax.ShapeDtypeStruct((kept, model), jnp.bfloat16),) * PLANE,
        in_specs=[planes, squares, flat],
        out_specs=(planes,) + (pl.BlockSpec((kept, STEP), lambda step: (0, step)),) * PLANE,
        scratch_shapes=[pltpu.VMEM((pairs, slots, LANES), jnp.float32), flat_scratch],
        compiler_params=PARAMS,
        name="spatial_back",
    )(embedded, weights, returned)

    def to_partner(array, away):
        if away == 0:
            return array
        return lax.ppermute(array, "shard", [(i, i ^ away) for i in range(parts)])

    far_count = parts // PLANE
    assert parts == far_count * PLANE and parts & (parts - 1) == 0
    kept_shape = jax.ShapeDtypeStruct((kept, model), jnp.bfloat16)
    plane_parts = [to_partner(block, away) for away, block in enumerate(sums)]
    plane_sum = pl.pallas_call(
        plane_sum_kernel,
        out_shape=kept_shape,
        in_specs=[VMEM] * PLANE,
        out_specs=VMEM,
        compiler_params=PARAMS,
        name="plane_sum",
    )(*plane_parts)
    far_parts = [to_partner(plane_sum, far * PLANE) for far in range(far_count)]
    total = pl.pallas_call(
        far_sum_kernel,
        out_shape=kept_shape,
        in_specs=[VMEM] * far_count,
        out_specs=VMEM,
        scratch_shapes=[pltpu.VMEM((far_count, kept, model), jnp.float32)],
        compiler_params=PARAMS,
        name="far_sum",
    )(*far_parts)
    totals = [total] + [
        lax.ppermute(total, "group", [(i, (i + away) % groups) for i in range(groups)])
        for away in range(1, groups)
    ]
    everyone = [to_partner(rows, near) for rows in totals for near in range(PLANE)]
    table_rows = templates // groups
    table_grad = pl.pallas_call(
        functools.partial(table_kernel, groups),
        out_shape=jax.ShapeDtypeStruct((table_rows, model), jnp.float32),
        in_specs=[VMEM] * (groups + groups * PLANE),
        out_specs=HBM,
        scratch_shapes=[
            pltpu.VMEM((groups, slots, model), jnp.bfloat16),
            pltpu.VMEM((PIECES, table_rows // PIECES, model), jnp.float32),
            pltpu.SemaphoreType.DMA((PIECES,)),
        ],
        compiler_params=PARAMS,
        name="table",
    )(*layouts, *everyone)
    return (input_grad[None], table_grad)


def solution(mesh):
    placed = (
        P("group", "shard", None, None),
        P("group", None, "shard", None),
        P(),
        P("group", None),
        P("group", None),
        P("group", None),
    )
    return jax.shard_map(
        body,
        mesh=mesh,
        in_specs=placed,
        out_specs=(P("group", "shard", None, None), P("group", None)),
        check_vma=False,
    )
```

```python
import functools
import math

import jax
import jax.numpy as jnp
from jax import lax
from jax.experimental import pallas as pl
from jax.experimental.pallas import tpu as pltpu
from jax.sharding import PartitionSpec as P

HEADS = 16
BLOCK = 32
LANES = 128
MASKED = -1e30
SUBLANES = 8
STEP = 512
PIECES = 4
PLANE = 4
SPATIAL_GROUP = 32
TEMPORAL_GROUP = 8


def dot(left, right, over):
    return lax.dot_general(
        left, right, (((over[0],), (over[1],)), ((), ())), preferred_element_type=jnp.float32
    )


def head_masks(width, scale):
    lane = lax.broadcasted_iota(jnp.int32, (1, LANES), 1)
    first = jnp.where(lane < width, scale, 0.0).astype(jnp.bfloat16)
    second = jnp.where(lane < width, 0.0, scale).astype(jnp.bfloat16)
    return first, second


def head_rows(pair, masks):
    return jnp.concatenate([pair * masks[0], pair * masks[1]], axis=0)


def head_columns(rows, width):
    count = rows.shape[0] // 2
    lane = lax.broadcasted_iota(jnp.int32, (count, rows.shape[1]), 1)
    return jnp.where(lane < width, rows[:count], rows[count:])


def each(function, *lists):
    return [function(*items) for items in zip(*lists)]


def weights_by_key(scores):
    tops = each(lambda s: jnp.max(s, axis=0, keepdims=True), scores)
    exponents = each(lambda s, t: jnp.exp(s - t), scores, tops)
    shares = each(lambda e: 1.0 / jnp.sum(e, axis=0, keepdims=True), exponents)
    return each(lambda e, r: (e * r).astype(jnp.bfloat16), exponents, shares)


def by_query(shares, values, width):
    if 2 * values[0].shape[0] != LANES or len(values) % 2:
        return each(lambda s, v: head_columns(dot(s, v, (0, 0)), width), shares, values)
    results = []
    for first in range(0, len(values), 2):
        turned = jnp.transpose(jnp.concatenate(shares[first : first + 2], axis=0))
        one, other = values[first : first + 2]
        zero = jnp.zeros_like(one)
        apart = jnp.concatenate(
            [jnp.concatenate([one, zero], axis=1), jnp.concatenate([zero, other], axis=1)], axis=0
        )
        both = dot(turned, apart, (1, 0))
        results += [head_columns(both[:, :LANES], width), head_columns(both[:, LANES:], width)]
    return results


def back(values, scaled, cotangents, weights, grad_weights, heads_grads, width):
    wide = each(lambda w: w.astype(jnp.float32), weights)
    deltas = each(lambda w, g: jnp.sum(w * g, axis=0, keepdims=True), wide, grad_weights)
    grad_scores = each(
        lambda w, g, d: (w * (g - d)).astype(jnp.bfloat16), wide, grad_weights, deltas
    )
    length = values[0].shape[0]
    whole = length % LANES == 0
    both_ways = grad_scores
    if whole:
        both_ways = each(
            lambda g: jnp.concatenate(
                [
                    g[:, start : start + length] + jnp.transpose(g[:, start : start + length])
                    for start in (0, length)
                ],
                axis=1,
            ),
            grad_scores,
        )
    grads = each(
        lambda c, w, g, hg, hv: c.astype(jnp.float32)
        + dot(jnp.concatenate([w, g], axis=1), jnp.concatenate([hg, hv], axis=0), (1, 0)),
        cotangents,
        weights,
        both_ways,
        heads_grads,
        scaled,
    )
    if whole:
        return grads
    score_scale = 0.5 / math.sqrt(width)
    rest = by_query(grad_scores, values, width)
    return each(lambda g, r: g + score_scale * r, grads, rest)


def pair_bias(counts, offsets, slots):
    def sessions(slot):
        block = slot // BLOCK
        session = jnp.full(slot.shape, -1, jnp.int32)
        for j in range(offsets.shape[1]):
            session = session + (offsets[0, j] <= block).astype(jnp.int32)
        return session

    key_slot = lax.broadcasted_iota(jnp.int32, (slots, 2 * slots), 0)
    query_slot = lax.broadcasted_iota(jnp.int32, (slots, 2 * slots), 1) % slots
    key_session = sessions(key_slot)
    first = jnp.zeros_like(key_slot)
    live = jnp.zeros_like(key_slot)
    for j in range(offsets.shape[1]):
        chosen = key_session == j
        first = jnp.where(chosen, offsets[0, j] * BLOCK, first)
        live = jnp.where(chosen, counts[0, j], live)
    allowed = (key_session == sessions(query_slot)) & (key_slot - first < live)
    return jnp.where(allowed, 0.0, MASKED)


def pair_columns(pair):
    return pl.ds(pair * LANES, LANES)


def in_groups(pairs, rows, size):
    items = [(pair, row) for pair in range(pairs) for row in range(rows)]
    return [items[start : start + size] for start in range(0, len(items), size)]


def of_patch(patch, slots, patches):
    return pl.ds(patch, slots, stride=patches)


def attention(width, tokens, rows, bias, group):
    score_masks = head_masks(width, 0.5 / math.sqrt(width))
    values = [
        (
            tokens[p, :, pair_columns(pair)].astype(jnp.float32)
            + rows[:, pair * LANES : (pair + 1) * LANES]
        ).astype(jnp.bfloat16)
        for pair, p in group
    ]
    scores = each(lambda v: dot(v, head_rows(v, score_masks), (1, 1)) + bias[...], values)
    return values, weights_by_key(scores)


def spatial_kernel(
    width, counts, offsets, layout, embedding, tokens, rows, mixed, spread, bias, by_electrode
):
    patches, slots, model = tokens.shape
    templates = embedding.shape[0]
    pairs = model // LANES

    @pl.when(pl.program_id(0) == 0)
    def _():
        bias[...] = pair_bias(counts, offsets, slots)
        chosen = lax.broadcasted_iota(jnp.int32, (templates, slots), 0) == layout[...]
        spread[...] = jnp.transpose(chosen.astype(jnp.float32)).astype(jnp.bfloat16)

    chosen_rows = dot(spread[...], embedding[...], (1, 0))
    rows[...] = chosen_rows.astype(jnp.bfloat16)
    for group in in_groups(pairs, patches, SPATIAL_GROUP):
        values, shares = attention(width, tokens, chosen_rows, bias, group)
        attended = by_query(shares, values, width)
        for (pair, p), value, result in zip(group, values, attended):
            by_electrode[pair, of_patch(p, slots, patches), :] = value.astype(jnp.float32) + result
    for pair in range(pairs):
        mixed[:, pair_columns(pair)] = by_electrode[pair].astype(jnp.bfloat16)


def weights_kernel(width, counts, offsets, rows, tokens, embedded, weights, made, bias):
    made[...] = jnp.zeros_like(made)
    patches, slots, model = tokens.shape

    @pl.when(pl.program_id(0) == 0)
    def _():
        bias[...] = pair_bias(counts, offsets, slots)

    added = rows[...].astype(jnp.float32)
    for group in in_groups(model // LANES, patches, SPATIAL_GROUP):
        values, shares = attention(width, tokens, added, bias, group)
        for (pair, p), value, share in zip(group, values, shares):
            embedded[p, :, pair_columns(pair)] = value
            weights[p, pair] = share


def patches_first(local):
    return local % SUBLANES != 0


def electrode_rows(electrode, electrodes, parts, local):
    start, step = electrode * local, electrodes * local
    if patches_first(local):
        return [pl.ds(start + p, parts, stride=step) for p in range(local)]
    return [pl.ds(start + part * step, local) for part in range(parts)]


def temporal_kernel(width, parts, mixed, out_grad, *refs):
    mixed_grad, received, returned = refs[-3:]
    electrodes, patches, model = out_grad.shape
    local = patches // parts
    pairs = model // LANES
    score_masks = head_masks(width, 0.5 / math.sqrt(width))
    ones = head_masks(width, 1.0)
    for pair in range(pairs):
        received[pair] = mixed[:, pair_columns(pair)].astype(jnp.float32)
    for group in in_groups(pairs, electrodes, TEMPORAL_GROUP):
        places = [electrode_rows(e, electrodes, parts, local) for _, e in group]
        values = each(
            lambda item, place: jnp.concatenate(
                [received[item[0], rows, :] for rows in place], axis=0
            ).astype(jnp.bfloat16),
            group,
            places,
        )
        cotangents = [out_grad[e, :, pair_columns(pair)] for pair, e in group]
        scaled = each(lambda v: head_rows(v, score_masks), values)
        scores = each(lambda v, s: dot(v, s, (1, 1)), values, scaled)
        heads_grads = each(lambda g: head_rows(g, ones), cotangents)
        grad_weights = each(lambda v, g: dot(v, g, (1, 1)), values, heads_grads)
        shares = weights_by_key(scores)
        grads = back(values, scaled, cotangents, shares, grad_weights, heads_grads, width)
        for (pair, _), place, grad in zip(group, places, grads):
            start = 0
            for rows in place:
                returned[pair, rows, :] = grad[start : start + rows.size]
                start += rows.size
    for pair in range(pairs):
        mixed_grad[:, pair_columns(pair)] = returned[pair].astype(jnp.bfloat16)


def half_rows(bit, away, count):
    here = lax.bitwise_and(lax.shift_right_logical(lax.axis_index("shard"), bit), 1)
    return pl.ds(pl.multiple_of(lax.bitwise_xor(here, away) * count, count), count)


def spatial_back_kernel(width, embedded, weights, mixed_grad, input_grad, *refs):
    electrode_grads, (sums, received) = refs[:-2], refs[-2:]
    patches, slots, model = embedded.shape
    pairs = model // LANES
    score_masks = head_masks(width, 0.5 / math.sqrt(width))
    ones = head_masks(width, 1.0)
    totals = [jnp.zeros((slots, LANES), jnp.float32) for _ in range(pairs)]
    for pair in range(pairs):
        received[pair] = mixed_grad[:, pair_columns(pair)].astype(jnp.float32)
    for group in in_groups(pairs, patches, SPATIAL_GROUP):
        cotangents = [
            received[pair, of_patch(p, slots, patches), :].astype(jnp.bfloat16)
            for pair, p in group
        ]
        values = [embedded[p, :, pair_columns(pair)] for pair, p in group]
        shares = [weights[p, pair] for pair, p in group]
        scaled = each(lambda v: head_rows(v, score_masks), values)
        heads_grads = each(lambda g: head_rows(g, ones), cotangents)
        grad_weights = each(lambda v, g: dot(v, g, (1, 1)), values, heads_grads)
        grads = back(values, scaled, cotangents, shares, grad_weights, heads_grads, width)
        for (pair, p), grad in zip(group, grads):
            input_grad[p, :, pair_columns(pair)] = grad.astype(jnp.bfloat16)
            totals[pair] = totals[pair] + grad
    for pair in range(pairs):
        sums[pair] = totals[pair]
        for away, block in enumerate(electrode_grads):
            rows = sums[pair, half_rows(0, away, block.shape[0]), :]
            block[:, pair_columns(pair)] = rows.astype(jnp.bfloat16)


def add(one, other):
    return (one.astype(jnp.float32) + other.astype(jnp.float32)).astype(jnp.bfloat16)


def core_sum_kernel(own, arrived, total):
    total[...] = add(own[...], arrived[...])


def cross_sum_kernel(*refs):
    totals = refs[-1]
    for away in range(totals.shape[0]):
        totals[away] = add(refs[2 * away][...], refs[2 * away + 1][...])


def far_sum_kernel(*refs):
    parts, (total, ordered) = refs[:-2], refs[-2:]
    place = lax.div(lax.axis_index("shard"), PLANE)
    for away, part in enumerate(parts):
        ordered[lax.bitwise_xor(place, away)] = part[...].astype(jnp.float32)
    result = ordered[0]
    for index in range(1, len(parts)):
        result = result + ordered[index]
    total[...] = result.astype(jnp.bfloat16)


def join_kernel(bit, own, arrived, joined):
    for away, block in enumerate((own, arrived)):
        joined[:, half_rows(bit, away, block.shape[1]), :] = block[...]


def table_kernel(groups, *refs):
    layouts, blocks, (table, sources, pieces, sems) = refs[:groups], refs[groups:-4], refs[-4:]
    owner = lax.axis_index("group")
    count, rows, _ = pieces.shape
    slots = sources.shape[1]
    join_kernel(0, *blocks, sources)
    copies = []
    for piece in range(count):
        first = owner * (count * rows) + piece * rows
        template = lax.broadcasted_iota(jnp.int32, (rows, slots), 0) + first
        total = jnp.zeros(pieces.shape[1:], jnp.float32)
        for away in range(groups):
            spread = (template == layouts[away][...]).astype(jnp.float32).astype(jnp.bfloat16)
            total = total + dot(spread, sources[away], (1, 0))
        pieces[piece] = total
        copy = pltpu.make_async_copy(
            pieces.at[piece], table.at[pl.ds(piece * rows, rows)], sems.at[piece]
        )
        copy.start()
        copies.append(copy)
    for copy in copies:
        copy.wait()


VMEM = pl.BlockSpec(memory_space=pltpu.VMEM)
SMEM = pl.BlockSpec(memory_space=pltpu.SMEM)
HBM = pl.BlockSpec(memory_space=pltpu.HBM)
PARAMS = pltpu.CompilerParams(vmem_limit_bytes=32 * 1024 * 1024)
STREAMED = pltpu.CompilerParams(vmem_limit_bytes=56 * 1024 * 1024)


def body(activations, out_grad, embedding, counts, offsets, layout):
    tokens = activations[0]
    local, slots, model = tokens.shape
    groups = lax.axis_size("group")
    parts = lax.axis_size("shard")
    patches = local * parts
    own = slots // parts
    width = model // HEADS
    templates = embedding.shape[0]
    pairs = STEP // LANES
    steps = model // STEP

    layouts = [layout] + [
        lax.ppermute(layout, "group", [(i, (i + away) % groups) for i in range(groups)])
        for away in range(1, groups)
    ]
    order = (2, 1, 0, 3) if patches_first(local) else (2, 0, 1, 3)
    cotangent = jnp.transpose(out_grad[0].reshape(parts, local, own, model), order)
    cotangent = cotangent.reshape(own, patches, model)

    flat = pl.BlockSpec((slots * local, STEP), lambda step: (0, step))
    planes = pl.BlockSpec((local, slots, STEP), lambda step: (0, 0, step))
    squares = pl.BlockSpec((local, pairs, slots, 2 * slots), lambda step: (0, step, 0, 0))
    flat_shape = jax.ShapeDtypeStruct((slots * local, model), jnp.bfloat16)
    plane_shape = jax.ShapeDtypeStruct(tokens.shape, jnp.bfloat16)
    flat_scratch = pltpu.VMEM((pairs, slots * local, LANES), jnp.float32)

    strip = pl.BlockSpec((slots, STEP), lambda step: (0, step))
    rows, mixed = pl.pallas_call(
        functools.partial(spatial_kernel, width),
        grid=(steps,),
        out_shape=(jax.ShapeDtypeStruct((slots, model), jnp.bfloat16), flat_shape),
        in_specs=[SMEM, SMEM, VMEM, pl.BlockSpec((templates, STEP), lambda step: (0, step)), planes],
        out_specs=(strip, flat),
        scratch_shapes=[
            pltpu.VMEM((slots, templates), jnp.bfloat16),
            pltpu.VMEM((slots, 2 * slots), jnp.float32),
            flat_scratch,
        ],
        compiler_params=STREAMED,
        name="spatial",
    )(counts, offsets, layout, embedding, tokens)
    embedded, weights, made = pl.pallas_call(
        functools.partial(weights_kernel, width),
        grid=(steps,),
        out_shape=(
            plane_shape,
            jax.ShapeDtypeStruct((local, model // LANES, slots, 2 * slots), jnp.bfloat16),
            jax.ShapeDtypeStruct((SUBLANES, LANES), jnp.float32),
        ),
        in_specs=[SMEM, SMEM, strip, planes],
        out_specs=(planes, squares, pl.BlockSpec((SUBLANES, LANES), lambda step: (0, 0))),
        scratch_shapes=[pltpu.VMEM((slots, 2 * slots), jnp.float32)],
        compiler_params=STREAMED,
        cost_estimate=pl.CostEstimate(
            flops=4 * local * slots * slots * model, bytes_accessed=6 * tokens.size, transcendentals=0
        ),
        name="weights",
    )(counts, offsets, rows, tokens)

    gathered = lax.all_to_all(mixed, "shard", split_axis=0, concat_axis=0, tiled=True)
    mixed_grad = pl.pallas_call(
        functools.partial(temporal_kernel, width, parts),
        grid=(steps,),
        out_shape=flat_shape,
        in_specs=[flat, pl.BlockSpec((own, patches, STEP), lambda step: (0, 0, step))]
        + [pl.BlockSpec(memory_space=pl.ANY)] * groups,
        out_specs=flat,
        scratch_shapes=[flat_scratch, flat_scratch],
        compiler_params=PARAMS,
        name="temporal",
    )(gathered, cotangent, made, *layouts[1:])

    returned = lax.all_to_all(mixed_grad, "shard", split_axis=0, concat_axis=0, tiled=True)
    half = slots // 2
    input_grad, own_half, other_half = pl.pallas_call(
        functools.partial(spatial_back_kernel, width),
        grid=(steps,),
        out_shape=(plane_shape,) + (jax.ShapeDtypeStruct((half, model), jnp.bfloat16),) * 2,
        in_specs=[planes, squares, flat],
        out_specs=(planes,) + (pl.BlockSpec((half, STEP), lambda step: (0, step)),) * 2,
        scratch_shapes=[pltpu.VMEM((pairs, slots, LANES), jnp.float32), flat_scratch],
        compiler_params=PARAMS,
        name="spatial_back",
    )(embedded, weights, returned)

    far_count = parts // PLANE
    assert parts == far_count * PLANE and parts & (parts - 1) == 0

    def to_partner(array, group_away, shard_away):
        if group_away == 0 and shard_away == 0:
            return array
        pairs_of_devices = [
            (g * parts + i, (g + group_away) % groups * parts + (i ^ shard_away))
            for g in range(groups)
            for i in range(parts)
        ]
        return lax.ppermute(array, ("group", "shard"), pairs_of_devices)

    def summed(kernel, shape, operands, scratch=()):
        return pl.pallas_call(
            kernel,
            out_shape=jax.ShapeDtypeStruct(shape, jnp.bfloat16),
            in_specs=[VMEM] * len(operands),
            out_specs=VMEM,
            scratch_shapes=list(scratch),
            compiler_params=PARAMS,
            name="sums",
        )(*operands)

    halved = summed(core_sum_kernel, (half, model), (own_half, to_partner(other_half, 0, 1)))
    total = summed(
        far_sum_kernel,
        (half, model),
        [to_partner(halved, 0, far * PLANE) for far in range(far_count)],
        [pltpu.VMEM((far_count, half, model), jnp.float32)],
    )
    crossed = [
        to_partner(total, away, side) for away in reversed(range(groups)) for side in (2, 0)
    ]
    totals = summed(cross_sum_kernel, (groups, half, model), crossed[::-1])
    table_rows = templates // groups
    table_grad = pl.pallas_call(
        functools.partial(table_kernel, groups),
        out_shape=jax.ShapeDtypeStruct((table_rows, model), jnp.float32),
        in_specs=[VMEM] * (groups + 2),
        out_specs=HBM,
        scratch_shapes=[
            pltpu.VMEM((groups, slots, model), jnp.bfloat16),
            pltpu.VMEM((PIECES, table_rows // PIECES, model), jnp.float32),
            pltpu.SemaphoreType.DMA((PIECES,)),
        ],
        compiler_params=PARAMS,
        name="table",
    )(*layouts, totals, to_partner(totals, 0, 1))
    return (input_grad[None], table_grad)


def solution(mesh):
    placed = (
        P("group", "shard", None, None),
        P("group", None, "shard", None),
        P(),
        P("group", None),
        P("group", None),
        P("group", None),
    )
    return jax.shard_map(
        body,
        mesh=mesh,
        in_specs=placed,
        out_specs=(P("group", "shard", None, None), P("group", None)),
        check_vma=False,
    )
```

```python
import functools
import math

import jax
import jax.numpy as jnp
from jax import lax
from jax.experimental import pallas as pl
from jax.experimental.pallas import tpu as pltpu
from jax.sharding import PartitionSpec as P

HEADS = 16
BLOCK = 32
LANES = 128
MASKED = -1e30
SUBLANES = 8
STEP = 512
PIECES = 8
PLANE = 4
SPATIAL_GROUP = 32
TEMPORAL_GROUP = 8


def dot(left, right, over):
    return lax.dot_general(
        left, right, (((over[0],), (over[1],)), ((), ())), preferred_element_type=jnp.float32
    )


def head_masks(width, scale):
    lane = lax.broadcasted_iota(jnp.int32, (1, LANES), 1)
    first = jnp.where(lane < width, scale, 0.0).astype(jnp.bfloat16)
    second = jnp.where(lane < width, 0.0, scale).astype(jnp.bfloat16)
    return first, second


def head_rows(pair, masks):
    return jnp.concatenate([pair * masks[0], pair * masks[1]], axis=0)


def head_columns(rows, width):
    count = rows.shape[0] // 2
    lane = lax.broadcasted_iota(jnp.int32, (count, rows.shape[1]), 1)
    return jnp.where(lane < width, rows[:count], rows[count:])


def each(function, *lists):
    return [function(*items) for items in zip(*lists)]


def weights_by_key(scores):
    tops = each(lambda s: jnp.max(s, axis=0, keepdims=True), scores)
    exponents = each(lambda s, t: jnp.exp(s - t), scores, tops)
    shares = each(lambda e: 1.0 / jnp.sum(e, axis=0, keepdims=True), exponents)
    return each(lambda e, r: (e * r).astype(jnp.bfloat16), exponents, shares)


def by_query(shares, values, width):
    if 2 * values[0].shape[0] != LANES or len(values) % 2:
        return each(lambda s, v: head_columns(dot(s, v, (0, 0)), width), shares, values)
    results = []
    for first in range(0, len(values), 2):
        turned = jnp.transpose(jnp.concatenate(shares[first : first + 2], axis=0))
        one, other = values[first : first + 2]
        zero = jnp.zeros_like(one)
        apart = jnp.concatenate(
            [jnp.concatenate([one, zero], axis=1), jnp.concatenate([zero, other], axis=1)], axis=0
        )
        both = dot(turned, apart, (1, 0))
        results += [head_columns(both[:, :LANES], width), head_columns(both[:, LANES:], width)]
    return results


def back(values, scaled, cotangents, weights, grad_weights, heads_grads, width):
    wide = each(lambda w: w.astype(jnp.float32), weights)
    deltas = each(lambda w, g: jnp.sum(w * g, axis=0, keepdims=True), wide, grad_weights)
    grad_scores = each(
        lambda w, g, d: (w * (g - d)).astype(jnp.bfloat16), wide, grad_weights, deltas
    )
    length = values[0].shape[0]
    whole = length % LANES == 0
    both_ways = grad_scores
    if whole:
        both_ways = each(
            lambda g: jnp.concatenate(
                [
                    g[:, start : start + length] + jnp.transpose(g[:, start : start + length])
                    for start in (0, length)
                ],
                axis=1,
            ),
            grad_scores,
        )
    grads = each(
        lambda c, w, g, hg, hv: c.astype(jnp.float32)
        + dot(jnp.concatenate([w, g], axis=1), jnp.concatenate([hg, hv], axis=0), (1, 0)),
        cotangents,
        weights,
        both_ways,
        heads_grads,
        scaled,
    )
    if whole:
        return grads
    score_scale = 0.5 / math.sqrt(width)
    rest = by_query(grad_scores, values, width)
    return each(lambda g, r: g + score_scale * r, grads, rest)


def pair_bias(counts, offsets, slots):
    def sessions(slot):
        block = slot // BLOCK
        session = jnp.full(slot.shape, -1, jnp.int32)
        for j in range(offsets.shape[1]):
            session = session + (offsets[0, j] <= block).astype(jnp.int32)
        return session

    key_slot = lax.broadcasted_iota(jnp.int32, (slots, 2 * slots), 0)
    query_slot = lax.broadcasted_iota(jnp.int32, (slots, 2 * slots), 1) % slots
    key_session = sessions(key_slot)
    first = jnp.zeros_like(key_slot)
    live = jnp.zeros_like(key_slot)
    for j in range(offsets.shape[1]):
        chosen = key_session == j
        first = jnp.where(chosen, offsets[0, j] * BLOCK, first)
        live = jnp.where(chosen, counts[0, j], live)
    allowed = (key_session == sessions(query_slot)) & (key_slot - first < live)
    return jnp.where(allowed, 0.0, MASKED)


def pair_columns(pair):
    return pl.ds(pair * LANES, LANES)


def in_groups(pairs, rows, size):
    items = [(pair, row) for pair in range(pairs) for row in range(rows)]
    return [items[start : start + size] for start in range(0, len(items), size)]


def of_patch(patch, slots, patches):
    return pl.ds(patch, slots, stride=patches)


def attention(width, tokens, rows, bias, group):
    score_masks = head_masks(width, 0.5 / math.sqrt(width))
    values = [
        (
            tokens[p, :, pair_columns(pair)].astype(jnp.float32)
            + rows[:, pair * LANES : (pair + 1) * LANES]
        ).astype(jnp.bfloat16)
        for pair, p in group
    ]
    scores = each(lambda v: dot(v, head_rows(v, score_masks), (1, 1)) + bias[...], values)
    return values, weights_by_key(scores)


def spatial_kernel(
    width, counts, offsets, layout, embedding, tokens, rows, mixed, spread, bias, by_electrode
):
    patches, slots, model = tokens.shape
    templates = embedding.shape[0]
    pairs = model // LANES

    @pl.when(pl.program_id(0) == 0)
    def _():
        bias[...] = pair_bias(counts, offsets, slots)
        wanted = jnp.broadcast_to(layout[...].astype(jnp.float32), (LANES, slots))
        wanted = jnp.transpose(wanted).astype(jnp.int32)
        template = lax.broadcasted_iota(jnp.int32, (slots, LANES), 1)
        for first in range(0, templates, LANES):
            chosen = wanted == template + first
            spread[:, pl.ds(first, LANES)] = chosen.astype(jnp.float32).astype(jnp.bfloat16)

    chosen_rows = dot(spread[...], embedding[...], (1, 0))
    rows[...] = chosen_rows.astype(jnp.bfloat16)
    for group in in_groups(pairs, patches, SPATIAL_GROUP):
        values, shares = attention(width, tokens, chosen_rows, bias, group)
        attended = by_query(shares, values, width)
        for (pair, p), value, result in zip(group, values, attended):
            by_electrode[pair, of_patch(p, slots, patches), :] = value.astype(jnp.float32) + result
    for pair in range(pairs):
        mixed[:, pair_columns(pair)] = by_electrode[pair].astype(jnp.bfloat16)


def weights_kernel(width, counts, offsets, rows, tokens, embedded, weights, made, bias):
    made[...] = jnp.zeros_like(made)
    patches, slots, model = tokens.shape

    @pl.when(pl.program_id(0) == 0)
    def _():
        bias[...] = pair_bias(counts, offsets, slots)

    added = rows[...].astype(jnp.float32)
    for group in in_groups(model // LANES, patches, SPATIAL_GROUP):
        values, shares = attention(width, tokens, added, bias, group)
        for (pair, p), value, share in zip(group, values, shares):
            embedded[p, :, pair_columns(pair)] = value
            weights[p, pair] = share


def patches_first(local):
    return local % SUBLANES != 0


def electrode_rows(electrode, electrodes, parts, local):
    start, step = electrode * local, electrodes * local
    if patches_first(local):
        return [pl.ds(start + p, parts, stride=step) for p in range(local)]
    return [pl.ds(start + part * step, local) for part in range(parts)]


def temporal_kernel(width, parts, mixed, out_grad, *refs):
    mixed_grad, received, returned = refs[-3:]
    electrodes, patches, model = out_grad.shape
    local = patches // parts
    pairs = model // LANES
    score_masks = head_masks(width, 0.5 / math.sqrt(width))
    ones = head_masks(width, 1.0)
    for pair in range(pairs):
        received[pair] = mixed[:, pair_columns(pair)].astype(jnp.float32)
    for group in in_groups(pairs, electrodes, TEMPORAL_GROUP):
        places = [electrode_rows(e, electrodes, parts, local) for _, e in group]
        values = each(
            lambda item, place: jnp.concatenate(
                [received[item[0], rows, :] for rows in place], axis=0
            ).astype(jnp.bfloat16),
            group,
            places,
        )
        cotangents = [out_grad[e, :, pair_columns(pair)] for pair, e in group]
        scaled = each(lambda v: head_rows(v, score_masks), values)
        scores = each(lambda v, s: dot(v, s, (1, 1)), values, scaled)
        heads_grads = each(lambda g: head_rows(g, ones), cotangents)
        grad_weights = each(lambda v, g: dot(v, g, (1, 1)), values, heads_grads)
        shares = weights_by_key(scores)
        grads = back(values, scaled, cotangents, shares, grad_weights, heads_grads, width)
        for (pair, _), place, grad in zip(group, places, grads):
            start = 0
            for rows in place:
                returned[pair, rows, :] = grad[start : start + rows.size]
                start += rows.size
    for pair in range(pairs):
        mixed_grad[:, pair_columns(pair)] = returned[pair].astype(jnp.bfloat16)


def half_rows(bit, away, count):
    here = lax.bitwise_and(lax.shift_right_logical(lax.axis_index("shard"), bit), 1)
    return pl.ds(pl.multiple_of(lax.bitwise_xor(here, away) * count, count), count)


def spatial_back_kernel(width, embedded, weights, mixed_grad, input_grad, *refs):
    electrode_grads, (sums, received) = refs[:-2], refs[-2:]
    patches, slots, model = embedded.shape
    pairs = model // LANES
    score_masks = head_masks(width, 0.5 / math.sqrt(width))
    ones = head_masks(width, 1.0)
    totals = [jnp.zeros((slots, LANES), jnp.float32) for _ in range(pairs)]
    for pair in range(pairs):
        received[pair] = mixed_grad[:, pair_columns(pair)].astype(jnp.float32)
    for group in in_groups(pairs, patches, SPATIAL_GROUP):
        cotangents = [
            received[pair, of_patch(p, slots, patches), :].astype(jnp.bfloat16)
            for pair, p in group
        ]
        values = [embedded[p, :, pair_columns(pair)] for pair, p in group]
        shares = [weights[p, pair] for pair, p in group]
        scaled = each(lambda v: head_rows(v, score_masks), values)
        heads_grads = each(lambda g: head_rows(g, ones), cotangents)
        grad_weights = each(lambda v, g: dot(v, g, (1, 1)), values, heads_grads)
        grads = back(values, scaled, cotangents, shares, grad_weights, heads_grads, width)
        for (pair, p), grad in zip(group, grads):
            input_grad[p, :, pair_columns(pair)] = grad.astype(jnp.bfloat16)
            totals[pair] = totals[pair] + grad
    for pair in range(pairs):
        sums[pair] = totals[pair]
        for away, block in enumerate(electrode_grads):
            rows = sums[pair, half_rows(0, away, block.shape[0]), :]
            block[:, pair_columns(pair)] = rows.astype(jnp.bfloat16)


def add(one, other):
    return (one.astype(jnp.float32) + other.astype(jnp.float32)).astype(jnp.bfloat16)


def core_sum_kernel(own, arrived, total):
    total[...] = add(own[...], arrived[...])


def cross_sum_kernel(*refs):
    totals = refs[-1]
    for away in range(totals.shape[0]):
        totals[away] = add(refs[2 * away][...], refs[2 * away + 1][...])


def far_sum_kernel(*refs):
    parts, (total, ordered) = refs[:-2], refs[-2:]
    place = lax.div(lax.axis_index("shard"), PLANE)
    for away, part in enumerate(parts):
        ordered[lax.bitwise_xor(place, away)] = part[...].astype(jnp.float32)
    result = ordered[0]
    for index in range(1, len(parts)):
        result = result + ordered[index]
    total[...] = result.astype(jnp.bfloat16)


def join_kernel(bit, own, arrived, joined):
    for away, block in enumerate((own, arrived)):
        joined[:, half_rows(bit, away, block.shape[1]), :] = block[...]


def table_kernel(groups, *refs):
    layouts, blocks, (table, sources, pieces, sems) = refs[:groups], refs[groups:-4], refs[-4:]
    owner = lax.axis_index("group")
    count, rows, _ = pieces.shape
    slots = sources.shape[1]
    join_kernel(0, *blocks, sources)
    copies = []
    for piece in range(count):
        first = owner * (count * rows) + piece * rows
        template = lax.broadcasted_iota(jnp.int32, (rows, slots), 0) + first
        total = jnp.zeros(pieces.shape[1:], jnp.float32)
        for away in range(groups):
            spread = (template == layouts[away][...]).astype(jnp.float32).astype(jnp.bfloat16)
            total = total + dot(spread, sources[away], (1, 0))
        pieces[piece] = total
        copy = pltpu.make_async_copy(
            pieces.at[piece], table.at[pl.ds(piece * rows, rows)], sems.at[piece]
        )
        copy.start()
        copies.append(copy)
    for copy in copies:
        copy.wait()


VMEM = pl.BlockSpec(memory_space=pltpu.VMEM)
SMEM = pl.BlockSpec(memory_space=pltpu.SMEM)
HBM = pl.BlockSpec(memory_space=pltpu.HBM)
PARAMS = pltpu.CompilerParams(vmem_limit_bytes=32 * 1024 * 1024)
STREAMED = pltpu.CompilerParams(vmem_limit_bytes=56 * 1024 * 1024)


def body(activations, out_grad, embedding, counts, offsets, layout):
    tokens = activations[0]
    local, slots, model = tokens.shape
    groups = lax.axis_size("group")
    parts = lax.axis_size("shard")
    patches = local * parts
    own = slots // parts
    width = model // HEADS
    templates = embedding.shape[0]
    pairs = STEP // LANES
    steps = model // STEP

    layouts = [layout] + [
        lax.ppermute(layout, "group", [(i, (i + away) % groups) for i in range(groups)])
        for away in range(1, groups)
    ]
    order = (2, 1, 0, 3) if patches_first(local) else (2, 0, 1, 3)
    cotangent = jnp.transpose(out_grad[0].reshape(parts, local, own, model), order)
    cotangent = cotangent.reshape(own, patches, model)

    flat = pl.BlockSpec((slots * local, STEP), lambda step: (0, step))
    planes = pl.BlockSpec((local, slots, STEP), lambda step: (0, 0, step))
    squares = pl.BlockSpec((local, pairs, slots, 2 * slots), lambda step: (0, step, 0, 0))
    flat_shape = jax.ShapeDtypeStruct((slots * local, model), jnp.bfloat16)
    plane_shape = jax.ShapeDtypeStruct(tokens.shape, jnp.bfloat16)
    flat_scratch = pltpu.VMEM((pairs, slots * local, LANES), jnp.float32)

    strip = pl.BlockSpec((slots, STEP), lambda step: (0, step))
    rows, mixed = pl.pallas_call(
        functools.partial(spatial_kernel, width),
        grid=(steps,),
        out_shape=(jax.ShapeDtypeStruct((slots, model), jnp.bfloat16), flat_shape),
        in_specs=[SMEM, SMEM, VMEM, pl.BlockSpec((templates, STEP), lambda step: (0, step)), planes],
        out_specs=(strip, flat),
        scratch_shapes=[
            pltpu.VMEM((slots, templates), jnp.bfloat16),
            pltpu.VMEM((slots, 2 * slots), jnp.float32),
            flat_scratch,
        ],
        compiler_params=STREAMED,
        name="spatial",
    )(counts, offsets, layout, embedding, tokens)
    embedded, weights, made = pl.pallas_call(
        functools.partial(weights_kernel, width),
        grid=(steps,),
        out_shape=(
            plane_shape,
            jax.ShapeDtypeStruct((local, model // LANES, slots, 2 * slots), jnp.bfloat16),
            jax.ShapeDtypeStruct((SUBLANES, LANES), jnp.float32),
        ),
        in_specs=[SMEM, SMEM, strip, planes],
        out_specs=(planes, squares, pl.BlockSpec((SUBLANES, LANES), lambda step: (0, 0))),
        scratch_shapes=[pltpu.VMEM((slots, 2 * slots), jnp.float32)],
        compiler_params=STREAMED,
        cost_estimate=pl.CostEstimate(
            flops=4 * local * slots * slots * model, bytes_accessed=6 * tokens.size, transcendentals=0
        ),
        name="weights",
    )(counts, offsets, rows, tokens)

    gathered = lax.all_to_all(mixed, "shard", split_axis=0, concat_axis=0, tiled=True)
    mixed_grad = pl.pallas_call(
        functools.partial(temporal_kernel, width, parts),
        grid=(steps,),
        out_shape=flat_shape,
        in_specs=[flat, pl.BlockSpec((own, patches, STEP), lambda step: (0, 0, step))]
        + [pl.BlockSpec(memory_space=pl.ANY)] * groups,
        out_specs=flat,
        scratch_shapes=[flat_scratch, flat_scratch],
        compiler_params=PARAMS,
        name="temporal",
    )(gathered, cotangent, made, *layouts[1:])

    returned = lax.all_to_all(mixed_grad, "shard", split_axis=0, concat_axis=0, tiled=True)
    half = slots // 2
    input_grad, own_half, other_half = pl.pallas_call(
        functools.partial(spatial_back_kernel, width),
        grid=(steps,),
        out_shape=(plane_shape,) + (jax.ShapeDtypeStruct((half, model), jnp.bfloat16),) * 2,
        in_specs=[planes, squares, flat],
        out_specs=(planes,) + (pl.BlockSpec((half, STEP), lambda step: (0, step)),) * 2,
        scratch_shapes=[pltpu.VMEM((pairs, slots, LANES), jnp.float32), flat_scratch],
        compiler_params=PARAMS,
        name="spatial_back",
    )(embedded, weights, returned)

    far_count = parts // PLANE
    assert parts == far_count * PLANE and parts & (parts - 1) == 0

    def to_partner(array, group_away, shard_away):
        if group_away == 0 and shard_away == 0:
            return array
        pairs_of_devices = [
            (g * parts + i, (g + group_away) % groups * parts + (i ^ shard_away))
            for g in range(groups)
            for i in range(parts)
        ]
        return lax.ppermute(array, ("group", "shard"), pairs_of_devices)

    def summed(kernel, shape, operands, scratch=()):
        return pl.pallas_call(
            kernel,
            out_shape=jax.ShapeDtypeStruct(shape, jnp.bfloat16),
            in_specs=[VMEM] * len(operands),
            out_specs=VMEM,
            scratch_shapes=list(scratch),
            compiler_params=PARAMS,
            name="sums",
        )(*operands)

    halved = summed(core_sum_kernel, (half, model), (own_half, to_partner(other_half, 0, 1)))
    total = summed(
        far_sum_kernel,
        (half, model),
        [to_partner(halved, 0, far * PLANE) for far in reversed(range(far_count))][::-1],
        [pltpu.VMEM((far_count, half, model), jnp.float32)],
    )
    crossed = [
        to_partner(total, away, side) for away in reversed(range(groups)) for side in (2, 0)
    ]
    totals = summed(cross_sum_kernel, (groups, half, model), crossed[::-1])
    table_rows = templates // groups
    table_grad = pl.pallas_call(
        functools.partial(table_kernel, groups),
        out_shape=jax.ShapeDtypeStruct((table_rows, model), jnp.float32),
        in_specs=[VMEM] * (groups + 2),
        out_specs=HBM,
        scratch_shapes=[
            pltpu.VMEM((groups, slots, model), jnp.bfloat16),
            pltpu.VMEM((PIECES, table_rows // PIECES, model), jnp.float32),
            pltpu.SemaphoreType.DMA((PIECES,)),
        ],
        compiler_params=PARAMS,
        name="table",
    )(*layouts, totals, to_partner(totals, 0, 1))
    return (input_grad[None], table_grad)


def solution(mesh):
    placed = (
        P("group", "shard", None, None),
        P("group", None, "shard", None),
        P(),
        P("group", None),
        P("group", None),
        P("group", None),
    )
    return jax.shard_map(
        body,
        mesh=mesh,
        in_specs=placed,
        out_specs=(P("group", "shard", None, None), P("group", None)),
        check_vma=False,
    )
```

```python
import functools
import math

import jax
import jax.numpy as jnp
from jax import lax
from jax.experimental import pallas as pl
from jax.experimental.pallas import tpu as pltpu
from jax.sharding import PartitionSpec as P

HEADS = 16
BLOCK = 32
LANES = 128
MASKED = -1e30
SUBLANES = 8
STEP = 512
PIECES = 8
PLANE = 4
SPATIAL_GROUP = 32
TEMPORAL_GROUP = 8


def dot(left, right, over):
    return lax.dot_general(
        left, right, (((over[0],), (over[1],)), ((), ())), preferred_element_type=jnp.float32
    )


def head_masks(width, scale):
    lane = lax.broadcasted_iota(jnp.int32, (1, LANES), 1)
    first = jnp.where(lane < width, scale, 0.0).astype(jnp.bfloat16)
    second = jnp.where(lane < width, 0.0, scale).astype(jnp.bfloat16)
    return first, second


def head_rows(pair, masks):
    return jnp.concatenate([pair * masks[0], pair * masks[1]], axis=0)


def head_columns(rows, width):
    count = rows.shape[0] // 2
    lane = lax.broadcasted_iota(jnp.int32, (count, rows.shape[1]), 1)
    return jnp.where(lane < width, rows[:count], rows[count:])


def each(function, *lists):
    return [function(*items) for items in zip(*lists)]


def weights_by_key(scores):
    tops = each(lambda s: jnp.max(s, axis=0, keepdims=True), scores)
    exponents = each(lambda s, t: jnp.exp(s - t), scores, tops)
    shares = each(lambda e: 1.0 / jnp.sum(e, axis=0, keepdims=True), exponents)
    return each(lambda e, r: (e * r).astype(jnp.bfloat16), exponents, shares)


def by_query(shares, values, width):
    if 2 * values[0].shape[0] != LANES or len(values) % 2:
        return each(lambda s, v: head_columns(dot(s, v, (0, 0)), width), shares, values)
    results = []
    for first in range(0, len(values), 2):
        turned = jnp.transpose(jnp.concatenate(shares[first : first + 2], axis=0))
        one, other = values[first : first + 2]
        zero = jnp.zeros_like(one)
        apart = jnp.concatenate(
            [jnp.concatenate([one, zero], axis=1), jnp.concatenate([zero, other], axis=1)], axis=0
        )
        both = dot(turned, apart, (1, 0))
        results += [head_columns(both[:, :LANES], width), head_columns(both[:, LANES:], width)]
    return results


def back(values, scaled, cotangents, weights, grad_weights, heads_grads, width):
    wide = each(lambda w: w.astype(jnp.float32), weights)
    deltas = each(lambda w, g: jnp.sum(w * g, axis=0, keepdims=True), wide, grad_weights)
    grad_scores = each(
        lambda w, g, d: (w * (g - d)).astype(jnp.bfloat16), wide, grad_weights, deltas
    )
    length = values[0].shape[0]
    whole = length % LANES == 0
    both_ways = grad_scores
    if whole:
        both_ways = each(
            lambda g: jnp.concatenate(
                [
                    g[:, start : start + length] + jnp.transpose(g[:, start : start + length])
                    for start in (0, length)
                ],
                axis=1,
            ),
            grad_scores,
        )
    grads = each(
        lambda c, w, g, hg, hv: c.astype(jnp.float32)
        + dot(jnp.concatenate([w, g], axis=1), jnp.concatenate([hg, hv], axis=0), (1, 0)),
        cotangents,
        weights,
        both_ways,
        heads_grads,
        scaled,
    )
    if whole:
        return grads
    score_scale = 0.5 / math.sqrt(width)
    rest = by_query(grad_scores, values, width)
    return each(lambda g, r: g + score_scale * r, grads, rest)


def pair_bias(counts, offsets, slots):
    def sessions(slot):
        block = slot // BLOCK
        session = jnp.full(slot.shape, -1, jnp.int32)
        for j in range(offsets.shape[1]):
            session = session + (offsets[0, j] <= block).astype(jnp.int32)
        return session

    key_slot = lax.broadcasted_iota(jnp.int32, (slots, 2 * slots), 0)
    query_slot = lax.broadcasted_iota(jnp.int32, (slots, 2 * slots), 1) % slots
    key_session = sessions(key_slot)
    first = jnp.zeros_like(key_slot)
    live = jnp.zeros_like(key_slot)
    for j in range(offsets.shape[1]):
        chosen = key_session == j
        first = jnp.where(chosen, offsets[0, j] * BLOCK, first)
        live = jnp.where(chosen, counts[0, j], live)
    allowed = (key_session == sessions(query_slot)) & (key_slot - first < live)
    return jnp.where(allowed, 0.0, MASKED)


def pair_columns(pair):
    return pl.ds(pair * LANES, LANES)


def step_columns(pair, width):
    start = pl.program_id(0) * width + pair * LANES
    return pl.ds(pl.multiple_of(start, LANES), LANES)


def in_groups(pairs, rows, size):
    items = [(pair, row) for pair in range(pairs) for row in range(rows)]
    return [items[start : start + size] for start in range(0, len(items), size)]


def of_patch(patch, slots, patches):
    return pl.ds(patch, slots, stride=patches)


def attention(width, tokens, rows, bias, group):
    score_masks = head_masks(width, 0.5 / math.sqrt(width))
    values = [
        (
            tokens[p, :, pair_columns(pair)].astype(jnp.float32)
            + rows[:, pair * LANES : (pair + 1) * LANES]
        ).astype(jnp.bfloat16)
        for pair, p in group
    ]
    scores = each(lambda v: dot(v, head_rows(v, score_masks), (1, 1)) + bias[...], values)
    return values, weights_by_key(scores)


def spatial_kernel(
    width, counts, offsets, layout, embedding, tokens, rows, mixed, spread, bias, by_electrode
):
    patches, slots, model = tokens.shape
    templates = embedding.shape[0]
    pairs = model // LANES

    @pl.when(pl.program_id(0) == 0)
    def _():
        bias[...] = pair_bias(counts, offsets, slots)
        wanted = jnp.broadcast_to(layout[...].astype(jnp.float32), (LANES, slots))
        wanted = jnp.transpose(wanted).astype(jnp.int32)
        template = lax.broadcasted_iota(jnp.int32, (slots, LANES), 1)
        for first in range(0, templates, LANES):
            chosen = wanted == template + first
            spread[:, pl.ds(first, LANES)] = chosen.astype(jnp.float32).astype(jnp.bfloat16)

    chosen_rows = dot(spread[...], embedding[...], (1, 0))
    rows[...] = chosen_rows.astype(jnp.bfloat16)
    for group in in_groups(pairs, patches, SPATIAL_GROUP):
        values, shares = attention(width, tokens, chosen_rows, bias, group)
        attended = by_query(shares, values, width)
        for (pair, p), value, result in zip(group, values, attended):
            by_electrode[pair, of_patch(p, slots, patches), :] = value.astype(jnp.float32) + result
    for pair in range(pairs):
        mixed[:, pair_columns(pair)] = by_electrode[pair].astype(jnp.bfloat16)


def weights_kernel(width, counts, offsets, rows, tokens, embedded, weights, made, bias):
    made[...] = jnp.zeros_like(made)
    patches, slots, model = tokens.shape

    @pl.when(pl.program_id(0) == 0)
    def _():
        bias[...] = pair_bias(counts, offsets, slots)

    added = rows[...].astype(jnp.float32)
    for group in in_groups(model // LANES, patches, SPATIAL_GROUP):
        values, shares = attention(width, tokens, added, bias, group)
        for (pair, p), value, share in zip(group, values, shares):
            embedded[p, :, pair_columns(pair)] = value
            weights[p, pair] = share


def patches_first(local):
    return local % SUBLANES != 0


def electrode_rows(electrode, electrodes, parts, local):
    start, step = electrode * local, electrodes * local
    if patches_first(local):
        return [pl.ds(start + p, parts, stride=step) for p in range(local)]
    return [pl.ds(start + part * step, local) for part in range(parts)]


def temporal_kernel(width, parts, mixed, out_grad, *refs):
    mixed_grad, received, returned = refs[-3:]
    electrodes, patches, _ = out_grad.shape
    model = mixed_grad.shape[1]
    local = patches // parts
    pairs = model // LANES
    score_masks = head_masks(width, 0.5 / math.sqrt(width))
    ones = head_masks(width, 1.0)
    for pair in range(pairs):
        received[pair] = mixed[:, step_columns(pair, model)].astype(jnp.float32)
    for group in in_groups(pairs, electrodes, TEMPORAL_GROUP):
        places = [electrode_rows(e, electrodes, parts, local) for _, e in group]
        values = each(
            lambda item, place: jnp.concatenate(
                [received[item[0], rows, :] for rows in place], axis=0
            ).astype(jnp.bfloat16),
            group,
            places,
        )
        cotangents = [out_grad[e, :, step_columns(pair, model)] for pair, e in group]
        scaled = each(lambda v: head_rows(v, score_masks), values)
        scores = each(lambda v, s: dot(v, s, (1, 1)), values, scaled)
        heads_grads = each(lambda g: head_rows(g, ones), cotangents)
        grad_weights = each(lambda v, g: dot(v, g, (1, 1)), values, heads_grads)
        shares = weights_by_key(scores)
        grads = back(values, scaled, cotangents, shares, grad_weights, heads_grads, width)
        for (pair, _), place, grad in zip(group, places, grads):
            start = 0
            for rows in place:
                returned[pair, rows, :] = grad[start : start + rows.size]
                start += rows.size
    for pair in range(pairs):
        mixed_grad[:, pair_columns(pair)] = returned[pair].astype(jnp.bfloat16)


def half_rows(bit, away, count):
    here = lax.bitwise_and(lax.shift_right_logical(lax.axis_index("shard"), bit), 1)
    return pl.ds(pl.multiple_of(lax.bitwise_xor(here, away) * count, count), count)


def spatial_back_kernel(width, embedded, weights, mixed_grad, input_grad, *refs):
    electrode_grads, (sums, received) = refs[:-2], refs[-2:]
    patches, slots, model = embedded.shape
    pairs = model // LANES
    score_masks = head_masks(width, 0.5 / math.sqrt(width))
    ones = head_masks(width, 1.0)
    totals = [jnp.zeros((slots, LANES), jnp.float32) for _ in range(pairs)]
    for pair in range(pairs):
        received[pair] = mixed_grad[:, step_columns(pair, model)].astype(jnp.float32)
    for group in in_groups(pairs, patches, SPATIAL_GROUP):
        cotangents = [
            received[pair, of_patch(p, slots, patches), :].astype(jnp.bfloat16)
            for pair, p in group
        ]
        values = [embedded[p, :, pair_columns(pair)] for pair, p in group]
        shares = [weights[p, pair] for pair, p in group]
        scaled = each(lambda v: head_rows(v, score_masks), values)
        heads_grads = each(lambda g: head_rows(g, ones), cotangents)
        grad_weights = each(lambda v, g: dot(v, g, (1, 1)), values, heads_grads)
        grads = back(values, scaled, cotangents, shares, grad_weights, heads_grads, width)
        for (pair, p), grad in zip(group, grads):
            input_grad[p, :, pair_columns(pair)] = grad.astype(jnp.bfloat16)
            totals[pair] = totals[pair] + grad
    for pair in range(pairs):
        sums[pair] = totals[pair]
        for away, block in enumerate(electrode_grads):
            rows = sums[pair, half_rows(0, away, block.shape[0]), :]
            block[:, pair_columns(pair)] = rows.astype(jnp.bfloat16)


def add(one, other):
    return (one.astype(jnp.float32) + other.astype(jnp.float32)).astype(jnp.bfloat16)


def core_sum_kernel(own, arrived, total):
    total[...] = add(own[...], arrived[...])


def cross_sum_kernel(*refs):
    totals = refs[-1]
    for away in range(totals.shape[0]):
        totals[away] = add(refs[2 * away][...], refs[2 * away + 1][...])


def far_sum_kernel(*refs):
    parts, (total, ordered) = refs[:-2], refs[-2:]
    place = lax.div(lax.axis_index("shard"), PLANE)
    for away, part in enumerate(parts):
        ordered[lax.bitwise_xor(place, away)] = part[...].astype(jnp.float32)
    result = ordered[0]
    for index in range(1, len(parts)):
        result = result + ordered[index]
    total[...] = result.astype(jnp.bfloat16)


def join_kernel(bit, own, arrived, joined):
    for away, block in enumerate((own, arrived)):
        joined[:, half_rows(bit, away, block.shape[1]), :] = block[...]


def table_kernel(groups, *refs):
    layouts, blocks, (table, sources, pieces, sems) = refs[:groups], refs[groups:-4], refs[-4:]
    owner = lax.axis_index("group")
    count, rows, _ = pieces.shape
    slots = sources.shape[1]
    join_kernel(0, *blocks, sources)
    copies = []
    for piece in range(count):
        first = owner * (count * rows) + piece * rows
        template = lax.broadcasted_iota(jnp.int32, (rows, slots), 0) + first
        total = jnp.zeros(pieces.shape[1:], jnp.float32)
        for away in range(groups):
            spread = (template == layouts[away][...]).astype(jnp.float32).astype(jnp.bfloat16)
            total = total + dot(spread, sources[away], (1, 0))
        pieces[piece] = total
        copy = pltpu.make_async_copy(
            pieces.at[piece], table.at[pl.ds(piece * rows, rows)], sems.at[piece]
        )
        copy.start()
        copies.append(copy)
    for copy in copies:
        copy.wait()


VMEM = pl.BlockSpec(memory_space=pltpu.VMEM)
SMEM = pl.BlockSpec(memory_space=pltpu.SMEM)
HBM = pl.BlockSpec(memory_space=pltpu.HBM)
PARAMS = pltpu.CompilerParams(vmem_limit_bytes=32 * 1024 * 1024)
STREAMED = pltpu.CompilerParams(vmem_limit_bytes=56 * 1024 * 1024)


def body(activations, out_grad, embedding, counts, offsets, layout):
    tokens = activations[0]
    local, slots, model = tokens.shape
    groups = lax.axis_size("group")
    parts = lax.axis_size("shard")
    patches = local * parts
    own = slots // parts
    width = model // HEADS
    templates = embedding.shape[0]
    pairs = STEP // LANES
    steps = model // STEP

    layouts = [layout] + [
        lax.ppermute(layout, "group", [(i, (i + away) % groups) for i in range(groups)])
        for away in range(1, groups)
    ]
    order = (2, 1, 0, 3) if patches_first(local) else (2, 0, 1, 3)
    cotangent = jnp.transpose(out_grad[0].reshape(parts, local, own, model), order)
    cotangent = cotangent.reshape(own, patches, model)

    flat = pl.BlockSpec((slots * local, STEP), lambda step: (0, step))
    planes = pl.BlockSpec((local, slots, STEP), lambda step: (0, 0, step))
    squares = pl.BlockSpec((local, pairs, slots, 2 * slots), lambda step: (0, step, 0, 0))
    flat_shape = jax.ShapeDtypeStruct((slots * local, model), jnp.bfloat16)
    plane_shape = jax.ShapeDtypeStruct(tokens.shape, jnp.bfloat16)
    flat_scratch = pltpu.VMEM((pairs, slots * local, LANES), jnp.float32)

    strip = pl.BlockSpec((slots, STEP), lambda step: (0, step))
    rows, mixed = pl.pallas_call(
        functools.partial(spatial_kernel, width),
        grid=(steps,),
        out_shape=(jax.ShapeDtypeStruct((slots, model), jnp.bfloat16), flat_shape),
        in_specs=[SMEM, SMEM, VMEM, pl.BlockSpec((templates, STEP), lambda step: (0, step)), planes],
        out_specs=(strip, flat),
        scratch_shapes=[
            pltpu.VMEM((slots, templates), jnp.bfloat16),
            pltpu.VMEM((slots, 2 * slots), jnp.float32),
            flat_scratch,
        ],
        compiler_params=STREAMED,
        name="spatial",
    )(counts, offsets, layout, embedding, tokens)
    embedded, weights, made = pl.pallas_call(
        functools.partial(weights_kernel, width),
        grid=(steps,),
        out_shape=(
            plane_shape,
            jax.ShapeDtypeStruct((local, model // LANES, slots, 2 * slots), jnp.bfloat16),
            jax.ShapeDtypeStruct((SUBLANES, LANES), jnp.float32),
        ),
        in_specs=[SMEM, SMEM, strip, planes],
        out_specs=(planes, squares, pl.BlockSpec((SUBLANES, LANES), lambda step: (0, 0))),
        scratch_shapes=[pltpu.VMEM((slots, 2 * slots), jnp.float32)],
        compiler_params=STREAMED,
        cost_estimate=pl.CostEstimate(
            flops=4 * local * slots * slots * model, bytes_accessed=6 * tokens.size, transcendentals=0
        ),
        name="weights",
    )(counts, offsets, rows, tokens)

    gathered = lax.all_to_all(mixed, "shard", split_axis=0, concat_axis=0, tiled=True)
    mixed_grad = pl.pallas_call(
        functools.partial(temporal_kernel, width, parts),
        grid=(steps,),
        out_shape=flat_shape,
        in_specs=[VMEM, VMEM]
        + [pl.BlockSpec(memory_space=pl.ANY)] * groups,
        out_specs=flat,
        scratch_shapes=[flat_scratch, flat_scratch],
        compiler_params=PARAMS,
        name="temporal",
    )(gathered, cotangent, made, *layouts[1:])

    returned = lax.all_to_all(mixed_grad, "shard", split_axis=0, concat_axis=0, tiled=True)
    half = slots // 2
    input_grad, own_half, other_half = pl.pallas_call(
        functools.partial(spatial_back_kernel, width),
        grid=(steps,),
        out_shape=(plane_shape,) + (jax.ShapeDtypeStruct((half, model), jnp.bfloat16),) * 2,
        in_specs=[planes, squares, VMEM],
        out_specs=(planes,) + (pl.BlockSpec((half, STEP), lambda step: (0, step)),) * 2,
        scratch_shapes=[pltpu.VMEM((pairs, slots, LANES), jnp.float32), flat_scratch],
        compiler_params=PARAMS,
        name="spatial_back",
    )(embedded, weights, returned)

    far_count = parts // PLANE
    assert parts == far_count * PLANE and parts & (parts - 1) == 0

    def to_partner(array, group_away, shard_away):
        if group_away == 0 and shard_away == 0:
            return array
        pairs_of_devices = [
            (g * parts + i, (g + group_away) % groups * parts + (i ^ shard_away))
            for g in range(groups)
            for i in range(parts)
        ]
        return lax.ppermute(array, ("group", "shard"), pairs_of_devices)

    def summed(kernel, shape, operands, scratch=()):
        return pl.pallas_call(
            kernel,
            out_shape=jax.ShapeDtypeStruct(shape, jnp.bfloat16),
            in_specs=[VMEM] * len(operands),
            out_specs=VMEM,
            scratch_shapes=list(scratch),
            compiler_params=PARAMS,
            name="sums",
        )(*operands)

    halved = summed(core_sum_kernel, (half, model), (own_half, to_partner(other_half, 0, 1)))
    total = summed(
        far_sum_kernel,
        (half, model),
        [to_partner(halved, 0, far * PLANE) for far in reversed(range(far_count))][::-1],
        [pltpu.VMEM((far_count, half, model), jnp.float32)],
    )
    crossed = [
        to_partner(total, away, side) for away in reversed(range(groups)) for side in (2, 0)
    ]
    totals = summed(cross_sum_kernel, (groups, half, model), crossed[::-1])
    table_rows = templates // groups
    table_grad = pl.pallas_call(
        functools.partial(table_kernel, groups),
        out_shape=jax.ShapeDtypeStruct((table_rows, model), jnp.float32),
        in_specs=[VMEM] * (groups + 2),
        out_specs=HBM,
        scratch_shapes=[
            pltpu.VMEM((groups, slots, model), jnp.bfloat16),
            pltpu.VMEM((PIECES, table_rows // PIECES, model), jnp.float32),
            pltpu.SemaphoreType.DMA((PIECES,)),
        ],
        compiler_params=PARAMS,
        name="table",
    )(*layouts, totals, to_partner(totals, 0, 1))
    return (input_grad[None], table_grad)


def solution(mesh):
    placed = (
        P("group", "shard", None, None),
        P("group", None, "shard", None),
        P(),
        P("group", None),
        P("group", None),
        P("group", None),
    )
    return jax.shard_map(
        body,
        mesh=mesh,
        in_specs=placed,
        out_specs=(P("group", "shard", None, None), P("group", None)),
        check_vma=False,
    )
```

```python
import functools
import math

import jax
import jax.numpy as jnp
from jax import lax
from jax.experimental import pallas as pl
from jax.experimental.pallas import tpu as pltpu
from jax.sharding import PartitionSpec as P

HEADS = 16
BLOCK = 32
LANES = 128
MASKED = -1e30
SUBLANES = 8
STEP = 512
PIECES = 8
PIECE = 256
AHEAD = 2
PLANE = 4
SPATIAL_GROUP = 32
TEMPORAL_GROUP = 8


def dot(left, right, over):
    return lax.dot_general(
        left, right, (((over[0],), (over[1],)), ((), ())), preferred_element_type=jnp.float32
    )


def head_masks(width, scale):
    lane = lax.broadcasted_iota(jnp.int32, (1, LANES), 1)
    first = jnp.where(lane < width, scale, 0.0).astype(jnp.bfloat16)
    second = jnp.where(lane < width, 0.0, scale).astype(jnp.bfloat16)
    return first, second


def head_rows(pair, masks):
    return jnp.concatenate([pair * masks[0], pair * masks[1]], axis=0)


def head_columns(rows, width):
    count = rows.shape[0] // 2
    lane = lax.broadcasted_iota(jnp.int32, (count, rows.shape[1]), 1)
    return jnp.where(lane < width, rows[:count], rows[count:])


def each(function, *lists):
    return [function(*items) for items in zip(*lists)]


def weights_by_key(scores):
    tops = each(lambda s: jnp.max(s, axis=0, keepdims=True), scores)
    exponents = each(lambda s, t: jnp.exp(s - t), scores, tops)
    shares = each(lambda e: 1.0 / jnp.sum(e, axis=0, keepdims=True), exponents)
    return each(lambda e, r: (e * r).astype(jnp.bfloat16), exponents, shares)


def by_query(shares, values, width):
    if 2 * values[0].shape[0] != LANES or len(values) % 2:
        return each(lambda s, v: head_columns(dot(s, v, (0, 0)), width), shares, values)
    results = []
    for first in range(0, len(values), 2):
        turned = jnp.transpose(jnp.concatenate(shares[first : first + 2], axis=0))
        one, other = values[first : first + 2]
        zero = jnp.zeros_like(one)
        apart = jnp.concatenate(
            [jnp.concatenate([one, zero], axis=1), jnp.concatenate([zero, other], axis=1)], axis=0
        )
        both = dot(turned, apart, (1, 0))
        results += [head_columns(both[:, :LANES], width), head_columns(both[:, LANES:], width)]
    return results


def back(values, scaled, cotangents, weights, grad_weights, heads_grads, width):
    wide = each(lambda w: w.astype(jnp.float32), weights)
    deltas = each(lambda w, g: jnp.sum(w * g, axis=0, keepdims=True), wide, grad_weights)
    grad_scores = each(
        lambda w, g, d: (w * (g - d)).astype(jnp.bfloat16), wide, grad_weights, deltas
    )
    length = values[0].shape[0]
    whole = length % LANES == 0
    both_ways = grad_scores
    if whole:
        both_ways = each(
            lambda g: jnp.concatenate(
                [
                    g[:, start : start + length] + jnp.transpose(g[:, start : start + length])
                    for start in (0, length)
                ],
                axis=1,
            ),
            grad_scores,
        )
    grads = each(
        lambda c, w, g, hg, hv: c.astype(jnp.float32)
        + dot(jnp.concatenate([w, g], axis=1), jnp.concatenate([hg, hv], axis=0), (1, 0)),
        cotangents,
        weights,
        both_ways,
        heads_grads,
        scaled,
    )
    if whole:
        return grads
    score_scale = 0.5 / math.sqrt(width)
    rest = by_query(grad_scores, values, width)
    return each(lambda g, r: g + score_scale * r, grads, rest)


def pair_bias(counts, offsets, slots):
    def sessions(slot):
        block = slot // BLOCK
        session = jnp.full(slot.shape, -1, jnp.int32)
        for j in range(offsets.shape[1]):
            session = session + (offsets[0, j] <= block).astype(jnp.int32)
        return session

    key_slot = lax.broadcasted_iota(jnp.int32, (slots, 2 * slots), 0)
    query_slot = lax.broadcasted_iota(jnp.int32, (slots, 2 * slots), 1) % slots
    key_session = sessions(key_slot)
    first = jnp.zeros_like(key_slot)
    live = jnp.zeros_like(key_slot)
    for j in range(offsets.shape[1]):
        chosen = key_session == j
        first = jnp.where(chosen, offsets[0, j] * BLOCK, first)
        live = jnp.where(chosen, counts[0, j], live)
    allowed = (key_session == sessions(query_slot)) & (key_slot - first < live)
    return jnp.where(allowed, 0.0, MASKED)


def pair_columns(pair):
    return pl.ds(pair * LANES, LANES)


def step_columns(pair, width):
    start = pl.program_id(0) * width + pair * LANES
    return pl.ds(pl.multiple_of(start, LANES), LANES)


def in_groups(pairs, rows, size):
    items = [(pair, row) for pair in range(pairs) for row in range(rows)]
    return [items[start : start + size] for start in range(0, len(items), size)]


def of_patch(patch, slots, patches):
    return pl.ds(patch, slots, stride=patches)


def attention(width, tokens, rows, bias, group):
    score_masks = head_masks(width, 0.5 / math.sqrt(width))
    values = [
        (
            tokens[p, :, pair_columns(pair)].astype(jnp.float32)
            + rows[:, pair * LANES : (pair + 1) * LANES]
        ).astype(jnp.bfloat16)
        for pair, p in group
    ]
    scores = each(lambda v: dot(v, head_rows(v, score_masks), (1, 1)) + bias[...], values)
    return values, weights_by_key(scores)


def spatial_kernel(
    width, counts, offsets, layout, all_embedding, all_tokens, all_rows, all_mixed,
    spread, bias, by_electrode, embedding, tokens, rows, mixed, fetch_sems, write_sems,
):
    pieces, patches, slots, model = tokens.shape
    templates = embedding.shape[1]
    pairs = model // LANES

    def fetches(at):
        columns = pl.ds(at * model, model)
        return (
            pltpu.make_async_copy(
                all_tokens.at[:, :, columns], tokens.at[at], fetch_sems.at[at, 0]
            ),
            pltpu.make_async_copy(
                all_embedding.at[:, columns], embedding.at[at], fetch_sems.at[at, 1]
            ),
        )

    def writes(at):
        columns = pl.ds(at * model, model)
        return (
            pltpu.make_async_copy(rows.at[at], all_rows.at[:, columns], write_sems.at[at, 0]),
            pltpu.make_async_copy(mixed.at[at], all_mixed.at[:, columns], write_sems.at[at, 1]),
        )

    for at in range(min(AHEAD, pieces)):
        for copy in fetches(at):
            copy.start()
    bias[...] = pair_bias(counts, offsets, slots)
    wanted = jnp.broadcast_to(layout[...].astype(jnp.float32), (LANES, slots))
    wanted = jnp.transpose(wanted).astype(jnp.int32)
    template = lax.broadcasted_iota(jnp.int32, (slots, LANES), 1)
    for first in range(0, templates, LANES):
        chosen = wanted == template + first
        spread[:, pl.ds(first, LANES)] = chosen.astype(jnp.float32).astype(jnp.bfloat16)

    for at in range(pieces):
        for copy in fetches(at):
            copy.wait()
        if at + AHEAD < pieces:
            for copy in fetches(at + AHEAD):
                copy.start()
        chosen_rows = dot(spread[...], embedding[at], (1, 0))
        rows[at] = chosen_rows.astype(jnp.bfloat16)
        for group in in_groups(pairs, patches, SPATIAL_GROUP):
            values, shares = attention(width, tokens.at[at], chosen_rows, bias, group)
            attended = by_query(shares, values, width)
            for (pair, p), value, result in zip(group, values, attended):
                by_electrode[at * pairs + pair, of_patch(p, slots, patches), :] = (
                    value.astype(jnp.float32) + result
                )
        for pair in range(pairs):
            mixed[at, :, pair_columns(pair)] = by_electrode[at * pairs + pair].astype(jnp.bfloat16)
        for copy in writes(at):
            copy.start()
    for at in range(pieces):
        for copy in writes(at):
            copy.wait()


def weights_kernel(width, counts, offsets, rows, tokens, embedded, weights, made, bias):
    made[...] = jnp.zeros_like(made)
    patches, slots, model = tokens.shape

    @pl.when(pl.program_id(0) == 0)
    def _():
        bias[...] = pair_bias(counts, offsets, slots)

    added = rows[...].astype(jnp.float32)
    for group in in_groups(model // LANES, patches, SPATIAL_GROUP):
        values, shares = attention(width, tokens, added, bias, group)
        for (pair, p), value, share in zip(group, values, shares):
            embedded[p, :, pair_columns(pair)] = value
            weights[p, pair] = share


def patches_first(local):
    return local % SUBLANES != 0


def electrode_rows(electrode, electrodes, parts, local):
    start, step = electrode * local, electrodes * local
    if patches_first(local):
        return [pl.ds(start + p, parts, stride=step) for p in range(local)]
    return [pl.ds(start + part * step, local) for part in range(parts)]


def temporal_kernel(width, parts, mixed, out_grad, *refs):
    all_mixed_grad, received, returned, mixed_grad, sems = refs[-5:]
    electrodes, patches, _ = out_grad.shape
    pieces, _, model = mixed_grad.shape
    local = patches // parts
    pairs = model // LANES
    score_masks = head_masks(width, 0.5 / math.sqrt(width))
    ones = head_masks(width, 1.0)
    copies = []
    for at in range(pieces):
        first = at * pairs
        for pair in range(first, first + pairs):
            received[pair] = mixed[:, pair_columns(pair)].astype(jnp.float32)
        for group in in_groups(pairs, electrodes, TEMPORAL_GROUP):
            group = [(first + pair, e) for pair, e in group]
            places = [electrode_rows(e, electrodes, parts, local) for _, e in group]
            values = each(
                lambda item, place: jnp.concatenate(
                    [received[item[0], rows, :] for rows in place], axis=0
                ).astype(jnp.bfloat16),
                group,
                places,
            )
            cotangents = [out_grad[e, :, pair_columns(pair)] for pair, e in group]
            scaled = each(lambda v: head_rows(v, score_masks), values)
            scores = each(lambda v, s: dot(v, s, (1, 1)), values, scaled)
            heads_grads = each(lambda g: head_rows(g, ones), cotangents)
            grad_weights = each(lambda v, g: dot(v, g, (1, 1)), values, heads_grads)
            shares = weights_by_key(scores)
            grads = back(values, scaled, cotangents, shares, grad_weights, heads_grads, width)
            for (pair, _), place, grad in zip(group, places, grads):
                start = 0
                for rows in place:
                    returned[pair, rows, :] = grad[start : start + rows.size]
                    start += rows.size
        for pair in range(pairs):
            mixed_grad[at, :, pair_columns(pair)] = returned[first + pair].astype(jnp.bfloat16)
        copy = pltpu.make_async_copy(
            mixed_grad.at[at], all_mixed_grad.at[:, pl.ds(at * model, model)], sems.at[at]
        )
        copy.start()
        copies.append(copy)
    for copy in copies:
        copy.wait()


def half_rows(bit, away, count):
    here = lax.bitwise_and(lax.shift_right_logical(lax.axis_index("shard"), bit), 1)
    return pl.ds(pl.multiple_of(lax.bitwise_xor(here, away) * count, count), count)


def spatial_back_kernel(width, embedded, weights, mixed_grad, input_grad, *refs):
    electrode_grads, (sums, received) = refs[:-2], refs[-2:]
    patches, slots, model = embedded.shape
    pairs = model // LANES
    score_masks = head_masks(width, 0.5 / math.sqrt(width))
    ones = head_masks(width, 1.0)
    totals = [jnp.zeros((slots, LANES), jnp.float32) for _ in range(pairs)]
    for pair in range(pairs):
        received[pair] = mixed_grad[:, step_columns(pair, model)].astype(jnp.float32)
    for group in in_groups(pairs, patches, SPATIAL_GROUP):
        cotangents = [
            received[pair, of_patch(p, slots, patches), :].astype(jnp.bfloat16)
            for pair, p in group
        ]
        values = [embedded[p, :, pair_columns(pair)] for pair, p in group]
        shares = [weights[p, pair] for pair, p in group]
        scaled = each(lambda v: head_rows(v, score_masks), values)
        heads_grads = each(lambda g: head_rows(g, ones), cotangents)
        grad_weights = each(lambda v, g: dot(v, g, (1, 1)), values, heads_grads)
        grads = back(values, scaled, cotangents, shares, grad_weights, heads_grads, width)
        for (pair, p), grad in zip(group, grads):
            input_grad[p, :, pair_columns(pair)] = grad.astype(jnp.bfloat16)
            totals[pair] = totals[pair] + grad
    for pair in range(pairs):
        sums[pair] = totals[pair]
        for away, block in enumerate(electrode_grads):
            rows = sums[pair, half_rows(0, away, block.shape[0]), :]
            block[:, pair_columns(pair)] = rows.astype(jnp.bfloat16)


def add(one, other):
    return (one.astype(jnp.float32) + other.astype(jnp.float32)).astype(jnp.bfloat16)


def core_sum_kernel(own, arrived, total):
    total[...] = add(own[...], arrived[...])


def cross_sum_kernel(*refs):
    totals = refs[-1]
    for away in range(totals.shape[0]):
        totals[away] = add(refs[2 * away][...], refs[2 * away + 1][...])


def far_sum_kernel(*refs):
    parts, (total, ordered) = refs[:-2], refs[-2:]
    place = lax.div(lax.axis_index("shard"), PLANE)
    for away, part in enumerate(parts):
        ordered[lax.bitwise_xor(place, away)] = part[...].astype(jnp.float32)
    result = ordered[0]
    for index in range(1, len(parts)):
        result = result + ordered[index]
    total[...] = result.astype(jnp.bfloat16)


def join_kernel(bit, own, arrived, joined):
    for away, block in enumerate((own, arrived)):
        joined[:, half_rows(bit, away, block.shape[1]), :] = block[...]


def table_kernel(groups, *refs):
    layouts, blocks, (table, sources, pieces, sems) = refs[:groups], refs[groups:-4], refs[-4:]
    owner = lax.axis_index("group")
    count, rows, _ = pieces.shape
    slots = sources.shape[1]
    join_kernel(0, *blocks, sources)
    copies = []
    for piece in range(count):
        first = owner * (count * rows) + piece * rows
        template = lax.broadcasted_iota(jnp.int32, (rows, slots), 0) + first
        total = jnp.zeros(pieces.shape[1:], jnp.float32)
        for away in range(groups):
            spread = (template == layouts[away][...]).astype(jnp.float32).astype(jnp.bfloat16)
            total = total + dot(spread, sources[away], (1, 0))
        pieces[piece] = total
        copy = pltpu.make_async_copy(
            pieces.at[piece], table.at[pl.ds(piece * rows, rows)], sems.at[piece]
        )
        copy.start()
        copies.append(copy)
    for copy in copies:
        copy.wait()


VMEM = pl.BlockSpec(memory_space=pltpu.VMEM)
SMEM = pl.BlockSpec(memory_space=pltpu.SMEM)
HBM = pl.BlockSpec(memory_space=pltpu.HBM)
PARAMS = pltpu.CompilerParams(vmem_limit_bytes=32 * 1024 * 1024)
STREAMED = pltpu.CompilerParams(vmem_limit_bytes=56 * 1024 * 1024)


def body(activations, out_grad, embedding, counts, offsets, layout):
    tokens = activations[0]
    local, slots, model = tokens.shape
    groups = lax.axis_size("group")
    parts = lax.axis_size("shard")
    patches = local * parts
    own = slots // parts
    width = model // HEADS
    templates = embedding.shape[0]
    pairs = STEP // LANES
    steps = model // STEP

    layouts = [layout] + [
        lax.ppermute(layout, "group", [(i, (i + away) % groups) for i in range(groups)])
        for away in range(1, groups)
    ]
    order = (2, 1, 0, 3) if patches_first(local) else (2, 0, 1, 3)
    cotangent = jnp.transpose(out_grad[0].reshape(parts, local, own, model), order)
    cotangent = cotangent.reshape(own, patches, model)

    flat = pl.BlockSpec((slots * local, STEP), lambda step: (0, step))
    planes = pl.BlockSpec((local, slots, STEP), lambda step: (0, 0, step))
    squares = pl.BlockSpec((local, pairs, slots, 2 * slots), lambda step: (0, step, 0, 0))
    flat_shape = jax.ShapeDtypeStruct((slots * local, model), jnp.bfloat16)
    plane_shape = jax.ShapeDtypeStruct(tokens.shape, jnp.bfloat16)
    flat_scratch = pltpu.VMEM((pairs, slots * local, LANES), jnp.float32)

    strip = pl.BlockSpec((slots, STEP), lambda step: (0, step))
    pieces = model // PIECE
    all_pairs = pltpu.VMEM((model // LANES, slots * local, LANES), jnp.float32)
    flat_pieces = pltpu.VMEM((pieces, slots * local, PIECE), jnp.bfloat16)
    rows, mixed = pl.pallas_call(
        functools.partial(spatial_kernel, width),
        out_shape=(jax.ShapeDtypeStruct((slots, model), jnp.bfloat16), flat_shape),
        in_specs=[SMEM, SMEM, VMEM, HBM, HBM],
        out_specs=(HBM, HBM),
        scratch_shapes=[
            pltpu.VMEM((slots, templates), jnp.bfloat16),
            pltpu.VMEM((slots, 2 * slots), jnp.float32),
            all_pairs,
            pltpu.VMEM((pieces, templates, PIECE), jnp.bfloat16),
            pltpu.VMEM((pieces, local, slots, PIECE), jnp.bfloat16),
            pltpu.VMEM((pieces, slots, PIECE), jnp.bfloat16),
            flat_pieces,
            pltpu.SemaphoreType.DMA((pieces, 2)),
            pltpu.SemaphoreType.DMA((pieces, 2)),
        ],
        compiler_params=STREAMED,
        name="spatial",
    )(counts, offsets, layout, embedding, tokens)
    embedded, weights, made = pl.pallas_call(
        functools.partial(weights_kernel, width),
        grid=(steps,),
        out_shape=(
            plane_shape,
            jax.ShapeDtypeStruct((local, model // LANES, slots, 2 * slots), jnp.bfloat16),
            jax.ShapeDtypeStruct((SUBLANES, LANES), jnp.float32),
        ),
        in_specs=[SMEM, SMEM, strip, planes],
        out_specs=(planes, squares, pl.BlockSpec((SUBLANES, LANES), lambda step: (0, 0))),
        scratch_shapes=[pltpu.VMEM((slots, 2 * slots), jnp.float32)],
        compiler_params=STREAMED,
        cost_estimate=pl.CostEstimate(
            flops=4 * local * slots * slots * model, bytes_accessed=6 * tokens.size, transcendentals=0
        ),
        name="weights",
    )(counts, offsets, rows, tokens)

    gathered = lax.all_to_all(mixed, "shard", split_axis=0, concat_axis=0, tiled=True)
    mixed_grad = pl.pallas_call(
        functools.partial(temporal_kernel, width, parts),
        out_shape=flat_shape,
        in_specs=[VMEM, VMEM] + [pl.BlockSpec(memory_space=pl.ANY)] * groups,
        out_specs=HBM,
        scratch_shapes=[all_pairs, all_pairs, flat_pieces, pltpu.SemaphoreType.DMA((pieces,))],
        compiler_params=PARAMS,
        name="temporal",
    )(gathered, cotangent, made, *layouts[1:])

    returned = lax.all_to_all(mixed_grad, "shard", split_axis=0, concat_axis=0, tiled=True)
    half = slots // 2
    input_grad, own_half, other_half = pl.pallas_call(
        functools.partial(spatial_back_kernel, width),
        grid=(steps,),
        out_shape=(plane_shape,) + (jax.ShapeDtypeStruct((half, model), jnp.bfloat16),) * 2,
        in_specs=[planes, squares, VMEM],
        out_specs=(planes,) + (pl.BlockSpec((half, STEP), lambda step: (0, step)),) * 2,
        scratch_shapes=[pltpu.VMEM((pairs, slots, LANES), jnp.float32), flat_scratch],
        compiler_params=PARAMS,
        name="spatial_back",
    )(embedded, weights, returned)

    far_count = parts // PLANE
    assert parts == far_count * PLANE and parts & (parts - 1) == 0

    def to_partner(array, group_away, shard_away):
        if group_away == 0 and shard_away == 0:
            return array
        pairs_of_devices = [
            (g * parts + i, (g + group_away) % groups * parts + (i ^ shard_away))
            for g in range(groups)
            for i in range(parts)
        ]
        return lax.ppermute(array, ("group", "shard"), pairs_of_devices)

    def summed(kernel, shape, operands, scratch=()):
        return pl.pallas_call(
            kernel,
            out_shape=jax.ShapeDtypeStruct(shape, jnp.bfloat16),
            in_specs=[VMEM] * len(operands),
            out_specs=VMEM,
            scratch_shapes=list(scratch),
            compiler_params=PARAMS,
            name="sums",
        )(*operands)

    halved = summed(core_sum_kernel, (half, model), (own_half, to_partner(other_half, 0, 1)))
    total = summed(
        far_sum_kernel,
        (half, model),
        [to_partner(halved, 0, far * PLANE) for far in reversed(range(far_count))][::-1],
        [pltpu.VMEM((far_count, half, model), jnp.float32)],
    )
    crossed = [
        to_partner(total, away, side) for away in reversed(range(groups)) for side in (2, 0)
    ]
    totals = summed(cross_sum_kernel, (groups, half, model), crossed[::-1])
    table_rows = templates // groups
    table_grad = pl.pallas_call(
        functools.partial(table_kernel, groups),
        out_shape=jax.ShapeDtypeStruct((table_rows, model), jnp.float32),
        in_specs=[VMEM] * (groups + 2),
        out_specs=HBM,
        scratch_shapes=[
            pltpu.VMEM((groups, slots, model), jnp.bfloat16),
            pltpu.VMEM((PIECES, table_rows // PIECES, model), jnp.float32),
            pltpu.SemaphoreType.DMA((PIECES,)),
        ],
        compiler_params=PARAMS,
        name="table",
    )(*layouts, totals, to_partner(totals, 0, 1))
    return (input_grad[None], table_grad)


def solution(mesh):
    placed = (
        P("group", "shard", None, None),
        P("group", None, "shard", None),
        P(),
        P("group", None),
        P("group", None),
        P("group", None),
    )
    return jax.shard_map(
        body,
        mesh=mesh,
        in_specs=placed,
        out_specs=(P("group", "shard", None, None), P("group", None)),
        check_vma=False,
    )
```

```python
import functools
import math

import jax
import jax.numpy as jnp
from jax import lax
from jax.experimental import pallas as pl
from jax.experimental.pallas import tpu as pltpu
from jax.sharding import PartitionSpec as P

HEADS = 16
BLOCK = 32
LANES = 128
MASKED = -1e30
SUBLANES = 8
STEP = 512
PIECES = 8
PIECE = 256
PLANE = 4
SPATIAL_GROUP = 32
TEMPORAL_GROUP = 8


def dot(left, right, over):
    return lax.dot_general(
        left, right, (((over[0],), (over[1],)), ((), ())), preferred_element_type=jnp.float32
    )


def head_masks(width, scale):
    lane = lax.broadcasted_iota(jnp.int32, (1, LANES), 1)
    first = jnp.where(lane < width, scale, 0.0).astype(jnp.bfloat16)
    second = jnp.where(lane < width, 0.0, scale).astype(jnp.bfloat16)
    return first, second


def head_rows(pair, masks):
    return jnp.concatenate([pair * masks[0], pair * masks[1]], axis=0)


def head_columns(rows, width):
    count = rows.shape[0] // 2
    lane = lax.broadcasted_iota(jnp.int32, (count, rows.shape[1]), 1)
    return jnp.where(lane < width, rows[:count], rows[count:])


def each(function, *lists):
    return [function(*items) for items in zip(*lists)]


def weights_by_key(scores):
    tops = each(lambda s: jnp.max(s, axis=0, keepdims=True), scores)
    exponents = each(lambda s, t: jnp.exp(s - t), scores, tops)
    shares = each(lambda e: 1.0 / jnp.sum(e, axis=0, keepdims=True), exponents)
    return each(lambda e, r: (e * r).astype(jnp.bfloat16), exponents, shares)


def by_query(shares, values, width):
    if 2 * values[0].shape[0] != LANES or len(values) % 2:
        return each(lambda s, v: head_columns(dot(s, v, (0, 0)), width), shares, values)
    results = []
    for first in range(0, len(values), 2):
        turned = jnp.transpose(jnp.concatenate(shares[first : first + 2], axis=0))
        one, other = values[first : first + 2]
        zero = jnp.zeros_like(one)
        apart = jnp.concatenate(
            [jnp.concatenate([one, zero], axis=1), jnp.concatenate([zero, other], axis=1)], axis=0
        )
        both = dot(turned, apart, (1, 0))
        results += [head_columns(both[:, :LANES], width), head_columns(both[:, LANES:], width)]
    return results


def back(values, scaled, cotangents, weights, grad_weights, heads_grads, width):
    wide = each(lambda w: w.astype(jnp.float32), weights)
    deltas = each(lambda w, g: jnp.sum(w * g, axis=0, keepdims=True), wide, grad_weights)
    grad_scores = each(
        lambda w, g, d: (w * (g - d)).astype(jnp.bfloat16), wide, grad_weights, deltas
    )
    length = values[0].shape[0]
    whole = length % LANES == 0
    both_ways = grad_scores
    if whole:
        both_ways = each(
            lambda g: jnp.concatenate(
                [
                    g[:, start : start + length] + jnp.transpose(g[:, start : start + length])
                    for start in (0, length)
                ],
                axis=1,
            ),
            grad_scores,
        )
    grads = each(
        lambda c, w, g, hg, hv: c.astype(jnp.float32)
        + dot(jnp.concatenate([w, g], axis=1), jnp.concatenate([hg, hv], axis=0), (1, 0)),
        cotangents,
        weights,
        both_ways,
        heads_grads,
        scaled,
    )
    if whole:
        return grads
    score_scale = 0.5 / math.sqrt(width)
    rest = by_query(grad_scores, values, width)
    return each(lambda g, r: g + score_scale * r, grads, rest)


def pair_bias(counts, offsets, slots):
    def sessions(slot):
        block = slot // BLOCK
        session = jnp.full(slot.shape, -1, jnp.int32)
        for j in range(offsets.shape[1]):
            session = session + (offsets[0, j] <= block).astype(jnp.int32)
        return session

    key_slot = lax.broadcasted_iota(jnp.int32, (slots, 2 * slots), 0)
    query_slot = lax.broadcasted_iota(jnp.int32, (slots, 2 * slots), 1) % slots
    key_session = sessions(key_slot)
    first = jnp.zeros_like(key_slot)
    live = jnp.zeros_like(key_slot)
    for j in range(offsets.shape[1]):
        chosen = key_session == j
        first = jnp.where(chosen, offsets[0, j] * BLOCK, first)
        live = jnp.where(chosen, counts[0, j], live)
    allowed = (key_session == sessions(query_slot)) & (key_slot - first < live)
    return jnp.where(allowed, 0.0, MASKED)


def pair_columns(pair):
    return pl.ds(pair * LANES, LANES)


def step_columns(pair, width):
    start = pl.program_id(0) * width + pair * LANES
    return pl.ds(pl.multiple_of(start, LANES), LANES)


def in_groups(pairs, rows, size):
    items = [(pair, row) for pair in range(pairs) for row in range(rows)]
    return [items[start : start + size] for start in range(0, len(items), size)]


def of_patch(patch, slots, patches):
    return pl.ds(patch, slots, stride=patches)


def of_halves(halves, index):
    count = halves[0].shape[0]
    return halves[index // count].at[index % count]


def attention(width, tokens, rows, bias, group):
    score_masks = head_masks(width, 0.5 / math.sqrt(width))
    values = [
        (
            of_halves(tokens, p)[:, pair_columns(pair)].astype(jnp.float32)
            + rows[:, pair * LANES : (pair + 1) * LANES]
        ).astype(jnp.bfloat16)
        for pair, p in group
    ]
    scores = each(lambda v: dot(v, head_rows(v, score_masks), (1, 1)) + bias[...], values)
    return values, weights_by_key(scores)


def spatial_kernel(
    width, counts, offsets, layout, embedding, other_embedding, tokens, other_tokens,
    rows, mixed, spread, bias, by_electrode,
):
    half, slots, model = tokens.shape
    patches, tokens = 2 * half, (tokens, other_tokens)
    templates = 2 * embedding.shape[0]
    pairs = model // LANES

    @pl.when(pl.program_id(0) == 0)
    def _():
        bias[...] = pair_bias(counts, offsets, slots)
        wanted = jnp.broadcast_to(layout[...].astype(jnp.float32), (LANES, slots))
        wanted = jnp.transpose(wanted).astype(jnp.int32)
        template = lax.broadcasted_iota(jnp.int32, (slots, LANES), 1)
        for first in range(0, templates, LANES):
            chosen = wanted == template + first
            spread[:, pl.ds(first, LANES)] = chosen.astype(jnp.float32).astype(jnp.bfloat16)

    chosen_rows = dot(spread[:, : templates // 2], embedding[...], (1, 0))
    chosen_rows = chosen_rows + dot(spread[:, templates // 2 :], other_embedding[...], (1, 0))
    rows[...] = chosen_rows.astype(jnp.bfloat16)
    for group in in_groups(pairs, patches, SPATIAL_GROUP):
        values, shares = attention(width, tokens, chosen_rows, bias, group)
        attended = by_query(shares, values, width)
        for (pair, p), value, result in zip(group, values, attended):
            by_electrode[pair, of_patch(p, slots, patches), :] = value.astype(jnp.float32) + result
    for pair in range(pairs):
        mixed[:, pair_columns(pair)] = by_electrode[pair].astype(jnp.bfloat16)


def weights_kernel(width, counts, offsets, rows, tokens, embedded, weights, made, bias):
    made[...] = jnp.zeros_like(made)
    patches, slots, model = tokens.shape
    tokens = (tokens,)

    @pl.when(pl.program_id(0) == 0)
    def _():
        bias[...] = pair_bias(counts, offsets, slots)

    added = rows[...].astype(jnp.float32)
    for group in in_groups(model // LANES, patches, SPATIAL_GROUP):
        values, shares = attention(width, tokens, added, bias, group)
        for (pair, p), value, share in zip(group, values, shares):
            embedded[p, :, pair_columns(pair)] = value
            weights[p, pair] = share


def patches_first(local):
    return local % SUBLANES != 0


def electrode_rows(electrode, electrodes, parts, local):
    start, step = electrode * local, electrodes * local
    if patches_first(local):
        return [pl.ds(start + p, parts, stride=step) for p in range(local)]
    return [pl.ds(start + part * step, local) for part in range(parts)]


def temporal_kernel(width, parts, mixed, out_grad, *refs):
    all_mixed_grad, received, returned, mixed_grad, sems = refs[-5:]
    electrodes, patches, _ = out_grad.shape
    pieces, _, model = mixed_grad.shape
    local = patches // parts
    pairs = model // LANES
    score_masks = head_masks(width, 0.5 / math.sqrt(width))
    ones = head_masks(width, 1.0)
    copies = []
    for at in range(pieces):
        first = at * pairs
        for pair in range(first, first + pairs):
            received[pair] = mixed[:, pair_columns(pair)].astype(jnp.float32)
        for group in in_groups(pairs, electrodes, TEMPORAL_GROUP):
            group = [(first + pair, e) for pair, e in group]
            places = [electrode_rows(e, electrodes, parts, local) for _, e in group]
            values = each(
                lambda item, place: jnp.concatenate(
                    [received[item[0], rows, :] for rows in place], axis=0
                ).astype(jnp.bfloat16),
                group,
                places,
            )
            cotangents = [out_grad[e, :, pair_columns(pair)] for pair, e in group]
            scaled = each(lambda v: head_rows(v, score_masks), values)
            scores = each(lambda v, s: dot(v, s, (1, 1)), values, scaled)
            heads_grads = each(lambda g: head_rows(g, ones), cotangents)
            grad_weights = each(lambda v, g: dot(v, g, (1, 1)), values, heads_grads)
            shares = weights_by_key(scores)
            grads = back(values, scaled, cotangents, shares, grad_weights, heads_grads, width)
            for (pair, _), place, grad in zip(group, places, grads):
                start = 0
                for rows in place:
                    returned[pair, rows, :] = grad[start : start + rows.size]
                    start += rows.size
        for pair in range(pairs):
            mixed_grad[at, :, pair_columns(pair)] = returned[first + pair].astype(jnp.bfloat16)
    for at in range(pieces):
        copy = pltpu.make_async_copy(
            mixed_grad.at[at], all_mixed_grad.at[:, pl.ds(at * model, model)], sems.at[at]
        )
        copy.start()
        copies.append(copy)
    for copy in copies:
        copy.wait()


def half_rows(bit, away, count):
    here = lax.bitwise_and(lax.shift_right_logical(lax.axis_index("shard"), bit), 1)
    return pl.ds(pl.multiple_of(lax.bitwise_xor(here, away) * count, count), count)


def spatial_back_kernel(
    width, embedded, other_embedded, weights, other_weights, mixed_grad, input_grad, *refs
):
    electrode_grads, (sums, received) = refs[:-2], refs[-2:]
    patches, slots, model = input_grad.shape
    embedded, weights = (embedded, other_embedded), (weights, other_weights)
    pairs = model // LANES
    score_masks = head_masks(width, 0.5 / math.sqrt(width))
    ones = head_masks(width, 1.0)
    totals = [jnp.zeros((slots, LANES), jnp.float32) for _ in range(pairs)]
    for pair in range(pairs):
        received[pair] = mixed_grad[:, step_columns(pair, model)].astype(jnp.float32)
    for group in in_groups(pairs, patches, SPATIAL_GROUP):
        cotangents = [
            received[pair, of_patch(p, slots, patches), :].astype(jnp.bfloat16)
            for pair, p in group
        ]
        values = [of_halves(embedded, p)[:, pair_columns(pair)] for pair, p in group]
        shares = [of_halves(weights, p)[pair] for pair, p in group]
        scaled = each(lambda v: head_rows(v, score_masks), values)
        heads_grads = each(lambda g: head_rows(g, ones), cotangents)
        grad_weights = each(lambda v, g: dot(v, g, (1, 1)), values, heads_grads)
        grads = back(values, scaled, cotangents, shares, grad_weights, heads_grads, width)
        for (pair, p), grad in zip(group, grads):
            input_grad[p, :, pair_columns(pair)] = grad.astype(jnp.bfloat16)
            totals[pair] = totals[pair] + grad
    for pair in range(pairs):
        sums[pair] = totals[pair]
        for away, block in enumerate(electrode_grads):
            rows = sums[pair, half_rows(0, away, block.shape[0]), :]
            block[:, pair_columns(pair)] = rows.astype(jnp.bfloat16)


def add(one, other):
    return (one.astype(jnp.float32) + other.astype(jnp.float32)).astype(jnp.bfloat16)


def core_sum_kernel(own, arrived, total):
    total[...] = add(own[...], arrived[...])


def cross_sum_kernel(*refs):
    totals = refs[-1]
    for away in range(totals.shape[0]):
        totals[away] = add(refs[2 * away][...], refs[2 * away + 1][...])


def far_sum_kernel(*refs):
    parts, (total, ordered) = refs[:-2], refs[-2:]
    place = lax.div(lax.axis_index("shard"), PLANE)
    for away, part in enumerate(parts):
        ordered[lax.bitwise_xor(place, away)] = part[...].astype(jnp.float32)
    result = ordered[0]
    for index in range(1, len(parts)):
        result = result + ordered[index]
    total[...] = result.astype(jnp.bfloat16)


def join_kernel(bit, own, arrived, joined):
    for away, block in enumerate((own, arrived)):
        joined[:, half_rows(bit, away, block.shape[1]), :] = block[...]


def table_kernel(groups, *refs):
    layouts, blocks, (table, sources, pieces, sems) = refs[:groups], refs[groups:-4], refs[-4:]
    owner = lax.axis_index("group")
    count, rows, _ = pieces.shape
    slots = sources.shape[1]
    join_kernel(0, *blocks, sources)
    copies = []
    for piece in range(count):
        first = owner * (count * rows) + piece * rows
        template = lax.broadcasted_iota(jnp.int32, (rows, slots), 0) + first
        total = jnp.zeros(pieces.shape[1:], jnp.float32)
        for away in range(groups):
            spread = (template == layouts[away][...]).astype(jnp.float32).astype(jnp.bfloat16)
            total = total + dot(spread, sources[away], (1, 0))
        pieces[piece] = total
        copy = pltpu.make_async_copy(
            pieces.at[piece], table.at[pl.ds(piece * rows, rows)], sems.at[piece]
        )
        copy.start()
        copies.append(copy)
    for copy in copies:
        copy.wait()


VMEM = pl.BlockSpec(memory_space=pltpu.VMEM)
SMEM = pl.BlockSpec(memory_space=pltpu.SMEM)
HBM = pl.BlockSpec(memory_space=pltpu.HBM)
PARAMS = pltpu.CompilerParams(vmem_limit_bytes=32 * 1024 * 1024)
STREAMED = pltpu.CompilerParams(vmem_limit_bytes=56 * 1024 * 1024)


def body(activations, out_grad, embedding, counts, offsets, layout):
    tokens = activations[0]
    local, slots, model = tokens.shape
    groups = lax.axis_size("group")
    parts = lax.axis_size("shard")
    patches = local * parts
    own = slots // parts
    width = model // HEADS
    templates = embedding.shape[0]
    pairs = STEP // LANES
    steps = model // STEP

    layouts = [layout] + [
        lax.ppermute(layout, "group", [(i, (i + away) % groups) for i in range(groups)])
        for away in range(1, groups)
    ]
    order = (2, 1, 0, 3) if patches_first(local) else (2, 0, 1, 3)
    cotangent = jnp.transpose(out_grad[0].reshape(parts, local, own, model), order)
    cotangent = cotangent.reshape(own, patches, model)

    flat = pl.BlockSpec((slots * local, STEP), lambda step: (0, step))
    planes = pl.BlockSpec((local, slots, STEP), lambda step: (0, 0, step))
    squares = pl.BlockSpec((local, pairs, slots, 2 * slots), lambda step: (0, step, 0, 0))
    flat_shape = jax.ShapeDtypeStruct((slots * local, model), jnp.bfloat16)
    plane_shape = jax.ShapeDtypeStruct(tokens.shape, jnp.bfloat16)
    flat_scratch = pltpu.VMEM((pairs, slots * local, LANES), jnp.float32)

    strip = pl.BlockSpec((slots, STEP), lambda step: (0, step))
    pieces = model // PIECE
    all_pairs = pltpu.VMEM((model // LANES, slots * local, LANES), jnp.float32)
    flat_pieces = pltpu.VMEM((pieces, slots * local, PIECE), jnp.bfloat16)

    def halves_of(shape, axis):
        cut = tuple(size // 2 if place == axis else size for place, size in enumerate(shape[1]))
        return [
            pl.BlockSpec(
                cut,
                lambda step, half=half: tuple(
                    half if place == axis else step if place == shape[0] else 0
                    for place in range(len(cut))
                ),
            )
            for half in range(2)
        ]

    rows, mixed = pl.pallas_call(
        functools.partial(spatial_kernel, width),
        grid=(steps,),
        out_shape=(jax.ShapeDtypeStruct((slots, model), jnp.bfloat16), flat_shape),
        in_specs=[SMEM, SMEM, VMEM]
        + halves_of((1, (templates, STEP)), 0)
        + halves_of((2, (local, slots, STEP)), 0),
        out_specs=(strip, flat),
        scratch_shapes=[
            pltpu.VMEM((slots, templates), jnp.bfloat16),
            pltpu.VMEM((slots, 2 * slots), jnp.float32),
            flat_scratch,
        ],
        compiler_params=STREAMED,
        name="spatial",
    )(counts, offsets, layout, embedding, embedding, tokens, tokens)
    embedded, weights, made = pl.pallas_call(
        functools.partial(weights_kernel, width),
        grid=(steps,),
        out_shape=(
            plane_shape,
            jax.ShapeDtypeStruct((local, model // LANES, slots, 2 * slots), jnp.bfloat16),
            jax.ShapeDtypeStruct((SUBLANES, LANES), jnp.float32),
        ),
        in_specs=[SMEM, SMEM, strip, planes],
        out_specs=(planes, squares, pl.BlockSpec((SUBLANES, LANES), lambda step: (0, 0))),
        scratch_shapes=[pltpu.VMEM((slots, 2 * slots), jnp.float32)],
        compiler_params=STREAMED,
        cost_estimate=pl.CostEstimate(
            flops=4 * local * slots * slots * model, bytes_accessed=6 * tokens.size, transcendentals=0
        ),
        name="weights",
    )(counts, offsets, rows, tokens)

    gathered = lax.all_to_all(mixed, "shard", split_axis=0, concat_axis=0, tiled=True)
    mixed_grad = pl.pallas_call(
        functools.partial(temporal_kernel, width, parts),
        out_shape=flat_shape,
        in_specs=[VMEM, VMEM] + [pl.BlockSpec(memory_space=pl.ANY)] * groups,
        out_specs=HBM,
        scratch_shapes=[all_pairs, all_pairs, flat_pieces, pltpu.SemaphoreType.DMA((pieces,))],
        compiler_params=PARAMS,
        name="temporal",
    )(gathered, cotangent, made, *layouts[1:])

    returned = lax.all_to_all(mixed_grad, "shard", split_axis=0, concat_axis=0, tiled=True)
    half = slots // 2
    input_grad, own_half, other_half = pl.pallas_call(
        functools.partial(spatial_back_kernel, width),
        grid=(steps,),
        out_shape=(plane_shape,) + (jax.ShapeDtypeStruct((half, model), jnp.bfloat16),) * 2,
        in_specs=halves_of((2, (local, slots, STEP)), 0)
        + halves_of((1, (local, pairs, slots, 2 * slots)), 0)
        + [VMEM],
        out_specs=(planes,) + (pl.BlockSpec((half, STEP), lambda step: (0, step)),) * 2,
        scratch_shapes=[pltpu.VMEM((pairs, slots, LANES), jnp.float32), flat_scratch],
        compiler_params=PARAMS,
        name="spatial_back",
    )(embedded, embedded, weights, weights, returned)

    far_count = parts // PLANE
    assert parts == far_count * PLANE and parts & (parts - 1) == 0

    def to_partner(array, group_away, shard_away):
        if group_away == 0 and shard_away == 0:
            return array
        pairs_of_devices = [
            (g * parts + i, (g + group_away) % groups * parts + (i ^ shard_away))
            for g in range(groups)
            for i in range(parts)
        ]
        return lax.ppermute(array, ("group", "shard"), pairs_of_devices)

    def summed(kernel, shape, operands, scratch=()):
        return pl.pallas_call(
            kernel,
            out_shape=jax.ShapeDtypeStruct(shape, jnp.bfloat16),
            in_specs=[VMEM] * len(operands),
            out_specs=VMEM,
            scratch_shapes=list(scratch),
            compiler_params=PARAMS,
            name="sums",
        )(*operands)

    halved = summed(core_sum_kernel, (half, model), (own_half, to_partner(other_half, 0, 1)))
    total = summed(
        far_sum_kernel,
        (half, model),
        [to_partner(halved, 0, far * PLANE) for far in reversed(range(far_count))][::-1],
        [pltpu.VMEM((far_count, half, model), jnp.float32)],
    )
    crossed = [
        to_partner(total, away, side) for away in reversed(range(groups)) for side in (2, 0)
    ]
    totals = summed(cross_sum_kernel, (groups, half, model), crossed[::-1])
    table_rows = templates // groups
    table_grad = pl.pallas_call(
        functools.partial(table_kernel, groups),
        out_shape=jax.ShapeDtypeStruct((table_rows, model), jnp.float32),
        in_specs=[VMEM] * (groups + 2),
        out_specs=HBM,
        scratch_shapes=[
            pltpu.VMEM((groups, slots, model), jnp.bfloat16),
            pltpu.VMEM((PIECES, table_rows // PIECES, model), jnp.float32),
            pltpu.SemaphoreType.DMA((PIECES,)),
        ],
        compiler_params=PARAMS,
        name="table",
    )(*layouts, totals, to_partner(totals, 0, 1))
    return (input_grad[None], table_grad)


def solution(mesh):
    placed = (
        P("group", "shard", None, None),
        P("group", None, "shard", None),
        P(),
        P("group", None),
        P("group", None),
        P("group", None),
    )
    return jax.shard_map(
        body,
        mesh=mesh,
        in_specs=placed,
        out_specs=(P("group", "shard", None, None), P("group", None)),
        check_vma=False,
    )
```

```python
import functools
import math

import jax
import jax.numpy as jnp
from jax import lax
from jax.experimental import pallas as pl
from jax.experimental.pallas import tpu as pltpu
from jax.sharding import PartitionSpec as P

HEADS = 16
BLOCK = 32
LANES = 128
MASKED = -1e30
SUBLANES = 8
STEP = 512
PIECES = 8
PIECE = 256
PLANE = 4
SPATIAL_GROUP = 16
TEMPORAL_GROUP = 4


def dot(left, right, over):
    return lax.dot_general(
        left, right, (((over[0],), (over[1],)), ((), ())), preferred_element_type=jnp.float32
    )


def head_masks(width, scale):
    lane = lax.broadcasted_iota(jnp.int32, (1, LANES), 1)
    first = jnp.where(lane < width, scale, 0.0).astype(jnp.bfloat16)
    second = jnp.where(lane < width, 0.0, scale).astype(jnp.bfloat16)
    return first, second


def head_rows(pair, masks):
    return jnp.concatenate([pair * masks[0], pair * masks[1]], axis=0)


def head_columns(rows, width):
    count = rows.shape[0] // 2
    lane = lax.broadcasted_iota(jnp.int32, (count, rows.shape[1]), 1)
    return jnp.where(lane < width, rows[:count], rows[count:])


def each(function, *lists):
    return [function(*items) for items in zip(*lists)]


def weights_by_key(scores):
    tops = each(lambda s: jnp.max(s, axis=0, keepdims=True), scores)
    exponents = each(lambda s, t: jnp.exp(s - t), scores, tops)
    shares = each(lambda e: 1.0 / jnp.sum(e, axis=0, keepdims=True), exponents)
    return each(lambda e, r: (e * r).astype(jnp.bfloat16), exponents, shares)


def by_query(shares, values, width):
    if 2 * values[0].shape[0] != LANES or len(values) % 2:
        return each(lambda s, v: head_columns(dot(s, v, (0, 0)), width), shares, values)
    results = []
    for first in range(0, len(values), 2):
        turned = jnp.transpose(jnp.concatenate(shares[first : first + 2], axis=0))
        one, other = values[first : first + 2]
        zero = jnp.zeros_like(one)
        apart = jnp.concatenate(
            [jnp.concatenate([one, zero], axis=1), jnp.concatenate([zero, other], axis=1)], axis=0
        )
        both = dot(turned, apart, (1, 0))
        results += [head_columns(both[:, :LANES], width), head_columns(both[:, LANES:], width)]
    return results


def back(values, scaled, cotangents, weights, grad_weights, heads_grads, width):
    wide = each(lambda w: w.astype(jnp.float32), weights)
    deltas = each(lambda w, g: jnp.sum(w * g, axis=0, keepdims=True), wide, grad_weights)
    grad_scores = each(
        lambda w, g, d: (w * (g - d)).astype(jnp.bfloat16), wide, grad_weights, deltas
    )
    length = values[0].shape[0]
    whole = length % LANES == 0
    both_ways = grad_scores
    if whole:
        both_ways = each(
            lambda g: jnp.concatenate(
                [
                    g[:, start : start + length] + jnp.transpose(g[:, start : start + length])
                    for start in (0, length)
                ],
                axis=1,
            ),
            grad_scores,
        )
    grads = each(
        lambda c, w, g, hg, hv: c.astype(jnp.float32)
        + dot(jnp.concatenate([w, g], axis=1), jnp.concatenate([hg, hv], axis=0), (1, 0)),
        cotangents,
        weights,
        both_ways,
        heads_grads,
        scaled,
    )
    if whole:
        return grads
    score_scale = 0.5 / math.sqrt(width)
    rest = by_query(grad_scores, values, width)
    return each(lambda g, r: g + score_scale * r, grads, rest)


def pair_bias(counts, offsets, slots):
    def sessions(slot):
        block = slot // BLOCK
        session = jnp.full(slot.shape, -1, jnp.int32)
        for j in range(offsets.shape[1]):
            session = session + (offsets[0, j] <= block).astype(jnp.int32)
        return session

    key_slot = lax.broadcasted_iota(jnp.int32, (slots, 2 * slots), 0)
    query_slot = lax.broadcasted_iota(jnp.int32, (slots, 2 * slots), 1) % slots
    key_session = sessions(key_slot)
    first = jnp.zeros_like(key_slot)
    live = jnp.zeros_like(key_slot)
    for j in range(offsets.shape[1]):
        chosen = key_session == j
        first = jnp.where(chosen, offsets[0, j] * BLOCK, first)
        live = jnp.where(chosen, counts[0, j], live)
    allowed = (key_session == sessions(query_slot)) & (key_slot - first < live)
    return jnp.where(allowed, 0.0, MASKED)


def pair_columns(pair):
    return pl.ds(pair * LANES, LANES)


def step_columns(pair, width):
    start = pl.program_id(0) * width + pair * LANES
    return pl.ds(pl.multiple_of(start, LANES), LANES)


def in_groups(pairs, rows, size):
    items = [(pair, row) for pair in range(pairs) for row in range(rows)]
    return [items[start : start + size] for start in range(0, len(items), size)]


def of_patch(patch, slots, patches):
    return pl.ds(patch, slots, stride=patches)


def of_halves(halves, index):
    count = halves[0].shape[0]
    return halves[index // count].at[index % count]


def attention(width, tokens, rows, bias, group):
    score_masks = head_masks(width, 0.5 / math.sqrt(width))
    values = [
        (
            of_halves(tokens, p)[:, pair_columns(pair)].astype(jnp.float32)
            + rows[:, pair * LANES : (pair + 1) * LANES]
        ).astype(jnp.bfloat16)
        for pair, p in group
    ]
    scores = each(lambda v: dot(v, head_rows(v, score_masks), (1, 1)) + bias[...], values)
    return values, weights_by_key(scores)


def spatial_kernel(
    width, counts, offsets, layout, embedding, other_embedding, tokens, other_tokens,
    rows, mixed, spread, bias, by_electrode,
):
    half, slots, model = tokens.shape
    patches, tokens = 2 * half, (tokens, other_tokens)
    templates = 2 * embedding.shape[0]
    pairs = model // LANES

    @pl.when(pl.program_id(0) == 0)
    def _():
        bias[...] = pair_bias(counts, offsets, slots)
        wanted = jnp.broadcast_to(layout[...].astype(jnp.float32), (LANES, slots))
        wanted = jnp.transpose(wanted).astype(jnp.int32)
        template = lax.broadcasted_iota(jnp.int32, (slots, LANES), 1)
        for first in range(0, templates, LANES):
            chosen = wanted == template + first
            spread[:, pl.ds(first, LANES)] = chosen.astype(jnp.float32).astype(jnp.bfloat16)

    chosen_rows = dot(spread[:, : templates // 2], embedding[...], (1, 0))
    chosen_rows = chosen_rows + dot(spread[:, templates // 2 :], other_embedding[...], (1, 0))
    rows[...] = chosen_rows.astype(jnp.bfloat16)
    for group in in_groups(pairs, patches, SPATIAL_GROUP):
        values, shares = attention(width, tokens, chosen_rows, bias, group)
        attended = by_query(shares, values, width)
        for (pair, p), value, result in zip(group, values, attended):
            by_electrode[pair, of_patch(p, slots, patches), :] = value.astype(jnp.float32) + result
    for pair in range(pairs):
        mixed[:, pair_columns(pair)] = by_electrode[pair].astype(jnp.bfloat16)


def weights_kernel(width, counts, offsets, rows, tokens, embedded, weights, made, bias):
    made[...] = jnp.zeros_like(made)
    patches, slots, model = tokens.shape
    tokens = (tokens,)

    @pl.when(pl.program_id(0) == 0)
    def _():
        bias[...] = pair_bias(counts, offsets, slots)

    added = rows[...].astype(jnp.float32)
    for group in in_groups(model // LANES, patches, SPATIAL_GROUP):
        values, shares = attention(width, tokens, added, bias, group)
        for (pair, p), value, share in zip(group, values, shares):
            embedded[p, :, pair_columns(pair)] = value
            weights[p, pair] = share


def patches_first(local):
    return local % SUBLANES != 0


def electrode_rows(electrode, electrodes, parts, local):
    start, step = electrode * local, electrodes * local
    if patches_first(local):
        return [pl.ds(start + p, parts, stride=step) for p in range(local)]
    return [pl.ds(start + part * step, local) for part in range(parts)]


def temporal_kernel(width, parts, mixed, out_grad, *refs):
    all_mixed_grad, received, returned, mixed_grad, sems = refs[-5:]
    electrodes, patches, _ = out_grad.shape
    pieces, _, model = mixed_grad.shape
    local = patches // parts
    pairs = model // LANES
    score_masks = head_masks(width, 0.5 / math.sqrt(width))
    ones = head_masks(width, 1.0)
    copies = []
    for at in range(pieces):
        first = at * pairs
        for pair in range(first, first + pairs):
            received[pair] = mixed[:, pair_columns(pair)].astype(jnp.float32)
        for group in in_groups(pairs, electrodes, TEMPORAL_GROUP):
            group = [(first + pair, e) for pair, e in group]
            places = [electrode_rows(e, electrodes, parts, local) for _, e in group]
            values = each(
                lambda item, place: jnp.concatenate(
                    [received[item[0], rows, :] for rows in place], axis=0
                ).astype(jnp.bfloat16),
                group,
                places,
            )
            cotangents = [out_grad[e, :, pair_columns(pair)] for pair, e in group]
            scaled = each(lambda v: head_rows(v, score_masks), values)
            scores = each(lambda v, s: dot(v, s, (1, 1)), values, scaled)
            heads_grads = each(lambda g: head_rows(g, ones), cotangents)
            grad_weights = each(lambda v, g: dot(v, g, (1, 1)), values, heads_grads)
            shares = weights_by_key(scores)
            grads = back(values, scaled, cotangents, shares, grad_weights, heads_grads, width)
            for (pair, _), place, grad in zip(group, places, grads):
                start = 0
                for rows in place:
                    returned[pair, rows, :] = grad[start : start + rows.size]
                    start += rows.size
        for pair in range(pairs):
            mixed_grad[at, :, pair_columns(pair)] = returned[first + pair].astype(jnp.bfloat16)
    for at in range(pieces):
        copy = pltpu.make_async_copy(
            mixed_grad.at[at], all_mixed_grad.at[:, pl.ds(at * model, model)], sems.at[at]
        )
        copy.start()
        copies.append(copy)
    for copy in copies:
        copy.wait()


def half_rows(bit, away, count):
    here = lax.bitwise_and(lax.shift_right_logical(lax.axis_index("shard"), bit), 1)
    return pl.ds(pl.multiple_of(lax.bitwise_xor(here, away) * count, count), count)


def spatial_back_kernel(
    width, embedded, other_embedded, weights, other_weights, mixed_grad, input_grad, *refs
):
    electrode_grads, (sums, received) = refs[:-2], refs[-2:]
    patches, slots, model = input_grad.shape
    embedded, weights = (embedded, other_embedded), (weights, other_weights)
    pairs = model // LANES
    score_masks = head_masks(width, 0.5 / math.sqrt(width))
    ones = head_masks(width, 1.0)
    totals = [jnp.zeros((slots, LANES), jnp.float32) for _ in range(pairs)]
    for pair in range(pairs):
        received[pair] = mixed_grad[:, step_columns(pair, model)].astype(jnp.float32)
    for group in in_groups(pairs, patches, SPATIAL_GROUP):
        cotangents = [
            received[pair, of_patch(p, slots, patches), :].astype(jnp.bfloat16)
            for pair, p in group
        ]
        values = [of_halves(embedded, p)[:, pair_columns(pair)] for pair, p in group]
        shares = [of_halves(weights, p)[pair] for pair, p in group]
        scaled = each(lambda v: head_rows(v, score_masks), values)
        heads_grads = each(lambda g: head_rows(g, ones), cotangents)
        grad_weights = each(lambda v, g: dot(v, g, (1, 1)), values, heads_grads)
        grads = back(values, scaled, cotangents, shares, grad_weights, heads_grads, width)
        for (pair, p), grad in zip(group, grads):
            input_grad[p, :, pair_columns(pair)] = grad.astype(jnp.bfloat16)
            totals[pair] = totals[pair] + grad
    for pair in range(pairs):
        sums[pair] = totals[pair]
        for away, block in enumerate(electrode_grads):
            rows = sums[pair, half_rows(0, away, block.shape[0]), :]
            block[:, pair_columns(pair)] = rows.astype(jnp.bfloat16)


def add(one, other):
    return (one.astype(jnp.float32) + other.astype(jnp.float32)).astype(jnp.bfloat16)


def core_sum_kernel(own, arrived, total):
    total[...] = add(own[...], arrived[...])


def cross_sum_kernel(*refs):
    totals = refs[-1]
    for away in range(totals.shape[0]):
        totals[away] = add(refs[2 * away][...], refs[2 * away + 1][...])


def far_sum_kernel(*refs):
    parts, (total, ordered) = refs[:-2], refs[-2:]
    place = lax.div(lax.axis_index("shard"), PLANE)
    for away, part in enumerate(parts):
        ordered[lax.bitwise_xor(place, away)] = part[...].astype(jnp.float32)
    result = ordered[0]
    for index in range(1, len(parts)):
        result = result + ordered[index]
    total[...] = result.astype(jnp.bfloat16)


def join_kernel(bit, own, arrived, joined):
    for away, block in enumerate((own, arrived)):
        joined[:, half_rows(bit, away, block.shape[1]), :] = block[...]


def table_kernel(groups, *refs):
    layouts, blocks, (table, sources, pieces, sems) = refs[:groups], refs[groups:-4], refs[-4:]
    owner = lax.axis_index("group")
    count, rows, _ = pieces.shape
    slots = sources.shape[1]
    join_kernel(0, *blocks, sources)
    copies = []
    for piece in range(count):
        first = owner * (count * rows) + piece * rows
        template = lax.broadcasted_iota(jnp.int32, (rows, slots), 0) + first
        total = jnp.zeros(pieces.shape[1:], jnp.float32)
        for away in range(groups):
            spread = (template == layouts[away][...]).astype(jnp.float32).astype(jnp.bfloat16)
            total = total + dot(spread, sources[away], (1, 0))
        pieces[piece] = total
        copy = pltpu.make_async_copy(
            pieces.at[piece], table.at[pl.ds(piece * rows, rows)], sems.at[piece]
        )
        copy.start()
        copies.append(copy)
    for copy in copies:
        copy.wait()


VMEM = pl.BlockSpec(memory_space=pltpu.VMEM)
SMEM = pl.BlockSpec(memory_space=pltpu.SMEM)
HBM = pl.BlockSpec(memory_space=pltpu.HBM)
PARAMS = pltpu.CompilerParams(vmem_limit_bytes=32 * 1024 * 1024)
STREAMED = pltpu.CompilerParams(vmem_limit_bytes=56 * 1024 * 1024)


def body(activations, out_grad, embedding, counts, offsets, layout):
    tokens = activations[0]
    local, slots, model = tokens.shape
    groups = lax.axis_size("group")
    parts = lax.axis_size("shard")
    patches = local * parts
    own = slots // parts
    width = model // HEADS
    templates = embedding.shape[0]
    pairs = STEP // LANES
    steps = model // STEP

    layouts = [layout] + [
        lax.ppermute(layout, "group", [(i, (i + away) % groups) for i in range(groups)])
        for away in range(1, groups)
    ]
    order = (2, 1, 0, 3) if patches_first(local) else (2, 0, 1, 3)
    cotangent = jnp.transpose(out_grad[0].reshape(parts, local, own, model), order)
    cotangent = cotangent.reshape(own, patches, model)

    flat = pl.BlockSpec((slots * local, STEP), lambda step: (0, step))
    planes = pl.BlockSpec((local, slots, STEP), lambda step: (0, 0, step))
    squares = pl.BlockSpec((local, pairs, slots, 2 * slots), lambda step: (0, step, 0, 0))
    flat_shape = jax.ShapeDtypeStruct((slots * local, model), jnp.bfloat16)
    plane_shape = jax.ShapeDtypeStruct(tokens.shape, jnp.bfloat16)
    flat_scratch = pltpu.VMEM((pairs, slots * local, LANES), jnp.float32)

    strip = pl.BlockSpec((slots, STEP), lambda step: (0, step))
    pieces = model // PIECE
    all_pairs = pltpu.VMEM((model // LANES, slots * local, LANES), jnp.float32)
    flat_pieces = pltpu.VMEM((pieces, slots * local, PIECE), jnp.bfloat16)

    def halves_of(shape, axis):
        cut = tuple(size // 2 if place == axis else size for place, size in enumerate(shape[1]))
        return [
            pl.BlockSpec(
                cut,
                lambda step, half=half: tuple(
                    half if place == axis else step if place == shape[0] else 0
                    for place in range(len(cut))
                ),
            )
            for half in range(2)
        ]

    rows, mixed = pl.pallas_call(
        functools.partial(spatial_kernel, width),
        grid=(steps,),
        out_shape=(jax.ShapeDtypeStruct((slots, model), jnp.bfloat16), flat_shape),
        in_specs=[SMEM, SMEM, VMEM]
        + halves_of((1, (templates, STEP)), 0)
        + halves_of((2, (local, slots, STEP)), 0),
        out_specs=(strip, flat),
        scratch_shapes=[
            pltpu.VMEM((slots, templates), jnp.bfloat16),
            pltpu.VMEM((slots, 2 * slots), jnp.float32),
            flat_scratch,
        ],
        compiler_params=STREAMED,
        name="spatial",
    )(counts, offsets, layout, embedding, embedding, tokens, tokens)
    embedded, weights, made = pl.pallas_call(
        functools.partial(weights_kernel, width),
        grid=(steps,),
        out_shape=(
            plane_shape,
            jax.ShapeDtypeStruct((local, model // LANES, slots, 2 * slots), jnp.bfloat16),
            jax.ShapeDtypeStruct((SUBLANES, LANES), jnp.float32),
        ),
        in_specs=[SMEM, SMEM, strip, planes],
        out_specs=(planes, squares, pl.BlockSpec((SUBLANES, LANES), lambda step: (0, 0))),
        scratch_shapes=[pltpu.VMEM((slots, 2 * slots), jnp.float32)],
        compiler_params=STREAMED,
        cost_estimate=pl.CostEstimate(
            flops=4 * local * slots * slots * model, bytes_accessed=6 * tokens.size, transcendentals=0
        ),
        name="weights",
    )(counts, offsets, rows, tokens)

    gathered = lax.all_to_all(mixed, "shard", split_axis=0, concat_axis=0, tiled=True)
    mixed_grad = pl.pallas_call(
        functools.partial(temporal_kernel, width, parts),
        out_shape=flat_shape,
        in_specs=[VMEM, VMEM] + [pl.BlockSpec(memory_space=pl.ANY)] * groups,
        out_specs=HBM,
        scratch_shapes=[all_pairs, all_pairs, flat_pieces, pltpu.SemaphoreType.DMA((pieces,))],
        compiler_params=PARAMS,
        name="temporal",
    )(gathered, cotangent, made, *layouts[1:])

    returned = lax.all_to_all(mixed_grad, "shard", split_axis=0, concat_axis=0, tiled=True)
    half = slots // 2
    input_grad, own_half, other_half = pl.pallas_call(
        functools.partial(spatial_back_kernel, width),
        grid=(steps,),
        out_shape=(plane_shape,) + (jax.ShapeDtypeStruct((half, model), jnp.bfloat16),) * 2,
        in_specs=halves_of((2, (local, slots, STEP)), 0)
        + halves_of((1, (local, pairs, slots, 2 * slots)), 0)
        + [VMEM],
        out_specs=(planes,) + (pl.BlockSpec((half, STEP), lambda step: (0, step)),) * 2,
        scratch_shapes=[pltpu.VMEM((pairs, slots, LANES), jnp.float32), flat_scratch],
        compiler_params=PARAMS,
        name="spatial_back",
    )(embedded, embedded, weights, weights, returned)

    far_count = parts // PLANE
    assert parts == far_count * PLANE and parts & (parts - 1) == 0

    def to_partner(array, group_away, shard_away):
        if group_away == 0 and shard_away == 0:
            return array
        pairs_of_devices = [
            (g * parts + i, (g + group_away) % groups * parts + (i ^ shard_away))
            for g in range(groups)
            for i in range(parts)
        ]
        return lax.ppermute(array, ("group", "shard"), pairs_of_devices)

    def summed(kernel, shape, operands, scratch=()):
        return pl.pallas_call(
            kernel,
            out_shape=jax.ShapeDtypeStruct(shape, jnp.bfloat16),
            in_specs=[VMEM] * len(operands),
            out_specs=VMEM,
            scratch_shapes=list(scratch),
            compiler_params=PARAMS,
            name="sums",
        )(*operands)

    halved = summed(core_sum_kernel, (half, model), (own_half, to_partner(other_half, 0, 1)))
    total = summed(
        far_sum_kernel,
        (half, model),
        [to_partner(halved, 0, far * PLANE) for far in reversed(range(far_count))][::-1],
        [pltpu.VMEM((far_count, half, model), jnp.float32)],
    )
    crossed = [
        to_partner(total, away, side) for away in reversed(range(groups)) for side in (2, 0)
    ]
    totals = summed(cross_sum_kernel, (groups, half, model), crossed[::-1])
    table_rows = templates // groups
    table_grad = pl.pallas_call(
        functools.partial(table_kernel, groups),
        out_shape=jax.ShapeDtypeStruct((table_rows, model), jnp.float32),
        in_specs=[VMEM] * (groups + 2),
        out_specs=HBM,
        scratch_shapes=[
            pltpu.VMEM((groups, slots, model), jnp.bfloat16),
            pltpu.VMEM((PIECES, table_rows // PIECES, model), jnp.float32),
            pltpu.SemaphoreType.DMA((PIECES,)),
        ],
        compiler_params=PARAMS,
        name="table",
    )(*layouts, totals, to_partner(totals, 0, 1))
    return (input_grad[None], table_grad)


def solution(mesh):
    placed = (
        P("group", "shard", None, None),
        P("group", None, "shard", None),
        P(),
        P("group", None),
        P("group", None),
        P("group", None),
    )
    return jax.shard_map(
        body,
        mesh=mesh,
        in_specs=placed,
        out_specs=(P("group", "shard", None, None), P("group", None)),
        check_vma=False,
    )
```

```python
import functools
import math

import jax
import jax.numpy as jnp
from jax import lax
from jax.experimental import pallas as pl
from jax.experimental.pallas import tpu as pltpu
from jax.sharding import PartitionSpec as P

HEADS = 16
BLOCK = 32
LANES = 128
MASKED = -1e30
SUBLANES = 8
STEP = 512
PIECES = 8
PIECE = 256
PLANE = 4
SPATIAL_GROUP = 32
TEMPORAL_GROUP = 8


def dot(left, right, over):
    return lax.dot_general(
        left, right, (((over[0],), (over[1],)), ((), ())), preferred_element_type=jnp.float32
    )


def head_masks(width, scale):
    lane = lax.broadcasted_iota(jnp.int32, (1, LANES), 1)
    first = jnp.where(lane < width, scale, 0.0).astype(jnp.bfloat16)
    second = jnp.where(lane < width, 0.0, scale).astype(jnp.bfloat16)
    return first, second


def head_rows(pair, masks):
    return jnp.concatenate([pair * masks[0], pair * masks[1]], axis=0)


def head_columns(rows, width):
    count = rows.shape[0] // 2
    lane = lax.broadcasted_iota(jnp.int32, (count, rows.shape[1]), 1)
    return jnp.where(lane < width, rows[:count], rows[count:])


def each(function, *lists):
    return [function(*items) for items in zip(*lists)]


def weights_by_key(scores):
    tops = each(lambda s: jnp.max(s, axis=0, keepdims=True), scores)
    exponents = each(lambda s, t: jnp.exp(s - t), scores, tops)
    shares = each(lambda e: 1.0 / jnp.sum(e, axis=0, keepdims=True), exponents)
    return each(lambda e, r: (e * r).astype(jnp.bfloat16), exponents, shares)


def by_query(shares, values, width):
    if 2 * values[0].shape[0] != LANES or len(values) % 2:
        return each(lambda s, v: head_columns(dot(s, v, (0, 0)), width), shares, values)
    results = []
    for first in range(0, len(values), 2):
        turned = jnp.transpose(jnp.concatenate(shares[first : first + 2], axis=0))
        one, other = values[first : first + 2]
        zero = jnp.zeros_like(one)
        apart = jnp.concatenate(
            [jnp.concatenate([one, zero], axis=1), jnp.concatenate([zero, other], axis=1)], axis=0
        )
        both = dot(turned, apart, (1, 0))
        results += [head_columns(both[:, :LANES], width), head_columns(both[:, LANES:], width)]
    return results


def back(values, scaled, cotangents, weights, grad_weights, heads_grads, width):
    wide = each(lambda w: w.astype(jnp.float32), weights)
    deltas = each(lambda w, g: jnp.sum(w * g, axis=0, keepdims=True), wide, grad_weights)
    grad_scores = each(
        lambda w, g, d: (w * (g - d)).astype(jnp.bfloat16), wide, grad_weights, deltas
    )
    length = values[0].shape[0]
    whole = length % LANES == 0
    both_ways = grad_scores
    if whole:
        both_ways = each(
            lambda g: jnp.concatenate(
                [
                    g[:, start : start + length] + jnp.transpose(g[:, start : start + length])
                    for start in (0, length)
                ],
                axis=1,
            ),
            grad_scores,
        )
    grads = each(
        lambda c, w, g, hg, hv: c.astype(jnp.float32)
        + dot(jnp.concatenate([w, g], axis=1), jnp.concatenate([hg, hv], axis=0), (1, 0)),
        cotangents,
        weights,
        both_ways,
        heads_grads,
        scaled,
    )
    if whole:
        return grads
    score_scale = 0.5 / math.sqrt(width)
    rest = by_query(grad_scores, values, width)
    return each(lambda g, r: g + score_scale * r, grads, rest)


def pair_bias(counts, offsets, slots):
    def sessions(slot):
        block = slot // BLOCK
        session = jnp.full(slot.shape, -1, jnp.int32)
        for j in range(offsets.shape[1]):
            session = session + (offsets[0, j] <= block).astype(jnp.int32)
        return session

    key_slot = lax.broadcasted_iota(jnp.int32, (slots, 2 * slots), 0)
    query_slot = lax.broadcasted_iota(jnp.int32, (slots, 2 * slots), 1) % slots
    key_session = sessions(key_slot)
    first = jnp.zeros_like(key_slot)
    live = jnp.zeros_like(key_slot)
    for j in range(offsets.shape[1]):
        chosen = key_session == j
        first = jnp.where(chosen, offsets[0, j] * BLOCK, first)
        live = jnp.where(chosen, counts[0, j], live)
    allowed = (key_session == sessions(query_slot)) & (key_slot - first < live)
    return jnp.where(allowed, 0.0, MASKED)


def pair_columns(pair):
    return pl.ds(pair * LANES, LANES)


def step_columns(pair, width):
    start = pl.program_id(0) * width + pair * LANES
    return pl.ds(pl.multiple_of(start, LANES), LANES)


def in_groups(pairs, rows, size):
    items = [(pair, row) for pair in range(pairs) for row in range(rows)]
    return [items[start : start + size] for start in range(0, len(items), size)]


def turned_stride(patches):
    return patches + 1 if patches % SUBLANES == 0 else patches


def turned_scratch(pairs, slots, patches):
    return pltpu.VMEM((pairs, slots * turned_stride(patches), LANES), jnp.float32)


def read_turned(ref, pair, slots, patches):
    stride = turned_stride(patches)
    if stride == patches:
        return ref[pair]
    pieces = [ref[pair, pl.ds(slot * stride, patches), :] for slot in range(slots)]
    return jnp.concatenate(pieces, axis=0)


def write_turned(ref, pair, rows, slots, patches):
    stride = turned_stride(patches)
    if stride == patches:
        ref[pair] = rows
        return
    for slot in range(slots):
        ref[pair, pl.ds(slot * stride, patches), :] = rows[slot * patches : (slot + 1) * patches]


def of_patch(patch, slots, patches):
    return pl.ds(patch, slots, stride=turned_stride(patches))


def of_halves(halves, index):
    count = halves[0].shape[0]
    return halves[index // count].at[index % count]


def attention(width, tokens, rows, bias, group):
    score_masks = head_masks(width, 0.5 / math.sqrt(width))
    values = [
        (
            of_halves(tokens, p)[:, pair_columns(pair)].astype(jnp.float32)
            + rows[:, pair * LANES : (pair + 1) * LANES]
        ).astype(jnp.bfloat16)
        for pair, p in group
    ]
    scores = each(lambda v: dot(v, head_rows(v, score_masks), (1, 1)) + bias[...], values)
    return values, weights_by_key(scores)


def spatial_kernel(
    width, counts, offsets, layout, embedding, other_embedding, tokens, other_tokens,
    rows, mixed, spread, bias, by_electrode,
):
    half, slots, model = tokens.shape
    patches, tokens = 2 * half, (tokens, other_tokens)
    templates = 2 * embedding.shape[0]
    pairs = model // LANES

    @pl.when(pl.program_id(0) == 0)
    def _():
        bias[...] = pair_bias(counts, offsets, slots)
        wanted = jnp.broadcast_to(layout[...].astype(jnp.float32), (LANES, slots))
        wanted = jnp.transpose(wanted).astype(jnp.int32)
        template = lax.broadcasted_iota(jnp.int32, (slots, LANES), 1)
        for first in range(0, templates, LANES):
            chosen = wanted == template + first
            spread[:, pl.ds(first, LANES)] = chosen.astype(jnp.float32).astype(jnp.bfloat16)

    chosen_rows = dot(spread[:, : templates // 2], embedding[...], (1, 0))
    chosen_rows = chosen_rows + dot(spread[:, templates // 2 :], other_embedding[...], (1, 0))
    rows[...] = chosen_rows.astype(jnp.bfloat16)
    for group in in_groups(pairs, patches, SPATIAL_GROUP):
        values, shares = attention(width, tokens, chosen_rows, bias, group)
        attended = by_query(shares, values, width)
        for (pair, p), value, result in zip(group, values, attended):
            by_electrode[pair, of_patch(p, slots, patches), :] = value.astype(jnp.float32) + result
    for pair in range(pairs):
        mixed[:, pair_columns(pair)] = read_turned(by_electrode, pair, slots, patches).astype(
            jnp.bfloat16
        )


def weights_kernel(width, counts, offsets, rows, tokens, embedded, weights, made, bias):
    made[...] = jnp.zeros_like(made)
    patches, slots, model = tokens.shape
    tokens = (tokens,)

    @pl.when(pl.program_id(0) == 0)
    def _():
        bias[...] = pair_bias(counts, offsets, slots)

    added = rows[...].astype(jnp.float32)
    for group in in_groups(model // LANES, patches, SPATIAL_GROUP):
        values, shares = attention(width, tokens, added, bias, group)
        for (pair, p), value, share in zip(group, values, shares):
            embedded[p, :, pair_columns(pair)] = value
            weights[p, pair] = share


def patches_first(local):
    return local % SUBLANES != 0


def electrode_rows(electrode, electrodes, parts, local):
    start, step = electrode * local, electrodes * local
    if patches_first(local):
        return [pl.ds(start + p, parts, stride=step) for p in range(local)]
    return [pl.ds(start + part * step, local) for part in range(parts)]


def temporal_kernel(width, parts, mixed, out_grad, *refs):
    all_mixed_grad, received, returned, mixed_grad, sems = refs[-5:]
    electrodes, patches, _ = out_grad.shape
    pieces, _, model = mixed_grad.shape
    local = patches // parts
    pairs = model // LANES
    score_masks = head_masks(width, 0.5 / math.sqrt(width))
    ones = head_masks(width, 1.0)
    copies = []
    for at in range(pieces):
        first = at * pairs
        for pair in range(first, first + pairs):
            received[pair] = mixed[:, pair_columns(pair)].astype(jnp.float32)
        for group in in_groups(pairs, electrodes, TEMPORAL_GROUP):
            group = [(first + pair, e) for pair, e in group]
            places = [electrode_rows(e, electrodes, parts, local) for _, e in group]
            values = each(
                lambda item, place: jnp.concatenate(
                    [received[item[0], rows, :] for rows in place], axis=0
                ).astype(jnp.bfloat16),
                group,
                places,
            )
            cotangents = [out_grad[e, :, pair_columns(pair)] for pair, e in group]
            scaled = each(lambda v: head_rows(v, score_masks), values)
            scores = each(lambda v, s: dot(v, s, (1, 1)), values, scaled)
            heads_grads = each(lambda g: head_rows(g, ones), cotangents)
            grad_weights = each(lambda v, g: dot(v, g, (1, 1)), values, heads_grads)
            shares = weights_by_key(scores)
            grads = back(values, scaled, cotangents, shares, grad_weights, heads_grads, width)
            for (pair, _), place, grad in zip(group, places, grads):
                start = 0
                for rows in place:
                    returned[pair, rows, :] = grad[start : start + rows.size]
                    start += rows.size
        for pair in range(pairs):
            mixed_grad[at, :, pair_columns(pair)] = returned[first + pair].astype(jnp.bfloat16)
    for at in range(pieces):
        copy = pltpu.make_async_copy(
            mixed_grad.at[at], all_mixed_grad.at[:, pl.ds(at * model, model)], sems.at[at]
        )
        copy.start()
        copies.append(copy)
    for copy in copies:
        copy.wait()


def half_rows(bit, away, count):
    here = lax.bitwise_and(lax.shift_right_logical(lax.axis_index("shard"), bit), 1)
    return pl.ds(pl.multiple_of(lax.bitwise_xor(here, away) * count, count), count)


def spatial_back_kernel(
    width, embedded, other_embedded, weights, other_weights, mixed_grad, input_grad, *refs
):
    electrode_grads, (sums, received) = refs[:-2], refs[-2:]
    patches, slots, model = input_grad.shape
    embedded, weights = (embedded, other_embedded), (weights, other_weights)
    pairs = model // LANES
    score_masks = head_masks(width, 0.5 / math.sqrt(width))
    ones = head_masks(width, 1.0)
    totals = [jnp.zeros((slots, LANES), jnp.float32) for _ in range(pairs)]
    for pair in range(pairs):
        arrived = mixed_grad[:, step_columns(pair, model)].astype(jnp.float32)
        write_turned(received, pair, arrived, slots, patches)
    for group in in_groups(pairs, patches, SPATIAL_GROUP):
        cotangents = [
            received[pair, of_patch(p, slots, patches), :].astype(jnp.bfloat16)
            for pair, p in group
        ]
        values = [of_halves(embedded, p)[:, pair_columns(pair)] for pair, p in group]
        shares = [of_halves(weights, p)[pair] for pair, p in group]
        scaled = each(lambda v: head_rows(v, score_masks), values)
        heads_grads = each(lambda g: head_rows(g, ones), cotangents)
        grad_weights = each(lambda v, g: dot(v, g, (1, 1)), values, heads_grads)
        grads = back(values, scaled, cotangents, shares, grad_weights, heads_grads, width)
        for (pair, p), grad in zip(group, grads):
            input_grad[p, :, pair_columns(pair)] = grad.astype(jnp.bfloat16)
            totals[pair] = totals[pair] + grad
    for pair in range(pairs):
        sums[pair] = totals[pair]
        for away, block in enumerate(electrode_grads):
            rows = sums[pair, half_rows(0, away, block.shape[0]), :]
            block[:, pair_columns(pair)] = rows.astype(jnp.bfloat16)


def add(one, other):
    return (one.astype(jnp.float32) + other.astype(jnp.float32)).astype(jnp.bfloat16)


def core_sum_kernel(own, arrived, total):
    total[...] = add(own[...], arrived[...])


def cross_sum_kernel(*refs):
    totals = refs[-1]
    for away in range(totals.shape[0]):
        totals[away] = add(refs[2 * away][...], refs[2 * away + 1][...])


def far_sum_kernel(*refs):
    parts, (total, ordered) = refs[:-2], refs[-2:]
    place = lax.div(lax.axis_index("shard"), PLANE)
    for away, part in enumerate(parts):
        ordered[lax.bitwise_xor(place, away)] = part[...].astype(jnp.float32)
    result = ordered[0]
    for index in range(1, len(parts)):
        result = result + ordered[index]
    total[...] = result.astype(jnp.bfloat16)


def join_kernel(bit, own, arrived, joined):
    for away, block in enumerate((own, arrived)):
        joined[:, half_rows(bit, away, block.shape[1]), :] = block[...]


def table_kernel(groups, *refs):
    layouts, blocks, (table, sources, pieces, sems) = refs[:groups], refs[groups:-4], refs[-4:]
    owner = lax.axis_index("group")
    count, rows, _ = pieces.shape
    slots = sources.shape[1]
    join_kernel(0, *blocks, sources)
    copies = []
    for piece in range(count):
        first = owner * (count * rows) + piece * rows
        template = lax.broadcasted_iota(jnp.int32, (rows, slots), 0) + first
        total = jnp.zeros(pieces.shape[1:], jnp.float32)
        for away in range(groups):
            spread = (template == layouts[away][...]).astype(jnp.float32).astype(jnp.bfloat16)
            total = total + dot(spread, sources[away], (1, 0))
        pieces[piece] = total
        copy = pltpu.make_async_copy(
            pieces.at[piece], table.at[pl.ds(piece * rows, rows)], sems.at[piece]
        )
        copy.start()
        copies.append(copy)
    for copy in copies:
        copy.wait()


VMEM = pl.BlockSpec(memory_space=pltpu.VMEM)
SMEM = pl.BlockSpec(memory_space=pltpu.SMEM)
HBM = pl.BlockSpec(memory_space=pltpu.HBM)
PARAMS = pltpu.CompilerParams(vmem_limit_bytes=32 * 1024 * 1024)
STREAMED = pltpu.CompilerParams(vmem_limit_bytes=56 * 1024 * 1024)


def body(activations, out_grad, embedding, counts, offsets, layout):
    tokens = activations[0]
    local, slots, model = tokens.shape
    groups = lax.axis_size("group")
    parts = lax.axis_size("shard")
    patches = local * parts
    own = slots // parts
    width = model // HEADS
    templates = embedding.shape[0]
    pairs = STEP // LANES
    steps = model // STEP

    layouts = [layout] + [
        lax.ppermute(layout, "group", [(i, (i + away) % groups) for i in range(groups)])
        for away in range(1, groups)
    ]
    order = (2, 1, 0, 3) if patches_first(local) else (2, 0, 1, 3)
    cotangent = jnp.transpose(out_grad[0].reshape(parts, local, own, model), order)
    cotangent = cotangent.reshape(own, patches, model)

    flat = pl.BlockSpec((slots * local, STEP), lambda step: (0, step))
    planes = pl.BlockSpec((local, slots, STEP), lambda step: (0, 0, step))
    squares = pl.BlockSpec((local, pairs, slots, 2 * slots), lambda step: (0, step, 0, 0))
    flat_shape = jax.ShapeDtypeStruct((slots * local, model), jnp.bfloat16)
    plane_shape = jax.ShapeDtypeStruct(tokens.shape, jnp.bfloat16)
    flat_scratch = turned_scratch(pairs, slots, local)

    strip = pl.BlockSpec((slots, STEP), lambda step: (0, step))
    pieces = model // PIECE
    all_pairs = pltpu.VMEM((model // LANES, slots * local, LANES), jnp.float32)
    flat_pieces = pltpu.VMEM((pieces, slots * local, PIECE), jnp.bfloat16)

    def halves_of(shape, axis):
        cut = tuple(size // 2 if place == axis else size for place, size in enumerate(shape[1]))
        return [
            pl.BlockSpec(
                cut,
                lambda step, half=half: tuple(
                    half if place == axis else step if place == shape[0] else 0
                    for place in range(len(cut))
                ),
            )
            for half in range(2)
        ]

    rows, mixed = pl.pallas_call(
        functools.partial(spatial_kernel, width),
        grid=(steps,),
        out_shape=(jax.ShapeDtypeStruct((slots, model), jnp.bfloat16), flat_shape),
        in_specs=[SMEM, SMEM, VMEM]
        + halves_of((1, (templates, STEP)), 0)
        + halves_of((2, (local, slots, STEP)), 0),
        out_specs=(strip, flat),
        scratch_shapes=[
            pltpu.VMEM((slots, templates), jnp.bfloat16),
            pltpu.VMEM((slots, 2 * slots), jnp.float32),
            flat_scratch,
        ],
        compiler_params=STREAMED,
        name="spatial",
    )(counts, offsets, layout, embedding, embedding, tokens, tokens)
    embedded, weights, made = pl.pallas_call(
        functools.partial(weights_kernel, width),
        grid=(steps,),
        out_shape=(
            plane_shape,
            jax.ShapeDtypeStruct((local, model // LANES, slots, 2 * slots), jnp.bfloat16),
            jax.ShapeDtypeStruct((SUBLANES, LANES), jnp.float32),
        ),
        in_specs=[SMEM, SMEM, strip, planes],
        out_specs=(planes, squares, pl.BlockSpec((SUBLANES, LANES), lambda step: (0, 0))),
        scratch_shapes=[pltpu.VMEM((slots, 2 * slots), jnp.float32)],
        compiler_params=STREAMED,
        cost_estimate=pl.CostEstimate(
            flops=4 * local * slots * slots * model, bytes_accessed=6 * tokens.size, transcendentals=0
        ),
        name="weights",
    )(counts, offsets, rows, tokens)

    gathered = lax.all_to_all(mixed, "shard", split_axis=0, concat_axis=0, tiled=True)
    mixed_grad = pl.pallas_call(
        functools.partial(temporal_kernel, width, parts),
        out_shape=flat_shape,
        in_specs=[VMEM, VMEM] + [pl.BlockSpec(memory_space=pl.ANY)] * groups,
        out_specs=HBM,
        scratch_shapes=[all_pairs, all_pairs, flat_pieces, pltpu.SemaphoreType.DMA((pieces,))],
        compiler_params=PARAMS,
        name="temporal",
    )(gathered, cotangent, made, *layouts[1:])

    returned = lax.all_to_all(mixed_grad, "shard", split_axis=0, concat_axis=0, tiled=True)
    half = slots // 2
    input_grad, own_half, other_half = pl.pallas_call(
        functools.partial(spatial_back_kernel, width),
        grid=(steps,),
        out_shape=(plane_shape,) + (jax.ShapeDtypeStruct((half, model), jnp.bfloat16),) * 2,
        in_specs=halves_of((2, (local, slots, STEP)), 0)
        + halves_of((1, (local, pairs, slots, 2 * slots)), 0)
        + [VMEM],
        out_specs=(planes,) + (pl.BlockSpec((half, STEP), lambda step: (0, step)),) * 2,
        scratch_shapes=[pltpu.VMEM((pairs, slots, LANES), jnp.float32), flat_scratch],
        compiler_params=PARAMS,
        name="spatial_back",
    )(embedded, embedded, weights, weights, returned)

    far_count = parts // PLANE
    assert parts == far_count * PLANE and parts & (parts - 1) == 0

    def to_partner(array, group_away, shard_away):
        if group_away == 0 and shard_away == 0:
            return array
        pairs_of_devices = [
            (g * parts + i, (g + group_away) % groups * parts + (i ^ shard_away))
            for g in range(groups)
            for i in range(parts)
        ]
        return lax.ppermute(array, ("group", "shard"), pairs_of_devices)

    def summed(kernel, shape, operands, scratch=()):
        return pl.pallas_call(
            kernel,
            out_shape=jax.ShapeDtypeStruct(shape, jnp.bfloat16),
            in_specs=[VMEM] * len(operands),
            out_specs=VMEM,
            scratch_shapes=list(scratch),
            compiler_params=PARAMS,
            name="sums",
        )(*operands)

    halved = summed(core_sum_kernel, (half, model), (own_half, to_partner(other_half, 0, 1)))
    total = summed(
        far_sum_kernel,
        (half, model),
        [to_partner(halved, 0, far * PLANE) for far in reversed(range(far_count))][::-1],
        [pltpu.VMEM((far_count, half, model), jnp.float32)],
    )
    crossed = [
        to_partner(total, away, side) for away in reversed(range(groups)) for side in (2, 0)
    ]
    totals = summed(cross_sum_kernel, (groups, half, model), crossed[::-1])
    table_rows = templates // groups
    table_grad = pl.pallas_call(
        functools.partial(table_kernel, groups),
        out_shape=jax.ShapeDtypeStruct((table_rows, model), jnp.float32),
        in_specs=[VMEM] * (groups + 2),
        out_specs=HBM,
        scratch_shapes=[
            pltpu.VMEM((groups, slots, model), jnp.bfloat16),
            pltpu.VMEM((PIECES, table_rows // PIECES, model), jnp.float32),
            pltpu.SemaphoreType.DMA((PIECES,)),
        ],
        compiler_params=PARAMS,
        name="table",
    )(*layouts, totals, to_partner(totals, 0, 1))
    return (input_grad[None], table_grad)


def solution(mesh):
    placed = (
        P("group", "shard", None, None),
        P("group", None, "shard", None),
        P(),
        P("group", None),
        P("group", None),
        P("group", None),
    )
    return jax.shard_map(
        body,
        mesh=mesh,
        in_specs=placed,
        out_specs=(P("group", "shard", None, None), P("group", None)),
        check_vma=False,
    )
```

```python
import functools
import math

import jax
import jax.numpy as jnp
from jax import lax
from jax.experimental import pallas as pl
from jax.experimental.pallas import tpu as pltpu
from jax.sharding import PartitionSpec as P

HEADS = 16
BLOCK = 32
LANES = 128
MASKED = -1e30
SUBLANES = 8
STEP = 512
PIECES = 8
PIECE = 512
PLANE = 4
SPATIAL_GROUP = 32
TEMPORAL_GROUP = 8


def dot(left, right, over):
    return lax.dot_general(
        left, right, (((over[0],), (over[1],)), ((), ())), preferred_element_type=jnp.float32
    )


def head_masks(width, scale):
    lane = lax.broadcasted_iota(jnp.int32, (1, LANES), 1)
    first = jnp.where(lane < width, scale, 0.0).astype(jnp.bfloat16)
    second = jnp.where(lane < width, 0.0, scale).astype(jnp.bfloat16)
    return first, second


def head_rows(pair, masks):
    return jnp.concatenate([pair * masks[0], pair * masks[1]], axis=0)


def head_columns(rows, width):
    count = rows.shape[0] // 2
    lane = lax.broadcasted_iota(jnp.int32, (count, rows.shape[1]), 1)
    return jnp.where(lane < width, rows[:count], rows[count:])


def each(function, *lists):
    return [function(*items) for items in zip(*lists)]


def weights_by_key(scores):
    tops = each(lambda s: jnp.max(s, axis=0, keepdims=True), scores)
    exponents = each(lambda s, t: jnp.exp(s - t), scores, tops)
    shares = each(lambda e: 1.0 / jnp.sum(e, axis=0, keepdims=True), exponents)
    return each(lambda e, r: (e * r).astype(jnp.bfloat16), exponents, shares)


def by_query(shares, values, width):
    if 2 * values[0].shape[0] != LANES or len(values) % 2:
        return each(lambda s, v: head_columns(dot(s, v, (0, 0)), width), shares, values)
    results = []
    for first in range(0, len(values), 2):
        turned = jnp.transpose(jnp.concatenate(shares[first : first + 2], axis=0))
        one, other = values[first : first + 2]
        zero = jnp.zeros_like(one)
        apart = jnp.concatenate(
            [jnp.concatenate([one, zero], axis=1), jnp.concatenate([zero, other], axis=1)], axis=0
        )
        both = dot(turned, apart, (1, 0))
        results += [head_columns(both[:, :LANES], width), head_columns(both[:, LANES:], width)]
    return results


def back(values, scaled, cotangents, weights, grad_weights, heads_grads, width):
    wide = each(lambda w: w.astype(jnp.float32), weights)
    deltas = each(lambda w, g: jnp.sum(w * g, axis=0, keepdims=True), wide, grad_weights)
    grad_scores = each(
        lambda w, g, d: (w * (g - d)).astype(jnp.bfloat16), wide, grad_weights, deltas
    )
    length = values[0].shape[0]
    whole = length % LANES == 0
    both_ways = grad_scores
    if whole:
        both_ways = each(
            lambda g: jnp.concatenate(
                [
                    g[:, start : start + length] + jnp.transpose(g[:, start : start + length])
                    for start in (0, length)
                ],
                axis=1,
            ),
            grad_scores,
        )
    grads = each(
        lambda c, w, g, hg, hv: c.astype(jnp.float32)
        + dot(jnp.concatenate([w, g], axis=1), jnp.concatenate([hg, hv], axis=0), (1, 0)),
        cotangents,
        weights,
        both_ways,
        heads_grads,
        scaled,
    )
    if whole:
        return grads
    score_scale = 0.5 / math.sqrt(width)
    rest = by_query(grad_scores, values, width)
    return each(lambda g, r: g + score_scale * r, grads, rest)


def pair_bias(counts, offsets, slots):
    def sessions(slot):
        block = slot // BLOCK
        session = jnp.full(slot.shape, -1, jnp.int32)
        for j in range(offsets.shape[1]):
            session = session + (offsets[0, j] <= block).astype(jnp.int32)
        return session

    key_slot = lax.broadcasted_iota(jnp.int32, (slots, 2 * slots), 0)
    query_slot = lax.broadcasted_iota(jnp.int32, (slots, 2 * slots), 1) % slots
    key_session = sessions(key_slot)
    first = jnp.zeros_like(key_slot)
    live = jnp.zeros_like(key_slot)
    for j in range(offsets.shape[1]):
        chosen = key_session == j
        first = jnp.where(chosen, offsets[0, j] * BLOCK, first)
        live = jnp.where(chosen, counts[0, j], live)
    allowed = (key_session == sessions(query_slot)) & (key_slot - first < live)
    return jnp.where(allowed, 0.0, MASKED)


def pair_columns(pair):
    return pl.ds(pair * LANES, LANES)


def step_columns(pair, width):
    start = pl.program_id(0) * width + pair * LANES
    return pl.ds(pl.multiple_of(start, LANES), LANES)


def in_groups(pairs, rows, size):
    items = [(pair, row) for pair in range(pairs) for row in range(rows)]
    return [items[start : start + size] for start in range(0, len(items), size)]


def turned_stride(patches):
    return patches + 1 if patches % SUBLANES == 0 else patches


def turned_scratch(pairs, slots, patches):
    return pltpu.VMEM((pairs, slots * turned_stride(patches), LANES), jnp.float32)


def read_turned(ref, pair, slots, patches):
    stride = turned_stride(patches)
    if stride == patches:
        return ref[pair]
    pieces = [ref[pair, pl.ds(slot * stride, patches), :] for slot in range(slots)]
    return jnp.concatenate(pieces, axis=0)


def write_turned(ref, pair, rows, slots, patches):
    stride = turned_stride(patches)
    if stride == patches:
        ref[pair] = rows
        return
    for slot in range(slots):
        ref[pair, pl.ds(slot * stride, patches), :] = rows[slot * patches : (slot + 1) * patches]


def of_patch(patch, slots, patches):
    return pl.ds(patch, slots, stride=turned_stride(patches))


def of_halves(halves, index):
    count = halves[0].shape[0]
    return halves[index // count].at[index % count]


def attention(width, tokens, rows, bias, group):
    score_masks = head_masks(width, 0.5 / math.sqrt(width))
    values = [
        (
            of_halves(tokens, p)[:, pair_columns(pair)].astype(jnp.float32)
            + rows[:, pair * LANES : (pair + 1) * LANES]
        ).astype(jnp.bfloat16)
        for pair, p in group
    ]
    scores = each(lambda v: dot(v, head_rows(v, score_masks), (1, 1)) + bias[...], values)
    return values, weights_by_key(scores)


def spatial_kernel(
    width, counts, offsets, layout, embedding, other_embedding, tokens, other_tokens,
    rows, mixed, spread, bias, by_electrode,
):
    half, slots, model = tokens.shape
    patches, tokens = 2 * half, (tokens, other_tokens)
    templates = 2 * embedding.shape[0]
    pairs = model // LANES

    @pl.when(pl.program_id(0) == 0)
    def _():
        bias[...] = pair_bias(counts, offsets, slots)
        wanted = jnp.broadcast_to(layout[...].astype(jnp.float32), (LANES, slots))
        wanted = jnp.transpose(wanted).astype(jnp.int32)
        template = lax.broadcasted_iota(jnp.int32, (slots, LANES), 1)
        for first in range(0, templates, LANES):
            chosen = wanted == template + first
            spread[:, pl.ds(first, LANES)] = chosen.astype(jnp.float32).astype(jnp.bfloat16)

    chosen_rows = dot(spread[:, : templates // 2], embedding[...], (1, 0))
    chosen_rows = chosen_rows + dot(spread[:, templates // 2 :], other_embedding[...], (1, 0))
    rows[...] = chosen_rows.astype(jnp.bfloat16)
    for group in in_groups(pairs, patches, SPATIAL_GROUP):
        values, shares = attention(width, tokens, chosen_rows, bias, group)
        attended = by_query(shares, values, width)
        for (pair, p), value, result in zip(group, values, attended):
            by_electrode[pair, of_patch(p, slots, patches), :] = value.astype(jnp.float32) + result
    for pair in range(pairs):
        mixed[:, pair_columns(pair)] = read_turned(by_electrode, pair, slots, patches).astype(
            jnp.bfloat16
        )


def weights_kernel(width, counts, offsets, rows, tokens, embedded, weights, made, bias):
    made[...] = jnp.zeros_like(made)
    patches, slots, model = tokens.shape
    tokens = (tokens,)

    @pl.when(pl.program_id(0) == 0)
    def _():
        bias[...] = pair_bias(counts, offsets, slots)

    added = rows[...].astype(jnp.float32)
    for group in in_groups(model // LANES, patches, SPATIAL_GROUP):
        values, shares = attention(width, tokens, added, bias, group)
        for (pair, p), value, share in zip(group, values, shares):
            embedded[p, :, pair_columns(pair)] = value
            weights[p, pair] = share


def patches_first(local):
    return local % SUBLANES != 0


def electrode_rows(electrode, electrodes, parts, local):
    start, step = electrode * local, electrodes * local
    if patches_first(local):
        return [pl.ds(start + p, parts, stride=step) for p in range(local)]
    return [pl.ds(start + part * step, local) for part in range(parts)]


def temporal_kernel(width, parts, mixed, out_grad, *refs):
    all_mixed_grad, received, returned, mixed_grad, sems = refs[-5:]
    electrodes, patches, _ = out_grad.shape
    pieces, _, model = mixed_grad.shape
    local = patches // parts
    pairs = model // LANES
    score_masks = head_masks(width, 0.5 / math.sqrt(width))
    ones = head_masks(width, 1.0)
    copies = []
    for at in range(pieces):
        first = at * pairs
        for pair in range(first, first + pairs):
            received[pair] = mixed[:, pair_columns(pair)].astype(jnp.float32)
        for group in in_groups(pairs, electrodes, TEMPORAL_GROUP):
            group = [(first + pair, e) for pair, e in group]
            places = [electrode_rows(e, electrodes, parts, local) for _, e in group]
            values = each(
                lambda item, place: jnp.concatenate(
                    [received[item[0], rows, :] for rows in place], axis=0
                ).astype(jnp.bfloat16),
                group,
                places,
            )
            cotangents = [out_grad[e, :, pair_columns(pair)] for pair, e in group]
            scaled = each(lambda v: head_rows(v, score_masks), values)
            scores = each(lambda v, s: dot(v, s, (1, 1)), values, scaled)
            heads_grads = each(lambda g: head_rows(g, ones), cotangents)
            grad_weights = each(lambda v, g: dot(v, g, (1, 1)), values, heads_grads)
            shares = weights_by_key(scores)
            grads = back(values, scaled, cotangents, shares, grad_weights, heads_grads, width)
            for (pair, _), place, grad in zip(group, places, grads):
                start = 0
                for rows in place:
                    returned[pair, rows, :] = grad[start : start + rows.size]
                    start += rows.size
        for pair in range(pairs):
            mixed_grad[at, :, pair_columns(pair)] = returned[first + pair].astype(jnp.bfloat16)
    for at in range(pieces):
        copy = pltpu.make_async_copy(
            mixed_grad.at[at], all_mixed_grad.at[:, pl.ds(at * model, model)], sems.at[at]
        )
        copy.start()
        copies.append(copy)
    for copy in copies:
        copy.wait()


def half_rows(bit, away, count):
    here = lax.bitwise_and(lax.shift_right_logical(lax.axis_index("shard"), bit), 1)
    return pl.ds(pl.multiple_of(lax.bitwise_xor(here, away) * count, count), count)


def spatial_back_kernel(
    width, embedded, other_embedded, weights, other_weights, mixed_grad, input_grad, *refs
):
    electrode_grads, (sums, received) = refs[:-2], refs[-2:]
    patches, slots, model = input_grad.shape
    embedded, weights = (embedded, other_embedded), (weights, other_weights)
    pairs = model // LANES
    score_masks = head_masks(width, 0.5 / math.sqrt(width))
    ones = head_masks(width, 1.0)
    totals = [jnp.zeros((slots, LANES), jnp.float32) for _ in range(pairs)]
    for pair in range(pairs):
        arrived = mixed_grad[:, step_columns(pair, model)].astype(jnp.float32)
        write_turned(received, pair, arrived, slots, patches)
    for group in in_groups(pairs, patches, SPATIAL_GROUP):
        cotangents = [
            received[pair, of_patch(p, slots, patches), :].astype(jnp.bfloat16)
            for pair, p in group
        ]
        values = [of_halves(embedded, p)[:, pair_columns(pair)] for pair, p in group]
        shares = [of_halves(weights, p)[pair] for pair, p in group]
        scaled = each(lambda v: head_rows(v, score_masks), values)
        heads_grads = each(lambda g: head_rows(g, ones), cotangents)
        grad_weights = each(lambda v, g: dot(v, g, (1, 1)), values, heads_grads)
        grads = back(values, scaled, cotangents, shares, grad_weights, heads_grads, width)
        for (pair, p), grad in zip(group, grads):
            input_grad[p, :, pair_columns(pair)] = grad.astype(jnp.bfloat16)
            totals[pair] = totals[pair] + grad
    for pair in range(pairs):
        sums[pair] = totals[pair]
        for away, block in enumerate(electrode_grads):
            rows = sums[pair, half_rows(0, away, block.shape[0]), :]
            block[:, pair_columns(pair)] = rows.astype(jnp.bfloat16)


def add(one, other):
    return (one.astype(jnp.float32) + other.astype(jnp.float32)).astype(jnp.bfloat16)


def core_sum_kernel(own, arrived, total):
    total[...] = add(own[...], arrived[...])


def cross_sum_kernel(*refs):
    totals = refs[-1]
    for away in range(totals.shape[0]):
        totals[away] = add(refs[2 * away][...], refs[2 * away + 1][...])


def far_sum_kernel(*refs):
    parts, (total, ordered) = refs[:-2], refs[-2:]
    place = lax.div(lax.axis_index("shard"), PLANE)
    for away, part in enumerate(parts):
        ordered[lax.bitwise_xor(place, away)] = part[...].astype(jnp.float32)
    result = ordered[0]
    for index in range(1, len(parts)):
        result = result + ordered[index]
    total[...] = result.astype(jnp.bfloat16)


def join_kernel(bit, own, arrived, joined):
    for away, block in enumerate((own, arrived)):
        joined[:, half_rows(bit, away, block.shape[1]), :] = block[...]


def table_kernel(groups, *refs):
    layouts, blocks, (table, sources, pieces, sems) = refs[:groups], refs[groups:-4], refs[-4:]
    owner = lax.axis_index("group")
    count, rows, _ = pieces.shape
    slots = sources.shape[1]
    join_kernel(0, *blocks, sources)
    copies = []
    for piece in range(count):
        first = owner * (count * rows) + piece * rows
        template = lax.broadcasted_iota(jnp.int32, (rows, slots), 0) + first
        total = jnp.zeros(pieces.shape[1:], jnp.float32)
        for away in range(groups):
            spread = (template == layouts[away][...]).astype(jnp.float32).astype(jnp.bfloat16)
            total = total + dot(spread, sources[away], (1, 0))
        pieces[piece] = total
        copy = pltpu.make_async_copy(
            pieces.at[piece], table.at[pl.ds(piece * rows, rows)], sems.at[piece]
        )
        copy.start()
        copies.append(copy)
    for copy in copies:
        copy.wait()


VMEM = pl.BlockSpec(memory_space=pltpu.VMEM)
SMEM = pl.BlockSpec(memory_space=pltpu.SMEM)
HBM = pl.BlockSpec(memory_space=pltpu.HBM)
PARAMS = pltpu.CompilerParams(vmem_limit_bytes=32 * 1024 * 1024)
STREAMED = pltpu.CompilerParams(vmem_limit_bytes=56 * 1024 * 1024)


def body(activations, out_grad, embedding, counts, offsets, layout):
    tokens = activations[0]
    local, slots, model = tokens.shape
    groups = lax.axis_size("group")
    parts = lax.axis_size("shard")
    patches = local * parts
    own = slots // parts
    width = model // HEADS
    templates = embedding.shape[0]
    pairs = STEP // LANES
    steps = model // STEP

    layouts = [layout] + [
        lax.ppermute(layout, "group", [(i, (i + away) % groups) for i in range(groups)])
        for away in range(1, groups)
    ]
    order = (2, 1, 0, 3) if patches_first(local) else (2, 0, 1, 3)
    cotangent = jnp.transpose(out_grad[0].reshape(parts, local, own, model), order)
    cotangent = cotangent.reshape(own, patches, model)

    flat = pl.BlockSpec((slots * local, STEP), lambda step: (0, step))
    planes = pl.BlockSpec((local, slots, STEP), lambda step: (0, 0, step))
    squares = pl.BlockSpec((local, pairs, slots, 2 * slots), lambda step: (0, step, 0, 0))
    flat_shape = jax.ShapeDtypeStruct((slots * local, model), jnp.bfloat16)
    plane_shape = jax.ShapeDtypeStruct(tokens.shape, jnp.bfloat16)
    flat_scratch = turned_scratch(pairs, slots, local)

    strip = pl.BlockSpec((slots, STEP), lambda step: (0, step))
    pieces = model // PIECE
    all_pairs = pltpu.VMEM((model // LANES, slots * local, LANES), jnp.float32)
    flat_pieces = pltpu.VMEM((pieces, slots * local, PIECE), jnp.bfloat16)

    def halves_of(shape, axis):
        cut = tuple(size // 2 if place == axis else size for place, size in enumerate(shape[1]))
        return [
            pl.BlockSpec(
                cut,
                lambda step, half=half: tuple(
                    half if place == axis else step if place == shape[0] else 0
                    for place in range(len(cut))
                ),
            )
            for half in range(2)
        ]

    rows, mixed = pl.pallas_call(
        functools.partial(spatial_kernel, width),
        grid=(steps,),
        out_shape=(jax.ShapeDtypeStruct((slots, model), jnp.bfloat16), flat_shape),
        in_specs=[SMEM, SMEM, VMEM]
        + halves_of((1, (templates, STEP)), 0)
        + halves_of((2, (local, slots, STEP)), 0),
        out_specs=(strip, flat),
        scratch_shapes=[
            pltpu.VMEM((slots, templates), jnp.bfloat16),
            pltpu.VMEM((slots, 2 * slots), jnp.float32),
            flat_scratch,
        ],
        compiler_params=STREAMED,
        name="spatial",
    )(counts, offsets, layout, embedding, embedding, tokens, tokens)
    embedded, weights, made = pl.pallas_call(
        functools.partial(weights_kernel, width),
        grid=(steps,),
        out_shape=(
            plane_shape,
            jax.ShapeDtypeStruct((local, model // LANES, slots, 2 * slots), jnp.bfloat16),
            jax.ShapeDtypeStruct((SUBLANES, LANES), jnp.float32),
        ),
        in_specs=[SMEM, SMEM, strip, planes],
        out_specs=(planes, squares, pl.BlockSpec((SUBLANES, LANES), lambda step: (0, 0))),
        scratch_shapes=[pltpu.VMEM((slots, 2 * slots), jnp.float32)],
        compiler_params=STREAMED,
        cost_estimate=pl.CostEstimate(
            flops=4 * local * slots * slots * model, bytes_accessed=6 * tokens.size, transcendentals=0
        ),
        name="weights",
    )(counts, offsets, rows, tokens)

    gathered = lax.all_to_all(mixed, "shard", split_axis=0, concat_axis=0, tiled=True)
    mixed_grad = pl.pallas_call(
        functools.partial(temporal_kernel, width, parts),
        out_shape=flat_shape,
        in_specs=[VMEM, VMEM] + [pl.BlockSpec(memory_space=pl.ANY)] * groups,
        out_specs=HBM,
        scratch_shapes=[all_pairs, all_pairs, flat_pieces, pltpu.SemaphoreType.DMA((pieces,))],
        compiler_params=PARAMS,
        name="temporal",
    )(gathered, cotangent, made, *layouts[1:])

    returned = lax.all_to_all(mixed_grad, "shard", split_axis=0, concat_axis=0, tiled=True)
    half = slots // 2
    input_grad, own_half, other_half = pl.pallas_call(
        functools.partial(spatial_back_kernel, width),
        grid=(steps,),
        out_shape=(plane_shape,) + (jax.ShapeDtypeStruct((half, model), jnp.bfloat16),) * 2,
        in_specs=halves_of((2, (local, slots, STEP)), 0)
        + halves_of((1, (local, pairs, slots, 2 * slots)), 0)
        + [VMEM],
        out_specs=(planes,) + (pl.BlockSpec((half, STEP), lambda step: (0, step)),) * 2,
        scratch_shapes=[pltpu.VMEM((pairs, slots, LANES), jnp.float32), flat_scratch],
        compiler_params=PARAMS,
        name="spatial_back",
    )(embedded, embedded, weights, weights, returned)

    far_count = parts // PLANE
    assert parts == far_count * PLANE and parts & (parts - 1) == 0

    def to_partner(array, group_away, shard_away):
        if group_away == 0 and shard_away == 0:
            return array
        pairs_of_devices = [
            (g * parts + i, (g + group_away) % groups * parts + (i ^ shard_away))
            for g in range(groups)
            for i in range(parts)
        ]
        return lax.ppermute(array, ("group", "shard"), pairs_of_devices)

    def summed(kernel, shape, operands, scratch=()):
        return pl.pallas_call(
            kernel,
            out_shape=jax.ShapeDtypeStruct(shape, jnp.bfloat16),
            in_specs=[VMEM] * len(operands),
            out_specs=VMEM,
            scratch_shapes=list(scratch),
            compiler_params=PARAMS,
            name="sums",
        )(*operands)

    halved = summed(core_sum_kernel, (half, model), (own_half, to_partner(other_half, 0, 1)))
    total = summed(
        far_sum_kernel,
        (half, model),
        [to_partner(halved, 0, far * PLANE) for far in reversed(range(far_count))][::-1],
        [pltpu.VMEM((far_count, half, model), jnp.float32)],
    )
    crossed = [
        to_partner(total, away, side) for away in reversed(range(groups)) for side in (2, 0)
    ]
    totals = summed(cross_sum_kernel, (groups, half, model), crossed[::-1])
    table_rows = templates // groups
    table_grad = pl.pallas_call(
        functools.partial(table_kernel, groups),
        out_shape=jax.ShapeDtypeStruct((table_rows, model), jnp.float32),
        in_specs=[VMEM] * (groups + 2),
        out_specs=HBM,
        scratch_shapes=[
            pltpu.VMEM((groups, slots, model), jnp.bfloat16),
            pltpu.VMEM((PIECES, table_rows // PIECES, model), jnp.float32),
            pltpu.SemaphoreType.DMA((PIECES,)),
        ],
        compiler_params=PARAMS,
        name="table",
    )(*layouts, totals, to_partner(totals, 0, 1))
    return (input_grad[None], table_grad)


def solution(mesh):
    placed = (
        P("group", "shard", None, None),
        P("group", None, "shard", None),
        P(),
        P("group", None),
        P("group", None),
        P("group", None),
    )
    return jax.shard_map(
        body,
        mesh=mesh,
        in_specs=placed,
        out_specs=(P("group", "shard", None, None), P("group", None)),
        check_vma=False,
    )
```
